32 devices in a mesh: ctx: 8 (over y, x, core), fsdp: 4 (over z).
Axes of the slice: x: 2, y: 2, z: 4, core: 2. Of those that a mesh axis runs over, the one named last changes fastest.
Arguments:
- tokens: bfloat16 [4096, 2048], P(('ctx', 'fsdp')), may hold values from -6 to 6
- cotangent: bfloat16 [4096, 2048], P(('ctx', 'fsdp')), may hold values from -6 to 6
- gain_attn: float32 [2048], replicated, may hold values from 0.25 to 1.75
- gain_ffn: float32 [2048], replicated, may hold values from 0.25 to 1.75
- query_key_value_weight: bfloat16 [2048, 4096], P('fsdp'), may hold values from -0.125 to 0.125
- w_out: bfloat16 [2048, 2048], P('fsdp'), may hold values from -1 to 1
- w_gate: bfloat16 [2048, 8192], P('fsdp'), may hold values from -0.125 to 0.125
- w_up: bfloat16 [2048, 8192], P('fsdp'), may hold values from -0.125 to 0.125
- w_down: bfloat16 [8192, 2048], P('fsdp'), may hold values from -0.0625 to 0.0625
- pair_block: int32 [8], replicated, may hold values from 0 to 7, each once
Outputs:
- result: bfloat16 [4096, 2048], P(('ctx', 'fsdp'))
- grad_input: float32 [4096, 2048], P(('ctx', 'fsdp'))
- grad_gain_attn: float32 [2048], P(('ctx', 'fsdp'))
- grad_gain_ffn: float32 [2048], P(('ctx', 'fsdp'))
- grad_qkv: float32 [2048, 4096], P(('fsdp', 'ctx'))
- grad_out: float32 [2048, 2048], P(('fsdp', 'ctx'))
- grad_gate: float32 [2048, 8192], P(('fsdp', 'ctx'))
- grad_up: float32 [2048, 8192], P(('fsdp', 'ctx'))
- grad_down: float32 [8192, 2048], P(('fsdp', 'ctx'))
The draws below stay inside these ranges and needn't reach their ends.
Inputs may be any that keep to these rules, and one draw needn't show every extreme that they name: Ctx index c holds the blocks pair_block[c] and 15 - pair_block[c] of 64 tokens each of every sequence; every value appears once.
All inputs are finite; a program needn't handle non-finite values.
Results may differ from the reference program's by a relative error of at most 0.02.
Values may be sent and summed in bfloat16 or wider, within the bound.
A program may use at most 448 MiB of HBM per device.

```python
import math
from functools import partial
import jax
import jax.numpy as jnp
from jax import lax

MODEL_WIDTH = 2048
QUERY_HEADS = 16
KEY_VALUE_HEADS = 8
HEAD_SIZE = 128
FF = 8192
TOK_DEV = 128
SEQ_LEN = 1024
TOKEN_COUNT = 4096
N_CTX = 8
N_FSDP = 4


def shard_levels(own_key, dims, pieces, low, largest):
    factor_of = 1.0
    for dim, parts in pieces:
        steps = jax.random.uniform(jax.random.fold_in(jax.random.fold_in(own_key, 6), dim), (parts,), jnp.float32, low / len(pieces), largest / len(pieces))
        factor_of = factor_of * jnp.repeat(jnp.exp(steps), dims[dim] // parts).reshape((-1,) + (1,) * (len(dims) - 1 - dim))
    return factor_of


def centred(rng, dims, width, limit, cuts=(), kind=jnp.bfloat16):
    gain = shard_levels(rng, dims, cuts, -0.22, 0.18) if cuts else 1.0
    entries = jax.random.normal(rng, dims, jnp.float32) * width * gain
    return jnp.minimum(jnp.maximum(entries, -limit), limit).astype(kind)


def setup_inputs(seed: int = 0) -> dict:
    keys = jax.random.split(jax.random.key(seed), 11)
    return {
        "tokens": centred(keys[0], (TOKEN_COUNT, MODEL_WIDTH), 1.0, 6.0, ((0, 32),)),
        "cotangent": centred(keys[1], (TOKEN_COUNT, MODEL_WIDTH), 1.0, 6.0, ((0, 32),)),
        "gain_attn": jnp.clip(1.0 + 0.15 * jax.random.normal(keys[2], (MODEL_WIDTH,), jnp.float32), 0.25, 1.75),
        "gain_ffn": jnp.clip(1.0 + 0.15 * jax.random.normal(keys[3], (MODEL_WIDTH,), jnp.float32), 0.25, 1.75),
        "query_key_value_weight": centred(keys[4], (MODEL_WIDTH, (QUERY_HEADS + 2 * KEY_VALUE_HEADS) * HEAD_SIZE), MODEL_WIDTH ** -0.5, 0.125, ((0, 4),)),
        "w_out": centred(keys[5], (QUERY_HEADS * HEAD_SIZE, MODEL_WIDTH), (max(1, QUERY_HEADS * HEAD_SIZE * 16 // SEQ_LEN)) ** -0.5, 1.0, ((0, 4),)),
        "w_gate": centred(keys[6], (MODEL_WIDTH, FF), MODEL_WIDTH ** -0.5, 0.125, ((0, 4),)),
        "w_up": centred(keys[7], (MODEL_WIDTH, FF), MODEL_WIDTH ** -0.5, 0.125, ((0, 4),)),
        "w_down": centred(keys[8], (FF, MODEL_WIDTH), FF ** -0.5, 0.0625, ((0, 4),)),
        "pair_block": jax.random.permutation(keys[9], N_CTX).astype(jnp.int32),
    }


@jax.custom_vjp
def lower_block(v):
    return lax.optimization_barrier(v.astype(jnp.bfloat16)).astype(jnp.float32)

@jax.custom_vjp
def low_back(v):
    return v

def low_keep(v):
    return (lower_block(v), None)

def low_pass(kept, grad):
    return (grad,)

def back_keep(v):
    return (v, None)

def back_low(kept, grad):
    return (lower_block(grad),)
lower_block.defvjp(low_keep, low_pass)
low_back.defvjp(back_keep, back_low)
precise = lax.Precision.HIGHEST
norm_eps = 1e-05
rope_base = 1000000.0

def positions(pair_block):
    half_rows = TOK_DEV // 2
    row_index = jnp.arange(TOK_DEV, dtype=jnp.int32)
    first_block = pair_block.astype(jnp.int32)[:, None]
    which_block = jnp.where(row_index[None, :] < half_rows, first_block, 2 * N_CTX - 1 - first_block)
    pos_rows = which_block * half_rows + (row_index % half_rows)[None, :]
    pos_table = jnp.broadcast_to(pos_rows[:, None, :], (N_CTX, N_FSDP, TOK_DEV))
    seq_table = jnp.broadcast_to(jnp.arange(N_FSDP, dtype=jnp.int32)[None, :, None], (N_CTX, N_FSDP, TOK_DEV))
    return (pos_table.reshape(-1), seq_table.reshape(-1))

def rms_norm(vectors, gain_vec):
    return vectors * lax.rsqrt(lax.optimization_barrier(jnp.mean(vectors * vectors, axis=-1, keepdims=True)) + norm_eps) * gain_vec

def apply_rotation(vectors, where_pos):
    half_dim = vectors.shape[-1] // 2
    frequency = jnp.exp(jnp.arange(half_dim, dtype=jnp.float32) * (-2.0 * math.log(rope_base) / vectors.shape[-1]))
    angles = where_pos.astype(jnp.float32)[:, None] * frequency[None, :]
    cosine = jnp.cos(angles)[:, None, :]
    sine_val = jnp.sin(angles)[:, None, :]
    first_half = vectors[..., :half_dim]
    second_half = vectors[..., half_dim:]
    return jnp.concatenate([first_half * cosine - second_half * sine_val, second_half * cosine + first_half * sine_val], axis=-1)

def layer(token_position, token_seq, input_rows, gain_attn, gain_ffn, query_key_value_weight, w_out, w_gate, w_up, w_down):
    block_of_rows = min(1024, TOKEN_COUNT)
    query_block = min(256, TOKEN_COUNT)
    group_count = QUERY_HEADS // KEY_VALUE_HEADS
    score_scale = 1.0 / math.sqrt(HEAD_SIZE)

    def apply_projection(rows_in):
        normed = lower_block(rms_norm(rows_in, gain_attn))
        return low_back(jnp.dot(normed, query_key_value_weight, precision=precise))
    projected_rows = lax.map(jax.checkpoint(apply_projection), input_rows.reshape(-1, block_of_rows, MODEL_WIDTH)).reshape(TOKEN_COUNT, (QUERY_HEADS + 2 * KEY_VALUE_HEADS) * HEAD_SIZE)
    queries = lower_block(apply_rotation(projected_rows[:, :QUERY_HEADS * HEAD_SIZE].reshape(TOKEN_COUNT, QUERY_HEADS, HEAD_SIZE), token_position))
    key_rows = lower_block(apply_rotation(projected_rows[:, QUERY_HEADS * HEAD_SIZE:(QUERY_HEADS + KEY_VALUE_HEADS) * HEAD_SIZE].reshape(TOKEN_COUNT, KEY_VALUE_HEADS, HEAD_SIZE), token_position))
    value_rows = lower_block(projected_rows[:, (QUERY_HEADS + KEY_VALUE_HEADS) * HEAD_SIZE:].reshape(TOKEN_COUNT, KEY_VALUE_HEADS, HEAD_SIZE))

    def attend(block_in):
        query_portion, pos_part, seq_part = block_in
        grouped_rows = query_portion.reshape(-1, KEY_VALUE_HEADS, group_count, HEAD_SIZE)
        scores = low_back(jnp.einsum('qhgd,khd->hgqk', grouped_rows, key_rows, precision=precise) * score_scale)
        allowed = (token_position[None, :] <= pos_part[:, None]) & (token_seq[None, :] == seq_part[:, None])
        scores = jnp.where(allowed[None, None], scores, -1e+30)
        shifted = jnp.exp(scores - lax.optimization_barrier(jnp.max(scores, axis=-1, keepdims=True)))
        probs_low = lower_block(shifted / lax.optimization_barrier(jnp.sum(shifted, axis=-1, keepdims=True)))
        mixed = jnp.einsum('hgqk,khd->qhgd', probs_low, value_rows, precision=precise)
        return mixed.reshape(-1, QUERY_HEADS * HEAD_SIZE)
    attended = lax.map(jax.checkpoint(attend), (queries.reshape(-1, query_block, QUERY_HEADS, HEAD_SIZE), token_position.reshape(-1, query_block), token_seq.reshape(-1, query_block)))
    attended = lower_block(low_back(attended.reshape(TOKEN_COUNT, QUERY_HEADS * HEAD_SIZE)))

    def finish(block_in):
        rows_in, attended_part = block_in
        middle = rows_in + low_back(jnp.dot(attended_part, w_out, precision=precise))
        normed = lower_block(rms_norm(middle, gain_ffn))
        gate_val = low_back(jnp.dot(normed, w_gate, precision=precise))
        up_val = low_back(jnp.dot(normed, w_up, precision=precise))
        hidden = lower_block(jax.nn.silu(gate_val) * up_val)
        return middle + low_back(jnp.dot(hidden, w_down, precision=precise))
    output = lax.map(jax.checkpoint(finish), (input_rows.reshape(-1, block_of_rows, MODEL_WIDTH), attended.reshape(-1, block_of_rows, QUERY_HEADS * HEAD_SIZE)))
    return output.reshape(TOKEN_COUNT, MODEL_WIDTH)

def reference(tokens, cotangent, gain_attn, gain_ffn, query_key_value_weight, w_out, w_gate, w_up, w_down, pair_block):
    token_position, token_seq = positions(pair_block)
    result, pull_back = jax.vjp(partial(layer, token_position, token_seq), tokens.astype(jnp.float32), gain_attn.astype(jnp.float32), gain_ffn.astype(jnp.float32), query_key_value_weight.astype(jnp.float32), w_out.astype(jnp.float32), w_gate.astype(jnp.float32), w_up.astype(jnp.float32), w_down.astype(jnp.float32))
    grads = pull_back(cotangent.astype(jnp.float32))
    return (result.astype(jnp.bfloat16), grads[0], grads[1], grads[2], grads[3], grads[4], grads[5], grads[6], grads[7])
```

```python
import math

import jax
import jax.numpy as jnp
from jax import lax
from jax.sharding import PartitionSpec as P

QUERY_HEADS = 16
KEY_VALUE_HEADS = 8
HEAD_SIZE = 128


norm_eps = 1e-05
rope_base = 1000000.0


def rms_norm(vectors, gain_vec):
    return (
        vectors
        * lax.rsqrt(jnp.mean(vectors * vectors, axis=-1, keepdims=True) + norm_eps)
        * gain_vec
    )


def apply_rotation(vectors, where_pos):
    half_dim = vectors.shape[-1] // 2
    frequency = jnp.exp(
        jnp.arange(half_dim, dtype=jnp.float32) * (-2.0 * math.log(rope_base) / vectors.shape[-1])
    )
    angles = where_pos.astype(jnp.float32)[:, None] * frequency[None, :]
    cosine = jnp.cos(angles)[:, None, :]
    sine_val = jnp.sin(angles)[:, None, :]
    first_half = vectors[..., :half_dim]
    second_half = vectors[..., half_dim:]
    return jnp.concatenate(
        [
            first_half * cosine - second_half * sine_val,
            second_half * cosine + first_half * sine_val,
        ],
        axis=-1,
    )


def positions(pair_block, token_rows):
    n_ctx = lax.axis_size("ctx")
    half_rows = token_rows // 2
    row_index = jnp.arange(token_rows, dtype=jnp.int32)
    first_block = pair_block[:, None]
    which_block = jnp.where(
        row_index[None, :] < half_rows, first_block, 2 * n_ctx - 1 - first_block
    )
    pos_table = which_block * half_rows + (row_index % half_rows)[None, :]
    own_pos = lax.dynamic_slice(pos_table, (lax.axis_index("ctx"), 0), (1, token_rows)).reshape(
        token_rows
    )
    return (pos_table.reshape(-1), own_pos)


def to_groups(input_array, group_count):
    token_rows = input_array.shape[0]
    head_length = input_array.shape[-1] // (group_count * KEY_VALUE_HEADS)
    return (
        input_array.reshape(token_rows, KEY_VALUE_HEADS, group_count, head_length)
        .transpose(1, 2, 0, 3)
        .reshape(KEY_VALUE_HEADS, group_count * token_rows, head_length)
    )


def from_groups(input_array, group_count):
    head_length = input_array.shape[-1]
    token_rows = input_array.shape[1] // group_count
    return (
        input_array.reshape(KEY_VALUE_HEADS, group_count, token_rows, head_length)
        .transpose(2, 0, 1, 3)
        .reshape(token_rows, KEY_VALUE_HEADS * group_count * head_length)
    )


def split_keys(every_key, every_value, key_pos):
    total_keys = every_key.shape[0]
    block_length = min(1024, total_keys)
    block_count = total_keys // block_length
    return (
        every_key.reshape(block_count, block_length, KEY_VALUE_HEADS, HEAD_SIZE),
        every_value.reshape(block_count, block_length, KEY_VALUE_HEADS, HEAD_SIZE),
        key_pos.reshape(block_count, block_length),
    )


def contract_last(left, right):
    return lax.dot_general(
        left, right, (((1,), (1,)), ((), ())), preferred_element_type=jnp.float32
    )


def contract_first(left, right):
    return lax.dot_general(
        left, right, (((0,), (0,)), ((), ())), preferred_element_type=jnp.float32
    )


def local_general(
    tokens,
    cotangent,
    gain_attn,
    gain_ffn,
    query_key_value_weight,
    w_out,
    w_gate,
    w_up,
    w_down,
    pair_block,
):
    token_rows = tokens.shape[0]
    query_columns = QUERY_HEADS * HEAD_SIZE
    key_value_columns = KEY_VALUE_HEADS * HEAD_SIZE
    group_count = QUERY_HEADS // KEY_VALUE_HEADS
    score_scale = 1.0 / math.sqrt(HEAD_SIZE)
    ff_cols = w_gate.shape[1]
    key_pos, own_pos = positions(pair_block, token_rows)
    query_pos = jnp.tile(own_pos, group_count)
    inputs_f = tokens.astype(jnp.float32)
    qkv_full, out_full = (
        lax.all_gather(query_key_value_weight, "fsdp", axis=0, tiled=True),
        lax.all_gather(w_out, "fsdp", axis=0, tiled=True),
    )
    normed_one_b = rms_norm(inputs_f, gain_attn).astype(jnp.bfloat16)
    projected_rows = jnp.dot(normed_one_b, qkv_full, preferred_element_type=jnp.float32)
    query_raw = projected_rows[:, :query_columns].reshape(token_rows, QUERY_HEADS, HEAD_SIZE)
    unrotated_key = projected_rows[:, query_columns : query_columns + key_value_columns].reshape(
        token_rows, KEY_VALUE_HEADS, HEAD_SIZE
    )
    query_b = (
        apply_rotation(query_raw, own_pos).astype(jnp.bfloat16).reshape(token_rows, query_columns)
    )
    keys_b = (
        apply_rotation(unrotated_key, own_pos)
        .astype(jnp.bfloat16)
        .reshape(token_rows, key_value_columns)
    )
    values_b = projected_rows[:, query_columns + key_value_columns :].astype(jnp.bfloat16)
    every_key, every_value = (
        lax.all_gather(keys_b, "ctx", axis=0, tiled=True),
        lax.all_gather(values_b, "ctx", axis=0, tiled=True),
    )
    query_grp = to_groups(query_b, group_count)
    key_blocks, value_blocks, pos_blocks = split_keys(every_key, every_value, key_pos)

    def forward_step(carry, block_in):
        run_max, run_total, weighted = carry
        key_block, value_block, block_pos = block_in
        causal = block_pos[None, None, :] <= query_pos[None, :, None]
        scores = (
            jnp.einsum("hqd,khd->hqk", query_grp, key_block, preferred_element_type=jnp.float32)
            * score_scale
        )
        scores = jnp.where(causal, scores, -1e30)
        new_max = jnp.maximum(run_max, jnp.max(scores, axis=-1))
        exp_scores = jnp.where(causal, jnp.exp(scores - new_max[..., None]), 0.0)
        fading = jnp.exp(run_max - new_max)
        run_total = run_total * fading + jnp.sum(exp_scores, axis=-1)
        weighted = weighted * fading[..., None] + jnp.einsum(
            "hqk,khd->hqd",
            exp_scores.astype(jnp.bfloat16),
            value_block,
            preferred_element_type=jnp.float32,
        )
        return ((new_max, run_total, weighted), None)

    initial_maximum = jnp.full((KEY_VALUE_HEADS, group_count * token_rows), -1e30, jnp.float32)
    initial_total = jnp.zeros((KEY_VALUE_HEADS, group_count * token_rows), jnp.float32)
    initial_weighted = jnp.zeros(
        (KEY_VALUE_HEADS, group_count * token_rows, HEAD_SIZE), jnp.float32
    )
    final_carry, ignored = lax.scan(
        forward_step,
        (initial_maximum, initial_total, initial_weighted),
        (key_blocks, value_blocks, pos_blocks),
    )
    run_max, run_total, weighted = final_carry
    log_total = run_max + jnp.log(run_total)
    attn_grp = weighted / run_total[..., None]
    attended_b = from_groups(attn_grp.astype(jnp.bfloat16), group_count)
    mid_rows = inputs_f + jnp.dot(attended_b, out_full, preferred_element_type=jnp.float32)
    gate_full, up_full, down_full = (
        lax.all_gather(w_gate, "fsdp", axis=0, tiled=True),
        lax.all_gather(w_up, "fsdp", axis=0, tiled=True),
        lax.all_gather(w_down, "fsdp", axis=0, tiled=True),
    )
    normed_two_b = rms_norm(mid_rows, gain_ffn).astype(jnp.bfloat16)
    gate_val = jnp.dot(normed_two_b, gate_full, preferred_element_type=jnp.float32)
    up_val = jnp.dot(normed_two_b, up_full, preferred_element_type=jnp.float32)
    hidden_b = (jax.nn.silu(gate_val) * up_val).astype(jnp.bfloat16)
    output_f = mid_rows + jnp.dot(hidden_b, down_full, preferred_element_type=jnp.float32)
    result = output_f.astype(jnp.bfloat16)
    normed_one_x, attended_x, normed_two_x, hidden_x = (
        lax.all_to_all(normed_one_b, "fsdp", split_axis=1, concat_axis=0, tiled=True),
        lax.all_to_all(attended_b, "fsdp", split_axis=1, concat_axis=0, tiled=True),
        lax.all_to_all(normed_two_b, "fsdp", split_axis=1, concat_axis=0, tiled=True),
        lax.all_to_all(hidden_b, "fsdp", split_axis=1, concat_axis=0, tiled=True),
    )
    grad_out_f = cotangent.astype(jnp.float32)
    gate_back, up_back, down_back = (
        lax.all_gather(w_gate, "fsdp", axis=0, tiled=True),
        lax.all_gather(w_up, "fsdp", axis=0, tiled=True),
        lax.all_gather(w_down, "fsdp", axis=0, tiled=True),
    )
    grad_hidden = contract_last(cotangent, down_back)
    ignored, ffn_back = jax.vjp(
        lambda gate_in, up_in: jax.nn.silu(gate_in) * up_in, gate_val, up_val
    )
    grad_gate_f, grad_up_f = ffn_back(grad_hidden)
    grad_gate_b = grad_gate_f.astype(jnp.bfloat16)
    grad_up_b = grad_up_f.astype(jnp.bfloat16)
    grad_normed_two = contract_last(grad_gate_b, gate_back) + contract_last(grad_up_b, up_back)
    ignored, norm_two_back = jax.vjp(rms_norm, mid_rows, gain_ffn)
    grad_mid_part, gain_ffn_part = norm_two_back(grad_normed_two)
    grad_mid = grad_out_f + grad_mid_part
    gate_up_b = jnp.concatenate([grad_gate_b, grad_up_b], axis=1)
    qkv_back, out_back = (
        lax.all_gather(query_key_value_weight, "fsdp", axis=0, tiled=True),
        lax.all_gather(w_out, "fsdp", axis=0, tiled=True),
    )
    grad_proj_b = grad_mid.astype(jnp.bfloat16)
    grad_att_b = contract_last(grad_proj_b, out_back).astype(jnp.bfloat16)
    grad_att_grp = to_groups(grad_att_b, group_count)
    delta_rows = jnp.sum(grad_att_grp.astype(jnp.float32) * attn_grp, axis=-1)

    def backward_step(grad_query, block_in):
        key_block, value_block, block_pos = block_in
        causal = block_pos[None, None, :] <= query_pos[None, :, None]
        scores = (
            jnp.einsum("hqd,khd->hqk", query_grp, key_block, preferred_element_type=jnp.float32)
            * score_scale
        )
        probs = jnp.where(causal, jnp.exp(scores - log_total[..., None]), 0.0)
        grad_values = jnp.einsum(
            "hqk,hqd->khd",
            probs.astype(jnp.bfloat16),
            grad_att_grp,
            preferred_element_type=jnp.float32,
        )
        grad_probs = jnp.einsum(
            "hqd,khd->hqk", grad_att_grp, value_block, preferred_element_type=jnp.float32
        )
        grad_scores = (probs * (grad_probs - delta_rows[..., None])).astype(jnp.bfloat16)
        grad_query = grad_query + score_scale * jnp.einsum(
            "hqk,khd->hqd", grad_scores, key_block, preferred_element_type=jnp.float32
        )
        grad_keys = score_scale * jnp.einsum(
            "hqk,hqd->khd", grad_scores, query_grp, preferred_element_type=jnp.float32
        )
        return (grad_query, (grad_keys, grad_values))

    grad_query_grp, key_grads = lax.scan(
        backward_step,
        jnp.zeros((KEY_VALUE_HEADS, group_count * token_rows, HEAD_SIZE), jnp.float32),
        (key_blocks, value_blocks, pos_blocks),
    )
    total_keys = key_pos.shape[0]
    grad_keys_all = key_grads[0].reshape(total_keys, key_value_columns)
    grad_values_all = key_grads[1].reshape(total_keys, key_value_columns)
    key_sums, summed_values = (
        lax.psum_scatter(
            grad_keys_all.astype(jnp.bfloat16), "ctx", scatter_dimension=0, tiled=True
        ).astype(jnp.float32),
        lax.psum_scatter(
            grad_values_all.astype(jnp.bfloat16), "ctx", scatter_dimension=0, tiled=True
        ).astype(jnp.float32),
    )
    grad_query_rows = from_groups(grad_query_grp, group_count).reshape(
        token_rows, QUERY_HEADS, HEAD_SIZE
    )
    ignored, query_rope_back = jax.vjp(lambda vectors: apply_rotation(vectors, own_pos), query_raw)
    ignored, key_rotation_backward = jax.vjp(
        lambda vectors: apply_rotation(vectors, own_pos), unrotated_key
    )
    grad_query_raw = query_rope_back(grad_query_rows)[0]
    unrotated_key_gradient = key_rotation_backward(
        key_sums.reshape(token_rows, KEY_VALUE_HEADS, HEAD_SIZE)
    )[0]
    grad_projected_b = jnp.concatenate(
        [
            grad_query_raw.reshape(token_rows, query_columns),
            unrotated_key_gradient.reshape(token_rows, key_value_columns),
            summed_values,
        ],
        axis=1,
    ).astype(jnp.bfloat16)
    grad_normed_one = contract_last(grad_projected_b, qkv_back)
    ignored, norm_one_back = jax.vjp(rms_norm, inputs_f, gain_attn)
    grad_in_part, gain_attn_part = norm_one_back(grad_normed_one)
    grad_input = grad_mid + grad_in_part
    cot_group, gate_up_group, projected_group, proj_group = (
        lax.all_gather(cotangent, "fsdp", axis=0, tiled=True),
        lax.all_gather(gate_up_b, "fsdp", axis=0, tiled=True),
        lax.all_gather(grad_projected_b, "fsdp", axis=0, tiled=True),
        lax.all_gather(grad_proj_b, "fsdp", axis=0, tiled=True),
    )
    qkv_part = contract_first(normed_one_x, projected_group)
    out_part = contract_first(attended_x, proj_group)
    gate_up_part = contract_first(normed_two_x, gate_up_group)
    gate_part = gate_up_part[:, :ff_cols]
    up_part = gate_up_part[:, ff_cols:]
    down_part = contract_first(hidden_x, cot_group)
    grad_qkv, grad_out, grad_down = (
        lax.psum_scatter(
            qkv_part.astype(jnp.bfloat16), "ctx", scatter_dimension=0, tiled=True
        ).astype(jnp.float32),
        lax.psum_scatter(
            out_part.astype(jnp.bfloat16), "ctx", scatter_dimension=0, tiled=True
        ).astype(jnp.float32),
        lax.psum_scatter(
            down_part.astype(jnp.bfloat16), "ctx", scatter_dimension=0, tiled=True
        ).astype(jnp.float32),
    )
    grad_gate, grad_up = (
        lax.psum_scatter(
            gate_part.astype(jnp.bfloat16), "ctx", scatter_dimension=0, tiled=True
        ).astype(jnp.float32),
        lax.psum_scatter(
            up_part.astype(jnp.bfloat16), "ctx", scatter_dimension=0, tiled=True
        ).astype(jnp.float32),
    )
    grad_gain_attn, grad_gain_ffn = (
        lax.psum_scatter(gain_attn_part, ("ctx", "fsdp"), scatter_dimension=0, tiled=True),
        lax.psum_scatter(gain_ffn_part, ("ctx", "fsdp"), scatter_dimension=0, tiled=True),
    )
    return (
        result,
        grad_input,
        grad_gain_attn,
        grad_gain_ffn,
        grad_qkv,
        grad_out,
        grad_gate,
        grad_up,
        grad_down,
    )


def rotate_heads(vectors, cosine, sine_val, sign):
    half_dim = HEAD_SIZE // 2
    first_half = vectors[..., :half_dim]
    second_half = vectors[..., half_dim:]
    return jnp.concatenate(
        [
            first_half * cosine - sign * second_half * sine_val,
            second_half * cosine + sign * first_half * sine_val,
        ],
        axis=-1,
    )


def local_heads(
    tokens,
    cotangent,
    gain_attn,
    gain_ffn,
    query_key_value_weight,
    w_out,
    w_gate,
    w_up,
    w_down,
    pair_block,
):
    f32, bf16 = jnp.float32, jnp.bfloat16
    n_ctx, n_fsdp = lax.axis_size("ctx"), lax.axis_size("fsdp")
    ctx, fsdp = lax.axis_index("ctx"), lax.axis_index("fsdp")
    token_rows, width = tokens.shape
    group_count = QUERY_HEADS // KEY_VALUE_HEADS
    head_columns = group_count * HEAD_SIZE
    query_columns = QUERY_HEADS * HEAD_SIZE
    key_columns = KEY_VALUE_HEADS * HEAD_SIZE
    score_scale = 1.0 / math.sqrt(HEAD_SIZE)
    depth = query_key_value_weight.shape[0]
    hidden_cols = w_down.shape[0]
    share = depth // head_columns
    head = lax.rem(ctx + share * fsdp, n_ctx)
    plane_of = lambda c, f: ((c + share * f) % n_ctx) // share

    key_pos, own_pos = positions(pair_block, token_rows)

    def head_columns_of(matrix, h):
        return jnp.concatenate(
            [
                lax.dynamic_slice_in_dim(matrix, h * head_columns, head_columns, 1),
                lax.dynamic_slice_in_dim(matrix, query_columns + h * HEAD_SIZE, HEAD_SIZE, 1),
                lax.dynamic_slice_in_dim(
                    matrix, query_columns + key_columns + h * HEAD_SIZE, HEAD_SIZE, 1
                ),
            ],
            axis=1,
        )

    sends = jnp.stack(
        [
            head_columns_of(query_key_value_weight, lax.rem(ctx + share * f, n_ctx))
            for f in range(n_fsdp)
        ]
    )
    w_head = lax.all_to_all(sends, "fsdp", split_axis=0, concat_axis=0, tiled=True).reshape(
        width, head_columns + 2 * HEAD_SIZE
    )
    out_block = lax.dynamic_slice_in_dim(
        w_out, lax.rem(ctx, share) * head_columns, head_columns, 0
    )
    out_pairs = [
        (c * n_fsdp + plane_of(c, f), c * n_fsdp + f) for c in range(n_ctx) for f in range(n_fsdp)
    ]
    out_head = lax.ppermute(out_block, ("ctx", "fsdp"), out_pairs)

    def hidden_columns(matrix):
        mine = lax.dynamic_index_in_dim(
            matrix.reshape(depth, n_fsdp, n_ctx, hidden_cols // n_ctx), ctx, 2, keepdims=False
        )
        turned = lax.all_to_all(
            mine.transpose(1, 0, 2), "fsdp", split_axis=0, concat_axis=0, tiled=True
        ).reshape(width, hidden_cols // n_ctx)
        return lax.all_gather(turned, "ctx", axis=1, tiled=True)

    gate_w = hidden_columns(w_gate)
    up_w = hidden_columns(w_up)
    cot_group = lax.all_gather(cotangent, "fsdp", axis=0, tiled=True)

    inputs_f = tokens.astype(f32)
    normed_one_b = rms_norm(inputs_f, gain_attn).astype(bf16)
    normed_one_seq = lax.all_gather(normed_one_b, "ctx", axis=0, tiled=True)
    projected = jnp.dot(normed_one_seq, w_head, preferred_element_type=f32)
    frequency = jnp.exp(
        jnp.arange(HEAD_SIZE // 2, dtype=f32) * (-2.0 * math.log(rope_base) / HEAD_SIZE)
    )
    angles = key_pos.astype(f32)[:, None] * frequency[None, :]
    cosine, sine_val = jnp.cos(angles), jnp.sin(angles)
    heads = [
        rotate_heads(projected[:, i * HEAD_SIZE : (i + 1) * HEAD_SIZE], cosine, sine_val, 1.0)
        for i in range(group_count + 1)
    ]
    queries = jnp.stack(heads[:group_count]).astype(bf16)
    keys = heads[group_count].astype(bf16)
    values = projected[:, head_columns + HEAD_SIZE :].astype(bf16)
    causal = key_pos[None, :] <= key_pos[:, None]
    scores = jnp.einsum("gqd,kd->gqk", queries, keys, preferred_element_type=f32) * score_scale
    scores = jnp.where(causal, scores, -1e30)
    shifted = jnp.exp(scores - jnp.max(scores, axis=-1, keepdims=True))
    probs = shifted / jnp.sum(shifted, axis=-1, keepdims=True)
    probs_low = probs.astype(bf16)
    attended = jnp.einsum("gqk,kd->qgd", probs_low, values, preferred_element_type=f32)
    attended_b = attended.astype(bf16).reshape(-1, head_columns)
    out_part = jnp.dot(attended_b, out_head, preferred_element_type=f32)
    mid = inputs_f + lax.psum_scatter(
        out_part.astype(bf16), "ctx", scatter_dimension=0, tiled=True
    ).astype(f32)

    mid_scale = lax.rsqrt(jnp.mean(mid * mid, axis=-1, keepdims=True) + norm_eps)
    normed_two_b = (mid * mid_scale * gain_ffn).astype(bf16)
    normed_two_group = lax.all_gather(normed_two_b, "fsdp", axis=0, tiled=True)
    gate = jnp.dot(normed_two_group, gate_w, preferred_element_type=f32)
    up = jnp.dot(normed_two_group, up_w, preferred_element_type=f32)
    sig = jax.nn.sigmoid(gate)
    silu = gate * sig
    hidden_b = (silu * up).astype(bf16)
    down_part = jnp.dot(hidden_b, w_down, preferred_element_type=f32)
    grad_hidden = contract_last(cot_group, w_down)
    grad_gate_b = (grad_hidden * up * sig * (1.0 + gate * (1.0 - sig))).astype(bf16)
    grad_up_b = (grad_hidden * silu).astype(bf16)
    normed_part = contract_last(grad_gate_b, gate_w) + contract_last(grad_up_b, up_w)
    result = (
        mid
        + lax.psum_scatter(
            down_part.astype(bf16), "fsdp", scatter_dimension=0, tiled=True
        ).astype(f32)
    ).astype(bf16)
    grad_normed_two = lax.psum_scatter(
        normed_part.astype(bf16), "fsdp", scatter_dimension=0, tiled=True
    ).astype(f32)
    u = grad_normed_two * gain_ffn
    grad_mid = (
        cotangent.astype(f32)
        + mid_scale * u
        - mid * mid_scale**3 * jnp.mean(u * mid, axis=-1, keepdims=True)
    )

    grad_down_part = contract_first(hidden_b, cot_group)
    grad_gate_part = contract_first(normed_two_group, grad_gate_b)
    grad_up_part = contract_first(normed_two_group, grad_up_b)
    grad_down = lax.psum_scatter(
        grad_down_part.astype(bf16), "ctx", scatter_dimension=0, tiled=True
    ).astype(f32)

    def spread(part):
        blocks = part.astype(bf16).reshape(n_fsdp, n_ctx, depth // n_ctx, hidden_cols)
        blocks = blocks.transpose(1, 0, 2, 3).reshape(width, hidden_cols)
        mine = lax.psum_scatter(blocks, "ctx", scatter_dimension=0, tiled=True)
        mine = mine.reshape(n_fsdp, depth // n_ctx, hidden_cols)
        return lax.all_to_all(mine, "fsdp", split_axis=0, concat_axis=2, tiled=True).reshape(
            depth // n_ctx, n_fsdp * hidden_cols
        )

    grad_gate, grad_up = spread(grad_gate_part).astype(f32), spread(grad_up_part).astype(f32)

    grad_proj_b = grad_mid.astype(bf16)
    grad_proj_seq = lax.all_gather(grad_proj_b, "ctx", axis=0, tiled=True)
    grad_att = contract_last(grad_proj_seq, out_head).astype(bf16)
    grad_att = grad_att.reshape(-1, group_count, HEAD_SIZE).transpose(1, 0, 2)
    grad_out_part = contract_first(attended_b, grad_proj_seq)
    grad_values = jnp.einsum("gqk,gqd->kd", probs_low, grad_att, preferred_element_type=f32)
    grad_probs = jnp.einsum("gqd,kd->gqk", grad_att, values, preferred_element_type=f32)
    delta = jnp.sum(grad_probs * probs, axis=-1, keepdims=True)
    grad_scores = (probs * (grad_probs - delta)).astype(bf16)
    grad_queries = score_scale * jnp.einsum(
        "gqk,kd->gqd", grad_scores, keys, preferred_element_type=f32
    )
    grad_keys = score_scale * jnp.einsum(
        "gqk,gqd->kd", grad_scores, queries, preferred_element_type=f32
    )
    grad_projected = jnp.concatenate(
        [rotate_heads(grad_queries[g], cosine, sine_val, -1.0) for g in range(group_count)]
        + [rotate_heads(grad_keys, cosine, sine_val, -1.0), grad_values],
        axis=1,
    ).astype(bf16)
    normed_one_part = contract_last(grad_projected, w_head)
    grad_normed_one = lax.psum_scatter(
        normed_one_part.astype(bf16), "ctx", scatter_dimension=0, tiled=True
    ).astype(f32)
    in_scale = lax.rsqrt(jnp.mean(inputs_f * inputs_f, axis=-1, keepdims=True) + norm_eps)
    u = grad_normed_one * gain_attn
    grad_input = (
        grad_mid
        + in_scale * u
        - inputs_f * in_scale**3 * jnp.mean(u * inputs_f, axis=-1, keepdims=True)
    )

    grad_head_part = contract_first(normed_one_seq, grad_projected).astype(bf16)
    blocks = grad_head_part.reshape(n_fsdp, n_ctx, depth // n_ctx, -1).transpose(1, 0, 2, 3)
    blocks = blocks.reshape(n_ctx * n_fsdp, depth // n_ctx, -1)
    got = lax.all_to_all(blocks, ("ctx", "fsdp"), split_axis=0, concat_axis=0, tiled=True)
    got = got.astype(f32)
    sums = [
        sum(got[((h - share * f) % n_ctx) * n_fsdp + f] for f in range(n_fsdp))
        for h in range(KEY_VALUE_HEADS)
    ]
    grad_qkv = jnp.concatenate(
        [s[:, :head_columns] for s in sums]
        + [s[:, head_columns : head_columns + HEAD_SIZE] for s in sums]
        + [s[:, head_columns + HEAD_SIZE :] for s in sums],
        axis=1,
    )
    back_pairs = [(b, a) for a, b in out_pairs]
    out_got = lax.ppermute(grad_out_part.astype(bf16), ("ctx", "fsdp"), back_pairs)
    padded = lax.dynamic_update_slice_in_dim(
        jnp.zeros((depth, width), bf16), out_got, lax.rem(ctx, share) * head_columns, 0
    )
    grad_out = lax.psum_scatter(padded, "ctx", scatter_dimension=0, tiled=True).astype(f32)

    my_rows = ctx * (depth // n_ctx)
    rows_of = lambda matrix: lax.dynamic_slice_in_dim(
        matrix, my_rows, depth // n_ctx, 0
    ).astype(f32)
    attn_sum = jnp.sum(rows_of(query_key_value_weight) * grad_qkv, axis=1)
    ffn_sum = jnp.sum(rows_of(w_gate) * grad_gate, axis=1) + jnp.sum(
        rows_of(w_up) * grad_up, axis=1
    )
    gain_pairs = [
        (c * n_fsdp + f, f * n_ctx + c) for c in range(n_ctx) for f in range(n_fsdp)
    ]
    moved = lax.ppermute(jnp.stack([attn_sum, ffn_sum]), ("ctx", "fsdp"), gain_pairs)
    my_gain = (ctx * n_fsdp + fsdp) * (depth // n_ctx)
    grad_gain_attn = moved[0] / lax.dynamic_slice_in_dim(gain_attn, my_gain, depth // n_ctx)
    grad_gain_ffn = moved[1] / lax.dynamic_slice_in_dim(gain_ffn, my_gain, depth // n_ctx)
    return (
        result,
        grad_input,
        grad_gain_attn,
        grad_gain_ffn,
        grad_qkv,
        grad_out,
        grad_gate,
        grad_up,
        grad_down,
    )


def solution(mesh):
    local = local_heads if mesh.shape["ctx"] == KEY_VALUE_HEADS else local_general
    return jax.shard_map(
        local,
        mesh=mesh,
        in_specs=(
            P(("ctx", "fsdp"), None),
            P(("ctx", "fsdp"), None),
            P(),
            P(),
            P("fsdp", None),
            P("fsdp", None),
            P("fsdp", None),
            P("fsdp", None),
            P("fsdp", None),
            P(),
        ),
        out_specs=(
            P(("ctx", "fsdp"), None),
            P(("ctx", "fsdp"), None),
            P(("ctx", "fsdp")),
            P(("ctx", "fsdp")),
            P(("fsdp", "ctx"), None),
            P(("fsdp", "ctx"), None),
            P(("fsdp", "ctx"), None),
            P(("fsdp", "ctx"), None),
            P(("fsdp", "ctx"), None),
        ),
        check_vma=False,
    )
```

```python
import math

import jax
import jax.numpy as jnp
from jax import lax
from jax.experimental import pallas as pl
from jax.experimental.pallas import tpu as pltpu
from jax.sharding import PartitionSpec as P

QUERY_HEADS = 16
KEY_VALUE_HEADS = 8
HEAD_SIZE = 128


norm_eps = 1e-05
rope_base = 1000000.0


def rms_norm(vectors, gain_vec):
    return (
        vectors
        * lax.rsqrt(jnp.mean(vectors * vectors, axis=-1, keepdims=True) + norm_eps)
        * gain_vec
    )


def apply_rotation(vectors, where_pos):
    half_dim = vectors.shape[-1] // 2
    frequency = jnp.exp(
        jnp.arange(half_dim, dtype=jnp.float32) * (-2.0 * math.log(rope_base) / vectors.shape[-1])
    )
    angles = where_pos.astype(jnp.float32)[:, None] * frequency[None, :]
    cosine = jnp.cos(angles)[:, None, :]
    sine_val = jnp.sin(angles)[:, None, :]
    first_half = vectors[..., :half_dim]
    second_half = vectors[..., half_dim:]
    return jnp.concatenate(
        [
            first_half * cosine - second_half * sine_val,
            second_half * cosine + first_half * sine_val,
        ],
        axis=-1,
    )


def positions(pair_block, token_rows):
    n_ctx = lax.axis_size("ctx")
    half_rows = token_rows // 2
    row_index = jnp.arange(token_rows, dtype=jnp.int32)
    first_block = pair_block[:, None]
    which_block = jnp.where(
        row_index[None, :] < half_rows, first_block, 2 * n_ctx - 1 - first_block
    )
    pos_table = which_block * half_rows + (row_index % half_rows)[None, :]
    own_pos = lax.dynamic_slice(pos_table, (lax.axis_index("ctx"), 0), (1, token_rows)).reshape(
        token_rows
    )
    return (pos_table.reshape(-1), own_pos)


def to_groups(input_array, group_count):
    token_rows = input_array.shape[0]
    head_length = input_array.shape[-1] // (group_count * KEY_VALUE_HEADS)
    return (
        input_array.reshape(token_rows, KEY_VALUE_HEADS, group_count, head_length)
        .transpose(1, 2, 0, 3)
        .reshape(KEY_VALUE_HEADS, group_count * token_rows, head_length)
    )


def from_groups(input_array, group_count):
    head_length = input_array.shape[-1]
    token_rows = input_array.shape[1] // group_count
    return (
        input_array.reshape(KEY_VALUE_HEADS, group_count, token_rows, head_length)
        .transpose(2, 0, 1, 3)
        .reshape(token_rows, KEY_VALUE_HEADS * group_count * head_length)
    )


def split_keys(every_key, every_value, key_pos):
    total_keys = every_key.shape[0]
    block_length = min(1024, total_keys)
    block_count = total_keys // block_length
    return (
        every_key.reshape(block_count, block_length, KEY_VALUE_HEADS, HEAD_SIZE),
        every_value.reshape(block_count, block_length, KEY_VALUE_HEADS, HEAD_SIZE),
        key_pos.reshape(block_count, block_length),
    )


def contract_last(left, right):
    return lax.dot_general(
        left, right, (((1,), (1,)), ((), ())), preferred_element_type=jnp.float32
    )


def contract_first(left, right):
    return lax.dot_general(
        left, right, (((0,), (0,)), ((), ())), preferred_element_type=jnp.float32
    )


def local_general(
    tokens,
    cotangent,
    gain_attn,
    gain_ffn,
    query_key_value_weight,
    w_out,
    w_gate,
    w_up,
    w_down,
    pair_block,
):
    token_rows = tokens.shape[0]
    query_columns = QUERY_HEADS * HEAD_SIZE
    key_value_columns = KEY_VALUE_HEADS * HEAD_SIZE
    group_count = QUERY_HEADS // KEY_VALUE_HEADS
    score_scale = 1.0 / math.sqrt(HEAD_SIZE)
    ff_cols = w_gate.shape[1]
    key_pos, own_pos = positions(pair_block, token_rows)
    query_pos = jnp.tile(own_pos, group_count)
    inputs_f = tokens.astype(jnp.float32)
    qkv_full, out_full = (
        lax.all_gather(query_key_value_weight, "fsdp", axis=0, tiled=True),
        lax.all_gather(w_out, "fsdp", axis=0, tiled=True),
    )
    normed_one_b = rms_norm(inputs_f, gain_attn).astype(jnp.bfloat16)
    projected_rows = jnp.dot(normed_one_b, qkv_full, preferred_element_type=jnp.float32)
    query_raw = projected_rows[:, :query_columns].reshape(token_rows, QUERY_HEADS, HEAD_SIZE)
    unrotated_key = projected_rows[:, query_columns : query_columns + key_value_columns].reshape(
        token_rows, KEY_VALUE_HEADS, HEAD_SIZE
    )
    query_b = (
        apply_rotation(query_raw, own_pos).astype(jnp.bfloat16).reshape(token_rows, query_columns)
    )
    keys_b = (
        apply_rotation(unrotated_key, own_pos)
        .astype(jnp.bfloat16)
        .reshape(token_rows, key_value_columns)
    )
    values_b = projected_rows[:, query_columns + key_value_columns :].astype(jnp.bfloat16)
    every_key, every_value = (
        lax.all_gather(keys_b, "ctx", axis=0, tiled=True),
        lax.all_gather(values_b, "ctx", axis=0, tiled=True),
    )
    query_grp = to_groups(query_b, group_count)
    key_blocks, value_blocks, pos_blocks = split_keys(every_key, every_value, key_pos)

    def forward_step(carry, block_in):
        run_max, run_total, weighted = carry
        key_block, value_block, block_pos = block_in
        causal = block_pos[None, None, :] <= query_pos[None, :, None]
        scores = (
            jnp.einsum("hqd,khd->hqk", query_grp, key_block, preferred_element_type=jnp.float32)
            * score_scale
        )
        scores = jnp.where(causal, scores, -1e30)
        new_max = jnp.maximum(run_max, jnp.max(scores, axis=-1))
        exp_scores = jnp.where(causal, jnp.exp(scores - new_max[..., None]), 0.0)
        fading = jnp.exp(run_max - new_max)
        run_total = run_total * fading + jnp.sum(exp_scores, axis=-1)
        weighted = weighted * fading[..., None] + jnp.einsum(
            "hqk,khd->hqd",
            exp_scores.astype(jnp.bfloat16),
            value_block,
            preferred_element_type=jnp.float32,
        )
        return ((new_max, run_total, weighted), None)

    initial_maximum = jnp.full((KEY_VALUE_HEADS, group_count * token_rows), -1e30, jnp.float32)
    initial_total = jnp.zeros((KEY_VALUE_HEADS, group_count * token_rows), jnp.float32)
    initial_weighted = jnp.zeros(
        (KEY_VALUE_HEADS, group_count * token_rows, HEAD_SIZE), jnp.float32
    )
    final_carry, ignored = lax.scan(
        forward_step,
        (initial_maximum, initial_total, initial_weighted),
        (key_blocks, value_blocks, pos_blocks),
    )
    run_max, run_total, weighted = final_carry
    log_total = run_max + jnp.log(run_total)
    attn_grp = weighted / run_total[..., None]
    attended_b = from_groups(attn_grp.astype(jnp.bfloat16), group_count)
    mid_rows = inputs_f + jnp.dot(attended_b, out_full, preferred_element_type=jnp.float32)
    gate_full, up_full, down_full = (
        lax.all_gather(w_gate, "fsdp", axis=0, tiled=True),
        lax.all_gather(w_up, "fsdp", axis=0, tiled=True),
        lax.all_gather(w_down, "fsdp", axis=0, tiled=True),
    )
    normed_two_b = rms_norm(mid_rows, gain_ffn).astype(jnp.bfloat16)
    gate_val = jnp.dot(normed_two_b, gate_full, preferred_element_type=jnp.float32)
    up_val = jnp.dot(normed_two_b, up_full, preferred_element_type=jnp.float32)
    hidden_b = (jax.nn.silu(gate_val) * up_val).astype(jnp.bfloat16)
    output_f = mid_rows + jnp.dot(hidden_b, down_full, preferred_element_type=jnp.float32)
    result = output_f.astype(jnp.bfloat16)
    normed_one_x, attended_x, normed_two_x, hidden_x = (
        lax.all_to_all(normed_one_b, "fsdp", split_axis=1, concat_axis=0, tiled=True),
        lax.all_to_all(attended_b, "fsdp", split_axis=1, concat_axis=0, tiled=True),
        lax.all_to_all(normed_two_b, "fsdp", split_axis=1, concat_axis=0, tiled=True),
        lax.all_to_all(hidden_b, "fsdp", split_axis=1, concat_axis=0, tiled=True),
    )
    grad_out_f = cotangent.astype(jnp.float32)
    gate_back, up_back, down_back = (
        lax.all_gather(w_gate, "fsdp", axis=0, tiled=True),
        lax.all_gather(w_up, "fsdp", axis=0, tiled=True),
        lax.all_gather(w_down, "fsdp", axis=0, tiled=True),
    )
    grad_hidden = contract_last(cotangent, down_back)
    ignored, ffn_back = jax.vjp(
        lambda gate_in, up_in: jax.nn.silu(gate_in) * up_in, gate_val, up_val
    )
    grad_gate_f, grad_up_f = ffn_back(grad_hidden)
    grad_gate_b = grad_gate_f.astype(jnp.bfloat16)
    grad_up_b = grad_up_f.astype(jnp.bfloat16)
    grad_normed_two = contract_last(grad_gate_b, gate_back) + contract_last(grad_up_b, up_back)
    ignored, norm_two_back = jax.vjp(rms_norm, mid_rows, gain_ffn)
    grad_mid_part, gain_ffn_part = norm_two_back(grad_normed_two)
    grad_mid = grad_out_f + grad_mid_part
    gate_up_b = jnp.concatenate([grad_gate_b, grad_up_b], axis=1)
    qkv_back, out_back = (
        lax.all_gather(query_key_value_weight, "fsdp", axis=0, tiled=True),
        lax.all_gather(w_out, "fsdp", axis=0, tiled=True),
    )
    grad_proj_b = grad_mid.astype(jnp.bfloat16)
    grad_att_b = contract_last(grad_proj_b, out_back).astype(jnp.bfloat16)
    grad_att_grp = to_groups(grad_att_b, group_count)
    delta_rows = jnp.sum(grad_att_grp.astype(jnp.float32) * attn_grp, axis=-1)

    def backward_step(grad_query, block_in):
        key_block, value_block, block_pos = block_in
        causal = block_pos[None, None, :] <= query_pos[None, :, None]
        scores = (
            jnp.einsum("hqd,khd->hqk", query_grp, key_block, preferred_element_type=jnp.float32)
            * score_scale
        )
        probs = jnp.where(causal, jnp.exp(scores - log_total[..., None]), 0.0)
        grad_values = jnp.einsum(
            "hqk,hqd->khd",
            probs.astype(jnp.bfloat16),
            grad_att_grp,
            preferred_element_type=jnp.float32,
        )
        grad_probs = jnp.einsum(
            "hqd,khd->hqk", grad_att_grp, value_block, preferred_element_type=jnp.float32
        )
        grad_scores = (probs * (grad_probs - delta_rows[..., None])).astype(jnp.bfloat16)
        grad_query = grad_query + score_scale * jnp.einsum(
            "hqk,khd->hqd", grad_scores, key_block, preferred_element_type=jnp.float32
        )
        grad_keys = score_scale * jnp.einsum(
            "hqk,hqd->khd", grad_scores, query_grp, preferred_element_type=jnp.float32
        )
        return (grad_query, (grad_keys, grad_values))

    grad_query_grp, key_grads = lax.scan(
        backward_step,
        jnp.zeros((KEY_VALUE_HEADS, group_count * token_rows, HEAD_SIZE), jnp.float32),
        (key_blocks, value_blocks, pos_blocks),
    )
    total_keys = key_pos.shape[0]
    grad_keys_all = key_grads[0].reshape(total_keys, key_value_columns)
    grad_values_all = key_grads[1].reshape(total_keys, key_value_columns)
    key_sums, summed_values = (
        lax.psum_scatter(
            grad_keys_all.astype(jnp.bfloat16), "ctx", scatter_dimension=0, tiled=True
        ).astype(jnp.float32),
        lax.psum_scatter(
            grad_values_all.astype(jnp.bfloat16), "ctx", scatter_dimension=0, tiled=True
        ).astype(jnp.float32),
    )
    grad_query_rows = from_groups(grad_query_grp, group_count).reshape(
        token_rows, QUERY_HEADS, HEAD_SIZE
    )
    ignored, query_rope_back = jax.vjp(lambda vectors: apply_rotation(vectors, own_pos), query_raw)
    ignored, key_rotation_backward = jax.vjp(
        lambda vectors: apply_rotation(vectors, own_pos), unrotated_key
    )
    grad_query_raw = query_rope_back(grad_query_rows)[0]
    unrotated_key_gradient = key_rotation_backward(
        key_sums.reshape(token_rows, KEY_VALUE_HEADS, HEAD_SIZE)
    )[0]
    grad_projected_b = jnp.concatenate(
        [
            grad_query_raw.reshape(token_rows, query_columns),
            unrotated_key_gradient.reshape(token_rows, key_value_columns),
            summed_values,
        ],
        axis=1,
    ).astype(jnp.bfloat16)
    grad_normed_one = contract_last(grad_projected_b, qkv_back)
    ignored, norm_one_back = jax.vjp(rms_norm, inputs_f, gain_attn)
    grad_in_part, gain_attn_part = norm_one_back(grad_normed_one)
    grad_input = grad_mid + grad_in_part
    cot_group, gate_up_group, projected_group, proj_group = (
        lax.all_gather(cotangent, "fsdp", axis=0, tiled=True),
        lax.all_gather(gate_up_b, "fsdp", axis=0, tiled=True),
        lax.all_gather(grad_projected_b, "fsdp", axis=0, tiled=True),
        lax.all_gather(grad_proj_b, "fsdp", axis=0, tiled=True),
    )
    qkv_part = contract_first(normed_one_x, projected_group)
    out_part = contract_first(attended_x, proj_group)
    gate_up_part = contract_first(normed_two_x, gate_up_group)
    gate_part = gate_up_part[:, :ff_cols]
    up_part = gate_up_part[:, ff_cols:]
    down_part = contract_first(hidden_x, cot_group)
    grad_qkv, grad_out, grad_down = (
        lax.psum_scatter(
            qkv_part.astype(jnp.bfloat16), "ctx", scatter_dimension=0, tiled=True
        ).astype(jnp.float32),
        lax.psum_scatter(
            out_part.astype(jnp.bfloat16), "ctx", scatter_dimension=0, tiled=True
        ).astype(jnp.float32),
        lax.psum_scatter(
            down_part.astype(jnp.bfloat16), "ctx", scatter_dimension=0, tiled=True
        ).astype(jnp.float32),
    )
    grad_gate, grad_up = (
        lax.psum_scatter(
            gate_part.astype(jnp.bfloat16), "ctx", scatter_dimension=0, tiled=True
        ).astype(jnp.float32),
        lax.psum_scatter(
            up_part.astype(jnp.bfloat16), "ctx", scatter_dimension=0, tiled=True
        ).astype(jnp.float32),
    )
    grad_gain_attn, grad_gain_ffn = (
        lax.psum_scatter(gain_attn_part, ("ctx", "fsdp"), scatter_dimension=0, tiled=True),
        lax.psum_scatter(gain_ffn_part, ("ctx", "fsdp"), scatter_dimension=0, tiled=True),
    )
    return (
        result,
        grad_input,
        grad_gain_attn,
        grad_gain_ffn,
        grad_qkv,
        grad_out,
        grad_gate,
        grad_up,
        grad_down,
    )


MESH = pl.DeviceIdType.MESH
ACROSS_X, ACROSS_Y, ACROSS_CORE = 2, 4, 1


class Links:
    def __init__(self, sems, ctx, fsdp):
        self.send_sem, self.recv_sem, self.local_sem = sems
        self.ctx, self.fsdp = ctx, fsdp
        self.remote = self.locals = 0

    def to(self, src, dst, ctx, fsdp):
        index, self.remote = self.remote, self.remote + 1
        return pltpu.make_async_remote_copy(
            src_ref=src,
            dst_ref=dst,
            send_sem=self.send_sem.at[index],
            recv_sem=self.recv_sem.at[index],
            device_id=(ctx, fsdp),
            device_id_type=MESH,
        )

    def plane(self, src, dst, flip):
        return self.to(src, dst, lax.bitwise_xor(self.ctx, flip), self.fsdp)

    def column(self, src, dst, flip):
        return self.to(src, dst, self.ctx, lax.bitwise_xor(self.fsdp, flip))

    def here(self, src, dst):
        index, self.locals = self.locals, self.locals + 1
        return pltpu.make_async_copy(src, dst, self.local_sem.at[index])


def greet(ctx, fsdp):
    barrier = pltpu.get_barrier_semaphore()
    partners = [(lax.bitwise_xor(ctx, flip), fsdp) for flip in (1, 2, 4)]
    partners += [(ctx, lax.bitwise_xor(fsdp, flip)) for flip in (1, 2, 3)]
    for partner in partners:
        pl.semaphore_signal(barrier, inc=1, device_id=partner, device_id_type=MESH)
    pl.semaphore_wait(barrier, len(partners))


class PlaneGather:
    def __init__(self, links, blocks, halves):
        self.links, self.blocks, self.halves = links, blocks, halves
        self.ctx = links.ctx
        self.sent = []
        self.cores = []

    def _go(self, copies):
        for copy in copies:
            copy.start()
        self.sent += copies
        return copies

    def _core(self, index):
        refs = self.blocks(index)
        self.cores += self._go([self.links.plane(r, r, ACROSS_CORE) for r in refs])

    def begin(self):
        refs = self.blocks(self.ctx)
        self.from_x = self._go([self.links.plane(r, r, ACROSS_X) for r in refs])
        self.from_y = self._go([self.links.plane(r, r, ACROSS_Y) for r in refs])
        self._core(self.ctx)

    def forward(self):
        index = lax.bitwise_xor(self.ctx, ACROSS_X)
        for copy in self.from_x:
            copy.wait_recv()
        refs = self.halves(index, 0)
        self.corner = self._go([self.links.plane(r, r, ACROSS_Y) for r in refs])
        self._core(index)
        index = lax.bitwise_xor(self.ctx, ACROSS_Y)
        for copy in self.from_y:
            copy.wait_recv()
        refs = self.halves(index, 1)
        self.corner += self._go([self.links.plane(r, r, ACROSS_X) for r in refs])
        self._core(index)

    def finish(self):
        for copy in self.corner:
            copy.wait_recv()
        self._core(lax.bitwise_xor(self.ctx, ACROSS_X | ACROSS_Y))
        for copy in self.cores:
            copy.wait_recv()

    def drain(self):
        for copy in self.sent:
            copy.wait_send()


class PlaneScatter:
    def __init__(self, links, part, core_rx, half_rx, side_rx):
        self.links, self.part = links, part
        self.core_rx, self.half_rx, self.side_rx = core_rx, half_rx, side_rx
        self.chip, self.core = links.ctx // 2, lax.rem(links.ctx, 2)
        self.sent = []
        self.from_core = {}

    def order(self):
        return [(flip, lax.bitwise_xor(self.chip, flip)) for flip in (3, 1, 2, 0)]

    def _go(self, copy):
        copy.start()
        self.sent.append(copy)
        return copy

    def give(self, flip, chip):
        self.from_core[flip] = self._go(
            self.links.plane(
                self.part.at[2 * chip + 1 - self.core], self.core_rx.at[chip], ACROSS_CORE
            )
        )

    def _summed(self, flip):
        chip = lax.bitwise_xor(self.chip, flip)
        self.from_core[flip].wait_recv()
        mine = self.part.at[2 * chip + self.core]
        total = mine[...].astype(jnp.float32) + self.core_rx[chip].astype(jnp.float32)
        return mine, total

    def run(self):
        half = self.half_rx.shape[1]
        mine, total = self._summed(3)
        mine[...] = total.astype(jnp.bfloat16)
        top = self._go(
            self.links.plane(mine.at[pl.ds(0, half)], self.half_rx.at[0], ACROSS_Y)
        )
        bottom = self._go(
            self.links.plane(mine.at[pl.ds(half, half)], self.half_rx.at[1], ACROSS_X)
        )
        sides = []
        for flip, copy, slot in ((1, top, 0), (2, bottom, 1)):
            mine, total = self._summed(flip)
            mine[...] = total.astype(jnp.bfloat16)
            copy.wait_recv()
            rows = pl.ds(slot * half, half)
            mine[rows] = (
                total[slot * half : (slot + 1) * half]
                + self.half_rx[slot].astype(jnp.float32)
            ).astype(jnp.bfloat16)
            sides.append(
                self._go(
                    self.links.plane(
                        mine, self.side_rx.at[slot], ACROSS_X if slot == 0 else ACROSS_Y
                    )
                )
            )
        mine, total = self._summed(0)
        for slot, copy in enumerate(sides):
            copy.wait_recv()
            total = total + self.side_rx[slot].astype(jnp.float32)
        return total

    def drain(self):
        for copy in self.sent:
            copy.wait_send()


def head_of(ctx, fsdp):
    return lax.bitwise_xor(ctx, 4 * lax.rem(fsdp, 2))


def out_plane(ctx, fsdp):
    return lax.bitwise_xor(ctx // 2, 2 * lax.rem(fsdp, 2))


def turn(vectors, cos_rows, sin_rows, sign):
    return vectors * cos_rows + sign * pltpu.roll(vectors, HEAD_SIZE // 2, 1) * sin_rows


def attention_kernel(
    tokens_ref,
    cot_ref,
    gain_one_ref,
    gain_two_ref,
    qkv_w_ref,
    out_w_ref,
    gate_ref,
    up_ref,
    cos_ref,
    sin_ref,
    pos_col_ref,
    pos_row_ref,
    mid_ref,
    normed_two_group,
    cot_group,
    gate_w,
    up_w,
    qkv_out,
    attended_out,
    normed_one_out,
    w_head_out,
    out_head_out,
    normed,
    w_head,
    out_head,
    qkv,
    attended,
    part,
    core_rx,
    half_rx,
    side_rx,
    normed_two,
    send_sem,
    recv_sem,
    local_sem,
):
    f32, bf16 = jnp.float32, jnp.bfloat16
    ctx, fsdp = lax.axis_index("ctx"), lax.axis_index("fsdp")
    links = Links((send_sem, recv_sem, local_sem), ctx, fsdp)
    rows, width = tokens_ref.shape
    depth = qkv_w_ref.shape[0]
    head_columns = out_head.shape[0]
    n_ctx, n_fsdp = normed.shape[0], width // depth
    seq_rows = n_ctx * rows
    hidden = gate_w.shape[1]
    strip = hidden // n_ctx
    query_columns = QUERY_HEADS * HEAD_SIZE
    key_columns = KEY_VALUE_HEADS * HEAD_SIZE
    score_scale = 1.0 / math.sqrt(HEAD_SIZE)
    finals = []

    greet(ctx, fsdp)

    my_rows = pl.ds(pl.multiple_of(fsdp * depth, depth), depth)

    def head_parts(head):
        starts = (
            (head * head_columns, head_columns, 0),
            (query_columns + head * HEAD_SIZE, HEAD_SIZE, head_columns),
            (query_columns + key_columns + head * HEAD_SIZE, HEAD_SIZE, head_columns + HEAD_SIZE),
        )
        for start, size, place in starts:
            yield (
                qkv_w_ref.at[:, pl.ds(pl.multiple_of(start, HEAD_SIZE), size)],
                w_head.at[my_rows, pl.ds(place, size)],
            )

    head_copies = []
    for flip in (1, 2, 3):
        for src, dst in head_parts(head_of(ctx, lax.bitwise_xor(fsdp, flip))):
            head_copies.append(links.column(src, dst, flip))
    own_head = [links.here(src, dst) for src, dst in head_parts(head_of(ctx, fsdp))]
    for copy in head_copies + own_head:
        copy.start()

    inputs = tokens_ref[...].astype(f32)
    scale = lax.rsqrt(jnp.mean(inputs * inputs, axis=-1, keepdims=True) + norm_eps)
    normed[ctx] = (inputs * scale * gain_one_ref[...]).astype(bf16)
    half = rows // 2
    gather = PlaneGather(
        links,
        lambda j: [normed.at[j]],
        lambda j, which: [normed.at[j, pl.ds(which * half, half)]],
    )
    gather.begin()
    gather.forward()
    gather.finish()
    finals.append(links.here(normed, normed_one_out))
    finals[-1].start()
    for copy in own_head:
        copy.wait()
    for copy in head_copies:
        copy.wait_recv()

    out_block = out_w_ref.at[
        pl.ds(pl.multiple_of(lax.rem(ctx, 2) * head_columns, head_columns), head_columns)
    ]
    out_sends = []
    slot = links.remote
    out_slot = links.column(out_block, out_head, 1)
    out_home = links.here(out_block, out_head)
    home = out_plane(ctx, fsdp) == fsdp
    for target in range(n_fsdp):
        wanted = (out_plane(ctx, jnp.int32(target)) == fsdp) & (fsdp != target)
        copy = pltpu.make_async_remote_copy(
            src_ref=out_block,
            dst_ref=out_head,
            send_sem=send_sem.at[links.remote],
            recv_sem=recv_sem.at[slot],
            device_id=(ctx, jnp.int32(target)),
            device_id_type=MESH,
        )
        links.remote += 1
        out_sends.append((wanted, copy))

        @pl.when(wanted)
        def _(copy=copy):
            copy.start()

    @pl.when(home)
    def _():
        out_home.start()

    def strips(target, rows_of):
        cols = pl.ds(pl.multiple_of(target * hidden + ctx * strip, strip), strip)
        place = pl.ds(pl.multiple_of(ctx * strip, strip), strip)
        for source, dest in ((gate_ref, gate_w), (up_ref, up_w)):
            yield source.at[:, cols], dest.at[rows_of, place]

    strip_copies = []
    for flip in (1, 2, 3):
        for src, dst in strips(lax.bitwise_xor(fsdp, flip), my_rows):
            strip_copies.append(links.column(src, dst, flip))
    own_strips = [links.here(src, dst) for src, dst in strips(fsdp, my_rows)]
    for copy in strip_copies + own_strips:
        copy.start()

    block_rows = 2 * rows

    def project(step, carry):
        at = pl.multiple_of(step * block_rows, block_rows)
        tile = normed[pl.ds(step * 2, 2)].reshape(block_rows, width)
        out = jnp.dot(tile, w_head[...], preferred_element_type=f32)
        cos_rows, sin_rows = cos_ref[pl.ds(at, block_rows)], sin_ref[pl.ds(at, block_rows)]
        for column in range(0, head_columns + HEAD_SIZE, HEAD_SIZE):
            turned = turn(out[:, column : column + HEAD_SIZE], cos_rows, sin_rows, 1.0)
            qkv[pl.ds(at, block_rows), pl.ds(column, HEAD_SIZE)] = turned.astype(bf16)
        column = head_columns + HEAD_SIZE
        qkv[pl.ds(at, block_rows), pl.ds(column, HEAD_SIZE)] = out[:, column:].astype(bf16)
        return carry

    lax.fori_loop(0, seq_rows // block_rows, project, 0)

    def attend(step, carry):
        at = pl.multiple_of(step * block_rows, block_rows)
        keys = qkv[:, pl.ds(head_columns, HEAD_SIZE)]
        values = qkv[:, pl.ds(head_columns + HEAD_SIZE, HEAD_SIZE)]
        causal = pos_row_ref[...] <= pos_col_ref[pl.ds(at, block_rows)]
        for column in range(0, head_columns, HEAD_SIZE):
            query = qkv[pl.ds(at, block_rows), pl.ds(column, HEAD_SIZE)]
            scores = contract_last(query, keys) * score_scale
            scores = jnp.where(causal, scores, -1e30)
            shifted = jnp.exp(scores - jnp.max(scores, axis=-1, keepdims=True))
            probs = shifted * (1.0 / jnp.sum(shifted, axis=-1, keepdims=True))
            mixed = jnp.dot(probs.astype(bf16), values, preferred_element_type=f32)
            attended[pl.ds(at, block_rows), pl.ds(column, HEAD_SIZE)] = mixed.astype(bf16)
        return carry

    lax.fori_loop(0, seq_rows // block_rows, attend, 0)

    @pl.when(home)
    def _():
        out_home.wait()

    @pl.when(jnp.logical_not(home))
    def _():
        out_slot.wait_recv()

    for src, dst in (
        (qkv, qkv_out),
        (attended, attended_out),
        (w_head, w_head_out),
        (out_head, out_head_out),
    ):
        finals.append(links.here(src, dst))
        finals[-1].start()

    scatter = PlaneScatter(links, part, core_rx, half_rx, side_rx)
    for flip, chip in scatter.order():
        at = pl.multiple_of(chip * block_rows, block_rows)
        out = jnp.dot(
            attended[pl.ds(at, block_rows)], out_head[...], preferred_element_type=f32
        )
        part[pl.ds(chip * 2, 2)] = out.astype(bf16).reshape(2, rows, width)
        scatter.give(flip, chip)
    mid = tokens_ref[...].astype(f32) + scatter.run()
    mid_ref[...] = mid
    mid_scale = lax.rsqrt(jnp.mean(mid * mid, axis=-1, keepdims=True) + norm_eps)
    normed_two[...] = (mid * mid_scale * gain_two_ref[...]).astype(bf16)

    group_rows = pl.ds(pl.multiple_of(fsdp * rows, rows), rows)
    group_copies = []
    for source, dest in ((normed_two, normed_two_group), (cot_ref, cot_group)):
        for flip in (1, 2, 3):
            group_copies.append(links.column(source, dest.at[group_rows], flip))
        finals.append(links.here(source, dest.at[group_rows]))
        finals[-1].start()
    for copy in group_copies:
        copy.start()

    for copy in own_strips:
        copy.wait()
    for copy in strip_copies:
        copy.wait_recv()

    def columns_of(j):
        place = pl.ds(pl.multiple_of(j * strip, strip), strip)
        return [gate_w.at[:, place], up_w.at[:, place]]

    def halves_of(j, which):
        place = pl.ds(pl.multiple_of(j * strip, strip), strip)
        part_rows = pl.ds(which * (width // 2), width // 2)
        return [gate_w.at[part_rows, place], up_w.at[part_rows, place]]

    weights = PlaneGather(links, columns_of, halves_of)
    weights.begin()
    weights.forward()
    weights.finish()

    for copy in group_copies:
        copy.wait_recv()
    for copy in head_copies + strip_copies + group_copies:
        copy.wait_send()
    for wanted, copy in out_sends:

        @pl.when(wanted)
        def _(copy=copy):
            copy.wait_send()

    gather.drain()
    scatter.drain()
    weights.drain()
    for copy in finals:
        copy.wait()


def attention_forward(
    tokens, cotangent, gain_attn, gain_ffn, qkv_w, w_out, w_gate, w_up, cos, sin, key_pos
):
    f32, bf16 = jnp.float32, jnp.bfloat16
    n_ctx, n_fsdp = lax.axis_size("ctx"), lax.axis_size("fsdp")
    rows, width = tokens.shape
    depth = qkv_w.shape[0]
    hidden = w_gate.shape[1] // n_fsdp
    seq_rows = n_ctx * rows
    head_columns = QUERY_HEADS // KEY_VALUE_HEADS * HEAD_SIZE
    all_columns = head_columns + 2 * HEAD_SIZE
    vmem, hbm = pl.BlockSpec(memory_space=pltpu.VMEM), pl.BlockSpec(memory_space=pl.ANY)
    shape = jax.ShapeDtypeStruct
    return pl.pallas_call(
        attention_kernel,
        name="attention_forward",
        out_shape=[
            shape((rows, width), f32),
            shape((n_fsdp * rows, width), bf16),
            shape((n_fsdp * rows, width), bf16),
            shape((width, hidden), bf16),
            shape((width, hidden), bf16),
            shape((seq_rows, all_columns), bf16),
            shape((seq_rows, head_columns), bf16),
            shape((n_ctx, rows, width), bf16),
            shape((width, all_columns), bf16),
            shape((head_columns, width), bf16),
        ],
        in_specs=[vmem] * 4 + [hbm] * 4 + [vmem] * 4,
        out_specs=[vmem] + [hbm] * 9,
        scratch_shapes=[
            pltpu.VMEM((n_ctx, rows, width), bf16),
            pltpu.VMEM((width, all_columns), bf16),
            pltpu.VMEM((head_columns, width), bf16),
            pltpu.VMEM((seq_rows, all_columns), bf16),
            pltpu.VMEM((seq_rows, head_columns), bf16),
            pltpu.VMEM((n_ctx, rows, width), bf16),
            pltpu.VMEM((n_ctx // 2, rows, width), bf16),
            pltpu.VMEM((2, rows // 2, width), bf16),
            pltpu.VMEM((2, rows, width), bf16),
            pltpu.VMEM((rows, width), bf16),
            pltpu.SemaphoreType.DMA((80,)),
            pltpu.SemaphoreType.DMA((80,)),
            pltpu.SemaphoreType.DMA((24,)),
        ],
        compiler_params=pltpu.CompilerParams(
            collective_id=1, has_side_effects=True, vmem_limit_bytes=58 * 2**20
        ),
    )(
        tokens,
        cotangent,
        gain_attn[None],
        gain_ffn[None],
        qkv_w,
        w_out,
        w_gate,
        w_up,
        cos,
        sin,
        key_pos[:, None],
        key_pos[None],
    )


def rotate_heads(vectors, cosine, sine_val, sign):
    half_dim = HEAD_SIZE // 2
    first_half = vectors[..., :half_dim]
    second_half = vectors[..., half_dim:]
    return jnp.concatenate(
        [
            first_half * cosine - sign * second_half * sine_val,
            second_half * cosine + sign * first_half * sine_val,
        ],
        axis=-1,
    )


def local_heads(
    tokens,
    cotangent,
    gain_attn,
    gain_ffn,
    query_key_value_weight,
    w_out,
    w_gate,
    w_up,
    w_down,
    pair_block,
):
    f32, bf16 = jnp.float32, jnp.bfloat16
    n_ctx, n_fsdp = lax.axis_size("ctx"), lax.axis_size("fsdp")
    ctx, fsdp = lax.axis_index("ctx"), lax.axis_index("fsdp")
    token_rows, width = tokens.shape
    group_count = QUERY_HEADS // KEY_VALUE_HEADS
    head_columns = group_count * HEAD_SIZE
    query_columns = QUERY_HEADS * HEAD_SIZE
    key_columns = KEY_VALUE_HEADS * HEAD_SIZE
    score_scale = 1.0 / math.sqrt(HEAD_SIZE)
    depth = query_key_value_weight.shape[0]
    hidden_cols = w_down.shape[0]

    key_pos, own_pos = positions(pair_block, token_rows)

    frequency = jnp.exp(
        jnp.arange(HEAD_SIZE // 2, dtype=f32) * (-2.0 * math.log(rope_base) / HEAD_SIZE)
    )
    angles = key_pos.astype(f32)[:, None] * frequency[None, :]
    cosine, sine_val = jnp.cos(angles), jnp.sin(angles)
    (
        mid,
        normed_two_group,
        cot_group,
        gate_w,
        up_w,
        qkv,
        attended_b,
        normed_one_seq,
        w_head,
        out_head,
    ) = attention_forward(
        tokens,
        cotangent,
        gain_attn,
        gain_ffn,
        query_key_value_weight,
        w_out,
        w_gate,
        w_up,
        jnp.concatenate([cosine, cosine], axis=1),
        jnp.concatenate([-sine_val, sine_val], axis=1),
        key_pos,
    )
    inputs_f = tokens.astype(f32)
    normed_one_seq = normed_one_seq.reshape(-1, width)
    queries = qkv[:, :head_columns].reshape(-1, group_count, HEAD_SIZE).transpose(1, 0, 2)
    keys = qkv[:, head_columns : head_columns + HEAD_SIZE]
    values = qkv[:, head_columns + HEAD_SIZE :]
    causal = key_pos[None, :] <= key_pos[:, None]
    scores = jnp.einsum("gqd,kd->gqk", queries, keys, preferred_element_type=f32) * score_scale
    scores = jnp.where(causal, scores, -1e30)
    shifted = jnp.exp(scores - jnp.max(scores, axis=-1, keepdims=True))
    probs = shifted / jnp.sum(shifted, axis=-1, keepdims=True)
    probs_low = probs.astype(bf16)

    mid_scale = lax.rsqrt(jnp.mean(mid * mid, axis=-1, keepdims=True) + norm_eps)
    gate = jnp.dot(normed_two_group, gate_w, preferred_element_type=f32)
    up = jnp.dot(normed_two_group, up_w, preferred_element_type=f32)
    sig = jax.nn.sigmoid(gate)
    silu = gate * sig
    hidden_b = (silu * up).astype(bf16)
    down_part = jnp.dot(hidden_b, w_down, preferred_element_type=f32)
    grad_hidden = contract_last(cot_group, w_down)
    grad_gate_b = (grad_hidden * up * sig * (1.0 + gate * (1.0 - sig))).astype(bf16)
    grad_up_b = (grad_hidden * silu).astype(bf16)
    normed_part = contract_last(grad_gate_b, gate_w) + contract_last(grad_up_b, up_w)
    result = (
        mid
        + lax.psum_scatter(
            down_part.astype(bf16), "fsdp", scatter_dimension=0, tiled=True
        ).astype(f32)
    ).astype(bf16)
    grad_normed_two = lax.psum_scatter(
        normed_part.astype(bf16), "fsdp", scatter_dimension=0, tiled=True
    ).astype(f32)
    u = grad_normed_two * gain_ffn
    grad_mid = (
        cotangent.astype(f32)
        + mid_scale * u
        - mid * mid_scale**3 * jnp.mean(u * mid, axis=-1, keepdims=True)
    )

    grad_down_part = contract_first(hidden_b, cot_group)
    grad_gate_part = contract_first(normed_two_group, grad_gate_b)
    grad_up_part = contract_first(normed_two_group, grad_up_b)
    grad_down = lax.psum_scatter(
        grad_down_part.astype(bf16), "ctx", scatter_dimension=0, tiled=True
    ).astype(f32)

    def spread(part):
        blocks = part.astype(bf16).reshape(n_fsdp, n_ctx, depth // n_ctx, hidden_cols)
        blocks = blocks.transpose(1, 0, 2, 3).reshape(width, hidden_cols)
        mine = lax.psum_scatter(blocks, "ctx", scatter_dimension=0, tiled=True)
        mine = mine.reshape(n_fsdp, depth // n_ctx, hidden_cols)
        return lax.all_to_all(mine, "fsdp", split_axis=0, concat_axis=2, tiled=True).reshape(
            depth // n_ctx, n_fsdp * hidden_cols
        )

    grad_gate, grad_up = spread(grad_gate_part).astype(f32), spread(grad_up_part).astype(f32)

    grad_proj_b = grad_mid.astype(bf16)
    grad_proj_seq = lax.all_gather(grad_proj_b, "ctx", axis=0, tiled=True)
    grad_att = contract_last(grad_proj_seq, out_head).astype(bf16)
    grad_att = grad_att.reshape(-1, group_count, HEAD_SIZE).transpose(1, 0, 2)
    grad_out_part = contract_first(attended_b, grad_proj_seq)
    grad_values = jnp.einsum("gqk,gqd->kd", probs_low, grad_att, preferred_element_type=f32)
    grad_probs = jnp.einsum("gqd,kd->gqk", grad_att, values, preferred_element_type=f32)
    delta = jnp.sum(grad_probs * probs, axis=-1, keepdims=True)
    grad_scores = (probs * (grad_probs - delta)).astype(bf16)
    grad_queries = score_scale * jnp.einsum(
        "gqk,kd->gqd", grad_scores, keys, preferred_element_type=f32
    )
    grad_keys = score_scale * jnp.einsum(
        "gqk,gqd->kd", grad_scores, queries, preferred_element_type=f32
    )
    grad_projected = jnp.concatenate(
        [rotate_heads(grad_queries[g], cosine, sine_val, -1.0) for g in range(group_count)]
        + [rotate_heads(grad_keys, cosine, sine_val, -1.0), grad_values],
        axis=1,
    ).astype(bf16)
    normed_one_part = contract_last(grad_projected, w_head)
    grad_normed_one = lax.psum_scatter(
        normed_one_part.astype(bf16), "ctx", scatter_dimension=0, tiled=True
    ).astype(f32)
    in_scale = lax.rsqrt(jnp.mean(inputs_f * inputs_f, axis=-1, keepdims=True) + norm_eps)
    u = grad_normed_one * gain_attn
    grad_input = (
        grad_mid
        + in_scale * u
        - inputs_f * in_scale**3 * jnp.mean(u * inputs_f, axis=-1, keepdims=True)
    )

    grad_head_part = contract_first(normed_one_seq, grad_projected).astype(bf16)
    blocks = grad_head_part.reshape(n_fsdp, n_ctx, depth // n_ctx, -1).transpose(1, 0, 2, 3)
    blocks = blocks.reshape(n_ctx * n_fsdp, depth // n_ctx, -1)
    got = lax.all_to_all(blocks, ("ctx", "fsdp"), split_axis=0, concat_axis=0, tiled=True)
    got = got.astype(f32)
    sums = [
        sum(got[(h ^ (4 * (f % 2))) * n_fsdp + f] for f in range(n_fsdp))
        for h in range(KEY_VALUE_HEADS)
    ]
    grad_qkv = jnp.concatenate(
        [s[:, :head_columns] for s in sums]
        + [s[:, head_columns : head_columns + HEAD_SIZE] for s in sums]
        + [s[:, head_columns + HEAD_SIZE :] for s in sums],
        axis=1,
    )
    strip_rows = depth // n_ctx
    placed = lax.dynamic_update_slice(
        jnp.zeros((n_ctx, n_fsdp, strip_rows, width), bf16),
        grad_out_part.astype(bf16).reshape(-1, 1, strip_rows, width),
        (4 * lax.rem(ctx, 2), out_plane(ctx, fsdp), 0, 0),
    ).reshape(n_ctx * n_fsdp, strip_rows, width)
    out_got = lax.all_to_all(placed, ("ctx", "fsdp"), split_axis=0, concat_axis=0, tiled=True)
    grad_out = jnp.sum(out_got.astype(f32), axis=0)

    my_rows = ctx * (depth // n_ctx)
    rows_of = lambda matrix: lax.dynamic_slice_in_dim(
        matrix, my_rows, depth // n_ctx, 0
    ).astype(f32)
    attn_sum = jnp.sum(rows_of(query_key_value_weight) * grad_qkv, axis=1)
    ffn_sum = jnp.sum(rows_of(w_gate) * grad_gate, axis=1) + jnp.sum(
        rows_of(w_up) * grad_up, axis=1
    )
    gain_pairs = [
        (c * n_fsdp + f, f * n_ctx + c) for c in range(n_ctx) for f in range(n_fsdp)
    ]
    moved = lax.ppermute(jnp.stack([attn_sum, ffn_sum]), ("ctx", "fsdp"), gain_pairs)
    my_gain = (ctx * n_fsdp + fsdp) * (depth // n_ctx)
    grad_gain_attn = moved[0] / lax.dynamic_slice_in_dim(gain_attn, my_gain, depth // n_ctx)
    grad_gain_ffn = moved[1] / lax.dynamic_slice_in_dim(gain_ffn, my_gain, depth // n_ctx)
    return (
        result,
        grad_input,
        grad_gain_attn,
        grad_gain_ffn,
        grad_qkv,
        grad_out,
        grad_gate,
        grad_up,
        grad_down,
    )


def solution(mesh):
    local = local_heads if mesh.shape["ctx"] == KEY_VALUE_HEADS else local_general
    return jax.shard_map(
        local,
        mesh=mesh,
        in_specs=(
            P(("ctx", "fsdp"), None),
            P(("ctx", "fsdp"), None),
            P(),
            P(),
            P("fsdp", None),
            P("fsdp", None),
            P("fsdp", None),
            P("fsdp", None),
            P("fsdp", None),
            P(),
        ),
        out_specs=(
            P(("ctx", "fsdp"), None),
            P(("ctx", "fsdp"), None),
            P(("ctx", "fsdp")),
            P(("ctx", "fsdp")),
            P(("fsdp", "ctx"), None),
            P(("fsdp", "ctx"), None),
            P(("fsdp", "ctx"), None),
            P(("fsdp", "ctx"), None),
            P(("fsdp", "ctx"), None),
        ),
        check_vma=False,
    )
```

```python
import math

import jax
import jax.numpy as jnp
from jax import lax
from jax.experimental import pallas as pl
from jax.experimental.pallas import tpu as pltpu
from jax.sharding import PartitionSpec as P

QUERY_HEADS = 16
KEY_VALUE_HEADS = 8
HEAD_SIZE = 128


norm_eps = 1e-05
rope_base = 1000000.0


def rms_norm(vectors, gain_vec):
    return (
        vectors
        * lax.rsqrt(jnp.mean(vectors * vectors, axis=-1, keepdims=True) + norm_eps)
        * gain_vec
    )


def apply_rotation(vectors, where_pos):
    half_dim = vectors.shape[-1] // 2
    frequency = jnp.exp(
        jnp.arange(half_dim, dtype=jnp.float32) * (-2.0 * math.log(rope_base) / vectors.shape[-1])
    )
    angles = where_pos.astype(jnp.float32)[:, None] * frequency[None, :]
    cosine = jnp.cos(angles)[:, None, :]
    sine_val = jnp.sin(angles)[:, None, :]
    first_half = vectors[..., :half_dim]
    second_half = vectors[..., half_dim:]
    return jnp.concatenate(
        [
            first_half * cosine - second_half * sine_val,
            second_half * cosine + first_half * sine_val,
        ],
        axis=-1,
    )


def positions(pair_block, token_rows):
    n_ctx = lax.axis_size("ctx")
    half_rows = token_rows // 2
    row_index = jnp.arange(token_rows, dtype=jnp.int32)
    first_block = pair_block[:, None]
    which_block = jnp.where(
        row_index[None, :] < half_rows, first_block, 2 * n_ctx - 1 - first_block
    )
    pos_table = which_block * half_rows + (row_index % half_rows)[None, :]
    own_pos = lax.dynamic_slice(pos_table, (lax.axis_index("ctx"), 0), (1, token_rows)).reshape(
        token_rows
    )
    return (pos_table.reshape(-1), own_pos)


def to_groups(input_array, group_count):
    token_rows = input_array.shape[0]
    head_length = input_array.shape[-1] // (group_count * KEY_VALUE_HEADS)
    return (
        input_array.reshape(token_rows, KEY_VALUE_HEADS, group_count, head_length)
        .transpose(1, 2, 0, 3)
        .reshape(KEY_VALUE_HEADS, group_count * token_rows, head_length)
    )


def from_groups(input_array, group_count):
    head_length = input_array.shape[-1]
    token_rows = input_array.shape[1] // group_count
    return (
        input_array.reshape(KEY_VALUE_HEADS, group_count, token_rows, head_length)
        .transpose(2, 0, 1, 3)
        .reshape(token_rows, KEY_VALUE_HEADS * group_count * head_length)
    )


def split_keys(every_key, every_value, key_pos):
    total_keys = every_key.shape[0]
    block_length = min(1024, total_keys)
    block_count = total_keys // block_length
    return (
        every_key.reshape(block_count, block_length, KEY_VALUE_HEADS, HEAD_SIZE),
        every_value.reshape(block_count, block_length, KEY_VALUE_HEADS, HEAD_SIZE),
        key_pos.reshape(block_count, block_length),
    )


def contract_last(left, right):
    return lax.dot_general(
        left, right, (((1,), (1,)), ((), ())), preferred_element_type=jnp.float32
    )


def contract_first(left, right):
    return lax.dot_general(
        left, right, (((0,), (0,)), ((), ())), preferred_element_type=jnp.float32
    )


def local_general(
    tokens,
    cotangent,
    gain_attn,
    gain_ffn,
    query_key_value_weight,
    w_out,
    w_gate,
    w_up,
    w_down,
    pair_block,
):
    token_rows = tokens.shape[0]
    query_columns = QUERY_HEADS * HEAD_SIZE
    key_value_columns = KEY_VALUE_HEADS * HEAD_SIZE
    group_count = QUERY_HEADS // KEY_VALUE_HEADS
    score_scale = 1.0 / math.sqrt(HEAD_SIZE)
    ff_cols = w_gate.shape[1]
    key_pos, own_pos = positions(pair_block, token_rows)
    query_pos = jnp.tile(own_pos, group_count)
    inputs_f = tokens.astype(jnp.float32)
    qkv_full, out_full = (
        lax.all_gather(query_key_value_weight, "fsdp", axis=0, tiled=True),
        lax.all_gather(w_out, "fsdp", axis=0, tiled=True),
    )
    normed_one_b = rms_norm(inputs_f, gain_attn).astype(jnp.bfloat16)
    projected_rows = jnp.dot(normed_one_b, qkv_full, preferred_element_type=jnp.float32)
    query_raw = projected_rows[:, :query_columns].reshape(token_rows, QUERY_HEADS, HEAD_SIZE)
    unrotated_key = projected_rows[:, query_columns : query_columns + key_value_columns].reshape(
        token_rows, KEY_VALUE_HEADS, HEAD_SIZE
    )
    query_b = (
        apply_rotation(query_raw, own_pos).astype(jnp.bfloat16).reshape(token_rows, query_columns)
    )
    keys_b = (
        apply_rotation(unrotated_key, own_pos)
        .astype(jnp.bfloat16)
        .reshape(token_rows, key_value_columns)
    )
    values_b = projected_rows[:, query_columns + key_value_columns :].astype(jnp.bfloat16)
    every_key, every_value = (
        lax.all_gather(keys_b, "ctx", axis=0, tiled=True),
        lax.all_gather(values_b, "ctx", axis=0, tiled=True),
    )
    query_grp = to_groups(query_b, group_count)
    key_blocks, value_blocks, pos_blocks = split_keys(every_key, every_value, key_pos)

    def forward_step(carry, block_in):
        run_max, run_total, weighted = carry
        key_block, value_block, block_pos = block_in
        causal = block_pos[None, None, :] <= query_pos[None, :, None]
        scores = (
            jnp.einsum("hqd,khd->hqk", query_grp, key_block, preferred_element_type=jnp.float32)
            * score_scale
        )
        scores = jnp.where(causal, scores, -1e30)
        new_max = jnp.maximum(run_max, jnp.max(scores, axis=-1))
        exp_scores = jnp.where(causal, jnp.exp(scores - new_max[..., None]), 0.0)
        fading = jnp.exp(run_max - new_max)
        run_total = run_total * fading + jnp.sum(exp_scores, axis=-1)
        weighted = weighted * fading[..., None] + jnp.einsum(
            "hqk,khd->hqd",
            exp_scores.astype(jnp.bfloat16),
            value_block,
            preferred_element_type=jnp.float32,
        )
        return ((new_max, run_total, weighted), None)

    initial_maximum = jnp.full((KEY_VALUE_HEADS, group_count * token_rows), -1e30, jnp.float32)
    initial_total = jnp.zeros((KEY_VALUE_HEADS, group_count * token_rows), jnp.float32)
    initial_weighted = jnp.zeros(
        (KEY_VALUE_HEADS, group_count * token_rows, HEAD_SIZE), jnp.float32
    )
    final_carry, ignored = lax.scan(
        forward_step,
        (initial_maximum, initial_total, initial_weighted),
        (key_blocks, value_blocks, pos_blocks),
    )
    run_max, run_total, weighted = final_carry
    log_total = run_max + jnp.log(run_total)
    attn_grp = weighted / run_total[..., None]
    attended_b = from_groups(attn_grp.astype(jnp.bfloat16), group_count)
    mid_rows = inputs_f + jnp.dot(attended_b, out_full, preferred_element_type=jnp.float32)
    gate_full, up_full, down_full = (
        lax.all_gather(w_gate, "fsdp", axis=0, tiled=True),
        lax.all_gather(w_up, "fsdp", axis=0, tiled=True),
        lax.all_gather(w_down, "fsdp", axis=0, tiled=True),
    )
    normed_two_b = rms_norm(mid_rows, gain_ffn).astype(jnp.bfloat16)
    gate_val = jnp.dot(normed_two_b, gate_full, preferred_element_type=jnp.float32)
    up_val = jnp.dot(normed_two_b, up_full, preferred_element_type=jnp.float32)
    hidden_b = (jax.nn.silu(gate_val) * up_val).astype(jnp.bfloat16)
    output_f = mid_rows + jnp.dot(hidden_b, down_full, preferred_element_type=jnp.float32)
    result = output_f.astype(jnp.bfloat16)
    normed_one_x, attended_x, normed_two_x, hidden_x = (
        lax.all_to_all(normed_one_b, "fsdp", split_axis=1, concat_axis=0, tiled=True),
        lax.all_to_all(attended_b, "fsdp", split_axis=1, concat_axis=0, tiled=True),
        lax.all_to_all(normed_two_b, "fsdp", split_axis=1, concat_axis=0, tiled=True),
        lax.all_to_all(hidden_b, "fsdp", split_axis=1, concat_axis=0, tiled=True),
    )
    grad_out_f = cotangent.astype(jnp.float32)
    gate_back, up_back, down_back = (
        lax.all_gather(w_gate, "fsdp", axis=0, tiled=True),
        lax.all_gather(w_up, "fsdp", axis=0, tiled=True),
        lax.all_gather(w_down, "fsdp", axis=0, tiled=True),
    )
    grad_hidden = contract_last(cotangent, down_back)
    ignored, ffn_back = jax.vjp(
        lambda gate_in, up_in: jax.nn.silu(gate_in) * up_in, gate_val, up_val
    )
    grad_gate_f, grad_up_f = ffn_back(grad_hidden)
    grad_gate_b = grad_gate_f.astype(jnp.bfloat16)
    grad_up_b = grad_up_f.astype(jnp.bfloat16)
    grad_normed_two = contract_last(grad_gate_b, gate_back) + contract_last(grad_up_b, up_back)
    ignored, norm_two_back = jax.vjp(rms_norm, mid_rows, gain_ffn)
    grad_mid_part, gain_ffn_part = norm_two_back(grad_normed_two)
    grad_mid = grad_out_f + grad_mid_part
    gate_up_b = jnp.concatenate([grad_gate_b, grad_up_b], axis=1)
    qkv_back, out_back = (
        lax.all_gather(query_key_value_weight, "fsdp", axis=0, tiled=True),
        lax.all_gather(w_out, "fsdp", axis=0, tiled=True),
    )
    grad_proj_b = grad_mid.astype(jnp.bfloat16)
    grad_att_b = contract_last(grad_proj_b, out_back).astype(jnp.bfloat16)
    grad_att_grp = to_groups(grad_att_b, group_count)
    delta_rows = jnp.sum(grad_att_grp.astype(jnp.float32) * attn_grp, axis=-1)

    def backward_step(grad_query, block_in):
        key_block, value_block, block_pos = block_in
        causal = block_pos[None, None, :] <= query_pos[None, :, None]
        scores = (
            jnp.einsum("hqd,khd->hqk", query_grp, key_block, preferred_element_type=jnp.float32)
            * score_scale
        )
        probs = jnp.where(causal, jnp.exp(scores - log_total[..., None]), 0.0)
        grad_values = jnp.einsum(
            "hqk,hqd->khd",
            probs.astype(jnp.bfloat16),
            grad_att_grp,
            preferred_element_type=jnp.float32,
        )
        grad_probs = jnp.einsum(
            "hqd,khd->hqk", grad_att_grp, value_block, preferred_element_type=jnp.float32
        )
        grad_scores = (probs * (grad_probs - delta_rows[..., None])).astype(jnp.bfloat16)
        grad_query = grad_query + score_scale * jnp.einsum(
            "hqk,khd->hqd", grad_scores, key_block, preferred_element_type=jnp.float32
        )
        grad_keys = score_scale * jnp.einsum(
            "hqk,hqd->khd", grad_scores, query_grp, preferred_element_type=jnp.float32
        )
        return (grad_query, (grad_keys, grad_values))

    grad_query_grp, key_grads = lax.scan(
        backward_step,
        jnp.zeros((KEY_VALUE_HEADS, group_count * token_rows, HEAD_SIZE), jnp.float32),
        (key_blocks, value_blocks, pos_blocks),
    )
    total_keys = key_pos.shape[0]
    grad_keys_all = key_grads[0].reshape(total_keys, key_value_columns)
    grad_values_all = key_grads[1].reshape(total_keys, key_value_columns)
    key_sums, summed_values = (
        lax.psum_scatter(
            grad_keys_all.astype(jnp.bfloat16), "ctx", scatter_dimension=0, tiled=True
        ).astype(jnp.float32),
        lax.psum_scatter(
            grad_values_all.astype(jnp.bfloat16), "ctx", scatter_dimension=0, tiled=True
        ).astype(jnp.float32),
    )
    grad_query_rows = from_groups(grad_query_grp, group_count).reshape(
        token_rows, QUERY_HEADS, HEAD_SIZE
    )
    ignored, query_rope_back = jax.vjp(lambda vectors: apply_rotation(vectors, own_pos), query_raw)
    ignored, key_rotation_backward = jax.vjp(
        lambda vectors: apply_rotation(vectors, own_pos), unrotated_key
    )
    grad_query_raw = query_rope_back(grad_query_rows)[0]
    unrotated_key_gradient = key_rotation_backward(
        key_sums.reshape(token_rows, KEY_VALUE_HEADS, HEAD_SIZE)
    )[0]
    grad_projected_b = jnp.concatenate(
        [
            grad_query_raw.reshape(token_rows, query_columns),
            unrotated_key_gradient.reshape(token_rows, key_value_columns),
            summed_values,
        ],
        axis=1,
    ).astype(jnp.bfloat16)
    grad_normed_one = contract_last(grad_projected_b, qkv_back)
    ignored, norm_one_back = jax.vjp(rms_norm, inputs_f, gain_attn)
    grad_in_part, gain_attn_part = norm_one_back(grad_normed_one)
    grad_input = grad_mid + grad_in_part
    cot_group, gate_up_group, projected_group, proj_group = (
        lax.all_gather(cotangent, "fsdp", axis=0, tiled=True),
        lax.all_gather(gate_up_b, "fsdp", axis=0, tiled=True),
        lax.all_gather(grad_projected_b, "fsdp", axis=0, tiled=True),
        lax.all_gather(grad_proj_b, "fsdp", axis=0, tiled=True),
    )
    qkv_part = contract_first(normed_one_x, projected_group)
    out_part = contract_first(attended_x, proj_group)
    gate_up_part = contract_first(normed_two_x, gate_up_group)
    gate_part = gate_up_part[:, :ff_cols]
    up_part = gate_up_part[:, ff_cols:]
    down_part = contract_first(hidden_x, cot_group)
    grad_qkv, grad_out, grad_down = (
        lax.psum_scatter(
            qkv_part.astype(jnp.bfloat16), "ctx", scatter_dimension=0, tiled=True
        ).astype(jnp.float32),
        lax.psum_scatter(
            out_part.astype(jnp.bfloat16), "ctx", scatter_dimension=0, tiled=True
        ).astype(jnp.float32),
        lax.psum_scatter(
            down_part.astype(jnp.bfloat16), "ctx", scatter_dimension=0, tiled=True
        ).astype(jnp.float32),
    )
    grad_gate, grad_up = (
        lax.psum_scatter(
            gate_part.astype(jnp.bfloat16), "ctx", scatter_dimension=0, tiled=True
        ).astype(jnp.float32),
        lax.psum_scatter(
            up_part.astype(jnp.bfloat16), "ctx", scatter_dimension=0, tiled=True
        ).astype(jnp.float32),
    )
    grad_gain_attn, grad_gain_ffn = (
        lax.psum_scatter(gain_attn_part, ("ctx", "fsdp"), scatter_dimension=0, tiled=True),
        lax.psum_scatter(gain_ffn_part, ("ctx", "fsdp"), scatter_dimension=0, tiled=True),
    )
    return (
        result,
        grad_input,
        grad_gain_attn,
        grad_gain_ffn,
        grad_qkv,
        grad_out,
        grad_gate,
        grad_up,
        grad_down,
    )


MESH = pl.DeviceIdType.MESH
ACROSS_X, ACROSS_Y, ACROSS_CORE = 2, 4, 1
BLOCK = 256


class Links:
    def __init__(self, sems, ctx, fsdp):
        self.send_sem, self.recv_sem, self.local_sem = sems
        self.ctx, self.fsdp = ctx, fsdp
        self.remote = self.locals = 0

    def to(self, src, dst, ctx, fsdp):
        index, self.remote = self.remote, self.remote + 1
        return pltpu.make_async_remote_copy(
            src_ref=src,
            dst_ref=dst,
            send_sem=self.send_sem.at[index],
            recv_sem=self.recv_sem.at[index],
            device_id=(ctx, fsdp),
            device_id_type=MESH,
        )

    def plane(self, src, dst, flip):
        return self.to(src, dst, lax.bitwise_xor(self.ctx, flip), self.fsdp)

    def column(self, src, dst, flip):
        return self.to(src, dst, self.ctx, lax.bitwise_xor(self.fsdp, flip))

    def here(self, src, dst):
        index, self.locals = self.locals, self.locals + 1
        return pltpu.make_async_copy(src, dst, self.local_sem.at[index])


def greet(ctx, fsdp):
    barrier = pltpu.get_barrier_semaphore()
    partners = [(lax.bitwise_xor(ctx, flip), fsdp) for flip in (1, 2, 4)]
    partners += [(ctx, lax.bitwise_xor(fsdp, flip)) for flip in (1, 2, 3)]
    for partner in partners:
        pl.semaphore_signal(barrier, inc=1, device_id=partner, device_id_type=MESH)
    pl.semaphore_wait(barrier, len(partners))


class PlaneGather:
    def __init__(self, links, blocks, halves):
        self.links, self.blocks, self.halves = links, blocks, halves
        self.ctx = links.ctx
        self.sent = []
        self.cores = []

    def _go(self, copies):
        for copy in copies:
            copy.start()
        self.sent += copies
        return copies

    def _core(self, index):
        refs = self.blocks(index)
        self.cores += self._go([self.links.plane(r, r, ACROSS_CORE) for r in refs])

    def begin(self):
        refs = self.blocks(self.ctx)
        self.from_x = self._go([self.links.plane(r, r, ACROSS_X) for r in refs])
        self.from_y = self._go([self.links.plane(r, r, ACROSS_Y) for r in refs])
        self._core(self.ctx)

    def forward(self):
        index = lax.bitwise_xor(self.ctx, ACROSS_X)
        for copy in self.from_x:
            copy.wait_recv()
        refs = self.halves(index, 0)
        self.corner = self._go([self.links.plane(r, r, ACROSS_Y) for r in refs])
        self._core(index)
        index = lax.bitwise_xor(self.ctx, ACROSS_Y)
        for copy in self.from_y:
            copy.wait_recv()
        refs = self.halves(index, 1)
        self.corner += self._go([self.links.plane(r, r, ACROSS_X) for r in refs])
        self._core(index)

    def finish(self):
        for copy in self.corner:
            copy.wait_recv()
        self._core(lax.bitwise_xor(self.ctx, ACROSS_X | ACROSS_Y))
        for copy in self.cores:
            copy.wait_recv()

    def drain(self):
        for copy in self.sent:
            copy.wait_send()


class PlaneScatter:
    def __init__(self, links, part, core_rx, half_rx, side_rx):
        self.links, self.part = links, part
        self.core_rx, self.half_rx, self.side_rx = core_rx, half_rx, side_rx
        self.chip, self.core = links.ctx // 2, lax.rem(links.ctx, 2)
        self.sent = []
        self.from_core = {}

    def order(self):
        return [(flip, lax.bitwise_xor(self.chip, flip)) for flip in (3, 1, 2, 0)]

    def _go(self, copy):
        copy.start()
        self.sent.append(copy)
        return copy

    def give(self, flip, chip):
        self.from_core[flip] = self._go(
            self.links.plane(
                self.part.at[2 * chip + 1 - self.core], self.core_rx.at[chip], ACROSS_CORE
            )
        )

    def _summed(self, flip):
        chip = lax.bitwise_xor(self.chip, flip)
        self.from_core[flip].wait_recv()
        mine = self.part.at[2 * chip + self.core]
        total = mine[...].astype(jnp.float32) + self.core_rx[chip].astype(jnp.float32)
        return mine, total

    def run(self):
        half = self.half_rx.shape[1]
        mine, total = self._summed(3)
        mine[...] = total.astype(jnp.bfloat16)
        top = self._go(
            self.links.plane(mine.at[pl.ds(0, half)], self.half_rx.at[0], ACROSS_Y)
        )
        bottom = self._go(
            self.links.plane(mine.at[pl.ds(half, half)], self.half_rx.at[1], ACROSS_X)
        )
        sides = []
        for flip, copy, slot in ((1, top, 0), (2, bottom, 1)):
            mine, total = self._summed(flip)
            mine[...] = total.astype(jnp.bfloat16)
            copy.wait_recv()
            rows = pl.ds(slot * half, half)
            mine[rows] = (
                total[slot * half : (slot + 1) * half]
                + self.half_rx[slot].astype(jnp.float32)
            ).astype(jnp.bfloat16)
            sides.append(
                self._go(
                    self.links.plane(
                        mine, self.side_rx.at[slot], ACROSS_X if slot == 0 else ACROSS_Y
                    )
                )
            )
        mine, total = self._summed(0)
        for slot, copy in enumerate(sides):
            copy.wait_recv()
            total = total + self.side_rx[slot].astype(jnp.float32)
        return total

    def drain(self):
        for copy in self.sent:
            copy.wait_send()


def head_of(ctx, fsdp):
    return lax.bitwise_xor(ctx, 4 * lax.rem(fsdp, 2))


def out_plane(ctx, fsdp):
    return lax.bitwise_xor(ctx // 2, 2 * lax.rem(fsdp, 2))


def turn(vectors, cos_rows, sin_rows, sign):
    return vectors * cos_rows + sign * pltpu.roll(vectors, HEAD_SIZE // 2, 1) * sin_rows


def attention_kernel(
    tokens_ref,
    cot_ref,
    gain_one_ref,
    gain_two_ref,
    qkv_w_ref,
    out_w_ref,
    gate_ref,
    up_ref,
    cos_ref,
    sin_ref,
    pos_col_ref,
    pos_row_ref,
    mid_ref,
    normed_two_group,
    cot_group,
    gate_w,
    up_w,
    qkv_out,
    attended_out,
    normed_one_out,
    w_head_out,
    out_head_out,
    normed,
    w_head,
    out_head,
    qkv,
    attended,
    part,
    core_rx,
    half_rx,
    side_rx,
    normed_two,
    send_sem,
    recv_sem,
    local_sem,
):
    f32, bf16 = jnp.float32, jnp.bfloat16
    ctx, fsdp = lax.axis_index("ctx"), lax.axis_index("fsdp")
    links = Links((send_sem, recv_sem, local_sem), ctx, fsdp)
    rows, width = tokens_ref.shape
    depth = qkv_w_ref.shape[0]
    head_columns = out_head.shape[0]
    n_ctx, n_fsdp = normed.shape[0], width // depth
    seq_rows = n_ctx * rows
    hidden = gate_w.shape[2]
    strip = hidden // n_ctx
    depth_blocks = gate_ref.shape[0]
    query_columns = QUERY_HEADS * HEAD_SIZE
    key_columns = KEY_VALUE_HEADS * HEAD_SIZE
    score_scale = 1.0 / math.sqrt(HEAD_SIZE)
    finals = []

    greet(ctx, fsdp)

    my_rows = pl.ds(pl.multiple_of(fsdp * depth, depth), depth)

    def head_parts(head):
        starts = (
            (head * head_columns, head_columns, 0),
            (query_columns + head * HEAD_SIZE, HEAD_SIZE, head_columns),
            (query_columns + key_columns + head * HEAD_SIZE, HEAD_SIZE, head_columns + HEAD_SIZE),
        )
        for start, size, place in starts:
            yield (
                qkv_w_ref.at[:, pl.ds(pl.multiple_of(start, HEAD_SIZE), size)],
                w_head.at[my_rows, pl.ds(place, size)],
            )

    head_copies = []
    for flip in (1, 2, 3):
        for src, dst in head_parts(head_of(ctx, lax.bitwise_xor(fsdp, flip))):
            head_copies.append(links.column(src, dst, flip))
    own_head = [links.here(src, dst) for src, dst in head_parts(head_of(ctx, fsdp))]
    for copy in head_copies + own_head:
        copy.start()

    inputs = tokens_ref[...].astype(f32)
    scale = lax.rsqrt(jnp.mean(inputs * inputs, axis=-1, keepdims=True) + norm_eps)
    normed[ctx] = (inputs * scale * gain_one_ref[...]).astype(bf16)
    half = rows // 2
    gather = PlaneGather(
        links,
        lambda j: [normed.at[j]],
        lambda j, which: [normed.at[j, pl.ds(which * half, half)]],
    )
    gather.begin()
    gather.forward()
    gather.finish()
    finals.append(links.here(normed, normed_one_out))
    finals[-1].start()
    for copy in own_head:
        copy.wait()
    for copy in head_copies:
        copy.wait_recv()

    out_block = out_w_ref.at[
        pl.ds(pl.multiple_of(lax.rem(ctx, 2) * head_columns, head_columns), head_columns)
    ]
    out_sends = []
    slot = links.remote
    out_slot = links.column(out_block, out_head, 1)
    out_home = links.here(out_block, out_head)
    home = out_plane(ctx, fsdp) == fsdp
    for target in range(n_fsdp):
        wanted = (out_plane(ctx, jnp.int32(target)) == fsdp) & (fsdp != target)
        copy = pltpu.make_async_remote_copy(
            src_ref=out_block,
            dst_ref=out_head,
            send_sem=send_sem.at[links.remote],
            recv_sem=recv_sem.at[slot],
            device_id=(ctx, jnp.int32(target)),
            device_id_type=MESH,
        )
        links.remote += 1
        out_sends.append((wanted, copy))

        @pl.when(wanted)
        def _(copy=copy):
            copy.start()

    @pl.when(home)
    def _():
        out_home.start()

    block_rows_of = pl.ds(fsdp * depth_blocks, depth_blocks)

    def strips(target):
        cols = pl.ds(pl.multiple_of(target * hidden + ctx * strip, strip), strip)
        place = pl.ds(pl.multiple_of(ctx * strip, strip), strip)
        for source, dest in ((gate_ref, gate_w), (up_ref, up_w)):
            yield source.at[:, :, cols], dest.at[block_rows_of, :, place]

    strip_copies = []
    for flip in (1, 2, 3):
        for src, dst in strips(lax.bitwise_xor(fsdp, flip)):
            strip_copies.append(links.column(src, dst, flip))
    own_strips = [links.here(src, dst) for src, dst in strips(fsdp)]
    for copy in strip_copies + own_strips:
        copy.start()

    block_rows = 2 * rows

    def project(step, carry):
        at = pl.multiple_of(step * block_rows, block_rows)
        tile = normed[pl.ds(step * 2, 2)].reshape(block_rows, width)
        out = jnp.dot(tile, w_head[...], preferred_element_type=f32)
        cos_rows, sin_rows = cos_ref[pl.ds(at, block_rows)], sin_ref[pl.ds(at, block_rows)]
        for column in range(0, head_columns + HEAD_SIZE, HEAD_SIZE):
            turned = turn(out[:, column : column + HEAD_SIZE], cos_rows, sin_rows, 1.0)
            qkv[pl.ds(at, block_rows), pl.ds(column, HEAD_SIZE)] = turned.astype(bf16)
        column = head_columns + HEAD_SIZE
        qkv[pl.ds(at, block_rows), pl.ds(column, HEAD_SIZE)] = out[:, column:].astype(bf16)
        return carry

    lax.fori_loop(0, seq_rows // block_rows, project, 0)

    def attend(step, carry):
        at = pl.multiple_of(step * block_rows, block_rows)
        keys = qkv[:, pl.ds(head_columns, HEAD_SIZE)]
        values = qkv[:, pl.ds(head_columns + HEAD_SIZE, HEAD_SIZE)]
        causal = pos_row_ref[...] <= pos_col_ref[pl.ds(at, block_rows)]
        for column in range(0, head_columns, HEAD_SIZE):
            query = qkv[pl.ds(at, block_rows), pl.ds(column, HEAD_SIZE)]
            scores = contract_last(query, keys) * score_scale
            scores = jnp.where(causal, scores, -1e30)
            shifted = jnp.exp(scores - jnp.max(scores, axis=-1, keepdims=True))
            probs = shifted * (1.0 / jnp.sum(shifted, axis=-1, keepdims=True))
            mixed = jnp.dot(probs.astype(bf16), values, preferred_element_type=f32)
            attended[pl.ds(at, block_rows), pl.ds(column, HEAD_SIZE)] = mixed.astype(bf16)
        return carry

    lax.fori_loop(0, seq_rows // block_rows, attend, 0)

    @pl.when(home)
    def _():
        out_home.wait()

    @pl.when(jnp.logical_not(home))
    def _():
        out_slot.wait_recv()

    for src, dst in (
        (qkv, qkv_out),
        (attended, attended_out),
        (w_head, w_head_out),
        (out_head, out_head_out),
    ):
        finals.append(links.here(src, dst))
        finals[-1].start()

    scatter = PlaneScatter(links, part, core_rx, half_rx, side_rx)
    for flip, chip in scatter.order():
        at = pl.multiple_of(chip * block_rows, block_rows)
        out = jnp.dot(
            attended[pl.ds(at, block_rows)], out_head[...], preferred_element_type=f32
        )
        part[pl.ds(chip * 2, 2)] = out.astype(bf16).reshape(2, rows, width)
        scatter.give(flip, chip)
    mid = tokens_ref[...].astype(f32) + scatter.run()
    mid_ref[...] = mid
    mid_scale = lax.rsqrt(jnp.mean(mid * mid, axis=-1, keepdims=True) + norm_eps)
    normed_two[...] = (mid * mid_scale * gain_two_ref[...]).astype(bf16)

    group_rows = pl.ds(pl.multiple_of(fsdp * rows, rows), rows)
    group_copies = []
    for source, dest in ((normed_two, normed_two_group), (cot_ref, cot_group)):
        for flip in (1, 2, 3):
            group_copies.append(links.column(source, dest.at[group_rows], flip))
        finals.append(links.here(source, dest.at[group_rows]))
        finals[-1].start()
    for copy in group_copies:
        copy.start()

    for copy in own_strips:
        copy.wait()
    for copy in strip_copies:
        copy.wait_recv()

    def columns_of(j):
        place = pl.ds(pl.multiple_of(j * strip, strip), strip)
        return [gate_w.at[:, :, place], up_w.at[:, :, place]]

    def halves_of(j, which):
        place = pl.ds(pl.multiple_of(j * strip, strip), strip)
        blocks = gate_w.shape[0] // 2
        some = pl.ds(which * blocks, blocks)
        return [gate_w.at[some, :, place], up_w.at[some, :, place]]

    weights = PlaneGather(links, columns_of, halves_of)
    weights.begin()
    weights.forward()
    weights.finish()

    for copy in group_copies:
        copy.wait_recv()
    for copy in head_copies + strip_copies + group_copies:
        copy.wait_send()
    for wanted, copy in out_sends:

        @pl.when(wanted)
        def _(copy=copy):
            copy.wait_send()

    gather.drain()
    scatter.drain()
    weights.drain()
    for copy in finals:
        copy.wait()


def attention_forward(
    tokens, cotangent, gain_attn, gain_ffn, qkv_w, w_out, w_gate, w_up, cos, sin, key_pos
):
    f32, bf16 = jnp.float32, jnp.bfloat16
    n_ctx, n_fsdp = lax.axis_size("ctx"), lax.axis_size("fsdp")
    rows, width = tokens.shape
    depth = qkv_w.shape[0]
    hidden = w_gate.shape[1] // n_fsdp
    seq_rows = n_ctx * rows
    head_columns = QUERY_HEADS // KEY_VALUE_HEADS * HEAD_SIZE
    all_columns = head_columns + 2 * HEAD_SIZE
    vmem, hbm = pl.BlockSpec(memory_space=pltpu.VMEM), pl.BlockSpec(memory_space=pl.ANY)
    shape = jax.ShapeDtypeStruct
    return pl.pallas_call(
        attention_kernel,
        name="attention_forward",
        out_shape=[
            shape((rows, width), f32),
            shape((n_fsdp * rows, width), bf16),
            shape((n_fsdp * rows, width), bf16),
            shape((width // BLOCK, BLOCK, hidden), bf16),
            shape((width // BLOCK, BLOCK, hidden), bf16),
            shape((seq_rows, all_columns), bf16),
            shape((seq_rows, head_columns), bf16),
            shape((n_ctx, rows, width), bf16),
            shape((width, all_columns), bf16),
            shape((head_columns, width), bf16),
        ],
        in_specs=[vmem] * 4 + [hbm] * 4 + [vmem] * 4,
        out_specs=[vmem] + [hbm] * 9,
        scratch_shapes=[
            pltpu.VMEM((n_ctx, rows, width), bf16),
            pltpu.VMEM((width, all_columns), bf16),
            pltpu.VMEM((head_columns, width), bf16),
            pltpu.VMEM((seq_rows, all_columns), bf16),
            pltpu.VMEM((seq_rows, head_columns), bf16),
            pltpu.VMEM((n_ctx, rows, width), bf16),
            pltpu.VMEM((n_ctx // 2, rows, width), bf16),
            pltpu.VMEM((2, rows // 2, width), bf16),
            pltpu.VMEM((2, rows, width), bf16),
            pltpu.VMEM((rows, width), bf16),
            pltpu.SemaphoreType.DMA((80,)),
            pltpu.SemaphoreType.DMA((80,)),
            pltpu.SemaphoreType.DMA((24,)),
        ],
        compiler_params=pltpu.CompilerParams(
            collective_id=1, has_side_effects=True, vmem_limit_bytes=58 * 2**20
        ),
    )(
        tokens,
        cotangent,
        gain_attn[None],
        gain_ffn[None],
        qkv_w,
        w_out,
        w_gate.reshape(depth // BLOCK, BLOCK, -1),
        w_up.reshape(depth // BLOCK, BLOCK, -1),
        cos,
        sin,
        key_pos[:, None],
        key_pos[None],
    )


class ChipScatter:
    def __init__(self, links, part, halves, sides):
        self.links, self.part, self.halves, self.sides = links, part, halves, sides
        self.chip = links.ctx // 2
        self.sent = []

    def _go(self, copy):
        copy.start()
        self.sent.append(copy)
        return copy

    def begin(self):
        corner = self.part(lax.bitwise_xor(self.chip, 3))
        half = corner.shape[0] // 2
        self.half = half
        self.corner = [
            self._go(self.links.plane(corner.at[pl.ds(0, half)], self.halves[0], ACROSS_Y)),
            self._go(self.links.plane(corner.at[pl.ds(half, half)], self.halves[1], ACROSS_X)),
        ]

    def middle(self):
        self.side = []
        for slot, (flip, across) in enumerate(((1, ACROSS_X), (2, ACROSS_Y))):
            mine = self.part(lax.bitwise_xor(self.chip, flip))
            self.corner[slot].wait_recv()
            rows = mine.at[pl.ds(slot * self.half, self.half)]
            rows[...] = (
                rows[...].astype(jnp.float32) + self.halves[slot][...].astype(jnp.float32)
            ).astype(jnp.bfloat16)
            self.side.append(self._go(self.links.plane(mine, self.sides[slot], across)))

    def finish(self):
        mine = self.part(self.chip)
        for copy in self.side:
            copy.wait_recv()
        mine[...] = (
            mine[...].astype(jnp.float32)
            + self.sides[0][...].astype(jnp.float32)
            + self.sides[1][...].astype(jnp.float32)
        ).astype(jnp.bfloat16)
        return mine

    def drain(self):
        for copy in self.sent:
            copy.wait_send()


def feed_forward_kernel(
    mid_ref,
    cot_ref,
    gain_ref,
    normed_ref,
    cots_ref,
    gate_hbm,
    up_hbm,
    down_hbm,
    result_ref,
    grad_mid_ref,
    grad_proj_ref,
    down_sum,
    gate_sum,
    up_part,
    gate_v,
    up_v,
    down_v,
    hidden,
    grad_gate,
    grad_up,
    other_normed,
    other_cots,
    other_hidden,
    other_gate,
    other_up,
    stage,
    landed,
    send_sem,
    recv_sem,
    local_sem,
    load_sem,
    free_sem,
):
    f32, bf16 = jnp.float32, jnp.bfloat16
    ctx, fsdp = lax.axis_index("ctx"), lax.axis_index("fsdp")
    links = Links((send_sem, recv_sem, local_sem), ctx, fsdp)
    core = lax.rem(ctx, 2)
    rows, width = mid_ref.shape
    group_rows = normed_ref.shape[0]
    blocks = gate_v.shape[0]
    hidden_units = blocks * BLOCK
    half_units = hidden_units // 2
    n_fsdp = group_rows // rows

    def loads(j):
        cols = pl.ds(pl.multiple_of(j * BLOCK, BLOCK), BLOCK)
        return (
            pltpu.make_async_copy(
                gate_hbm.at[:, :, cols], gate_v.at[:, :, cols], load_sem.at[0, j]
            ),
            pltpu.make_async_copy(up_hbm.at[:, :, cols], up_v.at[:, :, cols], load_sem.at[1, j]),
            pltpu.make_async_copy(down_hbm.at[j], down_v.at[j], load_sem.at[2, j]),
        )

    for j in range(blocks):
        for copy in loads(j):
            copy.start()

    greet(ctx, fsdp)

    swaps = [
        links.plane(normed_ref, other_normed, ACROSS_CORE),
        links.plane(cots_ref, other_cots, ACROSS_CORE),
    ]
    for copy in swaps:
        copy.start()

    def activate(j, carry):
        for copy in loads(j):
            copy.wait()
        cols = pl.ds(pl.multiple_of(j * BLOCK, BLOCK), BLOCK)
        normed = normed_ref[...]
        gate = jnp.dot(
            normed, gate_v[:, :, cols].reshape(width, BLOCK), preferred_element_type=f32
        )
        up = jnp.dot(normed, up_v[:, :, cols].reshape(width, BLOCK), preferred_element_type=f32)
        grad_hidden = contract_last(cots_ref[...], down_v[j])
        sig = 1.0 / (1.0 + jnp.exp(-gate))
        silu = gate * sig
        hidden[:, cols] = (silu * up).astype(bf16)
        grad_gate[:, cols] = (grad_hidden * up * (sig * (1.0 + gate * (1.0 - sig)))).astype(bf16)
        grad_up[:, cols] = (grad_hidden * silu).astype(bf16)
        return carry

    lax.fori_loop(0, blocks, activate, 0)

    theirs = pl.ds(pl.multiple_of((1 - core) * half_units, half_units), half_units)
    acts = [
        links.plane(grad_gate.at[:, theirs], other_gate, ACROSS_CORE),
        links.plane(grad_up.at[:, theirs], other_up, ACROSS_CORE),
    ]
    for pair in range(blocks // 2):
        cols = pl.ds(pl.multiple_of((2 * pair + 1 - core) * BLOCK, BLOCK), BLOCK)
        acts.append(
            links.plane(
                hidden.at[:, cols], other_hidden.at[:, pl.ds(pair * BLOCK, BLOCK)], ACROSS_CORE
            )
        )
    for copy in acts:
        copy.start()

    piece = 2 * BLOCK
    group = []
    for n in range(width // piece):
        cols = pl.ds(n * piece, piece)
        some = pl.ds(n * 2, 2)
        back = contract_last(grad_gate[...], gate_v[some].reshape(piece, hidden_units))
        back = back + contract_last(grad_up[...], up_v[some].reshape(piece, hidden_units))
        stage[1, :, :, cols] = back.astype(bf16).reshape(n_fsdp, rows, piece)
        down = jnp.dot(
            hidden[...],
            down_v[:, :, cols].reshape(hidden_units, piece),
            preferred_element_type=f32,
        )
        stage[0, :, :, cols] = down.astype(bf16).reshape(n_fsdp, rows, piece)
        for which in (1, 0):
            for flip in (1, 2, 3):
                target = lax.bitwise_xor(fsdp, flip)
                copy = links.column(
                    stage.at[which, target, :, cols], landed.at[which, flip - 1, :, cols], flip
                )
                copy.start()
                group.append(copy)

    for flip in (ACROSS_X, ACROSS_Y):
        pl.semaphore_signal(
            free_sem,
            inc=1,
            device_id=(lax.bitwise_xor(ctx, flip), fsdp),
            device_id_type=MESH,
        )

    def rows_dot(left, right):
        return lax.dot_general(
            left, right, (((0,), (0,)), ((), ())), preferred_element_type=f32
        )

    for copy in swaps + acts:
        copy.wait_recv()
    down_rows = 4

    def down_block(step, carry):
        pair, part = step // 2, lax.rem(step, 2)
        cols = pl.ds(pl.multiple_of(part * (width // 2), width // 2), width // 2)
        own = pl.ds(pl.multiple_of((2 * pair + core) * BLOCK, BLOCK), BLOCK)
        other = pl.ds(pl.multiple_of(pair * BLOCK, BLOCK), BLOCK)
        total = rows_dot(hidden[:, own], cots_ref[:, cols]) + rows_dot(
            other_hidden[:, other], other_cots[:, cols]
        )
        gate_v[pair, :, cols] = total.astype(bf16)
        return carry

    lax.fori_loop(0, blocks, down_block, 0)
    pl.semaphore_wait(free_sem, 2)
    down_scatter = ChipScatter(
        links,
        lambda chip: gate_v.at[chip],
        [down_v.at[0, pl.ds(0, BLOCK // 2)], down_v.at[0, pl.ds(BLOCK // 2, BLOCK // 2)]],
        [down_v.at[1], down_v.at[2]],
    )
    down_scatter.begin()

    mine = pl.ds(pl.multiple_of(core * half_units, half_units), half_units)

    def gradient_into(own_grad, other_grad, place):
        def block(b, carry):
            cols = pl.ds(pl.multiple_of(b * BLOCK, BLOCK), BLOCK)
            total = rows_dot(normed_ref[:, cols], own_grad[:, mine]) + rows_dot(
                other_normed[:, cols], other_grad[...]
            )
            low = total.astype(bf16)
            plane, chip = b // 2, 2 * lax.rem(b, 2)
            at_row = pl.ds(pl.multiple_of((plane // 2) * (BLOCK // 2), BLOCK // 2), BLOCK // 2)
            at_col = pl.ds(
                pl.multiple_of(lax.rem(plane, 2) * (width // 2), width // 2), width // 2
            )
            place[chip, at_row, at_col] = low[: BLOCK // 2]
            place[chip + 1, at_row, at_col] = low[BLOCK // 2 :]
            return carry

        lax.fori_loop(0, blocks, block, 0)

    gate_place = gate_v.at[pl.ds(4, 4)]
    gradient_into(grad_gate, other_gate, gate_place)
    gate_scatter = ChipScatter(
        links,
        lambda chip: gate_v.at[4 + chip],
        [down_v.at[3, pl.ds(0, BLOCK // 2)], down_v.at[3, pl.ds(BLOCK // 2, BLOCK // 2)]],
        [down_v.at[4], down_v.at[5]],
    )
    down_scatter.middle()
    gate_scatter.begin()
    up_place = up_v.at[pl.ds(0, 4)]
    gradient_into(grad_up, other_up, up_place)
    up_copy = links.here(up_place, up_part)
    up_copy.start()
    gate_scatter.middle()
    down_copy = links.here(down_scatter.finish(), down_sum)
    down_copy.start()

    for copy in group:
        copy.wait_recv()
    mid = mid_ref[...]
    sums = []
    for which in (0, 1):
        total = stage[which, fsdp].astype(f32)
        for slot in range(n_fsdp - 1):
            total = total + landed[which, slot].astype(f32)
        sums.append(total)
    result_ref[...] = (mid + sums[0]).astype(bf16)
    scale = lax.rsqrt(jnp.mean(mid * mid, axis=-1, keepdims=True) + norm_eps)
    u = sums[1] * gain_ref[...]
    inner = jnp.mean(u * mid, axis=-1, keepdims=True)
    grad_mid = cot_ref[...].astype(f32) + scale * u - mid * (scale * scale * scale * inner)
    grad_mid_ref[...] = grad_mid
    grad_proj_ref[...] = grad_mid.astype(bf16)

    gate_copy = links.here(gate_scatter.finish(), gate_sum)
    gate_copy.start()
    for copy in swaps + acts + group:
        copy.wait_send()
    down_scatter.drain()
    gate_scatter.drain()
    for copy in (up_copy, down_copy, gate_copy):
        copy.wait()


def feed_forward(mid, cotangent, gain_ffn, normed_group, cot_group, gate_w, up_w, w_down):
    f32, bf16 = jnp.float32, jnp.bfloat16
    n_fsdp = lax.axis_size("fsdp")
    rows, width = mid.shape
    group_rows = normed_group.shape[0]
    units = w_down.shape[0] * BLOCK
    blocks = units // BLOCK
    vmem, hbm = pl.BlockSpec(memory_space=pltpu.VMEM), pl.BlockSpec(memory_space=pl.ANY)
    shape = jax.ShapeDtypeStruct
    return pl.pallas_call(
        feed_forward_kernel,
        name="feed_forward",
        out_shape=[
            shape((rows, width), bf16),
            shape((rows, width), f32),
            shape((rows, width), bf16),
            shape((BLOCK, width), bf16),
            shape((BLOCK, width), bf16),
            shape((blocks // 2, BLOCK, width), bf16),
        ],
        in_specs=[vmem] * 5 + [hbm] * 3,
        out_specs=[vmem] * 3 + [hbm] * 3,
        scratch_shapes=[
            pltpu.VMEM((width // BLOCK, BLOCK, units), bf16),
            pltpu.VMEM((width // BLOCK, BLOCK, units), bf16),
            pltpu.VMEM((blocks, BLOCK, width), bf16),
            pltpu.VMEM((group_rows, units), bf16),
            pltpu.VMEM((group_rows, units), bf16),
            pltpu.VMEM((group_rows, units), bf16),
            pltpu.VMEM((group_rows, width), bf16),
            pltpu.VMEM((group_rows, width), bf16),
            pltpu.VMEM((group_rows, units // 2), bf16),
            pltpu.VMEM((group_rows, units // 2), bf16),
            pltpu.VMEM((group_rows, units // 2), bf16),
            pltpu.VMEM((2, n_fsdp, rows, width), bf16),
            pltpu.VMEM((2, n_fsdp - 1, rows, width), bf16),
            pltpu.SemaphoreType.DMA((48,)),
            pltpu.SemaphoreType.DMA((48,)),
            pltpu.SemaphoreType.DMA((8,)),
            pltpu.SemaphoreType.DMA((3, blocks)),
            pltpu.SemaphoreType.REGULAR,
        ],
        compiler_params=pltpu.CompilerParams(
            collective_id=2, has_side_effects=True, vmem_limit_bytes=62 * 2**20
        ),
    )(mid, cotangent, gain_ffn[None], normed_group, cot_group, gate_w, up_w, w_down)


def attention_back_kernel(
    grad_proj_ref,
    grad_mid_ref,
    tokens_ref,
    gain_ref,
    w_head_ref,
    out_head_ref,
    qkv_ref,
    attended_ref,
    cos_ref,
    sin_ref,
    pos_col_ref,
    pos_row_ref,
    normed_hbm,
    gate_sum_hbm,
    up_part_hbm,
    grad_input_ref,
    qkv_sum,
    out_sum,
    gate_out,
    up_out,
    proj,
    normed,
    up_part,
    up_halves,
    up_sides,
    grad_att,
    grads,
    key_grad,
    value_grad,
    part,
    core_rx,
    half_rx,
    side_rx,
    out_stage,
    out_landed,
    head_stage,
    head_landed,
    send_sem,
    recv_sem,
    local_sem,
):
    f32, bf16 = jnp.float32, jnp.bfloat16
    ctx, fsdp = lax.axis_index("ctx"), lax.axis_index("fsdp")
    links = Links((send_sem, recv_sem, local_sem), ctx, fsdp)
    chip, core = ctx // 2, lax.rem(ctx, 2)
    n_ctx, rows, width = proj.shape
    n_fsdp = out_landed.shape[0]
    seq_rows = n_ctx * rows
    head_columns = out_head_ref.shape[0]
    strip_rows = out_landed.shape[1]
    score_scale = 1.0 / math.sqrt(HEAD_SIZE)
    loads = [links.here(normed_hbm, normed), links.here(up_part_hbm, up_part)]
    for copy in loads:
        copy.start()

    flips = [(a, b) for a in range(n_ctx) for b in range(n_fsdp) if a or b]
    barrier = pltpu.get_barrier_semaphore()
    for a, b in flips:
        pl.semaphore_signal(
            barrier,
            inc=1,
            device_id=(lax.bitwise_xor(ctx, a), lax.bitwise_xor(fsdp, b)),
            device_id_type=MESH,
        )
    pl.semaphore_wait(barrier, len(flips))

    proj[ctx] = grad_proj_ref[...]
    half = rows // 2
    gather = PlaneGather(
        links,
        lambda j: [proj.at[j]],
        lambda j, which: [proj.at[j, pl.ds(which * half, half)]],
    )
    gather.begin()

    def spread(source, dest):
        half_width = width // 2
        place = pl.ds(pl.multiple_of((2 * fsdp + core) * half_width, half_width), half_width)
        copies = []
        for a in (0, 1):
            for b in range(n_fsdp):
                plane = lax.bitwise_xor(fsdp, b)
                who = lax.bitwise_xor(core, a)
                at_row = (plane // 2) * (BLOCK // 2) + who * strip_rows
                block = source.at[
                    pl.ds(pl.multiple_of(at_row, strip_rows), strip_rows),
                    pl.ds(pl.multiple_of(lax.rem(plane, 2) * half_width, half_width), half_width),
                ]
                target = dest.at[:, place]
                if a or b:
                    copies.append(
                        links.to(block, target, lax.bitwise_xor(ctx, a), plane)
                    )
                else:
                    local = links.here(block, target)
                    locals_.append(local)
                    local.start()
        for copy in copies:
            copy.start()
        return copies

    locals_ = []
    gate_copies = spread(gate_sum_hbm, gate_out)
    gather.forward()
    loads[1].wait()
    up_scatter = ChipScatter(
        links,
        lambda q: up_part.at[q],
        [up_halves.at[0], up_halves.at[1]],
        [up_sides.at[0], up_sides.at[1]],
    )
    up_scatter.begin()
    gather.finish()

    total = jnp.zeros((head_columns, width), f32)
    for j in range(0, n_ctx, 2):
        total = total + lax.dot_general(
            attended_ref[pl.ds(j * rows, 2 * rows)],
            proj[pl.ds(j, 2)].reshape(2 * rows, width),
            (((0,), (0,)), ((), ())),
            preferred_element_type=f32,
        )
    out_stage[...] = total.astype(bf16).reshape(out_stage.shape)
    half_ctx = n_ctx // 2
    out_base = links.remote
    links.remote += n_fsdp
    out_copies = []
    plane = out_plane(ctx, fsdp)
    for j in range(half_ctx):
        target = half_ctx * core + j
        away = (target != ctx) | (plane != fsdp)
        index = links.remote
        links.remote += 1
        copy = pltpu.make_async_remote_copy(
            src_ref=out_stage.at[j],
            dst_ref=out_landed.at[fsdp],
            send_sem=send_sem.at[index],
            recv_sem=recv_sem.at[out_base + fsdp],
            device_id=(target, plane),
            device_id_type=MESH,
        )
        out_copies.append((away, copy))

        @pl.when(away)
        def _(copy=copy):
            copy.start()

    def out_source(source):
        head = 2 * fsdp + ctx // half_ctx
        return head_of(head, jnp.int32(source))

    own_out = links.here(out_stage.at[lax.rem(ctx, half_ctx)], out_landed.at[fsdp])
    own_is_mine = out_source(fsdp) == ctx

    @pl.when(own_is_mine)
    def _():
        own_out.start()

    def back(step, carry):
        at = pl.multiple_of(step * 2 * rows, 2 * rows)
        tile = proj[pl.ds(2 * step, 2)].reshape(2 * rows, width)
        grad_att[pl.ds(at, 2 * rows)] = contract_last(tile, out_head_ref[...]).astype(bf16)
        return carry

    lax.fori_loop(0, n_ctx // 2, back, 0)

    key_grad[...] = jnp.zeros_like(key_grad)
    value_grad[...] = jnp.zeros_like(value_grad)

    def attend(step, carry):
        at = pl.ds(pl.multiple_of(step * 2 * rows, 2 * rows), 2 * rows)
        keys = qkv_ref[:, pl.ds(head_columns, HEAD_SIZE)]
        values = qkv_ref[:, pl.ds(head_columns + HEAD_SIZE, HEAD_SIZE)]
        causal = pos_row_ref[...] <= pos_col_ref[at]
        for column in range(0, head_columns, HEAD_SIZE):
            cols = pl.ds(column, HEAD_SIZE)
            query, grad_mixed = qkv_ref[at, cols], grad_att[at, cols]
            scores = contract_last(query, keys) * score_scale
            scores = jnp.where(causal, scores, -1e30)
            shifted = jnp.exp(scores - jnp.max(scores, axis=-1, keepdims=True))
            probs = shifted * (1.0 / jnp.sum(shifted, axis=-1, keepdims=True))
            grad_probs = contract_last(grad_mixed, values)
            delta = jnp.sum(grad_probs * probs, axis=-1, keepdims=True)
            grad_scores = (probs * (grad_probs - delta)).astype(bf16)
            value_grad[...] += contract_first(probs.astype(bf16), grad_mixed)
            key_grad[...] += contract_first(grad_scores, query)
            grad_query = jnp.dot(grad_scores, keys, preferred_element_type=f32) * score_scale
            grads[at, cols] = turn(grad_query, cos_ref[at], sin_ref[at], -1.0).astype(bf16)
        return carry

    lax.fori_loop(0, n_ctx // 2, attend, 0)
    turned = turn(key_grad[...] * score_scale, cos_ref[...], sin_ref[...], -1.0)
    grads[:, pl.ds(head_columns, HEAD_SIZE)] = turned.astype(bf16)
    grads[:, pl.ds(head_columns + HEAD_SIZE, HEAD_SIZE)] = value_grad[...].astype(bf16)

    scatter = PlaneScatter(links, part, core_rx, half_rx, side_rx)
    for flip, q in scatter.order():
        at = pl.multiple_of(q * 2 * rows, 2 * rows)
        out = contract_last(grads[pl.ds(at, 2 * rows)], w_head_ref[...])
        part[pl.ds(2 * q, 2)] = out.astype(bf16).reshape(2, rows, width)
        scatter.give(flip, q)

    loads[0].wait()
    depth = n_ctx * strip_rows
    head_copies = []
    for b in (2, 1, 3, 0):
        plane = lax.bitwise_xor(fsdp, b)
        cols = pl.ds(pl.multiple_of(plane * depth, depth), depth)
        total = lax.dot_general(
            normed[:, :, cols].reshape(seq_rows, depth),
            grads[...],
            (((0,), (0,)), ((), ())),
            preferred_element_type=f32,
        )
        head_stage[plane] = total.astype(bf16).reshape(n_ctx, strip_rows, -1)
        for a in range(n_ctx):
            target = lax.bitwise_xor(ctx, a)
            if a or b:
                copy = links.to(
                    head_stage.at[plane, target], head_landed.at[ctx, fsdp], target, plane
                )
                head_copies.append(copy)
            else:
                copy = links.here(head_stage.at[plane, target], head_landed.at[ctx, fsdp])
                locals_.append(copy)
            copy.start()

    up_scatter.middle()
    grad_normed = scatter.run()
    inputs = tokens_ref[...].astype(f32)
    scale = lax.rsqrt(jnp.mean(inputs * inputs, axis=-1, keepdims=True) + norm_eps)
    u = grad_normed * gain_ref[...]
    inner = jnp.mean(u * inputs, axis=-1, keepdims=True)
    grad_input_ref[...] = (
        grad_mid_ref[...] + scale * u - inputs * (scale * scale * scale * inner)
    )
    up_copies = spread(up_scatter.finish(), up_out)

    for source in range(n_fsdp):
        arrival = pltpu.make_async_remote_copy(
            src_ref=out_stage.at[0],
            dst_ref=out_landed.at[source],
            send_sem=send_sem.at[out_base],
            recv_sem=recv_sem.at[out_base + source],
            device_id=(lax.bitwise_xor(ctx, 1), fsdp),
            device_id_type=MESH,
        )
        outside = (out_source(source) != ctx) | (fsdp != source)

        @pl.when(outside)
        def _(arrival=arrival):
            arrival.wait_recv()

    @pl.when(own_is_mine)
    def _():
        own_out.wait()

    total = out_landed[0].astype(f32)
    for source in range(1, n_fsdp):
        total = total + out_landed[source].astype(f32)
    out_sum[...] = total
    for copy in head_copies:
        copy.wait_recv()
    for copy in locals_:
        copy.wait()
    query_columns = QUERY_HEADS * HEAD_SIZE
    key_columns = KEY_VALUE_HEADS * HEAD_SIZE
    for head in range(KEY_VALUE_HEADS):
        total = head_landed[head, 0].astype(f32)
        for source in range(1, n_fsdp):
            total = total + head_landed[head ^ (4 * (source % 2)), source].astype(f32)
        qkv_sum[:, pl.ds(head * head_columns, head_columns)] = total[:, :head_columns]
        qkv_sum[:, pl.ds(query_columns + head * HEAD_SIZE, HEAD_SIZE)] = total[
            :, head_columns : head_columns + HEAD_SIZE
        ]
        qkv_sum[:, pl.ds(query_columns + key_columns + head * HEAD_SIZE, HEAD_SIZE)] = total[
            :, head_columns + HEAD_SIZE :
        ]
    for copy in gate_copies + up_copies:
        copy.wait_recv()
    for copy in gate_copies + up_copies + head_copies:
        copy.wait_send()
    for away, copy in out_copies:

        @pl.when(away)
        def _(copy=copy):
            copy.wait_send()

    gather.drain()
    scatter.drain()
    up_scatter.drain()


def attention_back(
    grad_proj,
    grad_mid,
    tokens,
    gain_attn,
    w_head,
    out_head,
    qkv,
    attended,
    cos,
    sin,
    key_pos,
    normed,
    gate_sum,
    up_part,
):
    f32, bf16 = jnp.float32, jnp.bfloat16
    n_ctx, n_fsdp = lax.axis_size("ctx"), lax.axis_size("fsdp")
    rows, width = tokens.shape
    seq_rows = n_ctx * rows
    strip_rows = width // (n_ctx * n_fsdp)
    head_columns, all_columns = attended.shape[1], qkv.shape[1]
    vmem, hbm = pl.BlockSpec(memory_space=pltpu.VMEM), pl.BlockSpec(memory_space=pl.ANY)
    shape = jax.ShapeDtypeStruct
    return pl.pallas_call(
        attention_back_kernel,
        name="attention_back",
        out_shape=[
            shape((rows, width), f32),
            shape((strip_rows, (QUERY_HEADS + 2 * KEY_VALUE_HEADS) * HEAD_SIZE), f32),
            shape((strip_rows, width), f32),
            shape((strip_rows, n_fsdp * width), bf16),
            shape((strip_rows, n_fsdp * width), bf16),
        ],
        in_specs=[vmem] * 12 + [hbm] * 3,
        out_specs=[vmem] * 3 + [hbm] * 2,
        scratch_shapes=[
            pltpu.VMEM((n_ctx, rows, width), bf16),
            pltpu.VMEM((n_ctx, rows, width), bf16),
            pltpu.VMEM(up_part.shape, bf16),
            pltpu.VMEM((2, BLOCK // 2, width), bf16),
            pltpu.VMEM((2, BLOCK, width), bf16),
            pltpu.VMEM((seq_rows, head_columns), bf16),
            pltpu.VMEM((seq_rows, all_columns), bf16),
            pltpu.VMEM((seq_rows, HEAD_SIZE), f32),
            pltpu.VMEM((seq_rows, HEAD_SIZE), f32),
            pltpu.VMEM((n_ctx, rows, width), bf16),
            pltpu.VMEM((n_ctx // 2, rows, width), bf16),
            pltpu.VMEM((2, rows // 2, width), bf16),
            pltpu.VMEM((2, rows, width), bf16),
            pltpu.VMEM((n_ctx // 2, strip_rows, width), bf16),
            pltpu.VMEM((n_fsdp, strip_rows, width), bf16),
            pltpu.VMEM((n_fsdp, n_ctx, strip_rows, all_columns), bf16),
            pltpu.VMEM((n_ctx, n_fsdp, strip_rows, all_columns), bf16),
            pltpu.SemaphoreType.DMA((96,)),
            pltpu.SemaphoreType.DMA((96,)),
            pltpu.SemaphoreType.DMA((8,)),
        ],
        compiler_params=pltpu.CompilerParams(
            collective_id=3, has_side_effects=True, vmem_limit_bytes=62 * 2**20
        ),
    )(
        grad_proj,
        grad_mid,
        tokens,
        gain_attn[None],
        w_head,
        out_head,
        qkv,
        attended,
        cos,
        sin,
        key_pos[:, None],
        key_pos[None],
        normed,
        gate_sum,
        up_part,
    )


def local_heads(
    tokens,
    cotangent,
    gain_attn,
    gain_ffn,
    query_key_value_weight,
    w_out,
    w_gate,
    w_up,
    w_down,
    pair_block,
):
    f32 = jnp.float32
    n_ctx, n_fsdp = lax.axis_size("ctx"), lax.axis_size("fsdp")
    ctx, fsdp = lax.axis_index("ctx"), lax.axis_index("fsdp")
    token_rows, width = tokens.shape
    depth = query_key_value_weight.shape[0]

    key_pos, own_pos = positions(pair_block, token_rows)
    frequency = jnp.exp(
        jnp.arange(HEAD_SIZE // 2, dtype=f32) * (-2.0 * math.log(rope_base) / HEAD_SIZE)
    )
    angles = key_pos.astype(f32)[:, None] * frequency[None, :]
    cosine, sine_val = jnp.cos(angles), jnp.sin(angles)
    cos = jnp.concatenate([cosine, cosine], axis=1)
    sin = jnp.concatenate([-sine_val, sine_val], axis=1)
    (
        mid,
        normed_two_group,
        cot_group,
        gate_w,
        up_w,
        qkv,
        attended,
        normed_one_seq,
        w_head,
        out_head,
    ) = attention_forward(
        tokens,
        cotangent,
        gain_attn,
        gain_ffn,
        query_key_value_weight,
        w_out,
        w_gate,
        w_up,
        cos,
        sin,
        key_pos,
    )
    result, grad_mid, grad_proj, down_sum, gate_sum, up_part = feed_forward(
        mid,
        cotangent,
        gain_ffn,
        normed_two_group,
        cot_group,
        gate_w,
        up_w,
        w_down.reshape(-1, BLOCK, width),
    )
    grad_input, grad_qkv, grad_out, gate_low, up_low = attention_back(
        grad_proj,
        grad_mid,
        tokens,
        gain_attn,
        w_head,
        out_head,
        qkv,
        attended,
        cos,
        sin,
        key_pos,
        normed_one_seq,
        gate_sum,
        up_part,
    )
    grad_down = down_sum.astype(f32)
    grad_gate, grad_up = gate_low.astype(f32), up_low.astype(f32)

    my_rows = ctx * (depth // n_ctx)
    rows_of = lambda matrix: lax.dynamic_slice_in_dim(
        matrix, my_rows, depth // n_ctx, 0
    ).astype(f32)
    attn_sum = jnp.sum(rows_of(query_key_value_weight) * grad_qkv, axis=1)
    ffn_sum = jnp.sum(rows_of(w_gate) * grad_gate, axis=1) + jnp.sum(
        rows_of(w_up) * grad_up, axis=1
    )
    gain_pairs = [
        (c * n_fsdp + f, f * n_ctx + c) for c in range(n_ctx) for f in range(n_fsdp)
    ]
    moved = lax.ppermute(jnp.stack([attn_sum, ffn_sum]), ("ctx", "fsdp"), gain_pairs)
    my_gain = (ctx * n_fsdp + fsdp) * (depth // n_ctx)
    grad_gain_attn = moved[0] / lax.dynamic_slice_in_dim(gain_attn, my_gain, depth // n_ctx)
    grad_gain_ffn = moved[1] / lax.dynamic_slice_in_dim(gain_ffn, my_gain, depth // n_ctx)
    return (
        result,
        grad_input,
        grad_gain_attn,
        grad_gain_ffn,
        grad_qkv,
        grad_out,
        grad_gate,
        grad_up,
        grad_down,
    )


def solution(mesh):
    local = local_heads if mesh.shape["ctx"] == KEY_VALUE_HEADS else local_general
    return jax.shard_map(
        local,
        mesh=mesh,
        in_specs=(
            P(("ctx", "fsdp"), None),
            P(("ctx", "fsdp"), None),
            P(),
            P(),
            P("fsdp", None),
            P("fsdp", None),
            P("fsdp", None),
            P("fsdp", None),
            P("fsdp", None),
            P(),
        ),
        out_specs=(
            P(("ctx", "fsdp"), None),
            P(("ctx", "fsdp"), None),
            P(("ctx", "fsdp")),
            P(("ctx", "fsdp")),
            P(("fsdp", "ctx"), None),
            P(("fsdp", "ctx"), None),
            P(("fsdp", "ctx"), None),
            P(("fsdp", "ctx"), None),
            P(("fsdp", "ctx"), None),
        ),
        check_vma=False,
    )
```

```python
import math

import jax
import jax.numpy as jnp
from jax import lax
from jax.experimental import pallas as pl
from jax.experimental.pallas import tpu as pltpu
from jax.sharding import PartitionSpec as P

QUERY_HEADS = 16
KEY_VALUE_HEADS = 8
HEAD_SIZE = 128


norm_eps = 1e-05
rope_base = 1000000.0


def rms_norm(vectors, gain_vec):
    return (
        vectors
        * lax.rsqrt(jnp.mean(vectors * vectors, axis=-1, keepdims=True) + norm_eps)
        * gain_vec
    )


def apply_rotation(vectors, where_pos):
    half_dim = vectors.shape[-1] // 2
    frequency = jnp.exp(
        jnp.arange(half_dim, dtype=jnp.float32) * (-2.0 * math.log(rope_base) / vectors.shape[-1])
    )
    angles = where_pos.astype(jnp.float32)[:, None] * frequency[None, :]
    cosine = jnp.cos(angles)[:, None, :]
    sine_val = jnp.sin(angles)[:, None, :]
    first_half = vectors[..., :half_dim]
    second_half = vectors[..., half_dim:]
    return jnp.concatenate(
        [
            first_half * cosine - second_half * sine_val,
            second_half * cosine + first_half * sine_val,
        ],
        axis=-1,
    )


def positions(pair_block, token_rows):
    n_ctx = lax.axis_size("ctx")
    half_rows = token_rows // 2
    row_index = jnp.arange(token_rows, dtype=jnp.int32)
    first_block = pair_block[:, None]
    which_block = jnp.where(
        row_index[None, :] < half_rows, first_block, 2 * n_ctx - 1 - first_block
    )
    pos_table = which_block * half_rows + (row_index % half_rows)[None, :]
    own_pos = lax.dynamic_slice(pos_table, (lax.axis_index("ctx"), 0), (1, token_rows)).reshape(
        token_rows
    )
    return (pos_table.reshape(-1), own_pos)


def to_groups(input_array, group_count):
    token_rows = input_array.shape[0]
    head_length = input_array.shape[-1] // (group_count * KEY_VALUE_HEADS)
    return (
        input_array.reshape(token_rows, KEY_VALUE_HEADS, group_count, head_length)
        .transpose(1, 2, 0, 3)
        .reshape(KEY_VALUE_HEADS, group_count * token_rows, head_length)
    )


def from_groups(input_array, group_count):
    head_length = input_array.shape[-1]
    token_rows = input_array.shape[1] // group_count
    return (
        input_array.reshape(KEY_VALUE_HEADS, group_count, token_rows, head_length)
        .transpose(2, 0, 1, 3)
        .reshape(token_rows, KEY_VALUE_HEADS * group_count * head_length)
    )


def split_keys(every_key, every_value, key_pos):
    total_keys = every_key.shape[0]
    block_length = min(1024, total_keys)
    block_count = total_keys // block_length
    return (
        every_key.reshape(block_count, block_length, KEY_VALUE_HEADS, HEAD_SIZE),
        every_value.reshape(block_count, block_length, KEY_VALUE_HEADS, HEAD_SIZE),
        key_pos.reshape(block_count, block_length),
    )


def contract_last(left, right):
    return lax.dot_general(
        left, right, (((1,), (1,)), ((), ())), preferred_element_type=jnp.float32
    )


def contract_first(left, right):
    return lax.dot_general(
        left, right, (((0,), (0,)), ((), ())), preferred_element_type=jnp.float32
    )


def local_general(
    tokens,
    cotangent,
    gain_attn,
    gain_ffn,
    query_key_value_weight,
    w_out,
    w_gate,
    w_up,
    w_down,
    pair_block,
):
    token_rows = tokens.shape[0]
    query_columns = QUERY_HEADS * HEAD_SIZE
    key_value_columns = KEY_VALUE_HEADS * HEAD_SIZE
    group_count = QUERY_HEADS // KEY_VALUE_HEADS
    score_scale = 1.0 / math.sqrt(HEAD_SIZE)
    ff_cols = w_gate.shape[1]
    key_pos, own_pos = positions(pair_block, token_rows)
    query_pos = jnp.tile(own_pos, group_count)
    inputs_f = tokens.astype(jnp.float32)
    qkv_full, out_full = (
        lax.all_gather(query_key_value_weight, "fsdp", axis=0, tiled=True),
        lax.all_gather(w_out, "fsdp", axis=0, tiled=True),
    )
    normed_one_b = rms_norm(inputs_f, gain_attn).astype(jnp.bfloat16)
    projected_rows = jnp.dot(normed_one_b, qkv_full, preferred_element_type=jnp.float32)
    query_raw = projected_rows[:, :query_columns].reshape(token_rows, QUERY_HEADS, HEAD_SIZE)
    unrotated_key = projected_rows[:, query_columns : query_columns + key_value_columns].reshape(
        token_rows, KEY_VALUE_HEADS, HEAD_SIZE
    )
    query_b = (
        apply_rotation(query_raw, own_pos).astype(jnp.bfloat16).reshape(token_rows, query_columns)
    )
    keys_b = (
        apply_rotation(unrotated_key, own_pos)
        .astype(jnp.bfloat16)
        .reshape(token_rows, key_value_columns)
    )
    values_b = projected_rows[:, query_columns + key_value_columns :].astype(jnp.bfloat16)
    every_key, every_value = (
        lax.all_gather(keys_b, "ctx", axis=0, tiled=True),
        lax.all_gather(values_b, "ctx", axis=0, tiled=True),
    )
    query_grp = to_groups(query_b, group_count)
    key_blocks, value_blocks, pos_blocks = split_keys(every_key, every_value, key_pos)

    def forward_step(carry, block_in):
        run_max, run_total, weighted = carry
        key_block, value_block, block_pos = block_in
        causal = block_pos[None, None, :] <= query_pos[None, :, None]
        scores = (
            jnp.einsum("hqd,khd->hqk", query_grp, key_block, preferred_element_type=jnp.float32)
            * score_scale
        )
        scores = jnp.where(causal, scores, -1e30)
        new_max = jnp.maximum(run_max, jnp.max(scores, axis=-1))
        exp_scores = jnp.where(causal, jnp.exp(scores - new_max[..., None]), 0.0)
        fading = jnp.exp(run_max - new_max)
        run_total = run_total * fading + jnp.sum(exp_scores, axis=-1)
        weighted = weighted * fading[..., None] + jnp.einsum(
            "hqk,khd->hqd",
            exp_scores.astype(jnp.bfloat16),
            value_block,
            preferred_element_type=jnp.float32,
        )
        return ((new_max, run_total, weighted), None)

    initial_maximum = jnp.full((KEY_VALUE_HEADS, group_count * token_rows), -1e30, jnp.float32)
    initial_total = jnp.zeros((KEY_VALUE_HEADS, group_count * token_rows), jnp.float32)
    initial_weighted = jnp.zeros(
        (KEY_VALUE_HEADS, group_count * token_rows, HEAD_SIZE), jnp.float32
    )
    final_carry, ignored = lax.scan(
        forward_step,
        (initial_maximum, initial_total, initial_weighted),
        (key_blocks, value_blocks, pos_blocks),
    )
    run_max, run_total, weighted = final_carry
    log_total = run_max + jnp.log(run_total)
    attn_grp = weighted / run_total[..., None]
    attended_b = from_groups(attn_grp.astype(jnp.bfloat16), group_count)
    mid_rows = inputs_f + jnp.dot(attended_b, out_full, preferred_element_type=jnp.float32)
    gate_full, up_full, down_full = (
        lax.all_gather(w_gate, "fsdp", axis=0, tiled=True),
        lax.all_gather(w_up, "fsdp", axis=0, tiled=True),
        lax.all_gather(w_down, "fsdp", axis=0, tiled=True),
    )
    normed_two_b = rms_norm(mid_rows, gain_ffn).astype(jnp.bfloat16)
    gate_val = jnp.dot(normed_two_b, gate_full, preferred_element_type=jnp.float32)
    up_val = jnp.dot(normed_two_b, up_full, preferred_element_type=jnp.float32)
    hidden_b = (jax.nn.silu(gate_val) * up_val).astype(jnp.bfloat16)
    output_f = mid_rows + jnp.dot(hidden_b, down_full, preferred_element_type=jnp.float32)
    result = output_f.astype(jnp.bfloat16)
    normed_one_x, attended_x, normed_two_x, hidden_x = (
        lax.all_to_all(normed_one_b, "fsdp", split_axis=1, concat_axis=0, tiled=True),
        lax.all_to_all(attended_b, "fsdp", split_axis=1, concat_axis=0, tiled=True),
        lax.all_to_all(normed_two_b, "fsdp", split_axis=1, concat_axis=0, tiled=True),
        lax.all_to_all(hidden_b, "fsdp", split_axis=1, concat_axis=0, tiled=True),
    )
    grad_out_f = cotangent.astype(jnp.float32)
    gate_back, up_back, down_back = (
        lax.all_gather(w_gate, "fsdp", axis=0, tiled=True),
        lax.all_gather(w_up, "fsdp", axis=0, tiled=True),
        lax.all_gather(w_down, "fsdp", axis=0, tiled=True),
    )
    grad_hidden = contract_last(cotangent, down_back)
    ignored, ffn_back = jax.vjp(
        lambda gate_in, up_in: jax.nn.silu(gate_in) * up_in, gate_val, up_val
    )
    grad_gate_f, grad_up_f = ffn_back(grad_hidden)
    grad_gate_b = grad_gate_f.astype(jnp.bfloat16)
    grad_up_b = grad_up_f.astype(jnp.bfloat16)
    grad_normed_two = contract_last(grad_gate_b, gate_back) + contract_last(grad_up_b, up_back)
    ignored, norm_two_back = jax.vjp(rms_norm, mid_rows, gain_ffn)
    grad_mid_part, gain_ffn_part = norm_two_back(grad_normed_two)
    grad_mid = grad_out_f + grad_mid_part
    gate_up_b = jnp.concatenate([grad_gate_b, grad_up_b], axis=1)
    qkv_back, out_back = (
        lax.all_gather(query_key_value_weight, "fsdp", axis=0, tiled=True),
        lax.all_gather(w_out, "fsdp", axis=0, tiled=True),
    )
    grad_proj_b = grad_mid.astype(jnp.bfloat16)
    grad_att_b = contract_last(grad_proj_b, out_back).astype(jnp.bfloat16)
    grad_att_grp = to_groups(grad_att_b, group_count)
    delta_rows = jnp.sum(grad_att_grp.astype(jnp.float32) * attn_grp, axis=-1)

    def backward_step(grad_query, block_in):
        key_block, value_block, block_pos = block_in
        causal = block_pos[None, None, :] <= query_pos[None, :, None]
        scores = (
            jnp.einsum("hqd,khd->hqk", query_grp, key_block, preferred_element_type=jnp.float32)
            * score_scale
        )
        probs = jnp.where(causal, jnp.exp(scores - log_total[..., None]), 0.0)
        grad_values = jnp.einsum(
            "hqk,hqd->khd",
            probs.astype(jnp.bfloat16),
            grad_att_grp,
            preferred_element_type=jnp.float32,
        )
        grad_probs = jnp.einsum(
            "hqd,khd->hqk", grad_att_grp, value_block, preferred_element_type=jnp.float32
        )
        grad_scores = (probs * (grad_probs - delta_rows[..., None])).astype(jnp.bfloat16)
        grad_query = grad_query + score_scale * jnp.einsum(
            "hqk,khd->hqd", grad_scores, key_block, preferred_element_type=jnp.float32
        )
        grad_keys = score_scale * jnp.einsum(
            "hqk,hqd->khd", grad_scores, query_grp, preferred_element_type=jnp.float32
        )
        return (grad_query, (grad_keys, grad_values))

    grad_query_grp, key_grads = lax.scan(
        backward_step,
        jnp.zeros((KEY_VALUE_HEADS, group_count * token_rows, HEAD_SIZE), jnp.float32),
        (key_blocks, value_blocks, pos_blocks),
    )
    total_keys = key_pos.shape[0]
    grad_keys_all = key_grads[0].reshape(total_keys, key_value_columns)
    grad_values_all = key_grads[1].reshape(total_keys, key_value_columns)
    key_sums, summed_values = (
        lax.psum_scatter(
            grad_keys_all.astype(jnp.bfloat16), "ctx", scatter_dimension=0, tiled=True
        ).astype(jnp.float32),
        lax.psum_scatter(
            grad_values_all.astype(jnp.bfloat16), "ctx", scatter_dimension=0, tiled=True
        ).astype(jnp.float32),
    )
    grad_query_rows = from_groups(grad_query_grp, group_count).reshape(
        token_rows, QUERY_HEADS, HEAD_SIZE
    )
    ignored, query_rope_back = jax.vjp(lambda vectors: apply_rotation(vectors, own_pos), query_raw)
    ignored, key_rotation_backward = jax.vjp(
        lambda vectors: apply_rotation(vectors, own_pos), unrotated_key
    )
    grad_query_raw = query_rope_back(grad_query_rows)[0]
    unrotated_key_gradient = key_rotation_backward(
        key_sums.reshape(token_rows, KEY_VALUE_HEADS, HEAD_SIZE)
    )[0]
    grad_projected_b = jnp.concatenate(
        [
            grad_query_raw.reshape(token_rows, query_columns),
            unrotated_key_gradient.reshape(token_rows, key_value_columns),
            summed_values,
        ],
        axis=1,
    ).astype(jnp.bfloat16)
    grad_normed_one = contract_last(grad_projected_b, qkv_back)
    ignored, norm_one_back = jax.vjp(rms_norm, inputs_f, gain_attn)
    grad_in_part, gain_attn_part = norm_one_back(grad_normed_one)
    grad_input = grad_mid + grad_in_part
    cot_group, gate_up_group, projected_group, proj_group = (
        lax.all_gather(cotangent, "fsdp", axis=0, tiled=True),
        lax.all_gather(gate_up_b, "fsdp", axis=0, tiled=True),
        lax.all_gather(grad_projected_b, "fsdp", axis=0, tiled=True),
        lax.all_gather(grad_proj_b, "fsdp", axis=0, tiled=True),
    )
    qkv_part = contract_first(normed_one_x, projected_group)
    out_part = contract_first(attended_x, proj_group)
    gate_up_part = contract_first(normed_two_x, gate_up_group)
    gate_part = gate_up_part[:, :ff_cols]
    up_part = gate_up_part[:, ff_cols:]
    down_part = contract_first(hidden_x, cot_group)
    grad_qkv, grad_out, grad_down = (
        lax.psum_scatter(
            qkv_part.astype(jnp.bfloat16), "ctx", scatter_dimension=0, tiled=True
        ).astype(jnp.float32),
        lax.psum_scatter(
            out_part.astype(jnp.bfloat16), "ctx", scatter_dimension=0, tiled=True
        ).astype(jnp.float32),
        lax.psum_scatter(
            down_part.astype(jnp.bfloat16), "ctx", scatter_dimension=0, tiled=True
        ).astype(jnp.float32),
    )
    grad_gate, grad_up = (
        lax.psum_scatter(
            gate_part.astype(jnp.bfloat16), "ctx", scatter_dimension=0, tiled=True
        ).astype(jnp.float32),
        lax.psum_scatter(
            up_part.astype(jnp.bfloat16), "ctx", scatter_dimension=0, tiled=True
        ).astype(jnp.float32),
    )
    grad_gain_attn, grad_gain_ffn = (
        lax.psum_scatter(gain_attn_part, ("ctx", "fsdp"), scatter_dimension=0, tiled=True),
        lax.psum_scatter(gain_ffn_part, ("ctx", "fsdp"), scatter_dimension=0, tiled=True),
    )
    return (
        result,
        grad_input,
        grad_gain_attn,
        grad_gain_ffn,
        grad_qkv,
        grad_out,
        grad_gate,
        grad_up,
        grad_down,
    )


MESH = pl.DeviceIdType.MESH
ACROSS_X, ACROSS_Y, ACROSS_CORE = 2, 4, 1
BLOCK = 256


class Links:
    def __init__(self, sems, ctx, fsdp):
        self.send_sem, self.recv_sem, self.local_sem = sems
        self.ctx, self.fsdp = ctx, fsdp
        self.remote = self.locals = 0

    def to(self, src, dst, ctx, fsdp):
        index, self.remote = self.remote, self.remote + 1
        return pltpu.make_async_remote_copy(
            src_ref=src,
            dst_ref=dst,
            send_sem=self.send_sem.at[index],
            recv_sem=self.recv_sem.at[index],
            device_id=(ctx, fsdp),
            device_id_type=MESH,
        )

    def flip(self, src, dst, ctx_flip, fsdp_flip):
        return self.to(
            src, dst, lax.bitwise_xor(self.ctx, ctx_flip), lax.bitwise_xor(self.fsdp, fsdp_flip)
        )

    def plane(self, src, dst, flip):
        return self.flip(src, dst, flip, 0)

    def column(self, src, dst, flip):
        return self.flip(src, dst, 0, flip)

    def here(self, src, dst):
        index, self.locals = self.locals, self.locals + 1
        return pltpu.make_async_copy(src, dst, self.local_sem.at[index])


PLANE_FLIPS = [(1, 0), (2, 0), (4, 0)]
COLUMN_FLIPS = [(0, 1), (0, 2), (0, 3)]


def greet(ctx, fsdp, flips):
    barrier = pltpu.get_barrier_semaphore()
    for a, b in flips:
        pl.semaphore_signal(
            barrier,
            inc=1,
            device_id=(lax.bitwise_xor(ctx, a), lax.bitwise_xor(fsdp, b)),
            device_id_type=MESH,
        )
    pl.semaphore_wait(barrier, len(flips))


def start_all(copies):
    for copy in copies:
        copy.start()


class LineGather:
    def __init__(self, links, own, group):
        self.links, self.group = links, group
        self.home = links.here(own, group.at[0])
        self.near = links.column(own, group.at[2], 1)
        self.far = links.column(own, group.at[1], 2)
        self.relay = links.column(group.at[1], group.at[3], 1)

    def begin(self):
        start_all([self.far, self.near, self.home])

    def forward(self):
        self.far.wait_recv()
        self.relay.start()

    def finish(self):
        self.near.wait_recv()
        self.relay.wait_recv()
        for copy in (self.near, self.far, self.relay):
            copy.wait_send()
        self.home.wait()


class PlaneGather:
    def __init__(self, links, blocks, halves):
        self.links, self.blocks, self.halves = links, blocks, halves
        self.ctx = links.ctx
        self.sent = []
        self.cores = []

    def _go(self, copies):
        for copy in copies:
            copy.start()
        self.sent += copies
        return copies

    def _core(self, index):
        refs = self.blocks(index)
        self.cores += self._go([self.links.plane(r, r, ACROSS_CORE) for r in refs])

    def begin(self, sources=None):
        refs = self.blocks(self.ctx)
        pairs = list(zip(sources or refs, refs))
        self.from_x = self._go([self.links.plane(s, r, ACROSS_X) for s, r in pairs])
        self.from_y = self._go([self.links.plane(s, r, ACROSS_Y) for s, r in pairs])
        self.cores += self._go([self.links.plane(s, r, ACROSS_CORE) for s, r in pairs])

    def forward(self):
        index = lax.bitwise_xor(self.ctx, ACROSS_X)
        for copy in self.from_x:
            copy.wait_recv()
        refs = self.halves(index, 0)
        self.corner = self._go([self.links.plane(r, r, ACROSS_Y) for r in refs])
        self._core(index)
        index = lax.bitwise_xor(self.ctx, ACROSS_Y)
        for copy in self.from_y:
            copy.wait_recv()
        refs = self.halves(index, 1)
        self.corner += self._go([self.links.plane(r, r, ACROSS_X) for r in refs])
        self._core(index)

    def finish(self):
        for copy in self.corner:
            copy.wait_recv()
        self._core(lax.bitwise_xor(self.ctx, ACROSS_X | ACROSS_Y))
        for copy in self.cores:
            copy.wait_recv()

    def drain(self):
        for copy in self.sent:
            copy.wait_send()


class PlaneScatter:
    def __init__(self, links, part, core_rx, half_rx, side_rx):
        self.links, self.part = links, part
        self.core_rx, self.half_rx, self.side_rx = core_rx, half_rx, side_rx
        self.chip, self.core = links.ctx // 2, lax.rem(links.ctx, 2)
        self.sent = []
        self.from_core = {}

    def order(self):
        return [(flip, lax.bitwise_xor(self.chip, flip)) for flip in (3, 1, 2, 0)]

    def _go(self, copy):
        copy.start()
        self.sent.append(copy)
        return copy

    def give(self, flip, chip):
        self.from_core[flip] = self._go(
            self.links.plane(
                self.part.at[2 * chip + 1 - self.core], self.core_rx.at[chip], ACROSS_CORE
            )
        )

    def _summed(self, flip):
        chip = lax.bitwise_xor(self.chip, flip)
        self.from_core[flip].wait_recv()
        mine = self.part.at[2 * chip + self.core]
        total = mine[...].astype(jnp.float32) + self.core_rx[chip].astype(jnp.float32)
        return mine, total

    def begin(self):
        half = self.half = self.half_rx.shape[1]
        mine, total = self._summed(3)
        mine[...] = total.astype(jnp.bfloat16)
        self.corner = [
            self._go(self.links.plane(mine.at[pl.ds(0, half)], self.half_rx.at[0], ACROSS_Y)),
            self._go(
                self.links.plane(mine.at[pl.ds(half, half)], self.half_rx.at[1], ACROSS_X)
            ),
        ]

    def middle(self):
        self.sides = []
        for flip, across, slot in ((1, ACROSS_X, 0), (2, ACROSS_Y, 1)):
            mine, total = self._summed(flip)
            mine[...] = total.astype(jnp.bfloat16)
            self.corner[slot].wait_recv()
            rows = pl.ds(slot * self.half, self.half)
            mine[rows] = (
                total[slot * self.half : (slot + 1) * self.half]
                + self.half_rx[slot].astype(jnp.float32)
            ).astype(jnp.bfloat16)
            self.sides.append(self._go(self.links.plane(mine, self.side_rx.at[slot], across)))

    def finish(self):
        mine, total = self._summed(0)
        for slot, copy in enumerate(self.sides):
            copy.wait_recv()
            total = total + self.side_rx[slot].astype(jnp.float32)
        return total

    def drain(self):
        for copy in self.sent:
            copy.wait_send()


def swap_bits(fsdp):
    return 2 * lax.rem(fsdp, 2) + fsdp // 2


def turn(vectors, cos_rows, sin_rows, sign):
    return vectors * cos_rows + sign * pltpu.roll(vectors, HEAD_SIZE // 2, 1) * sin_rows


def attention_kernel(
    tokens_ref,
    cot_ref,
    gain_one_ref,
    gain_two_ref,
    qkv_w_ref,
    out_w_ref,
    gate_ref,
    up_ref,
    cos_ref,
    sin_ref,
    pos_col_ref,
    pos_row_ref,
    mid_ref,
    normed_two_group,
    cot_near,
    cot_far,
    gate_w,
    up_w,
    qkv_out,
    attended_out,
    normed_one_out,
    w_head_out,
    out_head_out,
    normed,
    w_head,
    out_head,
    out_relay,
    qkv,
    attended,
    part,
    core_rx,
    half_rx,
    side_rx,
    normed_two,
    send_sem,
    recv_sem,
    local_sem,
):
    f32, bf16 = jnp.float32, jnp.bfloat16
    ctx, fsdp = lax.axis_index("ctx"), lax.axis_index("fsdp")
    links = Links((send_sem, recv_sem, local_sem), ctx, fsdp)
    rows, width = tokens_ref.shape
    depth = qkv_w_ref.shape[0]
    head_columns = out_head.shape[0]
    n_ctx, n_fsdp = normed.shape[0], width // depth
    seq_rows = n_ctx * rows
    hidden = gate_w.shape[2]
    strip = hidden // n_ctx
    depth_blocks = gate_ref.shape[0]
    query_columns = QUERY_HEADS * HEAD_SIZE
    key_columns = KEY_VALUE_HEADS * HEAD_SIZE
    score_scale = 1.0 / math.sqrt(HEAD_SIZE)
    finals = []

    greet(ctx, fsdp, PLANE_FLIPS + COLUMN_FLIPS + [(6, 0)])

    out_block = out_w_ref.at[
        pl.ds(pl.multiple_of(lax.rem(ctx, 2) * head_columns, head_columns), head_columns)
    ]
    out_target = swap_bits(lax.bitwise_xor(ctx // 2, fsdp))
    out_away = out_target != fsdp
    out_copy = links.to(out_block, out_relay, ctx, out_target)
    out_home = links.here(out_block, out_relay)
    out_flip = 2 * swap_bits(fsdp)
    out_moves = fsdp != 0
    out_last = links.to(out_relay, out_head, lax.bitwise_xor(ctx, out_flip), fsdp)
    out_stays = links.here(out_relay, out_head)

    @pl.when(out_away)
    def _():
        out_copy.start()

    @pl.when(jnp.logical_not(out_away))
    def _():
        out_home.start()

    def rows_of(plane):
        return pl.ds(pl.multiple_of(plane * depth, depth), depth)

    head_parts = []
    for start, size, place in (
        (ctx * head_columns, head_columns, 0),
        (query_columns + ctx * HEAD_SIZE, HEAD_SIZE, head_columns),
        (query_columns + key_columns + ctx * HEAD_SIZE, HEAD_SIZE, head_columns + HEAD_SIZE),
    ):
        head_parts.append(
            (
                qkv_w_ref.at[:, pl.ds(pl.multiple_of(start, HEAD_SIZE), size)],
                w_head.at[rows_of(fsdp), pl.ds(place, size)],
            )
        )
    head_far = [links.column(src, dst, 2) for src, dst in head_parts]
    head_near = [links.column(src, dst, 1) for src, dst in head_parts]
    own_head = [links.here(src, dst) for src, dst in head_parts]
    start_all(head_far + head_near + own_head)

    def place_of(j):
        return pl.ds(pl.multiple_of(j * strip, strip), strip)

    def strips(target):
        cols = pl.ds(pl.multiple_of(target * hidden + ctx * strip, strip), strip)
        blocks = pl.ds(fsdp * depth_blocks, depth_blocks)
        for source, dest in ((gate_ref, gate_w), (up_ref, up_w)):
            yield source.at[:, :, cols], dest.at[blocks, :, place_of(ctx)]

    strip_copies = [[links.here(src, dst) for src, dst in strips(fsdp)]]
    for flip in (1, 2, 3):
        strip_copies.append(
            [links.column(s, d, flip) for s, d in strips(lax.bitwise_xor(fsdp, flip))]
        )
    start_all(strip_copies[0])

    def strip_gather(flip):
        first = lax.bitwise_xor(fsdp, flip) * depth_blocks
        blocks = pl.ds(first, depth_blocks)
        return PlaneGather(
            links,
            lambda j: [w.at[blocks, :, place_of(j)] for w in (gate_w, up_w)],
            lambda j, which: [w.at[first + which, :, place_of(j)] for w in (gate_w, up_w)],
        )

    weights = [strip_gather(flip) for flip in range(n_fsdp)]

    inputs = tokens_ref[...].astype(f32)
    scale = lax.rsqrt(jnp.mean(inputs * inputs, axis=-1, keepdims=True) + norm_eps)
    normed[ctx] = (inputs * scale * gain_one_ref[...]).astype(bf16)
    half = rows // 2
    gather = PlaneGather(
        links,
        lambda j: [normed.at[j]],
        lambda j, which: [normed.at[j, pl.ds(which * half, half)]],
    )
    gather.begin()
    gather.forward()
    weights[0].begin([source for source, dest in strips(fsdp)])
    gather.finish()

    @pl.when(out_away)
    def _():
        out_copy.wait_recv()

    @pl.when(jnp.logical_not(out_away))
    def _():
        out_home.wait()

    @pl.when(out_moves)
    def _():
        out_last.start()

    @pl.when(jnp.logical_not(out_moves))
    def _():
        out_stays.start()

    weights[0].forward()
    for copy in head_far:
        copy.wait_recv()
    far_rows = w_head.at[rows_of(lax.bitwise_xor(fsdp, 2))]
    head_relay = links.column(far_rows, far_rows, 1)
    head_relay.start()
    weights[0].finish()
    finals.append(links.here(normed, normed_one_out))
    finals[-1].start()
    for copy in own_head:
        copy.wait()
    for copy in head_near + [head_relay]:
        copy.wait_recv()
    start_all(strip_copies[1] + strip_copies[2] + strip_copies[3])

    block_rows = 2 * rows

    def project(step, carry):
        at = pl.multiple_of(step * block_rows, block_rows)
        tile = normed[pl.ds(step * 2, 2)].reshape(block_rows, width)
        out = jnp.dot(tile, w_head[...], preferred_element_type=f32)
        cos_rows, sin_rows = cos_ref[pl.ds(at, block_rows)], sin_ref[pl.ds(at, block_rows)]
        for column in range(0, head_columns + HEAD_SIZE, HEAD_SIZE):
            turned = turn(out[:, column : column + HEAD_SIZE], cos_rows, sin_rows, 1.0)
            qkv[pl.ds(at, block_rows), pl.ds(column, HEAD_SIZE)] = turned.astype(bf16)
        column = head_columns + HEAD_SIZE
        qkv[pl.ds(at, block_rows), pl.ds(column, HEAD_SIZE)] = out[:, column:].astype(bf16)
        return carry

    lax.fori_loop(0, seq_rows // block_rows, project, 0)
    def attend(step, carry):
        at = pl.multiple_of(step * block_rows, block_rows)
        keys = qkv[:, pl.ds(head_columns, HEAD_SIZE)]
        values = qkv[:, pl.ds(head_columns + HEAD_SIZE, HEAD_SIZE)]
        causal = pos_row_ref[...] <= pos_col_ref[pl.ds(at, block_rows)]
        for column in range(0, head_columns, HEAD_SIZE):
            query = qkv[pl.ds(at, block_rows), pl.ds(column, HEAD_SIZE)]
            scores = contract_last(query, keys) * score_scale
            scores = jnp.where(causal, scores, -1e30)
            shifted = jnp.exp(scores - jnp.max(scores, axis=-1, keepdims=True))
            probs = shifted * (1.0 / jnp.sum(shifted, axis=-1, keepdims=True))
            mixed = jnp.dot(probs.astype(bf16), values, preferred_element_type=f32)
            attended[pl.ds(at, block_rows), pl.ds(column, HEAD_SIZE)] = mixed.astype(bf16)
        return carry

    lax.fori_loop(0, seq_rows // block_rows, attend, 0)

    @pl.when(out_moves)
    def _():
        out_last.wait_recv()

    @pl.when(jnp.logical_not(out_moves))
    def _():
        out_stays.wait()

    for src, dst in (        (qkv, qkv_out),
        (attended, attended_out),
        (w_head, w_head_out),
        (out_head, out_head_out),
    ):
        finals.append(links.here(src, dst))
        finals[-1].start()

    scatter = PlaneScatter(links, part, core_rx, half_rx, side_rx)
    for flip, chip in scatter.order():
        at = pl.multiple_of(chip * block_rows, block_rows)
        out = jnp.dot(
            attended[pl.ds(at, block_rows)], out_head[...], preferred_element_type=f32
        )
        part[pl.ds(chip * 2, 2)] = out.astype(bf16).reshape(2, rows, width)
        scatter.give(flip, chip)

    def arrived(flip):
        for copy in strip_copies[flip]:
            copy.wait_recv()
        weights[flip].begin()

    scatter.begin()
    scatter.middle()
    mid = tokens_ref[...].astype(f32) + scatter.finish()
    mid_ref[...] = mid
    mid_scale = lax.rsqrt(jnp.mean(mid * mid, axis=-1, keepdims=True) + norm_eps)
    normed_two[...] = (mid * mid_scale * gain_two_ref[...]).astype(bf16)

    group = LineGather(links, normed_two, normed_two_group)
    cot_copies = [links.column(cot_ref, cot_far, 2), links.column(cot_ref, cot_near, 1)]
    group.begin()
    start_all(cot_copies)
    arrived(1)
    arrived(2)
    weights[1].forward()
    arrived(3)
    weights[2].forward()
    weights[1].finish()
    group.forward()
    weights[3].forward()
    weights[2].finish()
    weights[3].finish()
    group.finish()
    for copy in cot_copies:
        copy.wait()
    for copy in strip_copies[0]:
        copy.wait()

    for copies in [head_far, head_near, [head_relay]] + strip_copies[1:]:
        for copy in copies:
            copy.wait_send()

    @pl.when(out_away)
    def _():
        out_copy.wait_send()

    @pl.when(out_moves)
    def _():
        out_last.wait_send()

    gather.drain()
    scatter.drain()
    for item in weights:
        item.drain()
    for copy in finals:
        copy.wait()


def attention_forward(
    tokens, cotangent, gain_attn, gain_ffn, qkv_w, w_out, w_gate, w_up, cos, sin, key_pos
):
    f32, bf16 = jnp.float32, jnp.bfloat16
    n_ctx, n_fsdp = lax.axis_size("ctx"), lax.axis_size("fsdp")
    rows, width = tokens.shape
    depth = qkv_w.shape[0]
    hidden = w_gate.shape[1] // n_fsdp
    seq_rows = n_ctx * rows
    head_columns = QUERY_HEADS // KEY_VALUE_HEADS * HEAD_SIZE
    all_columns = head_columns + 2 * HEAD_SIZE
    vmem, hbm = pl.BlockSpec(memory_space=pltpu.VMEM), pl.BlockSpec(memory_space=pl.ANY)
    shape = jax.ShapeDtypeStruct
    return pl.pallas_call(
        attention_kernel,
        name="attention_forward",
        out_shape=[
            shape((rows, width), f32),
            shape((n_fsdp, rows, width), bf16),
            shape((rows, width), bf16),
            shape((rows, width), bf16),
            shape((width // BLOCK, BLOCK, hidden), bf16),
            shape((width // BLOCK, BLOCK, hidden), bf16),
            shape((seq_rows, all_columns), bf16),
            shape((seq_rows, head_columns), bf16),
            shape((n_ctx, rows, width), bf16),
            shape((width, all_columns), bf16),
            shape((head_columns, width), bf16),
        ],
        in_specs=[vmem] * 4 + [hbm] * 4 + [vmem] * 4,
        out_specs=[vmem] + [hbm] * 10,
        scratch_shapes=[
            pltpu.VMEM((n_ctx, rows, width), bf16),
            pltpu.VMEM((width, all_columns), bf16),
            pltpu.VMEM((head_columns, width), bf16),
            pltpu.VMEM((head_columns, width), bf16),
            pltpu.VMEM((seq_rows, all_columns), bf16),
            pltpu.VMEM((seq_rows, head_columns), bf16),
            pltpu.VMEM((n_ctx, rows, width), bf16),
            pltpu.VMEM((n_ctx // 2, rows, width), bf16),
            pltpu.VMEM((2, rows // 2, width), bf16),
            pltpu.VMEM((2, rows, width), bf16),
            pltpu.VMEM((rows, width), bf16),
            pltpu.SemaphoreType.DMA((112,)),
            pltpu.SemaphoreType.DMA((112,)),
            pltpu.SemaphoreType.DMA((16,)),
        ],
        compiler_params=pltpu.CompilerParams(
            collective_id=1, has_side_effects=True, vmem_limit_bytes=58 * 2**20
        ),
    )(
        tokens,
        cotangent,
        gain_attn[None],
        gain_ffn[None],
        qkv_w,
        w_out,
        w_gate.reshape(depth // BLOCK, BLOCK, -1),
        w_up.reshape(depth // BLOCK, BLOCK, -1),
        cos,
        sin,
        key_pos[:, None],
        key_pos[None],
    )


class ChipScatter:
    def __init__(self, links, part, halves, sides):
        self.links, self.part, self.halves, self.sides = links, part, halves, sides
        self.chip = links.ctx // 2
        self.sent = []

    def _go(self, copy):
        copy.start()
        self.sent.append(copy)
        return copy

    def begin(self, source=None):
        corner = (source or self.part)(lax.bitwise_xor(self.chip, 3))
        half = corner.shape[0] // 2
        self.half = half
        self.corner = [
            self._go(self.links.plane(corner.at[pl.ds(0, half)], self.halves[0], ACROSS_Y)),
            self._go(self.links.plane(corner.at[pl.ds(half, half)], self.halves[1], ACROSS_X)),
        ]

    def middle(self):
        self.side = []
        for slot, (flip, across) in enumerate(((1, ACROSS_X), (2, ACROSS_Y))):
            mine = self.part(lax.bitwise_xor(self.chip, flip))
            self.corner[slot].wait_recv()
            rows = mine.at[pl.ds(slot * self.half, self.half)]
            rows[...] = (
                rows[...].astype(jnp.float32) + self.halves[slot][...].astype(jnp.float32)
            ).astype(jnp.bfloat16)
            self.side.append(self._go(self.links.plane(mine, self.sides[slot], across)))

    def finish(self):
        mine = self.part(self.chip)
        for copy in self.side:
            copy.wait_recv()
        mine[...] = (
            mine[...].astype(jnp.float32)
            + self.sides[0][...].astype(jnp.float32)
            + self.sides[1][...].astype(jnp.float32)
        ).astype(jnp.bfloat16)
        return mine

    def drain(self):
        for copy in self.sent:
            copy.wait_send()


def feed_forward_kernel(
    mid_ref,
    cot_ref,
    gain_ref,
    normed_ref,
    cot_near_ref,
    cot_far_ref,
    gate_hbm,
    up_hbm,
    down_hbm,
    result_ref,
    grad_mid_ref,
    grad_proj_ref,
    down_sum,
    gate_sum,
    up_part,
    gate_v,
    up_v,
    down_v,
    cots,
    hidden,
    grad_gate,
    grad_up,
    other_normed,
    other_cots,
    other_hidden,
    other_gate,
    other_up,
    stage,
    landed,
    send_sem,
    recv_sem,
    local_sem,
    load_sem,
    down_free,
    gate_free,
):
    f32, bf16 = jnp.float32, jnp.bfloat16
    ctx, fsdp = lax.axis_index("ctx"), lax.axis_index("fsdp")
    links = Links((send_sem, recv_sem, local_sem), ctx, fsdp)
    core = lax.rem(ctx, 2)
    rows, width = mid_ref.shape
    blocks = gate_v.shape[0]
    hidden_units = blocks * BLOCK
    half_units = hidden_units // 2
    n_fsdp = normed_ref.shape[0]
    group_rows = n_fsdp * rows

    def loads(j):
        cols = pl.ds(pl.multiple_of(j * BLOCK, BLOCK), BLOCK)
        return (
            pltpu.make_async_copy(
                gate_hbm.at[:, :, cols], gate_v.at[:, :, cols], load_sem.at[0, j]
            ),
            pltpu.make_async_copy(up_hbm.at[:, :, cols], up_v.at[:, :, cols], load_sem.at[1, j]),
            pltpu.make_async_copy(down_hbm.at[j], down_v.at[j], load_sem.at[2, j]),
        )

    for j in range(blocks):
        for copy in loads(j):
            copy.start()

    greet(ctx, fsdp, PLANE_FLIPS + COLUMN_FLIPS[:2])

    cot_relay = links.column(cot_far_ref, cots.at[3], 1)
    cot_relay.start()
    cots[0] = cot_ref[...]
    cots[1] = cot_far_ref[...]
    cots[2] = cot_near_ref[...]

    swaps = [links.plane(normed_ref, other_normed, ACROSS_CORE)]
    cot_swaps = [links.plane(cots.at[s], other_cots.at[s], ACROSS_CORE) for s in range(n_fsdp)]
    start_all(swaps + cot_swaps[:3])

    half_slots, half_rows = n_fsdp // 2, group_rows // 2

    def activate(j, carry):
        for copy in loads(j):
            copy.wait()
        cols = pl.ds(pl.multiple_of(j * BLOCK, BLOCK), BLOCK)
        normed = normed_ref[...].reshape(group_rows, width)
        gate = jnp.dot(
            normed, gate_v[:, :, cols].reshape(width, BLOCK), preferred_element_type=f32
        )
        up = jnp.dot(normed, up_v[:, :, cols].reshape(width, BLOCK), preferred_element_type=f32)
        sig = jax.nn.sigmoid(gate)
        silu = gate * sig
        hidden[:, cols] = (silu * up).astype(bf16)
        grad_gate[:, cols] = (up * (sig * (1.0 + gate * (1.0 - sig)))).astype(bf16)
        grad_up[:, cols] = silu.astype(bf16)
        return carry

    lax.fori_loop(0, blocks, activate, 0)

    piece = 2 * BLOCK
    pieces = width // piece

    def spot(n):
        return pl.ds(n * piece, piece)

    def put(which, first, n, value):
        stage[which, pl.ds(first, half_slots), :, spot(n)] = value.astype(bf16).reshape(
            half_slots, rows, piece
        )

    def down_out(first, n):
        value = jnp.dot(
            hidden[pl.ds(first * rows, half_rows)],
            down_v[:, :, spot(n)].reshape(hidden_units, piece),
            preferred_element_type=f32,
        )
        put(0, first, n, value)

    def back_out(first, n):
        at, some = pl.ds(first * rows, half_rows), pl.ds(n * 2, 2)
        value = contract_last(grad_gate[at], gate_v[some].reshape(piece, hidden_units))
        value = value + contract_last(grad_up[at], up_v[some].reshape(piece, hidden_units))
        put(1, first, n, value)

    near, far = {}, []

    def send_near(which, n):
        near[which, n] = [
            links.column(stage.at[which, 3, :, spot(n)], landed.at[which, 1, :, spot(n)], 1),
            links.column(stage.at[which, 2, :, spot(n)], landed.at[which, 0, :, spot(n)], 1),
        ]
        start_all(near[which, n])

    def relay(which, n):
        near[which, n][0].wait_recv()
        stage[which, 1, :, spot(n)] = (
            stage[which, 1, :, spot(n)].astype(f32) + landed[which, 1, :, spot(n)].astype(f32)
        ).astype(bf16)
        copy = links.column(stage.at[which, 1, :, spot(n)], landed.at[which, 2, :, spot(n)], 2)
        copy.start()
        far.append(copy)

    for n in range(pieces):
        down_out(half_slots, n)
        send_near(0, n)
        down_out(0, n)

    def activation_grads(first):
        at = pl.ds(first * rows, half_rows)

        def step(j, carry):
            cols = pl.ds(pl.multiple_of(j * BLOCK, BLOCK), BLOCK)
            cot_rows = cots[pl.ds(first, half_slots)].reshape(half_rows, width)
            grad_hidden = contract_last(cot_rows, down_v[j])
            grad_gate[at, cols] = (grad_gate[at, cols].astype(f32) * grad_hidden).astype(bf16)
            grad_up[at, cols] = (grad_up[at, cols].astype(f32) * grad_hidden).astype(bf16)
            return carry

        lax.fori_loop(0, blocks, step, 0)

    hidden_acts = []
    for pair in range(blocks // 2):
        cols = pl.ds(pl.multiple_of((2 * pair + 1 - core) * BLOCK, BLOCK), BLOCK)
        hidden_acts.append(
            links.plane(
                hidden.at[:, cols], other_hidden.at[:, pl.ds(pair * BLOCK, BLOCK)], ACROSS_CORE
            )
        )
    start_all(hidden_acts)
    activation_grads(0)
    cot_relay.wait_recv()
    cot_swaps[3].start()
    activation_grads(half_slots)
    theirs = pl.ds(pl.multiple_of((1 - core) * half_units, half_units), half_units)
    acts = [
        links.plane(grad_gate.at[:, theirs], other_gate, ACROSS_CORE),
        links.plane(grad_up.at[:, theirs], other_up, ACROSS_CORE),
    ]
    start_all(acts)

    def free(sem):
        for flip in (ACROSS_X, ACROSS_Y):
            pl.semaphore_signal(
                sem,
                inc=1,
                device_id=(lax.bitwise_xor(ctx, flip), fsdp),
                device_id_type=MESH,
            )

    free(down_free)

    def flat(ref, cols):
        return ref[:, :, cols].reshape(group_rows, -1)

    for copy in cot_swaps + hidden_acts:
        copy.wait_recv()

    def down_block(pair, carry):
        own = pl.ds(pl.multiple_of((2 * pair + core) * BLOCK, BLOCK), BLOCK)
        other = pl.ds(pl.multiple_of(pair * BLOCK, BLOCK), BLOCK)
        left, right = hidden[:, own].T, other_hidden[:, other].T
        for cols in (pl.ds(0, width // 2), pl.ds(width // 2, width // 2)):
            total = jnp.dot(left, flat(cots, cols), preferred_element_type=f32)
            total = total + jnp.dot(right, flat(other_cots, cols), preferred_element_type=f32)
            down_v[pair, :, cols] = total.astype(bf16)
        return carry

    lax.fori_loop(0, blocks // 2, down_block, 0)
    pl.semaphore_wait(down_free, 2)

    def scatter_in(place):
        corner = place.at[4]
        return ChipScatter(
            links,
            lambda chip: place.at[chip],
            [corner.at[pl.ds(0, BLOCK // 2)], corner.at[pl.ds(BLOCK // 2, BLOCK // 2)]],
            [place.at[5], place.at[6]],
        )

    down_scatter = scatter_in(down_v)
    down_scatter.begin()
    for n in range(pieces):
        back_out(half_slots, n)
        send_near(1, n)
    for n in range(pieces):
        back_out(0, n)
    free(gate_free)
    relay(0, 0)
    relay(0, 1)

    mine = pl.ds(pl.multiple_of(core * half_units, half_units), half_units)

    def weight_block(b, carry):
        cols = pl.ds(pl.multiple_of(b * BLOCK, BLOCK), BLOCK)
        left, right = flat(normed_ref, cols).T, flat(other_normed, cols).T
        plane, chip = b // 2, 2 * lax.rem(b, 2)
        at_row = pl.ds(pl.multiple_of((plane // 2) * (BLOCK // 2), BLOCK // 2), BLOCK // 2)
        at_col = pl.ds(pl.multiple_of(lax.rem(plane, 2) * (width // 2), width // 2), width // 2)
        for own_grad, other_grad, place in (
            (grad_gate, other_gate, gate_v),
            (grad_up, other_up, up_v),
        ):
            total = jnp.dot(left, own_grad[:, mine], preferred_element_type=f32)
            total = total + jnp.dot(right, other_grad[...], preferred_element_type=f32)
            low = total.astype(bf16)
            place[chip, at_row, at_col] = low[: BLOCK // 2]
            place[chip + 1, at_row, at_col] = low[BLOCK // 2 :]
        return carry

    for copy in swaps + acts:
        copy.wait_recv()
    lax.fori_loop(0, blocks // 2, weight_block, 0)
    relay(0, 2)
    down_scatter.middle()
    lax.fori_loop(blocks // 2, blocks, weight_block, 0)
    pl.semaphore_wait(gate_free, 2)
    gate_scatter = scatter_in(gate_v)
    gate_scatter.begin()
    up_copy = links.here(up_v.at[pl.ds(0, 4)], up_part)
    up_copy.start()
    relay(0, 3)
    relay(1, 0)
    relay(1, 1)
    relay(1, 2)
    relay(1, 3)
    gate_scatter.middle()
    down_copy = links.here(down_scatter.finish(), down_sum)
    down_copy.start()

    for copy in [pair[1] for pair in near.values()] + far:
        copy.wait_recv()
    mid = mid_ref[...]
    sums = []
    for which in (0, 1):
        total = stage[which, 0].astype(f32) + landed[which, 0].astype(f32)
        sums.append(total + landed[which, 2].astype(f32))
    result_ref[...] = (mid + sums[0]).astype(bf16)
    scale = lax.rsqrt(jnp.mean(mid * mid, axis=-1, keepdims=True) + norm_eps)
    u = sums[1] * gain_ref[...]
    inner = jnp.mean(u * mid, axis=-1, keepdims=True)
    grad_mid = cot_ref[...].astype(f32) + scale * u - mid * (scale * scale * scale * inner)
    grad_mid_ref[...] = grad_mid
    grad_proj_ref[...] = grad_mid.astype(bf16)

    gate_copy = links.here(gate_scatter.finish(), gate_sum)
    gate_copy.start()
    sent = [copy for pair in near.values() for copy in pair] + far + swaps + cot_swaps
    for copy in sent + hidden_acts + acts + [cot_relay]:
        copy.wait_send()
    down_scatter.drain()
    gate_scatter.drain()
    for copy in (up_copy, down_copy, gate_copy):
        copy.wait()


def feed_forward(
    mid, cotangent, gain_ffn, normed_group, cot_near, cot_far, gate_w, up_w, w_down
):
    f32, bf16 = jnp.float32, jnp.bfloat16
    n_fsdp = lax.axis_size("fsdp")
    rows, width = mid.shape
    group_rows = n_fsdp * rows
    units = w_down.shape[0] * BLOCK
    blocks = units // BLOCK
    vmem, hbm = pl.BlockSpec(memory_space=pltpu.VMEM), pl.BlockSpec(memory_space=pl.ANY)
    shape = jax.ShapeDtypeStruct
    return pl.pallas_call(
        feed_forward_kernel,
        name="feed_forward",
        out_shape=[
            shape((rows, width), bf16),
            shape((rows, width), f32),
            shape((rows, width), bf16),
            shape((BLOCK, width), bf16),
            shape((BLOCK, width), bf16),
            shape((blocks // 2, BLOCK, width), bf16),
        ],
        in_specs=[vmem] * 6 + [hbm] * 3,
        out_specs=[vmem] * 3 + [hbm] * 3,
        scratch_shapes=[
            pltpu.VMEM((width // BLOCK, BLOCK, units), bf16),
            pltpu.VMEM((width // BLOCK, BLOCK, units), bf16),
            pltpu.VMEM((blocks, BLOCK, width), bf16),
            pltpu.VMEM((n_fsdp, rows, width), bf16),
            pltpu.VMEM((group_rows, units), bf16),
            pltpu.VMEM((group_rows, units), bf16),
            pltpu.VMEM((group_rows, units), bf16),
            pltpu.VMEM((n_fsdp, rows, width), bf16),
            pltpu.VMEM((n_fsdp, rows, width), bf16),
            pltpu.VMEM((group_rows, units // 2), bf16),
            pltpu.VMEM((group_rows, units // 2), bf16),
            pltpu.VMEM((group_rows, units // 2), bf16),
            pltpu.VMEM((2, n_fsdp, rows, width), bf16),
            pltpu.VMEM((2, n_fsdp - 1, rows, width), bf16),
            pltpu.SemaphoreType.DMA((48,)),
            pltpu.SemaphoreType.DMA((48,)),
            pltpu.SemaphoreType.DMA((8,)),
            pltpu.SemaphoreType.DMA((3, blocks)),
            pltpu.SemaphoreType.REGULAR,
            pltpu.SemaphoreType.REGULAR,
        ],
        compiler_params=pltpu.CompilerParams(
            collective_id=2, has_side_effects=True, vmem_limit_bytes=62 * 2**20
        ),
    )(mid, cotangent, gain_ffn[None], normed_group, cot_near, cot_far, gate_w, up_w, w_down)


def attention_back_kernel(
    grad_proj_ref,
    grad_mid_ref,
    tokens_ref,
    gain_ref,
    w_head_ref,
    out_head_ref,
    qkv_ref,
    attended_ref,
    cos_ref,
    sin_ref,
    pos_col_ref,
    pos_row_ref,
    normed_hbm,
    gate_sum_hbm,
    up_part_hbm,
    grad_input_ref,
    qkv_sum,
    out_sum,
    gate_out,
    up_out,
    proj,
    normed,
    up_part,
    up_halves,
    up_sides,
    grad_att,
    grads,
    key_grad,
    value_grad,
    part,
    core_rx,
    half_rx,
    side_rx,
    out_stage,
    out_landed,
    out_summed,
    head_stage,
    head_summed,
    head_landed,
    send_sem,
    recv_sem,
    local_sem,
):
    f32, bf16 = jnp.float32, jnp.bfloat16
    ctx, fsdp = lax.axis_index("ctx"), lax.axis_index("fsdp")
    links = Links((send_sem, recv_sem, local_sem), ctx, fsdp)
    chip, core = ctx // 2, lax.rem(ctx, 2)
    n_ctx, rows, width = proj.shape
    n_fsdp = out_landed.shape[0]
    seq_rows = n_ctx * rows
    head_columns = out_head_ref.shape[0]
    strip_rows = out_landed.shape[1]
    score_scale = 1.0 / math.sqrt(HEAD_SIZE)
    loads = [links.here(normed_hbm, normed), links.here(up_part_hbm, up_part)]
    for copy in loads:
        copy.start()

    flips = [(a, 0) for a in range(1, n_ctx)] + COLUMN_FLIPS + [(1, b) for b in (1, 2, 3)]
    greet(ctx, fsdp, flips)

    proj[ctx] = grad_proj_ref[...]
    half = rows // 2
    gather = PlaneGather(
        links,
        lambda j: [proj.at[j]],
        lambda j, which: [proj.at[j, pl.ds(which * half, half)]],
    )
    gather.begin()

    def spread(source, dest):
        half_width = width // 2
        place = pl.ds(pl.multiple_of((2 * fsdp + core) * half_width, half_width), half_width)
        copies = []
        for a in (0, 1):
            for b in range(n_fsdp):
                plane = lax.bitwise_xor(fsdp, b)
                who = lax.bitwise_xor(core, a)
                at_row = (plane // 2) * (BLOCK // 2) + who * strip_rows
                block = source.at[
                    pl.ds(pl.multiple_of(at_row, strip_rows), strip_rows),
                    pl.ds(pl.multiple_of(lax.rem(plane, 2) * half_width, half_width), half_width),
                ]
                target = dest.at[:, place]
                if a or b:
                    copies.append(
                        links.to(block, target, lax.bitwise_xor(ctx, a), plane)
                    )
                else:
                    local = links.here(block, target)
                    locals_.append(local)
                    local.start()
        for copy in copies:
            copy.start()
        return copies

    locals_ = []
    up_scatter = ChipScatter(
        links,
        lambda q: up_part.at[q],
        [up_halves.at[0], up_halves.at[1]],
        [up_sides.at[0], up_sides.at[1]],
    )
    gate_copies = spread(gate_sum_hbm, gate_out)
    gather.forward()
    up_scatter.begin(lambda q: up_part_hbm.at[q])
    gather.finish()

    total = jnp.zeros((head_columns, width), f32)
    for j in range(0, n_ctx, 2):
        total = total + lax.dot_general(
            attended_ref[pl.ds(j * rows, 2 * rows)],
            proj[pl.ds(j, 2)].reshape(2 * rows, width),
            (((0,), (0,)), ((), ())),
            preferred_element_type=f32,
        )
    out_stage[...] = total.astype(bf16).reshape(out_stage.shape)
    half_ctx = n_ctx // 2
    out_base = links.remote
    links.remote += half_ctx
    out_copies = []
    for j in range(half_ctx):
        target = half_ctx * core + j
        copy = pltpu.make_async_remote_copy(
            src_ref=out_stage.at[j],
            dst_ref=out_landed.at[chip],
            send_sem=send_sem.at[out_base + j],
            recv_sem=recv_sem.at[out_base + chip],
            device_id=(target, fsdp),
            device_id_type=MESH,
        )
        out_copies.append((target != ctx, copy))

        @pl.when(target != ctx)
        def _(copy=copy):
            copy.start()

    own_out = links.here(out_stage.at[lax.rem(ctx, half_ctx)], out_landed.at[chip])
    out_own_chip = lax.rem(ctx, 2) == ctx // half_ctx

    @pl.when(out_own_chip)
    def _():
        own_out.start()

    def out_arrivals():
        for source in range(half_ctx):
            arrival = pltpu.make_async_remote_copy(
                src_ref=out_stage.at[0],
                dst_ref=out_landed.at[source],
                send_sem=send_sem.at[out_base],
                recv_sem=recv_sem.at[out_base + source],
                device_id=(lax.bitwise_xor(ctx, 1), fsdp),
                device_id_type=MESH,
            )

            @pl.when(2 * source + ctx // half_ctx != ctx)
            def _(arrival=arrival):
                arrival.wait_recv()

        @pl.when(out_own_chip)
        def _():
            own_out.wait()

    def out_begin():
        out_arrivals()
        copies = [
            links.column(
                out_landed.at[lax.bitwise_xor(fsdp, flip)], out_summed.at[slot], 1
            )
            for flip, slot in ((3, 1), (1, 0))
        ]
        start_all(copies)
        return copies

    def out_relay(copies):
        copies[0].wait_recv()
        across = lax.bitwise_xor(fsdp, 2)
        out_landed[across] = (
            out_landed[across].astype(f32) + out_summed[1].astype(f32)
        ).astype(bf16)
        copy = links.column(out_landed.at[across], out_summed.at[2], 2)
        copy.start()
        return copy

    def back(step, carry):
        at = pl.multiple_of(step * 2 * rows, 2 * rows)
        tile = proj[pl.ds(2 * step, 2)].reshape(2 * rows, width)
        grad_att[pl.ds(at, 2 * rows)] = contract_last(tile, out_head_ref[...]).astype(bf16)
        return carry

    lax.fori_loop(0, n_ctx // 2, back, 0)

    key_grad[...] = jnp.zeros_like(key_grad)
    value_grad[...] = jnp.zeros_like(value_grad)

    def attend_head(column):
        cols = pl.ds(column, HEAD_SIZE)

        def step(index, carry):
            at = pl.ds(pl.multiple_of(index * 2 * rows, 2 * rows), 2 * rows)
            keys = qkv_ref[:, pl.ds(head_columns, HEAD_SIZE)]
            values = qkv_ref[:, pl.ds(head_columns + HEAD_SIZE, HEAD_SIZE)]
            causal = pos_row_ref[...] <= pos_col_ref[at]
            query, grad_mixed = qkv_ref[at, cols], grad_att[at, cols]
            scores = contract_last(query, keys) * score_scale
            scores = jnp.where(causal, scores, -1e30)
            shifted = jnp.exp(scores - jnp.max(scores, axis=-1, keepdims=True))
            probs = shifted * (1.0 / jnp.sum(shifted, axis=-1, keepdims=True))
            grad_probs = contract_last(grad_mixed, values)
            delta = jnp.sum(grad_probs * probs, axis=-1, keepdims=True)
            grad_scores = (probs * (grad_probs - delta)).astype(bf16)
            value_grad[...] += contract_first(probs.astype(bf16), grad_mixed)
            key_grad[...] += contract_first(grad_scores, query)
            grad_query = jnp.dot(grad_scores, keys, preferred_element_type=f32) * score_scale
            grads[at, cols] = turn(grad_query, cos_ref[at], sin_ref[at], -1.0).astype(bf16)
            return carry

        lax.fori_loop(0, n_ctx // 2, step, 0)

    depth = n_ctx * strip_rows
    head_near, head_far = [], []

    def head_part(cols, slot):
        flip = (0, 2, 1, 3)[slot]
        places = pl.ds(pl.multiple_of(lax.bitwise_xor(fsdp, flip) * depth, depth), depth)
        total = contract_first(normed[:, :, places].reshape(seq_rows, depth), grads[:, cols])
        head_stage[slot, :, :, cols] = total.astype(bf16).reshape(n_ctx, strip_rows, -1)

    def head_begin(cols):
        copies = []
        for slot in (3, 2):
            head_part(cols, slot)
            copy = links.flip(
                head_stage.at[slot, :, :, cols],
                head_summed.at[slot - 2, :, :, cols],
                0,
                1,
            )
            copy.start()
            copies.append(copy)
        head_near.append(copies)
        for slot in (1, 0):
            head_part(cols, slot)

    def head_relay(index, cols):
        head_near[index][0].wait_recv()
        head_stage[1, :, :, cols] = (
            head_stage[1, :, :, cols].astype(f32) + head_summed[1, :, :, cols].astype(f32)
        ).astype(bf16)
        copy = links.flip(
            head_stage.at[1, :, :, cols], head_summed.at[2, :, :, cols], 0, 2
        )
        copy.start()
        head_far.append(copy)

    first_cols = pl.ds(0, HEAD_SIZE)
    rest_cols = pl.ds(HEAD_SIZE, grads.shape[1] - HEAD_SIZE)
    attend_head(0)
    loads[1].wait()
    up_scatter.middle()
    out_near = out_begin()
    loads[0].wait()
    head_begin(first_cols)
    for column in range(HEAD_SIZE, head_columns, HEAD_SIZE):
        attend_head(column)
    out_far = out_relay(out_near)
    turned = turn(key_grad[...] * score_scale, cos_ref[...], sin_ref[...], -1.0)
    grads[:, pl.ds(head_columns, HEAD_SIZE)] = turned.astype(bf16)
    grads[:, pl.ds(head_columns + HEAD_SIZE, HEAD_SIZE)] = value_grad[...].astype(bf16)
    head_begin(rest_cols)

    scatter = PlaneScatter(links, part, core_rx, half_rx, side_rx)
    for flip, q in scatter.order():
        at = pl.multiple_of(q * 2 * rows, 2 * rows)
        out = contract_last(grads[pl.ds(at, 2 * rows)], w_head_ref[...])
        part[pl.ds(2 * q, 2)] = out.astype(bf16).reshape(2, rows, width)
        scatter.give(flip, q)

    scatter.begin()
    head_relay(0, first_cols)
    scatter.middle()
    head_relay(1, rest_cols)
    up_copies = spread(up_scatter.finish(), up_out)
    grad_normed = scatter.finish()
    inputs = tokens_ref[...].astype(f32)
    scale = lax.rsqrt(jnp.mean(inputs * inputs, axis=-1, keepdims=True) + norm_eps)
    u = grad_normed * gain_ref[...]
    inner = jnp.mean(u * inputs, axis=-1, keepdims=True)
    grad_input_ref[...] = (
        grad_mid_ref[...] + scale * u - inputs * (scale * scale * scale * inner)
    )
    for copy in [pair[1] for pair in head_near] + head_far:
        copy.wait_recv()
    head_stage[0] = (
        head_stage[0].astype(f32) + head_summed[0].astype(f32) + head_summed[2].astype(f32)
    ).astype(bf16)
    head_copies = [
        links.plane(
            head_stage.at[0, lax.bitwise_xor(ctx, a)], head_landed.at[ctx], a
        )
        for a in range(1, n_ctx)
    ]
    start_all(head_copies)
    head_landed[ctx] = head_stage[0, ctx]

    for copy in (out_near[1], out_far):
        copy.wait_recv()
    out_sum[...] = (
        out_landed[fsdp].astype(f32) + out_summed[0].astype(f32) + out_summed[2].astype(f32)
    )
    for copy in head_copies:
        copy.wait_recv()
    for copy in locals_:
        copy.wait()
    query_columns = QUERY_HEADS * HEAD_SIZE
    key_columns = KEY_VALUE_HEADS * HEAD_SIZE
    for head in range(KEY_VALUE_HEADS):
        total = head_landed[head].astype(f32)
        qkv_sum[:, pl.ds(head * head_columns, head_columns)] = total[:, :head_columns]
        qkv_sum[:, pl.ds(query_columns + head * HEAD_SIZE, HEAD_SIZE)] = total[
            :, head_columns : head_columns + HEAD_SIZE
        ]
        qkv_sum[:, pl.ds(query_columns + key_columns + head * HEAD_SIZE, HEAD_SIZE)] = total[
            :, head_columns + HEAD_SIZE :
        ]
    for copy in gate_copies + up_copies:
        copy.wait_recv()
    for copy in gate_copies + up_copies + head_copies + head_far + head_near[0] + head_near[1]:
        copy.wait_send()
    for copy in out_near + [out_far]:
        copy.wait_send()
    for away, copy in out_copies:

        @pl.when(away)
        def _(copy=copy):
            copy.wait_send()

    gather.drain()
    scatter.drain()
    up_scatter.drain()


def attention_back(
    grad_proj,
    grad_mid,
    tokens,
    gain_attn,
    w_head,
    out_head,
    qkv,
    attended,
    cos,
    sin,
    key_pos,
    normed,
    gate_sum,
    up_part,
):
    f32, bf16 = jnp.float32, jnp.bfloat16
    n_ctx, n_fsdp = lax.axis_size("ctx"), lax.axis_size("fsdp")
    rows, width = tokens.shape
    seq_rows = n_ctx * rows
    strip_rows = width // (n_ctx * n_fsdp)
    head_columns, all_columns = attended.shape[1], qkv.shape[1]
    vmem, hbm = pl.BlockSpec(memory_space=pltpu.VMEM), pl.BlockSpec(memory_space=pl.ANY)
    shape = jax.ShapeDtypeStruct
    return pl.pallas_call(
        attention_back_kernel,
        name="attention_back",
        out_shape=[
            shape((rows, width), f32),
            shape((strip_rows, (QUERY_HEADS + 2 * KEY_VALUE_HEADS) * HEAD_SIZE), f32),
            shape((strip_rows, width), f32),
            shape((strip_rows, n_fsdp * width), bf16),
            shape((strip_rows, n_fsdp * width), bf16),
        ],
        in_specs=[vmem] * 12 + [hbm] * 3,
        out_specs=[vmem] * 3 + [hbm] * 2,
        scratch_shapes=[
            pltpu.VMEM((n_ctx, rows, width), bf16),
            pltpu.VMEM((n_ctx, rows, width), bf16),
            pltpu.VMEM(up_part.shape, bf16),
            pltpu.VMEM((2, BLOCK // 2, width), bf16),
            pltpu.VMEM((2, BLOCK, width), bf16),
            pltpu.VMEM((seq_rows, head_columns), bf16),
            pltpu.VMEM((seq_rows, all_columns), bf16),
            pltpu.VMEM((seq_rows, HEAD_SIZE), f32),
            pltpu.VMEM((seq_rows, HEAD_SIZE), f32),
            pltpu.VMEM((n_ctx, rows, width), bf16),
            pltpu.VMEM((n_ctx // 2, rows, width), bf16),
            pltpu.VMEM((2, rows // 2, width), bf16),
            pltpu.VMEM((2, rows, width), bf16),
            pltpu.VMEM((n_ctx // 2, strip_rows, width), bf16),
            pltpu.VMEM((n_fsdp, strip_rows, width), bf16),
            pltpu.VMEM((n_fsdp - 1, strip_rows, width), bf16),
            pltpu.VMEM((n_fsdp, n_ctx, strip_rows, all_columns), bf16),
            pltpu.VMEM((n_fsdp - 1, n_ctx, strip_rows, all_columns), bf16),
            pltpu.VMEM((n_ctx, strip_rows, all_columns), bf16),
            pltpu.SemaphoreType.DMA((96,)),
            pltpu.SemaphoreType.DMA((96,)),
            pltpu.SemaphoreType.DMA((8,)),
        ],
        compiler_params=pltpu.CompilerParams(
            collective_id=3, has_side_effects=True, vmem_limit_bytes=62 * 2**20
        ),
    )(
        grad_proj,
        grad_mid,
        tokens,
        gain_attn[None],
        w_head,
        out_head,
        qkv,
        attended,
        cos,
        sin,
        key_pos[:, None],
        key_pos[None],
        normed,
        gate_sum,
        up_part,
    )


def local_heads(
    tokens,
    cotangent,
    gain_attn,
    gain_ffn,
    query_key_value_weight,
    w_out,
    w_gate,
    w_up,
    w_down,
    pair_block,
):
    f32 = jnp.float32
    n_ctx, n_fsdp = lax.axis_size("ctx"), lax.axis_size("fsdp")
    ctx, fsdp = lax.axis_index("ctx"), lax.axis_index("fsdp")
    token_rows, width = tokens.shape
    depth = query_key_value_weight.shape[0]

    key_pos, own_pos = positions(pair_block, token_rows)
    frequency = jnp.exp(
        jnp.arange(HEAD_SIZE // 2, dtype=f32) * (-2.0 * math.log(rope_base) / HEAD_SIZE)
    )
    angles = key_pos.astype(f32)[:, None] * frequency[None, :]
    cosine, sine_val = jnp.cos(angles), jnp.sin(angles)
    cos = jnp.concatenate([cosine, cosine], axis=1)
    sin = jnp.concatenate([-sine_val, sine_val], axis=1)
    (
        mid,
        normed_two_group,
        cot_near,
        cot_far,
        gate_w,
        up_w,
        qkv,
        attended,
        normed_one_seq,
        w_head,
        out_head,
    ) = attention_forward(
        tokens,
        cotangent,
        gain_attn,
        gain_ffn,
        query_key_value_weight,
        w_out,
        w_gate,
        w_up,
        cos,
        sin,
        key_pos,
    )
    result, grad_mid, grad_proj, down_sum, gate_sum, up_part = feed_forward(
        mid,
        cotangent,
        gain_ffn,
        normed_two_group,
        cot_near,
        cot_far,
        gate_w,
        up_w,
        w_down.reshape(-1, BLOCK, width),
    )
    grad_input, grad_qkv, grad_out, gate_low, up_low = attention_back(
        grad_proj,
        grad_mid,
        tokens,
        gain_attn,
        w_head,
        out_head,
        qkv,
        attended,
        cos,
        sin,
        key_pos,
        normed_one_seq,
        gate_sum,
        up_part,
    )
    grad_down = down_sum.astype(f32)
    grad_gate, grad_up = gate_low.astype(f32), up_low.astype(f32)

    my_rows = ctx * (depth // n_ctx)
    rows_of = lambda matrix: lax.dynamic_slice_in_dim(
        matrix, my_rows, depth // n_ctx, 0
    ).astype(f32)
    attn_sum = jnp.sum(rows_of(query_key_value_weight) * grad_qkv, axis=1)
    ffn_sum = jnp.sum(rows_of(w_gate) * grad_gate, axis=1) + jnp.sum(
        rows_of(w_up) * grad_up, axis=1
    )
    gain_pairs = [
        (c * n_fsdp + f, f * n_ctx + c) for c in range(n_ctx) for f in range(n_fsdp)
    ]
    moved = lax.ppermute(jnp.stack([attn_sum, ffn_sum]), ("ctx", "fsdp"), gain_pairs)
    my_gain = (ctx * n_fsdp + fsdp) * (depth // n_ctx)
    grad_gain_attn = moved[0] / lax.dynamic_slice_in_dim(gain_attn, my_gain, depth // n_ctx)
    grad_gain_ffn = moved[1] / lax.dynamic_slice_in_dim(gain_ffn, my_gain, depth // n_ctx)
    return (
        result,
        grad_input,
        grad_gain_attn,
        grad_gain_ffn,
        grad_qkv,
        grad_out,
        grad_gate,
        grad_up,
        grad_down,
    )


def solution(mesh):
    fits = mesh.shape["ctx"] == KEY_VALUE_HEADS and mesh.shape["fsdp"] == KEY_VALUE_HEADS // 2
    local = local_heads if fits else local_general
    return jax.shard_map(
        local,
        mesh=mesh,
        in_specs=(
            P(("ctx", "fsdp"), None),
            P(("ctx", "fsdp"), None),
            P(),
            P(),
            P("fsdp", None),
            P("fsdp", None),
            P("fsdp", None),
            P("fsdp", None),
            P("fsdp", None),
            P(),
        ),
        out_specs=(
            P(("ctx", "fsdp"), None),
            P(("ctx", "fsdp"), None),
            P(("ctx", "fsdp")),
            P(("ctx", "fsdp")),
            P(("fsdp", "ctx"), None),
            P(("fsdp", "ctx"), None),
            P(("fsdp", "ctx"), None),
            P(("fsdp", "ctx"), None),
            P(("fsdp", "ctx"), None),
        ),
        check_vma=False,
    )
```

```python
import math

import jax
import jax.numpy as jnp
from jax import lax
from jax.experimental import pallas as pl
from jax.experimental.pallas import tpu as pltpu
from jax.sharding import PartitionSpec as P

QUERY_HEADS = 16
KEY_VALUE_HEADS = 8
HEAD_SIZE = 128


norm_eps = 1e-05
rope_base = 1000000.0


def rms_norm(vectors, gain_vec):
    return (
        vectors
        * lax.rsqrt(jnp.mean(vectors * vectors, axis=-1, keepdims=True) + norm_eps)
        * gain_vec
    )


def apply_rotation(vectors, where_pos):
    half_dim = vectors.shape[-1] // 2
    frequency = jnp.exp(
        jnp.arange(half_dim, dtype=jnp.float32) * (-2.0 * math.log(rope_base) / vectors.shape[-1])
    )
    angles = where_pos.astype(jnp.float32)[:, None] * frequency[None, :]
    cosine = jnp.cos(angles)[:, None, :]
    sine_val = jnp.sin(angles)[:, None, :]
    first_half = vectors[..., :half_dim]
    second_half = vectors[..., half_dim:]
    return jnp.concatenate(
        [
            first_half * cosine - second_half * sine_val,
            second_half * cosine + first_half * sine_val,
        ],
        axis=-1,
    )


def positions(pair_block, token_rows):
    n_ctx = lax.axis_size("ctx")
    half_rows = token_rows // 2
    row_index = jnp.arange(token_rows, dtype=jnp.int32)
    first_block = pair_block[:, None]
    which_block = jnp.where(
        row_index[None, :] < half_rows, first_block, 2 * n_ctx - 1 - first_block
    )
    pos_table = which_block * half_rows + (row_index % half_rows)[None, :]
    own_pos = lax.dynamic_slice(pos_table, (lax.axis_index("ctx"), 0), (1, token_rows)).reshape(
        token_rows
    )
    return (pos_table.reshape(-1), own_pos)


def to_groups(input_array, group_count):
    token_rows = input_array.shape[0]
    head_length = input_array.shape[-1] // (group_count * KEY_VALUE_HEADS)
    return (
        input_array.reshape(token_rows, KEY_VALUE_HEADS, group_count, head_length)
        .transpose(1, 2, 0, 3)
        .reshape(KEY_VALUE_HEADS, group_count * token_rows, head_length)
    )


def from_groups(input_array, group_count):
    head_length = input_array.shape[-1]
    token_rows = input_array.shape[1] // group_count
    return (
        input_array.reshape(KEY_VALUE_HEADS, group_count, token_rows, head_length)
        .transpose(2, 0, 1, 3)
        .reshape(token_rows, KEY_VALUE_HEADS * group_count * head_length)
    )


def split_keys(every_key, every_value, key_pos):
    total_keys = every_key.shape[0]
    block_length = min(1024, total_keys)
    block_count = total_keys // block_length
    return (
        every_key.reshape(block_count, block_length, KEY_VALUE_HEADS, HEAD_SIZE),
        every_value.reshape(block_count, block_length, KEY_VALUE_HEADS, HEAD_SIZE),
        key_pos.reshape(block_count, block_length),
    )


def contract_last(left, right):
    return lax.dot_general(
        left, right, (((1,), (1,)), ((), ())), preferred_element_type=jnp.float32
    )


def contract_first(left, right):
    return lax.dot_general(
        left, right, (((0,), (0,)), ((), ())), preferred_element_type=jnp.float32
    )


def local_general(
    tokens,
    cotangent,
    gain_attn,
    gain_ffn,
    query_key_value_weight,
    w_out,
    w_gate,
    w_up,
    w_down,
    pair_block,
):
    token_rows = tokens.shape[0]
    query_columns = QUERY_HEADS * HEAD_SIZE
    key_value_columns = KEY_VALUE_HEADS * HEAD_SIZE
    group_count = QUERY_HEADS // KEY_VALUE_HEADS
    score_scale = 1.0 / math.sqrt(HEAD_SIZE)
    ff_cols = w_gate.shape[1]
    key_pos, own_pos = positions(pair_block, token_rows)
    query_pos = jnp.tile(own_pos, group_count)
    inputs_f = tokens.astype(jnp.float32)
    qkv_full, out_full = (
        lax.all_gather(query_key_value_weight, "fsdp", axis=0, tiled=True),
        lax.all_gather(w_out, "fsdp", axis=0, tiled=True),
    )
    normed_one_b = rms_norm(inputs_f, gain_attn).astype(jnp.bfloat16)
    projected_rows = jnp.dot(normed_one_b, qkv_full, preferred_element_type=jnp.float32)
    query_raw = projected_rows[:, :query_columns].reshape(token_rows, QUERY_HEADS, HEAD_SIZE)
    unrotated_key = projected_rows[:, query_columns : query_columns + key_value_columns].reshape(
        token_rows, KEY_VALUE_HEADS, HEAD_SIZE
    )
    query_b = (
        apply_rotation(query_raw, own_pos).astype(jnp.bfloat16).reshape(token_rows, query_columns)
    )
    keys_b = (
        apply_rotation(unrotated_key, own_pos)
        .astype(jnp.bfloat16)
        .reshape(token_rows, key_value_columns)
    )
    values_b = projected_rows[:, query_columns + key_value_columns :].astype(jnp.bfloat16)
    every_key, every_value = (
        lax.all_gather(keys_b, "ctx", axis=0, tiled=True),
        lax.all_gather(values_b, "ctx", axis=0, tiled=True),
    )
    query_grp = to_groups(query_b, group_count)
    key_blocks, value_blocks, pos_blocks = split_keys(every_key, every_value, key_pos)

    def forward_step(carry, block_in):
        run_max, run_total, weighted = carry
        key_block, value_block, block_pos = block_in
        causal = block_pos[None, None, :] <= query_pos[None, :, None]
        scores = (
            jnp.einsum("hqd,khd->hqk", query_grp, key_block, preferred_element_type=jnp.float32)
            * score_scale
        )
        scores = jnp.where(causal, scores, -1e30)
        new_max = jnp.maximum(run_max, jnp.max(scores, axis=-1))
        exp_scores = jnp.where(causal, jnp.exp(scores - new_max[..., None]), 0.0)
        fading = jnp.exp(run_max - new_max)
        run_total = run_total * fading + jnp.sum(exp_scores, axis=-1)
        weighted = weighted * fading[..., None] + jnp.einsum(
            "hqk,khd->hqd",
            exp_scores.astype(jnp.bfloat16),
            value_block,
            preferred_element_type=jnp.float32,
        )
        return ((new_max, run_total, weighted), None)

    initial_maximum = jnp.full((KEY_VALUE_HEADS, group_count * token_rows), -1e30, jnp.float32)
    initial_total = jnp.zeros((KEY_VALUE_HEADS, group_count * token_rows), jnp.float32)
    initial_weighted = jnp.zeros(
        (KEY_VALUE_HEADS, group_count * token_rows, HEAD_SIZE), jnp.float32
    )
    final_carry, ignored = lax.scan(
        forward_step,
        (initial_maximum, initial_total, initial_weighted),
        (key_blocks, value_blocks, pos_blocks),
    )
    run_max, run_total, weighted = final_carry
    log_total = run_max + jnp.log(run_total)
    attn_grp = weighted / run_total[..., None]
    attended_b = from_groups(attn_grp.astype(jnp.bfloat16), group_count)
    mid_rows = inputs_f + jnp.dot(attended_b, out_full, preferred_element_type=jnp.float32)
    gate_full, up_full, down_full = (
        lax.all_gather(w_gate, "fsdp", axis=0, tiled=True),
        lax.all_gather(w_up, "fsdp", axis=0, tiled=True),
        lax.all_gather(w_down, "fsdp", axis=0, tiled=True),
    )
    normed_two_b = rms_norm(mid_rows, gain_ffn).astype(jnp.bfloat16)
    gate_val = jnp.dot(normed_two_b, gate_full, preferred_element_type=jnp.float32)
    up_val = jnp.dot(normed_two_b, up_full, preferred_element_type=jnp.float32)
    hidden_b = (jax.nn.silu(gate_val) * up_val).astype(jnp.bfloat16)
    output_f = mid_rows + jnp.dot(hidden_b, down_full, preferred_element_type=jnp.float32)
    result = output_f.astype(jnp.bfloat16)
    normed_one_x, attended_x, normed_two_x, hidden_x = (
        lax.all_to_all(normed_one_b, "fsdp", split_axis=1, concat_axis=0, tiled=True),
        lax.all_to_all(attended_b, "fsdp", split_axis=1, concat_axis=0, tiled=True),
        lax.all_to_all(normed_two_b, "fsdp", split_axis=1, concat_axis=0, tiled=True),
        lax.all_to_all(hidden_b, "fsdp", split_axis=1, concat_axis=0, tiled=True),
    )
    grad_out_f = cotangent.astype(jnp.float32)
    gate_back, up_back, down_back = (
        lax.all_gather(w_gate, "fsdp", axis=0, tiled=True),
        lax.all_gather(w_up, "fsdp", axis=0, tiled=True),
        lax.all_gather(w_down, "fsdp", axis=0, tiled=True),
    )
    grad_hidden = contract_last(cotangent, down_back)
    ignored, ffn_back = jax.vjp(
        lambda gate_in, up_in: jax.nn.silu(gate_in) * up_in, gate_val, up_val
    )
    grad_gate_f, grad_up_f = ffn_back(grad_hidden)
    grad_gate_b = grad_gate_f.astype(jnp.bfloat16)
    grad_up_b = grad_up_f.astype(jnp.bfloat16)
    grad_normed_two = contract_last(grad_gate_b, gate_back) + contract_last(grad_up_b, up_back)
    ignored, norm_two_back = jax.vjp(rms_norm, mid_rows, gain_ffn)
    grad_mid_part, gain_ffn_part = norm_two_back(grad_normed_two)
    grad_mid = grad_out_f + grad_mid_part
    gate_up_b = jnp.concatenate([grad_gate_b, grad_up_b], axis=1)
    qkv_back, out_back = (
        lax.all_gather(query_key_value_weight, "fsdp", axis=0, tiled=True),
        lax.all_gather(w_out, "fsdp", axis=0, tiled=True),
    )
    grad_proj_b = grad_mid.astype(jnp.bfloat16)
    grad_att_b = contract_last(grad_proj_b, out_back).astype(jnp.bfloat16)
    grad_att_grp = to_groups(grad_att_b, group_count)
    delta_rows = jnp.sum(grad_att_grp.astype(jnp.float32) * attn_grp, axis=-1)

    def backward_step(grad_query, block_in):
        key_block, value_block, block_pos = block_in
        causal = block_pos[None, None, :] <= query_pos[None, :, None]
        scores = (
            jnp.einsum("hqd,khd->hqk", query_grp, key_block, preferred_element_type=jnp.float32)
            * score_scale
        )
        probs = jnp.where(causal, jnp.exp(scores - log_total[..., None]), 0.0)
        grad_values = jnp.einsum(
            "hqk,hqd->khd",
            probs.astype(jnp.bfloat16),
            grad_att_grp,
            preferred_element_type=jnp.float32,
        )
        grad_probs = jnp.einsum(
            "hqd,khd->hqk", grad_att_grp, value_block, preferred_element_type=jnp.float32
        )
        grad_scores = (probs * (grad_probs - delta_rows[..., None])).astype(jnp.bfloat16)
        grad_query = grad_query + score_scale * jnp.einsum(
            "hqk,khd->hqd", grad_scores, key_block, preferred_element_type=jnp.float32
        )
        grad_keys = score_scale * jnp.einsum(
            "hqk,hqd->khd", grad_scores, query_grp, preferred_element_type=jnp.float32
        )
        return (grad_query, (grad_keys, grad_values))

    grad_query_grp, key_grads = lax.scan(
        backward_step,
        jnp.zeros((KEY_VALUE_HEADS, group_count * token_rows, HEAD_SIZE), jnp.float32),
        (key_blocks, value_blocks, pos_blocks),
    )
    total_keys = key_pos.shape[0]
    grad_keys_all = key_grads[0].reshape(total_keys, key_value_columns)
    grad_values_all = key_grads[1].reshape(total_keys, key_value_columns)
    key_sums, summed_values = (
        lax.psum_scatter(
            grad_keys_all.astype(jnp.bfloat16), "ctx", scatter_dimension=0, tiled=True
        ).astype(jnp.float32),
        lax.psum_scatter(
            grad_values_all.astype(jnp.bfloat16), "ctx", scatter_dimension=0, tiled=True
        ).astype(jnp.float32),
    )
    grad_query_rows = from_groups(grad_query_grp, group_count).reshape(
        token_rows, QUERY_HEADS, HEAD_SIZE
    )
    ignored, query_rope_back = jax.vjp(lambda vectors: apply_rotation(vectors, own_pos), query_raw)
    ignored, key_rotation_backward = jax.vjp(
        lambda vectors: apply_rotation(vectors, own_pos), unrotated_key
    )
    grad_query_raw = query_rope_back(grad_query_rows)[0]
    unrotated_key_gradient = key_rotation_backward(
        key_sums.reshape(token_rows, KEY_VALUE_HEADS, HEAD_SIZE)
    )[0]
    grad_projected_b = jnp.concatenate(
        [
            grad_query_raw.reshape(token_rows, query_columns),
            unrotated_key_gradient.reshape(token_rows, key_value_columns),
            summed_values,
        ],
        axis=1,
    ).astype(jnp.bfloat16)
    grad_normed_one = contract_last(grad_projected_b, qkv_back)
    ignored, norm_one_back = jax.vjp(rms_norm, inputs_f, gain_attn)
    grad_in_part, gain_attn_part = norm_one_back(grad_normed_one)
    grad_input = grad_mid + grad_in_part
    cot_group, gate_up_group, projected_group, proj_group = (
        lax.all_gather(cotangent, "fsdp", axis=0, tiled=True),
        lax.all_gather(gate_up_b, "fsdp", axis=0, tiled=True),
        lax.all_gather(grad_projected_b, "fsdp", axis=0, tiled=True),
        lax.all_gather(grad_proj_b, "fsdp", axis=0, tiled=True),
    )
    qkv_part = contract_first(normed_one_x, projected_group)
    out_part = contract_first(attended_x, proj_group)
    gate_up_part = contract_first(normed_two_x, gate_up_group)
    gate_part = gate_up_part[:, :ff_cols]
    up_part = gate_up_part[:, ff_cols:]
    down_part = contract_first(hidden_x, cot_group)
    grad_qkv, grad_out, grad_down = (
        lax.psum_scatter(
            qkv_part.astype(jnp.bfloat16), "ctx", scatter_dimension=0, tiled=True
        ).astype(jnp.float32),
        lax.psum_scatter(
            out_part.astype(jnp.bfloat16), "ctx", scatter_dimension=0, tiled=True
        ).astype(jnp.float32),
        lax.psum_scatter(
            down_part.astype(jnp.bfloat16), "ctx", scatter_dimension=0, tiled=True
        ).astype(jnp.float32),
    )
    grad_gate, grad_up = (
        lax.psum_scatter(
            gate_part.astype(jnp.bfloat16), "ctx", scatter_dimension=0, tiled=True
        ).astype(jnp.float32),
        lax.psum_scatter(
            up_part.astype(jnp.bfloat16), "ctx", scatter_dimension=0, tiled=True
        ).astype(jnp.float32),
    )
    grad_gain_attn, grad_gain_ffn = (
        lax.psum_scatter(gain_attn_part, ("ctx", "fsdp"), scatter_dimension=0, tiled=True),
        lax.psum_scatter(gain_ffn_part, ("ctx", "fsdp"), scatter_dimension=0, tiled=True),
    )
    return (
        result,
        grad_input,
        grad_gain_attn,
        grad_gain_ffn,
        grad_qkv,
        grad_out,
        grad_gate,
        grad_up,
        grad_down,
    )


MESH = pl.DeviceIdType.MESH
ACROSS_X, ACROSS_Y, ACROSS_CORE = 2, 4, 1
BLOCK = 256


class Links:
    def __init__(self, sems, ctx, fsdp):
        self.send_sem, self.recv_sem, self.local_sem = sems
        self.ctx, self.fsdp = ctx, fsdp
        self.remote = self.locals = 0

    def to(self, src, dst, ctx, fsdp):
        index, self.remote = self.remote, self.remote + 1
        return pltpu.make_async_remote_copy(
            src_ref=src,
            dst_ref=dst,
            send_sem=self.send_sem.at[index],
            recv_sem=self.recv_sem.at[index],
            device_id=(ctx, fsdp),
            device_id_type=MESH,
        )

    def flip(self, src, dst, ctx_flip, fsdp_flip):
        return self.to(
            src, dst, lax.bitwise_xor(self.ctx, ctx_flip), lax.bitwise_xor(self.fsdp, fsdp_flip)
        )

    def plane(self, src, dst, flip):
        return self.flip(src, dst, flip, 0)

    def column(self, src, dst, flip):
        return self.flip(src, dst, 0, flip)

    def here(self, src, dst):
        index, self.locals = self.locals, self.locals + 1
        return pltpu.make_async_copy(src, dst, self.local_sem.at[index])


PLANE_FLIPS = [(1, 0), (2, 0), (4, 0)]
COLUMN_FLIPS = [(0, 1), (0, 2), (0, 3)]


def greet(ctx, fsdp, flips):
    barrier = pltpu.get_barrier_semaphore()
    for a, b in flips:
        pl.semaphore_signal(
            barrier,
            inc=1,
            device_id=(lax.bitwise_xor(ctx, a), lax.bitwise_xor(fsdp, b)),
            device_id_type=MESH,
        )
    pl.semaphore_wait(barrier, len(flips))


def start_all(copies):
    for copy in copies:
        copy.start()


class LineGather:
    def __init__(self, links, own, group):
        self.links, self.group = links, group
        self.home = links.here(own, group.at[0])
        self.near = links.column(own, group.at[2], 1)
        self.far = links.column(own, group.at[1], 2)
        self.relay = links.column(group.at[1], group.at[3], 1)

    def begin(self):
        start_all([self.far, self.near, self.home])

    def forward(self):
        self.far.wait_recv()
        self.relay.start()

    def finish(self):
        self.near.wait_recv()
        self.relay.wait_recv()
        for copy in (self.near, self.far, self.relay):
            copy.wait_send()
        self.home.wait()


class PlaneGather:
    def __init__(self, links, blocks, halves):
        self.links, self.blocks, self.halves = links, blocks, halves
        self.ctx = links.ctx
        self.sent = []
        self.cores = []

    def _go(self, copies):
        for copy in copies:
            copy.start()
        self.sent += copies
        return copies

    def _core(self, index):
        refs = self.blocks(index)
        self.cores += self._go([self.links.plane(r, r, ACROSS_CORE) for r in refs])

    def begin(self, sources=None):
        refs = self.blocks(self.ctx)
        pairs = list(zip(sources or refs, refs))
        self.from_x = self._go([self.links.plane(s, r, ACROSS_X) for s, r in pairs])
        self.from_y = self._go([self.links.plane(s, r, ACROSS_Y) for s, r in pairs])
        self.cores += self._go([self.links.plane(s, r, ACROSS_CORE) for s, r in pairs])

    def forward(self):
        index = lax.bitwise_xor(self.ctx, ACROSS_X)
        for copy in self.from_x:
            copy.wait_recv()
        refs = self.halves(index, 0)
        self.corner = self._go([self.links.plane(r, r, ACROSS_Y) for r in refs])
        self._core(index)
        index = lax.bitwise_xor(self.ctx, ACROSS_Y)
        for copy in self.from_y:
            copy.wait_recv()
        refs = self.halves(index, 1)
        self.corner += self._go([self.links.plane(r, r, ACROSS_X) for r in refs])
        self._core(index)

    def finish(self):
        for copy in self.corner:
            copy.wait_recv()
        self._core(lax.bitwise_xor(self.ctx, ACROSS_X | ACROSS_Y))
        for copy in self.cores:
            copy.wait_recv()

    def drain(self):
        for copy in self.sent:
            copy.wait_send()


class PlaneScatter:
    def __init__(self, links, part, core_rx, half_rx, side_rx):
        self.links, self.part = links, part
        self.core_rx, self.half_rx, self.side_rx = core_rx, half_rx, side_rx
        self.chip, self.core = links.ctx // 2, lax.rem(links.ctx, 2)
        self.sent = []
        self.from_core = {}

    def order(self):
        return [(flip, lax.bitwise_xor(self.chip, flip)) for flip in (3, 1, 2, 0)]

    def _go(self, copy):
        copy.start()
        self.sent.append(copy)
        return copy

    def give(self, flip, chip):
        self.from_core[flip] = self._go(
            self.links.plane(
                self.part.at[2 * chip + 1 - self.core], self.core_rx.at[chip], ACROSS_CORE
            )
        )

    def _summed(self, flip):
        chip = lax.bitwise_xor(self.chip, flip)
        self.from_core[flip].wait_recv()
        mine = self.part.at[2 * chip + self.core]
        total = mine[...].astype(jnp.float32) + self.core_rx[chip].astype(jnp.float32)
        return mine, total

    def begin(self):
        half = self.half = self.half_rx.shape[1]
        mine, total = self._summed(3)
        mine[...] = total.astype(jnp.bfloat16)
        self.corner = [
            self._go(self.links.plane(mine.at[pl.ds(0, half)], self.half_rx.at[0], ACROSS_Y)),
            self._go(
                self.links.plane(mine.at[pl.ds(half, half)], self.half_rx.at[1], ACROSS_X)
            ),
        ]

    def middle(self):
        self.sides = []
        for flip, across, slot in ((1, ACROSS_X, 0), (2, ACROSS_Y, 1)):
            mine, total = self._summed(flip)
            mine[...] = total.astype(jnp.bfloat16)
            self.corner[slot].wait_recv()
            rows = pl.ds(slot * self.half, self.half)
            mine[rows] = (
                total[slot * self.half : (slot + 1) * self.half]
                + self.half_rx[slot].astype(jnp.float32)
            ).astype(jnp.bfloat16)
            self.sides.append(self._go(self.links.plane(mine, self.side_rx.at[slot], across)))

    def finish(self):
        mine, total = self._summed(0)
        for slot, copy in enumerate(self.sides):
            copy.wait_recv()
            total = total + self.side_rx[slot].astype(jnp.float32)
        return total

    def drain(self):
        for copy in self.sent:
            copy.wait_send()


def swap_bits(fsdp):
    return 2 * lax.rem(fsdp, 2) + fsdp // 2


def place_positions(pair_ref, pos_col, pos_row, rows):
    half, n_ctx = rows // 2, pos_col.shape[0] // rows
    down = lax.broadcasted_iota(jnp.int32, (rows, 1), 0)
    along = lax.broadcasted_iota(jnp.int32, (1, rows), 1)
    for j in range(n_ctx):
        first = pair_ref[j] * half
        second = (2 * n_ctx - 1 - pair_ref[j]) * half - half
        pos_col[pl.ds(j * rows, rows)] = down + jnp.where(down < half, first, second)
        pos_row[:, pl.ds(j * rows, rows)] = along + jnp.where(along < half, first, second)


def turn(vectors, cos_rows, sin_rows, sign):
    return vectors * cos_rows + sign * pltpu.roll(vectors, HEAD_SIZE // 2, 1) * sin_rows


def attention_kernel(
    tokens_ref,
    cot_ref,
    gain_one_ref,
    gain_two_ref,
    qkv_w_ref,
    out_w_ref,
    gate_ref,
    up_ref,
    pair_ref,
    mid_ref,
    normed_two_group,
    cot_near,
    cot_far,
    gate_w,
    up_w,
    qkv_out,
    attended_out,
    normed_one_out,
    w_head_out,
    out_head_out,
    cos_out,
    sin_out,
    normed,
    w_head,
    out_head,
    out_relay,
    qkv,
    attended,
    part,
    core_rx,
    half_rx,
    side_rx,
    normed_two,
    cos_ref,
    sin_ref,
    pos_col_ref,
    pos_row_ref,
    send_sem,
    recv_sem,
    local_sem,
):
    f32, bf16 = jnp.float32, jnp.bfloat16
    ctx, fsdp = lax.axis_index("ctx"), lax.axis_index("fsdp")
    links = Links((send_sem, recv_sem, local_sem), ctx, fsdp)
    rows, width = tokens_ref.shape
    depth = qkv_w_ref.shape[0]
    head_columns = out_head.shape[0]
    n_ctx, n_fsdp = normed.shape[0], width // depth
    seq_rows = n_ctx * rows
    hidden = gate_w.shape[2]
    strip = hidden // n_ctx
    depth_blocks = gate_ref.shape[0]
    query_columns = QUERY_HEADS * HEAD_SIZE
    key_columns = KEY_VALUE_HEADS * HEAD_SIZE
    score_scale = 1.0 / math.sqrt(HEAD_SIZE)
    finals = []

    greet(ctx, fsdp, PLANE_FLIPS + COLUMN_FLIPS + [(6, 0)])

    out_block = out_w_ref.at[
        pl.ds(pl.multiple_of(lax.rem(ctx, 2) * head_columns, head_columns), head_columns)
    ]
    out_target = swap_bits(lax.bitwise_xor(ctx // 2, fsdp))
    out_away = out_target != fsdp
    out_copy = links.to(out_block, out_relay, ctx, out_target)
    out_home = links.here(out_block, out_relay)
    out_flip = 2 * swap_bits(fsdp)
    out_moves = fsdp != 0
    out_last = links.to(out_relay, out_head, lax.bitwise_xor(ctx, out_flip), fsdp)
    out_stays = links.here(out_relay, out_head)

    @pl.when(out_away)
    def _():
        out_copy.start()

    @pl.when(jnp.logical_not(out_away))
    def _():
        out_home.start()

    def rows_of(plane):
        return pl.ds(pl.multiple_of(plane * depth, depth), depth)

    head_parts, places = [], []
    for start, size, place in (
        (ctx * head_columns, head_columns, 0),
        (query_columns + ctx * HEAD_SIZE, HEAD_SIZE, head_columns),
        (query_columns + key_columns + ctx * HEAD_SIZE, HEAD_SIZE, head_columns + HEAD_SIZE),
    ):
        places.append(pl.ds(place, size))
        head_parts.append(
            (
                qkv_w_ref.at[:, pl.ds(pl.multiple_of(start, HEAD_SIZE), size)],
                w_head.at[rows_of(fsdp), pl.ds(place, size)],
            )
        )
    head_far = [links.column(src, dst, 2) for src, dst in head_parts]
    head_near = [links.column(src, dst, 1) for src, dst in head_parts]
    own_head = [links.here(src, dst) for src, dst in head_parts]
    start_all(head_far + head_near + own_head)

    def place_of(j):
        return pl.ds(pl.multiple_of(j * strip, strip), strip)

    def strips(target):
        cols = pl.ds(pl.multiple_of(target * hidden + ctx * strip, strip), strip)
        blocks = pl.ds(fsdp * depth_blocks, depth_blocks)
        for source, dest in ((gate_ref, gate_w), (up_ref, up_w)):
            yield source.at[:, :, cols], dest.at[blocks, :, place_of(ctx)]

    strip_copies = [[links.here(src, dst) for src, dst in strips(fsdp)]]
    for flip in (1, 2, 3):
        strip_copies.append(
            [links.column(s, d, flip) for s, d in strips(lax.bitwise_xor(fsdp, flip))]
        )
    start_all(strip_copies[0])

    def strip_gather(flip):
        first = lax.bitwise_xor(fsdp, flip) * depth_blocks
        blocks = pl.ds(first, depth_blocks)
        return PlaneGather(
            links,
            lambda j: [w.at[blocks, :, place_of(j)] for w in (gate_w, up_w)],
            lambda j, which: [w.at[first + which, :, place_of(j)] for w in (gate_w, up_w)],
        )

    weights = [strip_gather(flip) for flip in range(n_fsdp)]

    inputs = tokens_ref[...].astype(f32)
    scale = lax.rsqrt(jnp.mean(inputs * inputs, axis=-1, keepdims=True) + norm_eps)
    normed[ctx] = (inputs * scale * gain_one_ref[...]).astype(bf16)
    half = rows // 2
    gather = PlaneGather(
        links,
        lambda j: [normed.at[j]],
        lambda j, which: [normed.at[j, pl.ds(which * half, half)]],
    )
    gather.begin()

    place_positions(pair_ref, pos_col_ref, pos_row_ref, rows)
    lane = lax.broadcasted_iota(jnp.int32, (1, HEAD_SIZE), 1)
    lane_half = lax.rem(lane, HEAD_SIZE // 2).astype(f32)
    frequency = jnp.exp(lane_half * (-2.0 * math.log(rope_base) / HEAD_SIZE))
    side = jnp.where(lane < HEAD_SIZE // 2, -1.0, 1.0)

    def tables(step, carry):
        at = pl.ds(pl.multiple_of(step * rows, rows), rows)
        angles = pos_col_ref[at].astype(f32) * frequency
        cos_ref[at] = jnp.cos(angles)
        sin_ref[at] = side * jnp.sin(angles)
        return carry

    lax.fori_loop(0, n_ctx, tables, 0)
    for src, dst in ((cos_ref, cos_out), (sin_ref, sin_out)):
        finals.append(links.here(src, dst))
        finals[-1].start()
    gather.forward()
    weights[0].begin([source for source, dest in strips(fsdp)])
    gather.finish()

    @pl.when(out_away)
    def _():
        out_copy.wait_recv()

    @pl.when(jnp.logical_not(out_away))
    def _():
        out_home.wait()

    @pl.when(out_moves)
    def _():
        out_last.start()

    @pl.when(jnp.logical_not(out_moves))
    def _():
        out_stays.start()

    weights[0].forward()
    cot_copies = [links.column(cot_ref, cot_far, 2), links.column(cot_ref, cot_near, 1)]
    head_relay = []
    far_rows = rows_of(lax.bitwise_xor(fsdp, 2))
    for copy, place in zip(head_far, places):
        copy.wait_recv()
        block = w_head.at[far_rows, place]
        head_relay.append(links.column(block, block, 1))
        head_relay[-1].start()
    start_all(cot_copies[:1])
    weights[0].finish()
    finals.append(links.here(normed, normed_one_out))
    finals[-1].start()
    for copy in own_head:
        copy.wait()
    for copy in head_near + head_relay:
        copy.wait_recv()
    start_all(strip_copies[1] + strip_copies[2] + strip_copies[3])

    block_rows = 2 * rows

    def project(step, carry):
        at = pl.multiple_of(step * block_rows, block_rows)
        tile = normed[pl.ds(step * 2, 2)].reshape(block_rows, width)
        out = jnp.dot(tile, w_head[...], preferred_element_type=f32)
        cos_rows, sin_rows = cos_ref[pl.ds(at, block_rows)], sin_ref[pl.ds(at, block_rows)]
        for column in range(0, head_columns + HEAD_SIZE, HEAD_SIZE):
            turned = turn(out[:, column : column + HEAD_SIZE], cos_rows, sin_rows, 1.0)
            qkv[pl.ds(at, block_rows), pl.ds(column, HEAD_SIZE)] = turned.astype(bf16)
        column = head_columns + HEAD_SIZE
        qkv[pl.ds(at, block_rows), pl.ds(column, HEAD_SIZE)] = out[:, column:].astype(bf16)
        return carry

    lax.fori_loop(0, seq_rows // block_rows, project, 0)
    def attend(step, carry):
        at = pl.multiple_of(step * block_rows, block_rows)
        keys = qkv[:, pl.ds(head_columns, HEAD_SIZE)]
        values = qkv[:, pl.ds(head_columns + HEAD_SIZE, HEAD_SIZE)]
        causal = pos_row_ref[...] <= pos_col_ref[pl.ds(at, block_rows)]
        for column in range(0, head_columns, HEAD_SIZE):
            query = qkv[pl.ds(at, block_rows), pl.ds(column, HEAD_SIZE)]
            scores = contract_last(query, keys) * score_scale
            scores = jnp.where(causal, scores, -1e30)
            shifted = jnp.exp(scores - jnp.max(scores, axis=-1, keepdims=True))
            probs = shifted * (1.0 / jnp.sum(shifted, axis=-1, keepdims=True))
            mixed = jnp.dot(probs.astype(bf16), values, preferred_element_type=f32)
            attended[pl.ds(at, block_rows), pl.ds(column, HEAD_SIZE)] = mixed.astype(bf16)
        return carry

    lax.fori_loop(0, seq_rows // block_rows, attend, 0)

    @pl.when(out_moves)
    def _():
        out_last.wait_recv()

    @pl.when(jnp.logical_not(out_moves))
    def _():
        out_stays.wait()

    for src, dst in (        (qkv, qkv_out),
        (attended, attended_out),
        (w_head, w_head_out),
        (out_head, out_head_out),
    ):
        finals.append(links.here(src, dst))
        finals[-1].start()

    scatter = PlaneScatter(links, part, core_rx, half_rx, side_rx)
    for flip, chip in scatter.order():
        at = pl.multiple_of(chip * block_rows, block_rows)
        out = jnp.dot(
            attended[pl.ds(at, block_rows)], out_head[...], preferred_element_type=f32
        )
        part[pl.ds(chip * 2, 2)] = out.astype(bf16).reshape(2, rows, width)
        scatter.give(flip, chip)

    def arrived(flip):
        for copy in strip_copies[flip]:
            copy.wait_recv()
        weights[flip].begin()

    scatter.begin()
    scatter.middle()
    mid = tokens_ref[...].astype(f32) + scatter.finish()
    mid_ref[...] = mid
    mid_scale = lax.rsqrt(jnp.mean(mid * mid, axis=-1, keepdims=True) + norm_eps)
    normed_two[...] = (mid * mid_scale * gain_two_ref[...]).astype(bf16)

    group = LineGather(links, normed_two, normed_two_group)
    group.begin()
    arrived(1)
    arrived(2)
    weights[1].forward()
    group.forward()
    start_all(cot_copies[1:])
    arrived(3)
    weights[2].forward()
    weights[1].finish()
    weights[3].forward()
    weights[2].finish()
    weights[3].finish()
    group.finish()
    for copy in cot_copies:
        copy.wait()
    for copy in strip_copies[0]:
        copy.wait()

    for copies in [head_far, head_near, head_relay] + strip_copies[1:]:
        for copy in copies:
            copy.wait_send()

    @pl.when(out_away)
    def _():
        out_copy.wait_send()

    @pl.when(out_moves)
    def _():
        out_last.wait_send()

    gather.drain()
    scatter.drain()
    for item in weights:
        item.drain()
    for copy in finals:
        copy.wait()


def attention_forward(
    tokens, cotangent, gain_attn, gain_ffn, qkv_w, w_out, w_gate, w_up, pair_block
):
    f32, bf16 = jnp.float32, jnp.bfloat16
    n_ctx, n_fsdp = lax.axis_size("ctx"), lax.axis_size("fsdp")
    rows, width = tokens.shape
    depth = qkv_w.shape[0]
    hidden = w_gate.shape[1] // n_fsdp
    seq_rows = n_ctx * rows
    head_columns = QUERY_HEADS // KEY_VALUE_HEADS * HEAD_SIZE
    all_columns = head_columns + 2 * HEAD_SIZE
    vmem, hbm = pl.BlockSpec(memory_space=pltpu.VMEM), pl.BlockSpec(memory_space=pl.ANY)
    shape = jax.ShapeDtypeStruct
    return pl.pallas_call(
        attention_kernel,
        name="attention_forward",
        out_shape=[
            shape((rows, width), f32),
            shape((n_fsdp, rows, width), bf16),
            shape((rows, width), bf16),
            shape((rows, width), bf16),
            shape((width // BLOCK, BLOCK, hidden), bf16),
            shape((width // BLOCK, BLOCK, hidden), bf16),
            shape((seq_rows, all_columns), bf16),
            shape((seq_rows, head_columns), bf16),
            shape((n_ctx, rows, width), bf16),
            shape((width, all_columns), bf16),
            shape((head_columns, width), bf16),
            shape((seq_rows, HEAD_SIZE), f32),
            shape((seq_rows, HEAD_SIZE), f32),
        ],
        in_specs=[vmem] * 4 + [hbm] * 4 + [pl.BlockSpec(memory_space=pltpu.SMEM)],
        out_specs=[vmem] + [hbm] * 12,
        scratch_shapes=[
            pltpu.VMEM((n_ctx, rows, width), bf16),
            pltpu.VMEM((width, all_columns), bf16),
            pltpu.VMEM((head_columns, width), bf16),
            pltpu.VMEM((head_columns, width), bf16),
            pltpu.VMEM((seq_rows, all_columns), bf16),
            pltpu.VMEM((seq_rows, head_columns), bf16),
            pltpu.VMEM((n_ctx, rows, width), bf16),
            pltpu.VMEM((n_ctx // 2, rows, width), bf16),
            pltpu.VMEM((2, rows // 2, width), bf16),
            pltpu.VMEM((2, rows, width), bf16),
            pltpu.VMEM((rows, width), bf16),
            pltpu.VMEM((seq_rows, HEAD_SIZE), f32),
            pltpu.VMEM((seq_rows, HEAD_SIZE), f32),
            pltpu.VMEM((seq_rows, 1), jnp.int32),
            pltpu.VMEM((1, seq_rows), jnp.int32),
            pltpu.SemaphoreType.DMA((112,)),
            pltpu.SemaphoreType.DMA((112,)),
            pltpu.SemaphoreType.DMA((16,)),
        ],
        compiler_params=pltpu.CompilerParams(
            collective_id=1, has_side_effects=True, vmem_limit_bytes=58 * 2**20
        ),
    )(
        tokens,
        cotangent,
        gain_attn[None],
        gain_ffn[None],
        qkv_w,
        w_out,
        w_gate.reshape(depth // BLOCK, BLOCK, -1),
        w_up.reshape(depth // BLOCK, BLOCK, -1),
        pair_block,
    )


class ChipScatter:
    def __init__(self, links, parts, halves, sides):
        self.links, self.parts, self.halves, self.sides = links, parts, halves, sides
        self.sent = []

    def _go(self, copy):
        copy.start()
        self.sent.append(copy)
        return copy

    def begin(self, source=None):
        corner = self.parts[3] if source is None else source
        half = corner.shape[0] // 2
        self.half = half
        self.corner = [
            self._go(self.links.plane(corner.at[pl.ds(0, half)], self.halves[0], ACROSS_Y)),
            self._go(self.links.plane(corner.at[pl.ds(half, half)], self.halves[1], ACROSS_X)),
        ]

    def middle(self):
        self.side = []
        for slot, (flip, across) in enumerate(((1, ACROSS_X), (2, ACROSS_Y))):
            mine = self.parts[flip]
            self.corner[slot].wait_recv()
            rows = mine.at[pl.ds(slot * self.half, self.half)]
            rows[...] = (
                rows[...].astype(jnp.float32) + self.halves[slot][...].astype(jnp.float32)
            ).astype(jnp.bfloat16)
            self.side.append(self._go(self.links.plane(mine, self.sides[slot], across)))

    def finish(self):
        mine = self.parts[0]
        for copy in self.side:
            copy.wait_recv()
        mine[...] = (
            mine[...].astype(jnp.float32)
            + self.sides[0][...].astype(jnp.float32)
            + self.sides[1][...].astype(jnp.float32)
        ).astype(jnp.bfloat16)
        return mine

    def drain(self):
        for copy in self.sent:
            copy.wait_send()


def feed_forward_kernel(
    mid_ref,
    cot_ref,
    gain_ref,
    normed_ref,
    cot_near_ref,
    cot_far_ref,
    gate_hbm,
    up_hbm,
    down_hbm,
    result_ref,
    grad_mid_ref,
    grad_proj_ref,
    down_sum,
    gate_sum,
    up_part,
    gate_v,
    up_v,
    down_v,
    cots,
    hidden,
    grad_gate,
    grad_up,
    other_normed,
    other_cots,
    other_hidden,
    other_gate,
    other_up,
    stage,
    landed,
    down_parts,
    down_halves,
    send_sem,
    recv_sem,
    local_sem,
    load_sem,
    down_free,
    gate_free,
):
    f32, bf16 = jnp.float32, jnp.bfloat16
    ctx, fsdp = lax.axis_index("ctx"), lax.axis_index("fsdp")
    links = Links((send_sem, recv_sem, local_sem), ctx, fsdp)
    core = lax.rem(ctx, 2)
    rows, width = mid_ref.shape
    blocks = gate_v.shape[0]
    hidden_units = blocks * BLOCK
    half_units = hidden_units // 2
    n_fsdp = normed_ref.shape[0]
    group_rows = n_fsdp * rows

    def loads(j):
        cols = pl.ds(pl.multiple_of(j * BLOCK, BLOCK), BLOCK)
        return (
            pltpu.make_async_copy(
                gate_hbm.at[:, :, cols], gate_v.at[:, :, cols], load_sem.at[0, j]
            ),
            pltpu.make_async_copy(up_hbm.at[:, :, cols], up_v.at[:, :, cols], load_sem.at[1, j]),
            pltpu.make_async_copy(down_hbm.at[j], down_v.at[j], load_sem.at[2, j]),
        )

    for j in range(blocks):
        for copy in loads(j):
            copy.start()

    greet(ctx, fsdp, PLANE_FLIPS + COLUMN_FLIPS[:2])

    cot_relay = links.column(cot_far_ref, cots.at[3], 1)
    cot_relay.start()
    cots[0] = cot_ref[...]
    cots[1] = cot_far_ref[...]
    cots[2] = cot_near_ref[...]
    mid_load = links.here(mid_ref, grad_mid_ref)
    mid_load.start()

    swaps = [links.plane(normed_ref, other_normed, ACROSS_CORE)]
    cot_swaps = [links.plane(cots.at[s], other_cots.at[s], ACROSS_CORE) for s in range(n_fsdp)]
    start_all(swaps + cot_swaps[:3])

    half_slots, half_rows = n_fsdp // 2, group_rows // 2

    def activate(j, carry):
        for copy in loads(j):
            copy.wait()
        cols = pl.ds(pl.multiple_of(j * BLOCK, BLOCK), BLOCK)
        for first in (0, half_slots):
            at = pl.ds(first * rows, half_rows)
            normed = normed_ref[pl.ds(first, half_slots)].reshape(half_rows, width)
            gate = jnp.dot(
                normed, gate_v[:, :, cols].reshape(width, BLOCK), preferred_element_type=f32
            )
            up = jnp.dot(
                normed, up_v[:, :, cols].reshape(width, BLOCK), preferred_element_type=f32
            )
            sig = jax.nn.sigmoid(gate)
            silu = gate * sig
            hidden[at, cols] = (silu * up).astype(bf16)
            grad_gate[at, cols] = (up * (sig * (1.0 + gate * (1.0 - sig)))).astype(bf16)
            grad_up[at, cols] = silu.astype(bf16)
        return carry

    lax.fori_loop(0, blocks, activate, 0)

    hidden_acts = []
    for pair in range(blocks // 2):
        cols = pl.ds(pl.multiple_of((2 * pair + 1 - core) * BLOCK, BLOCK), BLOCK)
        hidden_acts.append(
            links.plane(
                hidden.at[:, cols], other_hidden.at[:, pl.ds(pair * BLOCK, BLOCK)], ACROSS_CORE
            )
        )
    start_all(hidden_acts)
    piece = 2 * BLOCK
    pieces = width // piece

    def spot(n):
        return pl.ds(n * piece, piece)

    def put(which, first, n, value):
        stage[which, pl.ds(first, half_slots), :, spot(n)] = value.astype(bf16).reshape(
            half_slots, rows, piece
        )

    def down_out(first, n):
        value = jnp.dot(
            hidden[pl.ds(first * rows, half_rows)],
            down_v[:, :, spot(n)].reshape(hidden_units, piece),
            preferred_element_type=f32,
        )
        put(0, first, n, value)

    def back_out(first, n):
        at, some = pl.ds(first * rows, half_rows), pl.ds(n * 2, 2)
        value = contract_last(grad_gate[at], gate_v[some].reshape(piece, hidden_units))
        value = value + contract_last(grad_up[at], up_v[some].reshape(piece, hidden_units))
        put(1, first, n, value)

    near, far = {}, []

    def send_near(which, n):
        near[which, n] = [
            links.column(stage.at[which, 3, :, spot(n)], landed.at[which, 1, :, spot(n)], 1),
            links.column(stage.at[which, 2, :, spot(n)], landed.at[which, 0, :, spot(n)], 1),
        ]
        start_all(near[which, n])

    def relay(which, n):
        near[which, n][0].wait_recv()
        stage[which, 1, :, spot(n)] = (
            stage[which, 1, :, spot(n)].astype(f32) + landed[which, 1, :, spot(n)].astype(f32)
        ).astype(bf16)
        copy = links.column(stage.at[which, 1, :, spot(n)], landed.at[which, 2, :, spot(n)], 2)
        copy.start()
        far.append(copy)

    for n in range(pieces):
        down_out(half_slots, n)
        send_near(0, n)
        down_out(0, n)

    def activation_grads(first):
        at = pl.ds(first * rows, half_rows)

        def step(j, carry):
            cols = pl.ds(pl.multiple_of(j * BLOCK, BLOCK), BLOCK)
            cot_rows = cots[pl.ds(first, half_slots)].reshape(half_rows, width)
            grad_hidden = contract_last(cot_rows, down_v[j])
            grad_gate[at, cols] = (grad_gate[at, cols].astype(f32) * grad_hidden).astype(bf16)
            grad_up[at, cols] = (grad_up[at, cols].astype(f32) * grad_hidden).astype(bf16)
            return carry

        lax.fori_loop(0, blocks, step, 0)

    for copy in [cot_relay]:
        copy.wait_recv()
    start_all(cot_swaps[3:])
    def flat(ref, cols):
        return ref[:, :, cols].reshape(group_rows, -1)

    for copy in cot_swaps + hidden_acts:
        copy.wait_recv()

    def down_block(pair, place):
        own = pl.ds(pl.multiple_of((2 * pair + core) * BLOCK, BLOCK), BLOCK)
        other = pl.ds(pl.multiple_of(pair * BLOCK, BLOCK), BLOCK)
        left, right = hidden[:, own].T, other_hidden[:, other].T
        for cols in (pl.ds(0, width // 2), pl.ds(width // 2, width // 2)):
            total = jnp.dot(left, flat(cots, cols), preferred_element_type=f32)
            total = total + jnp.dot(right, flat(other_cots, cols), preferred_element_type=f32)
            place[:, cols] = total.astype(bf16)

    def halves_of(ref):
        return [ref.at[pl.ds(0, BLOCK // 2)], ref.at[pl.ds(BLOCK // 2, BLOCK // 2)]]

    chip = ctx // 2
    down_scatter = ChipScatter(
        links,
        [down_v.at[2]] + [down_parts.at[flip - 1] for flip in (1, 2, 3)],
        halves_of(down_halves),
        [down_v.at[0], down_v.at[1]],
    )
    down_block(lax.bitwise_xor(chip, 3), down_parts.at[2])
    down_scatter.begin()

    def down_side(flip, carry):
        down_block(lax.bitwise_xor(chip, flip), down_parts.at[flip - 1])
        return carry

    lax.fori_loop(1, 3, down_side, 0)
    activation_grads(0)
    activation_grads(half_slots)
    down_block(chip, down_v.at[2])
    theirs = pl.ds(pl.multiple_of((1 - core) * half_units, half_units), half_units)
    acts = [
        links.plane(grad_gate.at[:, theirs], other_gate, ACROSS_CORE),
        links.plane(grad_up.at[:, theirs], other_up, ACROSS_CORE),
    ]
    start_all(acts)

    def free(sem):
        for flip in (ACROSS_X, ACROSS_Y):
            pl.semaphore_signal(
                sem,
                inc=1,
                device_id=(lax.bitwise_xor(ctx, flip), fsdp),
                device_id_type=MESH,
            )

    free(down_free)

    for n in range(pieces):
        back_out(half_slots, n)
        send_near(1, n)
    pl.semaphore_wait(down_free, 2)
    down_scatter.middle()
    for n in range(pieces):
        back_out(0, n)
    free(gate_free)
    relay(0, 0)
    relay(0, 1)

    mine = pl.ds(pl.multiple_of(core * half_units, half_units), half_units)

    def weight_block(b, carry):
        cols = pl.ds(pl.multiple_of(b * BLOCK, BLOCK), BLOCK)
        left, right = flat(normed_ref, cols).T, flat(other_normed, cols).T
        plane, first = b // 2, 2 * lax.rem(b, 2)
        at_row = pl.ds(pl.multiple_of((plane // 2) * (BLOCK // 2), BLOCK // 2), BLOCK // 2)
        at_col = pl.ds(pl.multiple_of(lax.rem(plane, 2) * (width // 2), width // 2), width // 2)
        for own_grad, other_grad, place in (
            (grad_gate, other_gate, gate_v),
            (grad_up, other_up, up_v),
        ):
            total = jnp.dot(left, own_grad[:, mine], preferred_element_type=f32)
            total = total + jnp.dot(right, other_grad[...], preferred_element_type=f32)
            low = total.astype(bf16)
            place[first, at_row, at_col] = low[: BLOCK // 2]
            place[first + 1, at_row, at_col] = low[BLOCK // 2 :]
        return carry

    for copy in swaps + acts:
        copy.wait_recv()
    lax.fori_loop(0, blocks // 2, weight_block, 0)
    relay(0, 2)
    lax.fori_loop(blocks // 2, blocks, weight_block, 0)
    pl.semaphore_wait(gate_free, 2)
    gate_scatter = ChipScatter(
        links,
        [gate_v.at[lax.bitwise_xor(chip, flip)] for flip in range(4)],
        halves_of(gate_v.at[4]),
        [gate_v.at[5], gate_v.at[6]],
    )
    gate_scatter.begin()
    up_copy = links.here(up_v.at[pl.ds(0, 4)], up_part)
    up_copy.start()
    relay(0, 3)
    relay(1, 0)
    relay(1, 1)
    relay(1, 2)
    relay(1, 3)
    gate_scatter.middle()
    down_copy = links.here(down_scatter.finish(), down_sum)
    down_copy.start()

    for copy in [pair[1] for pair in near.values()] + far:
        copy.wait_recv()
    for copies in near.values():
        for copy in copies:
            copy.wait_send()
    mid_load.wait()
    chunk = 32

    def close(step, carry):
        at = pl.ds(pl.multiple_of(step * chunk, chunk), chunk)

        def summed(which):
            total = stage[which, 0, at].astype(f32) + landed[which, 0, at].astype(f32)
            return total + landed[which, 2, at].astype(f32)

        mid = grad_mid_ref[at]
        stage[0, 2, at] = (mid + summed(0)).astype(bf16)
        scale = lax.rsqrt(jnp.mean(mid * mid, axis=-1, keepdims=True) + norm_eps)
        u = summed(1) * gain_ref[...]
        inner = jnp.mean(u * mid, axis=-1, keepdims=True)
        grad_mid = (
            cots[0, at].astype(f32) + scale * u - mid * (scale * scale * scale * inner)
        )
        grad_mid_ref[at] = grad_mid
        stage[1, 2, at] = grad_mid.astype(bf16)
        return carry

    lax.fori_loop(0, rows // chunk, close, 0)
    row_copies = [
        links.here(stage.at[0, 2], result_ref),
        links.here(stage.at[1, 2], grad_proj_ref),
    ]
    start_all(row_copies)

    gate_copy = links.here(gate_scatter.finish(), gate_sum)
    gate_copy.start()
    sent = far + swaps + cot_swaps
    for copy in sent + hidden_acts + acts + [cot_relay]:
        copy.wait_send()
    down_scatter.drain()
    gate_scatter.drain()
    for copy in row_copies + [up_copy, down_copy, gate_copy]:
        copy.wait()


def feed_forward(
    mid, cotangent, gain_ffn, normed_group, cot_near, cot_far, gate_w, up_w, w_down
):
    f32, bf16 = jnp.float32, jnp.bfloat16
    n_fsdp = lax.axis_size("fsdp")
    rows, width = mid.shape
    group_rows = n_fsdp * rows
    units = w_down.shape[0] * BLOCK
    blocks = units // BLOCK
    vmem, hbm = pl.BlockSpec(memory_space=pltpu.VMEM), pl.BlockSpec(memory_space=pl.ANY)
    shape = jax.ShapeDtypeStruct
    return pl.pallas_call(
        feed_forward_kernel,
        name="feed_forward",
        out_shape=[
            shape((rows, width), bf16),
            shape((rows, width), f32),
            shape((rows, width), bf16),
            shape((BLOCK, width), bf16),
            shape((BLOCK, width), bf16),
            shape((blocks // 2, BLOCK, width), bf16),
        ],
        in_specs=[hbm] + [vmem] * 5 + [hbm] * 3,
        out_specs=[hbm, vmem, hbm] + [hbm] * 3,
        scratch_shapes=[
            pltpu.VMEM((width // BLOCK, BLOCK, units), bf16),
            pltpu.VMEM((width // BLOCK, BLOCK, units), bf16),
            pltpu.VMEM((blocks, BLOCK, width), bf16),
            pltpu.VMEM((n_fsdp, rows, width), bf16),
            pltpu.VMEM((group_rows, units), bf16),
            pltpu.VMEM((group_rows, units), bf16),
            pltpu.VMEM((group_rows, units), bf16),
            pltpu.VMEM((n_fsdp, rows, width), bf16),
            pltpu.VMEM((n_fsdp, rows, width), bf16),
            pltpu.VMEM((group_rows, units // 2), bf16),
            pltpu.VMEM((group_rows, units // 2), bf16),
            pltpu.VMEM((group_rows, units // 2), bf16),
            pltpu.VMEM((2, n_fsdp, rows, width), bf16),
            pltpu.VMEM((2, n_fsdp - 1, rows, width), bf16),
            pltpu.VMEM((blocks // 2 - 1, BLOCK, width), bf16),
            pltpu.VMEM((BLOCK, width), bf16),
            pltpu.SemaphoreType.DMA((48,)),
            pltpu.SemaphoreType.DMA((48,)),
            pltpu.SemaphoreType.DMA((8,)),
            pltpu.SemaphoreType.DMA((3, blocks)),
            pltpu.SemaphoreType.REGULAR,
            pltpu.SemaphoreType.REGULAR,
        ],
        compiler_params=pltpu.CompilerParams(
            collective_id=2, has_side_effects=True, vmem_limit_bytes=62 * 2**20
        ),
    )(mid, cotangent, gain_ffn[None], normed_group, cot_near, cot_far, gate_w, up_w, w_down)


def attention_back_kernel(
    grad_proj_ref,
    grad_mid_ref,
    tokens_ref,
    gain_ref,
    w_head_ref,
    out_head_ref,
    qkv_ref,
    attended_ref,
    cos_ref,
    sin_ref,
    pair_ref,
    normed_hbm,
    gate_sum_hbm,
    up_part_hbm,
    grad_input_ref,
    qkv_sum,
    out_sum,
    gate_out,
    up_out,
    proj,
    normed,
    up_part,
    up_halves,
    up_sides,
    grad_att,
    grads,
    key_grad,
    value_grad,
    part,
    core_rx,
    half_rx,
    side_rx,
    out_stage,
    out_landed,
    out_summed,
    head_stage,
    head_summed,
    head_landed,
    pos_col_ref,
    pos_row_ref,
    send_sem,
    recv_sem,
    local_sem,
):
    f32, bf16 = jnp.float32, jnp.bfloat16
    ctx, fsdp = lax.axis_index("ctx"), lax.axis_index("fsdp")
    links = Links((send_sem, recv_sem, local_sem), ctx, fsdp)
    chip, core = ctx // 2, lax.rem(ctx, 2)
    n_ctx, rows, width = proj.shape
    n_fsdp = out_landed.shape[0]
    seq_rows = n_ctx * rows
    head_columns = out_head_ref.shape[0]
    strip_rows = out_landed.shape[1]
    score_scale = 1.0 / math.sqrt(HEAD_SIZE)
    loads = [links.here(normed_hbm, normed), links.here(up_part_hbm, up_part)]
    for copy in loads:
        copy.start()

    flips = [(a, 0) for a in range(1, n_ctx)] + COLUMN_FLIPS + [(1, b) for b in (1, 2, 3)]
    greet(ctx, fsdp, flips)

    proj[ctx] = grad_proj_ref[...]
    half = rows // 2
    gather = PlaneGather(
        links,
        lambda j: [proj.at[j]],
        lambda j, which: [proj.at[j, pl.ds(which * half, half)]],
    )
    gather.begin()
    place_positions(pair_ref, pos_col_ref, pos_row_ref, rows)

    def spread(source, dest):
        half_width = width // 2
        place = pl.ds(pl.multiple_of((2 * fsdp + core) * half_width, half_width), half_width)
        copies = []
        for a in (0, 1):
            for b in range(n_fsdp):
                plane = lax.bitwise_xor(fsdp, b)
                who = lax.bitwise_xor(core, a)
                at_row = (plane // 2) * (BLOCK // 2) + who * strip_rows
                block = source.at[
                    pl.ds(pl.multiple_of(at_row, strip_rows), strip_rows),
                    pl.ds(pl.multiple_of(lax.rem(plane, 2) * half_width, half_width), half_width),
                ]
                target = dest.at[:, place]
                if a or b:
                    copies.append(
                        links.to(block, target, lax.bitwise_xor(ctx, a), plane)
                    )
                else:
                    local = links.here(block, target)
                    locals_.append(local)
                    local.start()
        for copy in copies:
            copy.start()
        return copies

    locals_ = []
    up_scatter = ChipScatter(
        links,
        [up_part.at[lax.bitwise_xor(chip, flip)] for flip in range(4)],
        [up_halves.at[0], up_halves.at[1]],
        [up_sides.at[0], up_sides.at[1]],
    )
    gate_copies = spread(gate_sum_hbm, gate_out)
    gather.forward()
    gather.finish()

    total = jnp.zeros((head_columns, width), f32)
    for j in range(0, n_ctx, 2):
        total = total + lax.dot_general(
            attended_ref[pl.ds(j * rows, 2 * rows)],
            proj[pl.ds(j, 2)].reshape(2 * rows, width),
            (((0,), (0,)), ((), ())),
            preferred_element_type=f32,
        )
    out_stage[...] = total.astype(bf16).reshape(out_stage.shape)
    half_ctx = n_ctx // 2
    out_base = links.remote
    links.remote += half_ctx
    out_copies = []
    for j in range(half_ctx):
        target = half_ctx * core + j
        copy = pltpu.make_async_remote_copy(
            src_ref=out_stage.at[j],
            dst_ref=out_landed.at[chip],
            send_sem=send_sem.at[out_base + j],
            recv_sem=recv_sem.at[out_base + chip],
            device_id=(target, fsdp),
            device_id_type=MESH,
        )
        out_copies.append((target != ctx, copy))

        @pl.when(target != ctx)
        def _(copy=copy):
            copy.start()

    own_out = links.here(out_stage.at[lax.rem(ctx, half_ctx)], out_landed.at[chip])
    out_own_chip = lax.rem(ctx, 2) == ctx // half_ctx

    @pl.when(out_own_chip)
    def _():
        own_out.start()

    up_scatter.begin(up_part_hbm.at[lax.bitwise_xor(chip, 3)])

    def out_arrivals():
        for source in range(half_ctx):
            arrival = pltpu.make_async_remote_copy(
                src_ref=out_stage.at[0],
                dst_ref=out_landed.at[source],
                send_sem=send_sem.at[out_base],
                recv_sem=recv_sem.at[out_base + source],
                device_id=(lax.bitwise_xor(ctx, 1), fsdp),
                device_id_type=MESH,
            )

            @pl.when(2 * source + ctx // half_ctx != ctx)
            def _(arrival=arrival):
                arrival.wait_recv()

        @pl.when(out_own_chip)
        def _():
            own_out.wait()

    def out_begin():
        out_arrivals()
        copies = [
            links.column(
                out_landed.at[lax.bitwise_xor(fsdp, flip)], out_summed.at[slot], 1
            )
            for flip, slot in ((3, 1), (1, 0))
        ]
        start_all(copies)
        return copies

    def out_relay(copies):
        copies[0].wait_recv()
        across = lax.bitwise_xor(fsdp, 2)
        out_landed[across] = (
            out_landed[across].astype(f32) + out_summed[1].astype(f32)
        ).astype(bf16)
        copy = links.column(out_landed.at[across], out_summed.at[2], 2)
        copy.start()
        return copy

    def back(step, carry):
        at = pl.multiple_of(step * 2 * rows, 2 * rows)
        tile = proj[pl.ds(2 * step, 2)].reshape(2 * rows, width)
        grad_att[pl.ds(at, 2 * rows)] = contract_last(tile, out_head_ref[...]).astype(bf16)
        return carry

    lax.fori_loop(0, n_ctx // 2, back, 0)

    key_grad[...] = jnp.zeros_like(key_grad)
    value_grad[...] = jnp.zeros_like(value_grad)

    def attend_head(column):
        cols = pl.ds(column, HEAD_SIZE)

        def step(index, carry):
            at = pl.ds(pl.multiple_of(index * 2 * rows, 2 * rows), 2 * rows)
            keys = qkv_ref[:, pl.ds(head_columns, HEAD_SIZE)]
            values = qkv_ref[:, pl.ds(head_columns + HEAD_SIZE, HEAD_SIZE)]
            causal = pos_row_ref[...] <= pos_col_ref[at]
            query, grad_mixed = qkv_ref[at, cols], grad_att[at, cols]
            scores = contract_last(query, keys) * score_scale
            scores = jnp.where(causal, scores, -1e30)
            shifted = jnp.exp(scores - jnp.max(scores, axis=-1, keepdims=True))
            probs = shifted * (1.0 / jnp.sum(shifted, axis=-1, keepdims=True))
            grad_probs = contract_last(grad_mixed, values)
            delta = jnp.sum(grad_probs * probs, axis=-1, keepdims=True)
            grad_scores = (probs * (grad_probs - delta)).astype(bf16)
            value_grad[...] += contract_first(probs.astype(bf16), grad_mixed)
            key_grad[...] += contract_first(grad_scores, query)
            grad_query = jnp.dot(grad_scores, keys, preferred_element_type=f32) * score_scale
            grads[at, cols] = turn(grad_query, cos_ref[at], sin_ref[at], -1.0).astype(bf16)
            return carry

        lax.fori_loop(0, n_ctx // 2, step, 0)

    depth = n_ctx * strip_rows
    head_near, head_far = [], []

    def head_part(cols, slot):
        flip = (0, 2, 1, 3)[slot]
        places = pl.ds(pl.multiple_of(lax.bitwise_xor(fsdp, flip) * depth, depth), depth)
        total = contract_first(normed[:, :, places].reshape(seq_rows, depth), grads[:, cols])
        head_stage[slot, :, :, cols] = total.astype(bf16).reshape(n_ctx, strip_rows, -1)

    def head_begin(cols):
        copies = []
        for slot in (3, 2):
            head_part(cols, slot)
            copy = links.flip(
                head_stage.at[slot, :, :, cols],
                head_summed.at[slot - 2, :, :, cols],
                0,
                1,
            )
            copy.start()
            copies.append(copy)
        head_near.append(copies)
        for slot in (1, 0):
            head_part(cols, slot)

    def head_relay(index, cols):
        head_near[index][0].wait_recv()
        head_stage[1, :, :, cols] = (
            head_stage[1, :, :, cols].astype(f32) + head_summed[1, :, :, cols].astype(f32)
        ).astype(bf16)
        copy = links.flip(
            head_stage.at[1, :, :, cols], head_summed.at[2, :, :, cols], 0, 2
        )
        copy.start()
        head_far.append(copy)

    first_cols = pl.ds(0, HEAD_SIZE)
    rest_cols = pl.ds(HEAD_SIZE, grads.shape[1] - HEAD_SIZE)
    attend_head(0)
    loads[0].wait()
    head_begin(first_cols)
    out_near = out_begin()
    for column in range(HEAD_SIZE, head_columns, HEAD_SIZE):
        attend_head(column)
    loads[1].wait()
    up_scatter.middle()
    turned = turn(key_grad[...] * score_scale, cos_ref[...], sin_ref[...], -1.0)
    grads[:, pl.ds(head_columns, HEAD_SIZE)] = turned.astype(bf16)
    grads[:, pl.ds(head_columns + HEAD_SIZE, HEAD_SIZE)] = value_grad[...].astype(bf16)
    head_begin(rest_cols)

    scatter = PlaneScatter(links, part, core_rx, half_rx, side_rx)
    for flip, q in scatter.order():
        at = pl.multiple_of(q * 2 * rows, 2 * rows)
        out = contract_last(grads[pl.ds(at, 2 * rows)], w_head_ref[...])
        part[pl.ds(2 * q, 2)] = out.astype(bf16).reshape(2, rows, width)
        scatter.give(flip, q)

    scatter.begin()
    head_relay(0, first_cols)
    out_far = out_relay(out_near)
    head_relay(1, rest_cols)
    scatter.middle()
    up_copies = spread(up_scatter.finish(), up_out)
    grad_normed = scatter.finish()
    inputs = tokens_ref[...].astype(f32)
    scale = lax.rsqrt(jnp.mean(inputs * inputs, axis=-1, keepdims=True) + norm_eps)
    u = grad_normed * gain_ref[...]
    inner = jnp.mean(u * inputs, axis=-1, keepdims=True)
    grad_input_ref[...] = (
        grad_mid_ref[...] + scale * u - inputs * (scale * scale * scale * inner)
    )
    for copy in [pair[1] for pair in head_near] + head_far:
        copy.wait_recv()
    head_stage[0] = (
        head_stage[0].astype(f32) + head_summed[0].astype(f32) + head_summed[2].astype(f32)
    ).astype(bf16)
    head_copies = [
        links.plane(
            head_stage.at[0, lax.bitwise_xor(ctx, a)], head_landed.at[ctx], a
        )
        for a in range(1, n_ctx)
    ]
    start_all(head_copies)
    head_landed[ctx] = head_stage[0, ctx]

    for copy in (out_near[1], out_far):
        copy.wait_recv()
    out_sum[...] = (
        out_landed[fsdp].astype(f32) + out_summed[0].astype(f32) + out_summed[2].astype(f32)
    )
    for copy in head_copies:
        copy.wait_recv()
    for copy in locals_:
        copy.wait()
    query_columns = QUERY_HEADS * HEAD_SIZE
    key_columns = KEY_VALUE_HEADS * HEAD_SIZE
    for head in range(KEY_VALUE_HEADS):
        total = head_landed[head].astype(f32)
        qkv_sum[:, pl.ds(head * head_columns, head_columns)] = total[:, :head_columns]
        qkv_sum[:, pl.ds(query_columns + head * HEAD_SIZE, HEAD_SIZE)] = total[
            :, head_columns : head_columns + HEAD_SIZE
        ]
        qkv_sum[:, pl.ds(query_columns + key_columns + head * HEAD_SIZE, HEAD_SIZE)] = total[
            :, head_columns + HEAD_SIZE :
        ]
    for copy in gate_copies + up_copies:
        copy.wait_recv()
    for copy in gate_copies + up_copies + head_copies + head_far + head_near[0] + head_near[1]:
        copy.wait_send()
    for copy in out_near + [out_far]:
        copy.wait_send()
    for away, copy in out_copies:

        @pl.when(away)
        def _(copy=copy):
            copy.wait_send()

    gather.drain()
    scatter.drain()
    up_scatter.drain()


def attention_back(
    grad_proj,
    grad_mid,
    tokens,
    gain_attn,
    w_head,
    out_head,
    qkv,
    attended,
    cos,
    sin,
    pair_block,
    normed,
    gate_sum,
    up_part,
):
    f32, bf16 = jnp.float32, jnp.bfloat16
    n_ctx, n_fsdp = lax.axis_size("ctx"), lax.axis_size("fsdp")
    rows, width = tokens.shape
    seq_rows = n_ctx * rows
    strip_rows = width // (n_ctx * n_fsdp)
    head_columns, all_columns = attended.shape[1], qkv.shape[1]
    vmem, hbm = pl.BlockSpec(memory_space=pltpu.VMEM), pl.BlockSpec(memory_space=pl.ANY)
    shape = jax.ShapeDtypeStruct
    return pl.pallas_call(
        attention_back_kernel,
        name="attention_back",
        out_shape=[
            shape((rows, width), f32),
            shape((strip_rows, (QUERY_HEADS + 2 * KEY_VALUE_HEADS) * HEAD_SIZE), f32),
            shape((strip_rows, width), f32),
            shape((strip_rows, n_fsdp * width), bf16),
            shape((strip_rows, n_fsdp * width), bf16),
        ],
        in_specs=[vmem] * 10 + [pl.BlockSpec(memory_space=pltpu.SMEM)] + [hbm] * 3,
        out_specs=[vmem] * 3 + [hbm] * 2,
        scratch_shapes=[
            pltpu.VMEM((n_ctx, rows, width), bf16),
            pltpu.VMEM((n_ctx, rows, width), bf16),
            pltpu.VMEM(up_part.shape, bf16),
            pltpu.VMEM((2, BLOCK // 2, width), bf16),
            pltpu.VMEM((2, BLOCK, width), bf16),
            pltpu.VMEM((seq_rows, head_columns), bf16),
            pltpu.VMEM((seq_rows, all_columns), bf16),
            pltpu.VMEM((seq_rows, HEAD_SIZE), f32),
            pltpu.VMEM((seq_rows, HEAD_SIZE), f32),
            pltpu.VMEM((n_ctx, rows, width), bf16),
            pltpu.VMEM((n_ctx // 2, rows, width), bf16),
            pltpu.VMEM((2, rows // 2, width), bf16),
            pltpu.VMEM((2, rows, width), bf16),
            pltpu.VMEM((n_ctx // 2, strip_rows, width), bf16),
            pltpu.VMEM((n_fsdp, strip_rows, width), bf16),
            pltpu.VMEM((n_fsdp - 1, strip_rows, width), bf16),
            pltpu.VMEM((n_fsdp, n_ctx, strip_rows, all_columns), bf16),
            pltpu.VMEM((n_fsdp - 1, n_ctx, strip_rows, all_columns), bf16),
            pltpu.VMEM((n_ctx, strip_rows, all_columns), bf16),
            pltpu.VMEM((seq_rows, 1), jnp.int32),
            pltpu.VMEM((1, seq_rows), jnp.int32),
            pltpu.SemaphoreType.DMA((96,)),
            pltpu.SemaphoreType.DMA((96,)),
            pltpu.SemaphoreType.DMA((8,)),
        ],
        compiler_params=pltpu.CompilerParams(
            collective_id=3, has_side_effects=True, vmem_limit_bytes=62 * 2**20
        ),
    )(
        grad_proj,
        grad_mid,
        tokens,
        gain_attn[None],
        w_head,
        out_head,
        qkv,
        attended,
        cos,
        sin,
        pair_block,
        normed,
        gate_sum,
        up_part,
    )


def finish_kernel(
    gate_ref,
    up_ref,
    qkv_ref,
    gate_hbm,
    up_hbm,
    qkv_hbm,
    gate_out,
    up_out,
    qkv_out,
    sums_ref,
    gate_w,
    up_w,
    qkv_w,
    sem,
):
    f32 = jnp.float32
    rows = gate_w.shape[0]
    at = pl.ds(pl.multiple_of(lax.axis_index("ctx") * rows, rows), rows)
    copies = []
    for index, (source, dest) in enumerate(((gate_hbm, gate_w), (up_hbm, up_w), (qkv_hbm, qkv_w))):
        copies.append(pltpu.make_async_copy(source.at[at], dest, sem.at[index]))
        copies[-1].start()

    def spread(values, out, weights):
        out[...] = values[...].astype(f32)
        return jnp.sum(weights[...].astype(f32) * values[...].astype(f32), axis=1, keepdims=True)

    for copy in copies:
        copy.wait()
    ffn = spread(gate_ref, gate_out, gate_w) + spread(up_ref, up_out, up_w)
    attn = spread(qkv_ref, qkv_out, qkv_w)
    lane = lax.broadcasted_iota(jnp.int32, sums_ref.shape, 1)
    sums_ref[...] = jnp.where(lane == 0, attn, ffn)


def finish(gate_low, up_low, qkv_sum, w_gate, w_up, qkv_w):
    rows = gate_low.shape[0]
    vmem, hbm = pl.BlockSpec(memory_space=pltpu.VMEM), pl.BlockSpec(memory_space=pl.ANY)
    return pl.pallas_call(
        finish_kernel,
        name="finish",
        out_shape=[
            jax.ShapeDtypeStruct(gate_low.shape, jnp.float32),
            jax.ShapeDtypeStruct(up_low.shape, jnp.float32),
            jax.ShapeDtypeStruct(qkv_sum.shape, jnp.float32),
            jax.ShapeDtypeStruct((rows, 2), jnp.float32),
        ],
        in_specs=[vmem] * 3 + [hbm] * 3,
        out_specs=[vmem] * 4,
        scratch_shapes=[
            pltpu.VMEM(gate_low.shape, jnp.bfloat16),
            pltpu.VMEM(up_low.shape, jnp.bfloat16),
            pltpu.VMEM(qkv_sum.shape, jnp.bfloat16),
            pltpu.SemaphoreType.DMA((3,)),
        ],
        compiler_params=pltpu.CompilerParams(vmem_limit_bytes=62 * 2**20),
    )(gate_low, up_low, qkv_sum, w_gate, w_up, qkv_w)


def local_heads(
    tokens,
    cotangent,
    gain_attn,
    gain_ffn,
    query_key_value_weight,
    w_out,
    w_gate,
    w_up,
    w_down,
    pair_block,
):
    f32 = jnp.float32
    n_ctx, n_fsdp = lax.axis_size("ctx"), lax.axis_size("fsdp")
    ctx, fsdp = lax.axis_index("ctx"), lax.axis_index("fsdp")
    token_rows, width = tokens.shape
    depth = query_key_value_weight.shape[0]

    (
        mid,
        normed_two_group,
        cot_near,
        cot_far,
        gate_w,
        up_w,
        qkv,
        attended,
        normed_one_seq,
        w_head,
        out_head,
        cos,
        sin,
    ) = attention_forward(
        tokens,
        cotangent,
        gain_attn,
        gain_ffn,
        query_key_value_weight,
        w_out,
        w_gate,
        w_up,
        pair_block,
    )
    result, grad_mid, grad_proj, down_sum, gate_sum, up_part = feed_forward(
        mid,
        cotangent,
        gain_ffn,
        normed_two_group,
        cot_near,
        cot_far,
        gate_w,
        up_w,
        w_down.reshape(-1, BLOCK, width),
    )
    grad_input, qkv_sum, grad_out, gate_low, up_low = attention_back(
        grad_proj,
        grad_mid,
        tokens,
        gain_attn,
        w_head,
        out_head,
        qkv,
        attended,
        cos,
        sin,
        pair_block,
        normed_one_seq,
        gate_sum,
        up_part,
    )
    grad_down = down_sum.astype(f32)
    grad_gate, grad_up, grad_qkv, sums = finish(
        gate_low, up_low, qkv_sum, w_gate, w_up, query_key_value_weight
    )

    gain_pairs = [
        (c * n_fsdp + f, f * n_ctx + c) for c in range(n_ctx) for f in range(n_fsdp)
    ]
    moved = lax.ppermute(sums, ("ctx", "fsdp"), gain_pairs)
    my_gain = (ctx * n_fsdp + fsdp) * (depth // n_ctx)
    grad_gain_attn = moved[:, 0] / lax.dynamic_slice_in_dim(gain_attn, my_gain, depth // n_ctx)
    grad_gain_ffn = moved[:, 1] / lax.dynamic_slice_in_dim(gain_ffn, my_gain, depth // n_ctx)
    return (
        result,
        grad_input,
        grad_gain_attn,
        grad_gain_ffn,
        grad_qkv,
        grad_out,
        grad_gate,
        grad_up,
        grad_down,
    )


def solution(mesh):
    fits = mesh.shape["ctx"] == KEY_VALUE_HEADS and mesh.shape["fsdp"] == KEY_VALUE_HEADS // 2
    local = local_heads if fits else local_general
    return jax.shard_map(
        local,
        mesh=mesh,
        in_specs=(
            P(("ctx", "fsdp"), None),
            P(("ctx", "fsdp"), None),
            P(),
            P(),
            P("fsdp", None),
            P("fsdp", None),
            P("fsdp", None),
            P("fsdp", None),
            P("fsdp", None),
            P(),
        ),
        out_specs=(
            P(("ctx", "fsdp"), None),
            P(("ctx", "fsdp"), None),
            P(("ctx", "fsdp")),
            P(("ctx", "fsdp")),
            P(("fsdp", "ctx"), None),
            P(("fsdp", "ctx"), None),
            P(("fsdp", "ctx"), None),
            P(("fsdp", "ctx"), None),
            P(("fsdp", "ctx"), None),
        ),
        check_vma=False,
    )
```

```python
import functools
import math

import jax
import jax.numpy as jnp
from jax import lax
from jax.experimental import pallas as pl
from jax.experimental.pallas import tpu as pltpu
from jax.sharding import PartitionSpec as P

QUERY_HEADS = 16
KEY_VALUE_HEADS = 8
HEAD_SIZE = 128


norm_eps = 1e-05
rope_base = 1000000.0


def rms_norm(vectors, gain_vec):
    return (
        vectors
        * lax.rsqrt(jnp.mean(vectors * vectors, axis=-1, keepdims=True) + norm_eps)
        * gain_vec
    )


def apply_rotation(vectors, where_pos):
    half_dim = vectors.shape[-1] // 2
    frequency = jnp.exp(
        jnp.arange(half_dim, dtype=jnp.float32) * (-2.0 * math.log(rope_base) / vectors.shape[-1])
    )
    angles = where_pos.astype(jnp.float32)[:, None] * frequency[None, :]
    cosine = jnp.cos(angles)[:, None, :]
    sine_val = jnp.sin(angles)[:, None, :]
    first_half = vectors[..., :half_dim]
    second_half = vectors[..., half_dim:]
    return jnp.concatenate(
        [
            first_half * cosine - second_half * sine_val,
            second_half * cosine + first_half * sine_val,
        ],
        axis=-1,
    )


def positions(pair_block, token_rows):
    n_ctx = lax.axis_size("ctx")
    half_rows = token_rows // 2
    row_index = jnp.arange(token_rows, dtype=jnp.int32)
    first_block = pair_block[:, None]
    which_block = jnp.where(
        row_index[None, :] < half_rows, first_block, 2 * n_ctx - 1 - first_block
    )
    pos_table = which_block * half_rows + (row_index % half_rows)[None, :]
    own_pos = lax.dynamic_slice(pos_table, (lax.axis_index("ctx"), 0), (1, token_rows)).reshape(
        token_rows
    )
    return (pos_table.reshape(-1), own_pos)


def to_groups(input_array, group_count):
    token_rows = input_array.shape[0]
    head_length = input_array.shape[-1] // (group_count * KEY_VALUE_HEADS)
    return (
        input_array.reshape(token_rows, KEY_VALUE_HEADS, group_count, head_length)
        .transpose(1, 2, 0, 3)
        .reshape(KEY_VALUE_HEADS, group_count * token_rows, head_length)
    )


def from_groups(input_array, group_count):
    head_length = input_array.shape[-1]
    token_rows = input_array.shape[1] // group_count
    return (
        input_array.reshape(KEY_VALUE_HEADS, group_count, token_rows, head_length)
        .transpose(2, 0, 1, 3)
        .reshape(token_rows, KEY_VALUE_HEADS * group_count * head_length)
    )


def split_keys(every_key, every_value, key_pos):
    total_keys = every_key.shape[0]
    block_length = min(1024, total_keys)
    block_count = total_keys // block_length
    return (
        every_key.reshape(block_count, block_length, KEY_VALUE_HEADS, HEAD_SIZE),
        every_value.reshape(block_count, block_length, KEY_VALUE_HEADS, HEAD_SIZE),
        key_pos.reshape(block_count, block_length),
    )


def contract_last(left, right):
    return lax.dot_general(
        left, right, (((1,), (1,)), ((), ())), preferred_element_type=jnp.float32
    )


def contract_first(left, right):
    return lax.dot_general(
        left, right, (((0,), (0,)), ((), ())), preferred_element_type=jnp.float32
    )


def local_general(
    tokens,
    cotangent,
    gain_attn,
    gain_ffn,
    query_key_value_weight,
    w_out,
    w_gate,
    w_up,
    w_down,
    pair_block,
):
    token_rows = tokens.shape[0]
    query_columns = QUERY_HEADS * HEAD_SIZE
    key_value_columns = KEY_VALUE_HEADS * HEAD_SIZE
    group_count = QUERY_HEADS // KEY_VALUE_HEADS
    score_scale = 1.0 / math.sqrt(HEAD_SIZE)
    ff_cols = w_gate.shape[1]
    key_pos, own_pos = positions(pair_block, token_rows)
    query_pos = jnp.tile(own_pos, group_count)
    inputs_f = tokens.astype(jnp.float32)
    qkv_full, out_full = (
        lax.all_gather(query_key_value_weight, "fsdp", axis=0, tiled=True),
        lax.all_gather(w_out, "fsdp", axis=0, tiled=True),
    )
    normed_one_b = rms_norm(inputs_f, gain_attn).astype(jnp.bfloat16)
    projected_rows = jnp.dot(normed_one_b, qkv_full, preferred_element_type=jnp.float32)
    query_raw = projected_rows[:, :query_columns].reshape(token_rows, QUERY_HEADS, HEAD_SIZE)
    unrotated_key = projected_rows[:, query_columns : query_columns + key_value_columns].reshape(
        token_rows, KEY_VALUE_HEADS, HEAD_SIZE
    )
    query_b = (
        apply_rotation(query_raw, own_pos).astype(jnp.bfloat16).reshape(token_rows, query_columns)
    )
    keys_b = (
        apply_rotation(unrotated_key, own_pos)
        .astype(jnp.bfloat16)
        .reshape(token_rows, key_value_columns)
    )
    values_b = projected_rows[:, query_columns + key_value_columns :].astype(jnp.bfloat16)
    every_key, every_value = (
        lax.all_gather(keys_b, "ctx", axis=0, tiled=True),
        lax.all_gather(values_b, "ctx", axis=0, tiled=True),
    )
    query_grp = to_groups(query_b, group_count)
    key_blocks, value_blocks, pos_blocks = split_keys(every_key, every_value, key_pos)

    def forward_step(carry, block_in):
        run_max, run_total, weighted = carry
        key_block, value_block, block_pos = block_in
        causal = block_pos[None, None, :] <= query_pos[None, :, None]
        scores = (
            jnp.einsum("hqd,khd->hqk", query_grp, key_block, preferred_element_type=jnp.float32)
            * score_scale
        )
        scores = jnp.where(causal, scores, -1e30)
        new_max = jnp.maximum(run_max, jnp.max(scores, axis=-1))
        exp_scores = jnp.where(causal, jnp.exp(scores - new_max[..., None]), 0.0)
        fading = jnp.exp(run_max - new_max)
        run_total = run_total * fading + jnp.sum(exp_scores, axis=-1)
        weighted = weighted * fading[..., None] + jnp.einsum(
            "hqk,khd->hqd",
            exp_scores.astype(jnp.bfloat16),
            value_block,
            preferred_element_type=jnp.float32,
        )
        return ((new_max, run_total, weighted), None)

    initial_maximum = jnp.full((KEY_VALUE_HEADS, group_count * token_rows), -1e30, jnp.float32)
    initial_total = jnp.zeros((KEY_VALUE_HEADS, group_count * token_rows), jnp.float32)
    initial_weighted = jnp.zeros(
        (KEY_VALUE_HEADS, group_count * token_rows, HEAD_SIZE), jnp.float32
    )
    final_carry, ignored = lax.scan(
        forward_step,
        (initial_maximum, initial_total, initial_weighted),
        (key_blocks, value_blocks, pos_blocks),
    )
    run_max, run_total, weighted = final_carry
    log_total = run_max + jnp.log(run_total)
    attn_grp = weighted / run_total[..., None]
    attended_b = from_groups(attn_grp.astype(jnp.bfloat16), group_count)
    mid_rows = inputs_f + jnp.dot(attended_b, out_full, preferred_element_type=jnp.float32)
    gate_full, up_full, down_full = (
        lax.all_gather(w_gate, "fsdp", axis=0, tiled=True),
        lax.all_gather(w_up, "fsdp", axis=0, tiled=True),
        lax.all_gather(w_down, "fsdp", axis=0, tiled=True),
    )
    normed_two_b = rms_norm(mid_rows, gain_ffn).astype(jnp.bfloat16)
    gate_val = jnp.dot(normed_two_b, gate_full, preferred_element_type=jnp.float32)
    up_val = jnp.dot(normed_two_b, up_full, preferred_element_type=jnp.float32)
    hidden_b = (jax.nn.silu(gate_val) * up_val).astype(jnp.bfloat16)
    output_f = mid_rows + jnp.dot(hidden_b, down_full, preferred_element_type=jnp.float32)
    result = output_f.astype(jnp.bfloat16)
    normed_one_x, attended_x, normed_two_x, hidden_x = (
        lax.all_to_all(normed_one_b, "fsdp", split_axis=1, concat_axis=0, tiled=True),
        lax.all_to_all(attended_b, "fsdp", split_axis=1, concat_axis=0, tiled=True),
        lax.all_to_all(normed_two_b, "fsdp", split_axis=1, concat_axis=0, tiled=True),
        lax.all_to_all(hidden_b, "fsdp", split_axis=1, concat_axis=0, tiled=True),
    )
    grad_out_f = cotangent.astype(jnp.float32)
    gate_back, up_back, down_back = (
        lax.all_gather(w_gate, "fsdp", axis=0, tiled=True),
        lax.all_gather(w_up, "fsdp", axis=0, tiled=True),
        lax.all_gather(w_down, "fsdp", axis=0, tiled=True),
    )
    grad_hidden = contract_last(cotangent, down_back)
    ignored, ffn_back = jax.vjp(
        lambda gate_in, up_in: jax.nn.silu(gate_in) * up_in, gate_val, up_val
    )
    grad_gate_f, grad_up_f = ffn_back(grad_hidden)
    grad_gate_b = grad_gate_f.astype(jnp.bfloat16)
    grad_up_b = grad_up_f.astype(jnp.bfloat16)
    grad_normed_two = contract_last(grad_gate_b, gate_back) + contract_last(grad_up_b, up_back)
    ignored, norm_two_back = jax.vjp(rms_norm, mid_rows, gain_ffn)
    grad_mid_part, gain_ffn_part = norm_two_back(grad_normed_two)
    grad_mid = grad_out_f + grad_mid_part
    gate_up_b = jnp.concatenate([grad_gate_b, grad_up_b], axis=1)
    qkv_back, out_back = (
        lax.all_gather(query_key_value_weight, "fsdp", axis=0, tiled=True),
        lax.all_gather(w_out, "fsdp", axis=0, tiled=True),
    )
    grad_proj_b = grad_mid.astype(jnp.bfloat16)
    grad_att_b = contract_last(grad_proj_b, out_back).astype(jnp.bfloat16)
    grad_att_grp = to_groups(grad_att_b, group_count)
    delta_rows = jnp.sum(grad_att_grp.astype(jnp.float32) * attn_grp, axis=-1)

    def backward_step(grad_query, block_in):
        key_block, value_block, block_pos = block_in
        causal = block_pos[None, None, :] <= query_pos[None, :, None]
        scores = (
            jnp.einsum("hqd,khd->hqk", query_grp, key_block, preferred_element_type=jnp.float32)
            * score_scale
        )
        probs = jnp.where(causal, jnp.exp(scores - log_total[..., None]), 0.0)
        grad_values = jnp.einsum(
            "hqk,hqd->khd",
            probs.astype(jnp.bfloat16),
            grad_att_grp,
            preferred_element_type=jnp.float32,
        )
        grad_probs = jnp.einsum(
            "hqd,khd->hqk", grad_att_grp, value_block, preferred_element_type=jnp.float32
        )
        grad_scores = (probs * (grad_probs - delta_rows[..., None])).astype(jnp.bfloat16)
        grad_query = grad_query + score_scale * jnp.einsum(
            "hqk,khd->hqd", grad_scores, key_block, preferred_element_type=jnp.float32
        )
        grad_keys = score_scale * jnp.einsum(
            "hqk,hqd->khd", grad_scores, query_grp, preferred_element_type=jnp.float32
        )
        return (grad_query, (grad_keys, grad_values))

    grad_query_grp, key_grads = lax.scan(
        backward_step,
        jnp.zeros((KEY_VALUE_HEADS, group_count * token_rows, HEAD_SIZE), jnp.float32),
        (key_blocks, value_blocks, pos_blocks),
    )
    total_keys = key_pos.shape[0]
    grad_keys_all = key_grads[0].reshape(total_keys, key_value_columns)
    grad_values_all = key_grads[1].reshape(total_keys, key_value_columns)
    key_sums, summed_values = (
        lax.psum_scatter(
            grad_keys_all.astype(jnp.bfloat16), "ctx", scatter_dimension=0, tiled=True
        ).astype(jnp.float32),
        lax.psum_scatter(
            grad_values_all.astype(jnp.bfloat16), "ctx", scatter_dimension=0, tiled=True
        ).astype(jnp.float32),
    )
    grad_query_rows = from_groups(grad_query_grp, group_count).reshape(
        token_rows, QUERY_HEADS, HEAD_SIZE
    )
    ignored, query_rope_back = jax.vjp(lambda vectors: apply_rotation(vectors, own_pos), query_raw)
    ignored, key_rotation_backward = jax.vjp(
        lambda vectors: apply_rotation(vectors, own_pos), unrotated_key
    )
    grad_query_raw = query_rope_back(grad_query_rows)[0]
    unrotated_key_gradient = key_rotation_backward(
        key_sums.reshape(token_rows, KEY_VALUE_HEADS, HEAD_SIZE)
    )[0]
    grad_projected_b = jnp.concatenate(
        [
            grad_query_raw.reshape(token_rows, query_columns),
            unrotated_key_gradient.reshape(token_rows, key_value_columns),
            summed_values,
        ],
        axis=1,
    ).astype(jnp.bfloat16)
    grad_normed_one = contract_last(grad_projected_b, qkv_back)
    ignored, norm_one_back = jax.vjp(rms_norm, inputs_f, gain_attn)
    grad_in_part, gain_attn_part = norm_one_back(grad_normed_one)
    grad_input = grad_mid + grad_in_part
    cot_group, gate_up_group, projected_group, proj_group = (
        lax.all_gather(cotangent, "fsdp", axis=0, tiled=True),
        lax.all_gather(gate_up_b, "fsdp", axis=0, tiled=True),
        lax.all_gather(grad_projected_b, "fsdp", axis=0, tiled=True),
        lax.all_gather(grad_proj_b, "fsdp", axis=0, tiled=True),
    )
    qkv_part = contract_first(normed_one_x, projected_group)
    out_part = contract_first(attended_x, proj_group)
    gate_up_part = contract_first(normed_two_x, gate_up_group)
    gate_part = gate_up_part[:, :ff_cols]
    up_part = gate_up_part[:, ff_cols:]
    down_part = contract_first(hidden_x, cot_group)
    grad_qkv, grad_out, grad_down = (
        lax.psum_scatter(
            qkv_part.astype(jnp.bfloat16), "ctx", scatter_dimension=0, tiled=True
        ).astype(jnp.float32),
        lax.psum_scatter(
            out_part.astype(jnp.bfloat16), "ctx", scatter_dimension=0, tiled=True
        ).astype(jnp.float32),
        lax.psum_scatter(
            down_part.astype(jnp.bfloat16), "ctx", scatter_dimension=0, tiled=True
        ).astype(jnp.float32),
    )
    grad_gate, grad_up = (
        lax.psum_scatter(
            gate_part.astype(jnp.bfloat16), "ctx", scatter_dimension=0, tiled=True
        ).astype(jnp.float32),
        lax.psum_scatter(
            up_part.astype(jnp.bfloat16), "ctx", scatter_dimension=0, tiled=True
        ).astype(jnp.float32),
    )
    grad_gain_attn, grad_gain_ffn = (
        lax.psum_scatter(gain_attn_part, ("ctx", "fsdp"), scatter_dimension=0, tiled=True),
        lax.psum_scatter(gain_ffn_part, ("ctx", "fsdp"), scatter_dimension=0, tiled=True),
    )
    return (
        result,
        grad_input,
        grad_gain_attn,
        grad_gain_ffn,
        grad_qkv,
        grad_out,
        grad_gate,
        grad_up,
        grad_down,
    )


MESH = pl.DeviceIdType.MESH
ACROSS_X, ACROSS_Y, ACROSS_CORE = 2, 4, 1
BLOCK = 256


class Links:
    def __init__(self, sems, ctx, fsdp):
        self.send_sem, self.recv_sem, self.local_sem = sems
        self.ctx, self.fsdp = ctx, fsdp
        self.remote = self.locals = 0

    def to(self, src, dst, ctx, fsdp):
        index, self.remote = self.remote, self.remote + 1
        return pltpu.make_async_remote_copy(
            src_ref=src,
            dst_ref=dst,
            send_sem=self.send_sem.at[index],
            recv_sem=self.recv_sem.at[index],
            device_id=(ctx, fsdp),
            device_id_type=MESH,
        )

    def flip(self, src, dst, ctx_flip, fsdp_flip):
        return self.to(
            src, dst, lax.bitwise_xor(self.ctx, ctx_flip), lax.bitwise_xor(self.fsdp, fsdp_flip)
        )

    def plane(self, src, dst, flip):
        return self.flip(src, dst, flip, 0)

    def column(self, src, dst, flip):
        return self.flip(src, dst, 0, flip)

    def here(self, src, dst):
        index, self.locals = self.locals, self.locals + 1
        return pltpu.make_async_copy(src, dst, self.local_sem.at[index])


PLANE_FLIPS = [(1, 0), (2, 0), (4, 0)]
COLUMN_FLIPS = [(0, 1), (0, 2), (0, 3)]


def greet(ctx, fsdp, flips):
    barrier = pltpu.get_barrier_semaphore()
    for a, b in flips:
        pl.semaphore_signal(
            barrier,
            inc=1,
            device_id=(lax.bitwise_xor(ctx, a), lax.bitwise_xor(fsdp, b)),
            device_id_type=MESH,
        )
    pl.semaphore_wait(barrier, len(flips))


def start_all(copies):
    for copy in copies:
        copy.start()


class LineGather:
    def __init__(self, links, own, group):
        self.links, self.group = links, group
        self.home = links.here(own, group.at[0])
        self.near = links.column(own, group.at[2], 1)
        self.far = links.column(own, group.at[1], 2)
        self.relay = links.column(group.at[1], group.at[3], 1)

    def begin(self):
        start_all([self.far, self.near, self.home])

    def forward(self):
        self.far.wait_recv()
        self.relay.start()

    def finish(self):
        self.near.wait_recv()
        self.relay.wait_recv()
        for copy in (self.near, self.far, self.relay):
            copy.wait_send()
        self.home.wait()


class PlaneGather:
    def __init__(self, links, blocks, halves):
        self.links, self.blocks, self.halves = links, blocks, halves
        self.ctx = links.ctx
        self.sent = []
        self.cores = []

    def _go(self, copies):
        for copy in copies:
            copy.start()
        self.sent += copies
        return copies

    def _core(self, index):
        refs = self.blocks(index)
        self.cores += self._go([self.links.plane(r, r, ACROSS_CORE) for r in refs])

    def begin(self, sources=None):
        refs = self.blocks(self.ctx)
        pairs = list(zip(sources or refs, refs))
        self.from_x = self._go([self.links.plane(s, r, ACROSS_X) for s, r in pairs])
        self.from_y = self._go([self.links.plane(s, r, ACROSS_Y) for s, r in pairs])
        self.cores += self._go([self.links.plane(s, r, ACROSS_CORE) for s, r in pairs])

    def forward(self):
        index = lax.bitwise_xor(self.ctx, ACROSS_X)
        for copy in self.from_x:
            copy.wait_recv()
        refs = self.halves(index, 0)
        self.corner = self._go([self.links.plane(r, r, ACROSS_Y) for r in refs])
        self._core(index)
        index = lax.bitwise_xor(self.ctx, ACROSS_Y)
        for copy in self.from_y:
            copy.wait_recv()
        refs = self.halves(index, 1)
        self.corner += self._go([self.links.plane(r, r, ACROSS_X) for r in refs])
        self._core(index)

    def finish(self):
        for copy in self.corner:
            copy.wait_recv()
        self._core(lax.bitwise_xor(self.ctx, ACROSS_X | ACROSS_Y))
        for copy in self.cores:
            copy.wait_recv()

    def drain(self):
        for copy in self.sent:
            copy.wait_send()


class PlaneScatter:
    def __init__(self, links, part, core_rx, half_rx, side_rx):
        self.links, self.part = links, part
        self.core_rx, self.half_rx, self.side_rx = core_rx, half_rx, side_rx
        self.chip, self.core = links.ctx // 2, lax.rem(links.ctx, 2)
        self.sent = []
        self.from_core = {}

    def order(self):
        return [(flip, lax.bitwise_xor(self.chip, flip)) for flip in (3, 1, 2, 0)]

    def _go(self, copy):
        copy.start()
        self.sent.append(copy)
        return copy

    def give(self, flip, chip):
        self.from_core[flip] = self._go(
            self.links.plane(
                self.part.at[2 * chip + 1 - self.core], self.core_rx.at[chip], ACROSS_CORE
            )
        )

    def _summed(self, flip):
        chip = lax.bitwise_xor(self.chip, flip)
        self.from_core[flip].wait_recv()
        mine = self.part.at[2 * chip + self.core]
        total = mine[...].astype(jnp.float32) + self.core_rx[chip].astype(jnp.float32)
        return mine, total

    def begin(self):
        half = self.half = self.half_rx.shape[1]
        mine, total = self._summed(3)
        mine[...] = total.astype(jnp.bfloat16)
        self.corner = [
            self._go(self.links.plane(mine.at[pl.ds(0, half)], self.half_rx.at[0], ACROSS_Y)),
            self._go(
                self.links.plane(mine.at[pl.ds(half, half)], self.half_rx.at[1], ACROSS_X)
            ),
        ]

    def middle(self):
        self.sides = []
        for flip, across, slot in ((1, ACROSS_X, 0), (2, ACROSS_Y, 1)):
            mine, total = self._summed(flip)
            mine[...] = total.astype(jnp.bfloat16)
            self.corner[slot].wait_recv()
            rows = pl.ds(slot * self.half, self.half)
            mine[rows] = (
                total[slot * self.half : (slot + 1) * self.half]
                + self.half_rx[slot].astype(jnp.float32)
            ).astype(jnp.bfloat16)
            self.sides.append(self._go(self.links.plane(mine, self.side_rx.at[slot], across)))

    def finish(self):
        mine, total = self._summed(0)
        for slot, copy in enumerate(self.sides):
            copy.wait_recv()
            total = total + self.side_rx[slot].astype(jnp.float32)
        return total

    def drain(self):
        for copy in self.sent:
            copy.wait_send()


def swap_bits(fsdp):
    return 2 * lax.rem(fsdp, 2) + fsdp // 2


def place_positions(pair_ref, pos_col, pos_row, rows):
    half, n_ctx = rows // 2, pos_col.shape[0] // rows
    down = lax.broadcasted_iota(jnp.int32, (rows, 1), 0)
    along = lax.broadcasted_iota(jnp.int32, (1, rows), 1)
    for j in range(n_ctx):
        first = pair_ref[j] * half
        second = (2 * n_ctx - 1 - pair_ref[j]) * half - half
        pos_col[pl.ds(j * rows, rows)] = down + jnp.where(down < half, first, second)
        pos_row[:, pl.ds(j * rows, rows)] = along + jnp.where(along < half, first, second)


def turn(vectors, cos_rows, sin_rows, sign):
    return vectors * cos_rows + sign * pltpu.roll(vectors, HEAD_SIZE // 2, 1) * sin_rows


def attention_kernel(
    tokens_ref,
    cot_ref,
    gain_one_ref,
    gain_two_ref,
    qkv_w_ref,
    out_w_ref,
    gate_ref,
    up_ref,
    pair_ref,
    mid_ref,
    normed_two_group,
    cot_near,
    cot_far,
    gate_w,
    up_w,
    qkv_out,
    attended_out,
    normed_one_out,
    w_head_out,
    out_head_out,
    cos_out,
    sin_out,
    normed,
    w_head,
    out_head,
    out_relay,
    qkv,
    attended,
    part,
    core_rx,
    half_rx,
    side_rx,
    normed_two,
    cos_ref,
    sin_ref,
    pos_col_ref,
    pos_row_ref,
    send_sem,
    recv_sem,
    local_sem,
):
    f32, bf16 = jnp.float32, jnp.bfloat16
    ctx, fsdp = lax.axis_index("ctx"), lax.axis_index("fsdp")
    links = Links((send_sem, recv_sem, local_sem), ctx, fsdp)
    rows, width = tokens_ref.shape
    depth = qkv_w_ref.shape[0]
    head_columns = out_head.shape[0]
    n_ctx, n_fsdp = normed.shape[0], width // depth
    seq_rows = n_ctx * rows
    hidden = gate_w.shape[2]
    strip = hidden // n_ctx
    depth_blocks = gate_ref.shape[0]
    query_columns = QUERY_HEADS * HEAD_SIZE
    key_columns = KEY_VALUE_HEADS * HEAD_SIZE
    score_scale = 1.0 / math.sqrt(HEAD_SIZE)
    finals = []

    greet(ctx, fsdp, PLANE_FLIPS + COLUMN_FLIPS + [(6, 0)])

    out_block = out_w_ref.at[
        pl.ds(pl.multiple_of(lax.rem(ctx, 2) * head_columns, head_columns), head_columns)
    ]
    out_target = swap_bits(lax.bitwise_xor(ctx // 2, fsdp))
    out_away = out_target != fsdp
    out_copy = links.to(out_block, out_relay, ctx, out_target)
    out_home = links.here(out_block, out_relay)
    out_flip = 2 * swap_bits(fsdp)
    out_moves = fsdp != 0
    out_last = links.to(out_relay, out_head, lax.bitwise_xor(ctx, out_flip), fsdp)
    out_stays = links.here(out_relay, out_head)

    @pl.when(out_away)
    def _():
        out_copy.start()

    @pl.when(jnp.logical_not(out_away))
    def _():
        out_home.start()

    def rows_of(plane):
        return pl.ds(pl.multiple_of(plane * depth, depth), depth)

    head_parts, places = [], []
    for start, size, place in (
        (ctx * head_columns, head_columns, 0),
        (query_columns + ctx * HEAD_SIZE, HEAD_SIZE, head_columns),
        (query_columns + key_columns + ctx * HEAD_SIZE, HEAD_SIZE, head_columns + HEAD_SIZE),
    ):
        places.append(pl.ds(place, size))
        head_parts.append(
            (
                qkv_w_ref.at[:, pl.ds(pl.multiple_of(start, HEAD_SIZE), size)],
                w_head.at[rows_of(fsdp), pl.ds(place, size)],
            )
        )
    head_far = [links.column(src, dst, 2) for src, dst in head_parts]
    head_near = [links.column(src, dst, 1) for src, dst in head_parts]
    own_head = [links.here(src, dst) for src, dst in head_parts]
    start_all(head_far + head_near + own_head)

    def place_of(j):
        return pl.ds(pl.multiple_of(j * strip, strip), strip)

    def strips(target):
        cols = pl.ds(pl.multiple_of(target * hidden + ctx * strip, strip), strip)
        blocks = pl.ds(fsdp * depth_blocks, depth_blocks)
        for source, dest in ((gate_ref, gate_w), (up_ref, up_w)):
            yield source.at[:, :, cols], dest.at[blocks, :, place_of(ctx)]

    strip_copies = [[links.here(src, dst) for src, dst in strips(fsdp)]]
    for flip in (1, 2, 3):
        strip_copies.append(
            [links.column(s, d, flip) for s, d in strips(lax.bitwise_xor(fsdp, flip))]
        )
    start_all(strip_copies[0])

    def strip_gather(flip):
        first = lax.bitwise_xor(fsdp, flip) * depth_blocks
        blocks = pl.ds(first, depth_blocks)
        return PlaneGather(
            links,
            lambda j: [w.at[blocks, :, place_of(j)] for w in (gate_w, up_w)],
            lambda j, which: [w.at[first + which, :, place_of(j)] for w in (gate_w, up_w)],
        )

    weights = [strip_gather(flip) for flip in range(n_fsdp)]

    inputs = tokens_ref[...].astype(f32)
    scale = lax.rsqrt(jnp.mean(inputs * inputs, axis=-1, keepdims=True) + norm_eps)
    normed[ctx] = (inputs * scale * gain_one_ref[...]).astype(bf16)
    half = rows // 2
    gather = PlaneGather(
        links,
        lambda j: [normed.at[j]],
        lambda j, which: [normed.at[j, pl.ds(which * half, half)]],
    )
    gather.begin()

    place_positions(pair_ref, pos_col_ref, pos_row_ref, rows)
    lane = lax.broadcasted_iota(jnp.int32, (1, HEAD_SIZE), 1)
    lane_half = lax.rem(lane, HEAD_SIZE // 2).astype(f32)
    frequency = jnp.exp(lane_half * (-2.0 * math.log(rope_base) / HEAD_SIZE))
    side = jnp.where(lane < HEAD_SIZE // 2, -1.0, 1.0)

    def tables(step, carry):
        at = pl.ds(pl.multiple_of(step * rows, rows), rows)
        angles = pos_col_ref[at].astype(f32) * frequency
        cos_ref[at] = jnp.cos(angles)
        sin_ref[at] = side * jnp.sin(angles)
        return carry

    lax.fori_loop(0, n_ctx, tables, 0)
    for src, dst in ((cos_ref, cos_out), (sin_ref, sin_out)):
        finals.append(links.here(src, dst))
        finals[-1].start()
    gather.forward()
    weights[0].begin([source for source, dest in strips(fsdp)])
    gather.finish()

    @pl.when(out_away)
    def _():
        out_copy.wait_recv()

    @pl.when(jnp.logical_not(out_away))
    def _():
        out_home.wait()

    @pl.when(out_moves)
    def _():
        out_last.start()

    @pl.when(jnp.logical_not(out_moves))
    def _():
        out_stays.start()

    weights[0].forward()
    cot_copies = [links.column(cot_ref, cot_far, 2), links.column(cot_ref, cot_near, 1)]
    head_relay = []
    far_rows = rows_of(lax.bitwise_xor(fsdp, 2))
    for copy, place in zip(head_far, places):
        copy.wait_recv()
        block = w_head.at[far_rows, place]
        head_relay.append(links.column(block, block, 1))
        head_relay[-1].start()
    start_all(cot_copies[:1])
    weights[0].finish()
    finals.append(links.here(normed, normed_one_out))
    finals[-1].start()
    for copy in own_head:
        copy.wait()
    for copy in head_near + head_relay:
        copy.wait_recv()
    start_all(strip_copies[1] + strip_copies[2] + strip_copies[3])

    block_rows = 2 * rows

    def project(step, carry):
        at = pl.multiple_of(step * block_rows, block_rows)
        tile = normed[pl.ds(step * 2, 2)].reshape(block_rows, width)
        out = jnp.dot(tile, w_head[...], preferred_element_type=f32)
        cos_rows, sin_rows = cos_ref[pl.ds(at, block_rows)], sin_ref[pl.ds(at, block_rows)]
        for column in range(0, head_columns + HEAD_SIZE, HEAD_SIZE):
            turned = turn(out[:, column : column + HEAD_SIZE], cos_rows, sin_rows, 1.0)
            qkv[pl.ds(at, block_rows), pl.ds(column, HEAD_SIZE)] = turned.astype(bf16)
        column = head_columns + HEAD_SIZE
        qkv[pl.ds(at, block_rows), pl.ds(column, HEAD_SIZE)] = out[:, column:].astype(bf16)
        return carry

    lax.fori_loop(0, seq_rows // block_rows, project, 0)
    def attend(step, carry):
        at = pl.multiple_of(step * block_rows, block_rows)
        keys = qkv[:, pl.ds(head_columns, HEAD_SIZE)]
        values = qkv[:, pl.ds(head_columns + HEAD_SIZE, HEAD_SIZE)]
        causal = pos_row_ref[...] <= pos_col_ref[pl.ds(at, block_rows)]
        for column in range(0, head_columns, HEAD_SIZE):
            query = qkv[pl.ds(at, block_rows), pl.ds(column, HEAD_SIZE)]
            scores = contract_last(query, keys) * score_scale
            scores = jnp.where(causal, scores, -1e30)
            shifted = jnp.exp(scores - jnp.max(scores, axis=-1, keepdims=True))
            probs = shifted * (1.0 / jnp.sum(shifted, axis=-1, keepdims=True))
            mixed = jnp.dot(probs.astype(bf16), values, preferred_element_type=f32)
            attended[pl.ds(at, block_rows), pl.ds(column, HEAD_SIZE)] = mixed.astype(bf16)
        return carry

    lax.fori_loop(0, seq_rows // block_rows, attend, 0)

    @pl.when(out_moves)
    def _():
        out_last.wait_recv()

    @pl.when(jnp.logical_not(out_moves))
    def _():
        out_stays.wait()

    for src, dst in (        (qkv, qkv_out),
        (attended, attended_out),
        (w_head, w_head_out),
        (out_head, out_head_out),
    ):
        finals.append(links.here(src, dst))
        finals[-1].start()

    scatter = PlaneScatter(links, part, core_rx, half_rx, side_rx)
    for flip, chip in scatter.order():
        at = pl.multiple_of(chip * block_rows, block_rows)
        out = jnp.dot(
            attended[pl.ds(at, block_rows)], out_head[...], preferred_element_type=f32
        )
        part[pl.ds(chip * 2, 2)] = out.astype(bf16).reshape(2, rows, width)
        scatter.give(flip, chip)

    def arrived(flip):
        for copy in strip_copies[flip]:
            copy.wait_recv()
        weights[flip].begin()

    scatter.begin()
    scatter.middle()
    mid = tokens_ref[...].astype(f32) + scatter.finish()
    mid_ref[...] = mid
    mid_scale = lax.rsqrt(jnp.mean(mid * mid, axis=-1, keepdims=True) + norm_eps)
    normed_two[...] = (mid * mid_scale * gain_two_ref[...]).astype(bf16)

    group = LineGather(links, normed_two, normed_two_group)
    group.begin()
    arrived(1)
    arrived(2)
    weights[1].forward()
    group.forward()
    start_all(cot_copies[1:])
    arrived(3)
    weights[2].forward()
    weights[1].finish()
    weights[3].forward()
    weights[2].finish()
    weights[3].finish()
    group.finish()
    for copy in cot_copies:
        copy.wait()
    for copy in strip_copies[0]:
        copy.wait()

    for copies in [head_far, head_near, head_relay] + strip_copies[1:]:
        for copy in copies:
            copy.wait_send()

    @pl.when(out_away)
    def _():
        out_copy.wait_send()

    @pl.when(out_moves)
    def _():
        out_last.wait_send()

    gather.drain()
    scatter.drain()
    for item in weights:
        item.drain()
    for copy in finals:
        copy.wait()


def attention_forward(
    tokens, cotangent, gain_attn, gain_ffn, qkv_w, w_out, w_gate, w_up, pair_block
):
    f32, bf16 = jnp.float32, jnp.bfloat16
    n_ctx, n_fsdp = lax.axis_size("ctx"), lax.axis_size("fsdp")
    rows, width = tokens.shape
    depth = qkv_w.shape[0]
    hidden = w_gate.shape[1] // n_fsdp
    seq_rows = n_ctx * rows
    head_columns = QUERY_HEADS // KEY_VALUE_HEADS * HEAD_SIZE
    all_columns = head_columns + 2 * HEAD_SIZE
    vmem, hbm = pl.BlockSpec(memory_space=pltpu.VMEM), pl.BlockSpec(memory_space=pl.ANY)
    shape = jax.ShapeDtypeStruct
    return pl.pallas_call(
        attention_kernel,
        name="attention_forward",
        out_shape=[
            shape((rows, width), f32),
            shape((n_fsdp, rows, width), bf16),
            shape((rows, width), bf16),
            shape((rows, width), bf16),
            shape((width // BLOCK, BLOCK, hidden), bf16),
            shape((width // BLOCK, BLOCK, hidden), bf16),
            shape((seq_rows, all_columns), bf16),
            shape((seq_rows, head_columns), bf16),
            shape((n_ctx, rows, width), bf16),
            shape((width, all_columns), bf16),
            shape((head_columns, width), bf16),
            shape((seq_rows, HEAD_SIZE), f32),
            shape((seq_rows, HEAD_SIZE), f32),
        ],
        in_specs=[vmem] * 4 + [hbm] * 4 + [pl.BlockSpec(memory_space=pltpu.SMEM)],
        out_specs=[vmem] + [hbm] * 12,
        scratch_shapes=[
            pltpu.VMEM((n_ctx, rows, width), bf16),
            pltpu.VMEM((width, all_columns), bf16),
            pltpu.VMEM((head_columns, width), bf16),
            pltpu.VMEM((head_columns, width), bf16),
            pltpu.VMEM((seq_rows, all_columns), bf16),
            pltpu.VMEM((seq_rows, head_columns), bf16),
            pltpu.VMEM((n_ctx, rows, width), bf16),
            pltpu.VMEM((n_ctx // 2, rows, width), bf16),
            pltpu.VMEM((2, rows // 2, width), bf16),
            pltpu.VMEM((2, rows, width), bf16),
            pltpu.VMEM((rows, width), bf16),
            pltpu.VMEM((seq_rows, HEAD_SIZE), f32),
            pltpu.VMEM((seq_rows, HEAD_SIZE), f32),
            pltpu.VMEM((seq_rows, 1), jnp.int32),
            pltpu.VMEM((1, seq_rows), jnp.int32),
            pltpu.SemaphoreType.DMA((112,)),
            pltpu.SemaphoreType.DMA((112,)),
            pltpu.SemaphoreType.DMA((16,)),
        ],
        compiler_params=pltpu.CompilerParams(
            collective_id=1, has_side_effects=True, vmem_limit_bytes=58 * 2**20
        ),
    )(
        tokens,
        cotangent,
        gain_attn[None],
        gain_ffn[None],
        qkv_w,
        w_out,
        w_gate.reshape(depth // BLOCK, BLOCK, -1),
        w_up.reshape(depth // BLOCK, BLOCK, -1),
        pair_block,
    )


class ChipScatter:
    def __init__(self, links, parts, halves, sides):
        self.links, self.parts, self.halves, self.sides = links, parts, halves, sides
        self.sent = []

    def _go(self, copy):
        copy.start()
        self.sent.append(copy)
        return copy

    def begin(self, source=None):
        corner = self.parts[3] if source is None else source
        half = corner.shape[0] // 2
        self.half = half
        self.corner = [
            self._go(self.links.plane(corner.at[pl.ds(0, half)], self.halves[0], ACROSS_Y)),
            self._go(self.links.plane(corner.at[pl.ds(half, half)], self.halves[1], ACROSS_X)),
        ]

    def middle(self):
        self.side = []
        for slot, (flip, across) in enumerate(((1, ACROSS_X), (2, ACROSS_Y))):
            mine = self.parts[flip]
            self.corner[slot].wait_recv()
            rows = mine.at[pl.ds(slot * self.half, self.half)]
            rows[...] = (
                rows[...].astype(jnp.float32) + self.halves[slot][...].astype(jnp.float32)
            ).astype(jnp.bfloat16)
            self.side.append(self._go(self.links.plane(mine, self.sides[slot], across)))

    def finish(self):
        mine = self.parts[0]
        for copy in self.side:
            copy.wait_recv()
        mine[...] = (
            mine[...].astype(jnp.float32)
            + self.sides[0][...].astype(jnp.float32)
            + self.sides[1][...].astype(jnp.float32)
        ).astype(jnp.bfloat16)
        return mine

    def drain(self):
        for copy in self.sent:
            copy.wait_send()


def feed_forward_kernel(
    mid_ref,
    cot_ref,
    gain_ref,
    normed_ref,
    cot_near_ref,
    cot_far_ref,
    gate_hbm,
    up_hbm,
    down_hbm,
    result_ref,
    grad_mid_ref,
    grad_proj_ref,
    down_sum,
    gate_sum,
    up_part,
    gate_v,
    up_v,
    down_v,
    cots,
    hidden,
    grad_gate,
    grad_up,
    other_normed,
    other_cots,
    other_hidden,
    other_gate,
    other_up,
    stage,
    landed,
    down_parts,
    down_halves,
    send_sem,
    recv_sem,
    local_sem,
    load_sem,
    down_free,
    gate_free,
):
    f32, bf16 = jnp.float32, jnp.bfloat16
    ctx, fsdp = lax.axis_index("ctx"), lax.axis_index("fsdp")
    links = Links((send_sem, recv_sem, local_sem), ctx, fsdp)
    core = lax.rem(ctx, 2)
    rows, width = mid_ref.shape
    blocks = gate_v.shape[0]
    hidden_units = blocks * BLOCK
    half_units = hidden_units // 2
    n_fsdp = normed_ref.shape[0]
    group_rows = n_fsdp * rows

    def loads(j):
        cols = pl.ds(pl.multiple_of(j * BLOCK, BLOCK), BLOCK)
        return (
            pltpu.make_async_copy(
                gate_hbm.at[:, :, cols], gate_v.at[:, :, cols], load_sem.at[0, j]
            ),
            pltpu.make_async_copy(up_hbm.at[:, :, cols], up_v.at[:, :, cols], load_sem.at[1, j]),
            pltpu.make_async_copy(down_hbm.at[j], down_v.at[j], load_sem.at[2, j]),
        )

    for j in range(blocks):
        for copy in loads(j):
            copy.start()

    greet(ctx, fsdp, PLANE_FLIPS + COLUMN_FLIPS[:2])

    cot_relay = links.column(cot_far_ref, cots.at[3], 1)
    cot_relay.start()
    cots[0] = cot_ref[...]
    cots[1] = cot_far_ref[...]
    cots[2] = cot_near_ref[...]
    mid_load = links.here(mid_ref, grad_mid_ref)
    mid_load.start()

    swaps = [links.plane(normed_ref, other_normed, ACROSS_CORE)]
    cot_swaps = [links.plane(cots.at[s], other_cots.at[s], ACROSS_CORE) for s in range(n_fsdp)]
    start_all(swaps + cot_swaps[:3])

    half_slots, half_rows = n_fsdp // 2, group_rows // 2

    def activate(j, carry):
        for copy in loads(j):
            copy.wait()
        cols = pl.ds(pl.multiple_of(j * BLOCK, BLOCK), BLOCK)
        for first in (0, half_slots):
            at = pl.ds(first * rows, half_rows)
            normed = normed_ref[pl.ds(first, half_slots)].reshape(half_rows, width)
            gate = jnp.dot(
                normed, gate_v[:, :, cols].reshape(width, BLOCK), preferred_element_type=f32
            )
            up = jnp.dot(
                normed, up_v[:, :, cols].reshape(width, BLOCK), preferred_element_type=f32
            )
            sig = jax.nn.sigmoid(gate)
            silu = gate * sig
            hidden[at, cols] = (silu * up).astype(bf16)
            grad_gate[at, cols] = (up * (sig * (1.0 + gate * (1.0 - sig)))).astype(bf16)
            grad_up[at, cols] = silu.astype(bf16)
        return carry

    lax.fori_loop(0, blocks, activate, 0)

    hidden_acts = []
    for pair in range(blocks // 2):
        cols = pl.ds(pl.multiple_of((2 * pair + 1 - core) * BLOCK, BLOCK), BLOCK)
        hidden_acts.append(
            links.plane(
                hidden.at[:, cols], other_hidden.at[:, pl.ds(pair * BLOCK, BLOCK)], ACROSS_CORE
            )
        )
    start_all(hidden_acts)
    piece = 2 * BLOCK
    pieces = width // piece

    def spot(n):
        return pl.ds(n * piece, piece)

    def put(which, first, n, value):
        stage[which, pl.ds(first, half_slots), :, spot(n)] = value.astype(bf16).reshape(
            half_slots, rows, piece
        )

    def down_out(first, n):
        value = jnp.dot(
            hidden[pl.ds(first * rows, half_rows)],
            down_v[:, :, spot(n)].reshape(hidden_units, piece),
            preferred_element_type=f32,
        )
        put(0, first, n, value)

    def back_out(first, n):
        at, some = pl.ds(first * rows, half_rows), pl.ds(n * 2, 2)
        value = contract_last(grad_gate[at], gate_v[some].reshape(piece, hidden_units))
        value = value + contract_last(grad_up[at], up_v[some].reshape(piece, hidden_units))
        put(1, first, n, value)

    near, far = {}, []

    def send_near(which, n):
        near[which, n] = [
            links.column(stage.at[which, 3, :, spot(n)], landed.at[which, 1, :, spot(n)], 1),
            links.column(stage.at[which, 2, :, spot(n)], landed.at[which, 0, :, spot(n)], 1),
        ]
        start_all(near[which, n])

    def relay(which, n):
        near[which, n][0].wait_recv()
        stage[which, 1, :, spot(n)] = (
            stage[which, 1, :, spot(n)].astype(f32) + landed[which, 1, :, spot(n)].astype(f32)
        ).astype(bf16)
        copy = links.column(stage.at[which, 1, :, spot(n)], landed.at[which, 2, :, spot(n)], 2)
        copy.start()
        far.append(copy)

    for n in range(pieces):
        down_out(half_slots, n)
        send_near(0, n)
        down_out(0, n)

    def activation_grads(first):
        at = pl.ds(first * rows, half_rows)

        def step(j, carry):
            cols = pl.ds(pl.multiple_of(j * BLOCK, BLOCK), BLOCK)
            cot_rows = cots[pl.ds(first, half_slots)].reshape(half_rows, width)
            grad_hidden = contract_last(cot_rows, down_v[j])
            grad_gate[at, cols] = (grad_gate[at, cols].astype(f32) * grad_hidden).astype(bf16)
            grad_up[at, cols] = (grad_up[at, cols].astype(f32) * grad_hidden).astype(bf16)
            return carry

        lax.fori_loop(0, blocks, step, 0)

    for copy in [cot_relay]:
        copy.wait_recv()
    start_all(cot_swaps[3:])
    def flat(ref, cols):
        return ref[:, :, cols].reshape(group_rows, -1)

    for copy in cot_swaps + hidden_acts:
        copy.wait_recv()

    def down_block(pair, place):
        own = pl.ds(pl.multiple_of((2 * pair + core) * BLOCK, BLOCK), BLOCK)
        other = pl.ds(pl.multiple_of(pair * BLOCK, BLOCK), BLOCK)
        left, right = hidden[:, own].T, other_hidden[:, other].T
        for cols in (pl.ds(0, width // 2), pl.ds(width // 2, width // 2)):
            total = jnp.dot(left, flat(cots, cols), preferred_element_type=f32)
            total = total + jnp.dot(right, flat(other_cots, cols), preferred_element_type=f32)
            place[:, cols] = total.astype(bf16)

    def halves_of(ref):
        return [ref.at[pl.ds(0, BLOCK // 2)], ref.at[pl.ds(BLOCK // 2, BLOCK // 2)]]

    chip = ctx // 2
    down_scatter = ChipScatter(
        links,
        [down_v.at[2]] + [down_parts.at[flip - 1] for flip in (1, 2, 3)],
        halves_of(down_halves),
        [down_v.at[0], down_v.at[1]],
    )
    down_block(lax.bitwise_xor(chip, 3), down_parts.at[2])
    down_scatter.begin()

    def down_side(flip, carry):
        down_block(lax.bitwise_xor(chip, flip), down_parts.at[flip - 1])
        return carry

    lax.fori_loop(1, 3, down_side, 0)
    activation_grads(0)
    activation_grads(half_slots)
    down_block(chip, down_v.at[2])
    theirs = pl.ds(pl.multiple_of((1 - core) * half_units, half_units), half_units)
    acts = [
        links.plane(grad_gate.at[:, theirs], other_gate, ACROSS_CORE),
        links.plane(grad_up.at[:, theirs], other_up, ACROSS_CORE),
    ]
    start_all(acts)

    def free(sem):
        for flip in (ACROSS_X, ACROSS_Y):
            pl.semaphore_signal(
                sem,
                inc=1,
                device_id=(lax.bitwise_xor(ctx, flip), fsdp),
                device_id_type=MESH,
            )

    free(down_free)
    pl.semaphore_wait(down_free, 2)
    down_scatter.middle()

    for n in range(pieces):
        back_out(half_slots, n)
        send_near(1, n)
    for n in range(pieces):
        back_out(0, n)
    free(gate_free)
    relay(0, 0)
    relay(0, 1)

    mine = pl.ds(pl.multiple_of(core * half_units, half_units), half_units)

    def weight_block(b, carry):
        cols = pl.ds(pl.multiple_of(b * BLOCK, BLOCK), BLOCK)
        left, right = flat(normed_ref, cols).T, flat(other_normed, cols).T
        plane, first = b // 2, 2 * lax.rem(b, 2)
        at_row = pl.ds(pl.multiple_of((plane // 2) * (BLOCK // 2), BLOCK // 2), BLOCK // 2)
        at_col = pl.ds(pl.multiple_of(lax.rem(plane, 2) * (width // 2), width // 2), width // 2)
        for own_grad, other_grad, place in (
            (grad_gate, other_gate, gate_v),
            (grad_up, other_up, up_v),
        ):
            total = jnp.dot(left, own_grad[:, mine], preferred_element_type=f32)
            total = total + jnp.dot(right, other_grad[...], preferred_element_type=f32)
            low = total.astype(bf16)
            place[first, at_row, at_col] = low[: BLOCK // 2]
            place[first + 1, at_row, at_col] = low[BLOCK // 2 :]
        return carry

    for copy in swaps + acts:
        copy.wait_recv()
    lax.fori_loop(0, blocks // 2, weight_block, 0)
    relay(0, 2)
    lax.fori_loop(blocks // 2, blocks, weight_block, 0)
    pl.semaphore_wait(gate_free, 2)
    gate_scatter = ChipScatter(
        links,
        [gate_v.at[lax.bitwise_xor(chip, flip)] for flip in range(4)],
        halves_of(gate_v.at[4]),
        [gate_v.at[5], gate_v.at[6]],
    )
    gate_scatter.begin()
    up_copy = links.here(up_v.at[pl.ds(0, 4)], up_part)
    up_copy.start()
    relay(0, 3)
    relay(1, 0)
    relay(1, 1)
    relay(1, 2)
    relay(1, 3)
    gate_scatter.middle()
    down_copy = links.here(down_scatter.finish(), down_sum)
    down_copy.start()

    for copy in [pair[1] for pair in near.values()] + far:
        copy.wait_recv()
    for copies in near.values():
        for copy in copies:
            copy.wait_send()
    mid_load.wait()
    chunk = 32

    def close(step, carry):
        at = pl.ds(pl.multiple_of(step * chunk, chunk), chunk)

        def summed(which):
            total = stage[which, 0, at].astype(f32) + landed[which, 0, at].astype(f32)
            return total + landed[which, 2, at].astype(f32)

        mid = grad_mid_ref[at]
        stage[0, 2, at] = (mid + summed(0)).astype(bf16)
        scale = lax.rsqrt(jnp.mean(mid * mid, axis=-1, keepdims=True) + norm_eps)
        u = summed(1) * gain_ref[...]
        inner = jnp.mean(u * mid, axis=-1, keepdims=True)
        grad_mid = (
            cots[0, at].astype(f32) + scale * u - mid * (scale * scale * scale * inner)
        )
        grad_mid_ref[at] = grad_mid
        stage[1, 2, at] = grad_mid.astype(bf16)
        return carry

    lax.fori_loop(0, rows // chunk, close, 0)
    row_copies = [
        links.here(stage.at[0, 2], result_ref),
        links.here(stage.at[1, 2], grad_proj_ref),
    ]
    start_all(row_copies)

    gate_copy = links.here(gate_scatter.finish(), gate_sum)
    gate_copy.start()
    sent = far + swaps + cot_swaps
    for copy in sent + hidden_acts + acts + [cot_relay]:
        copy.wait_send()
    down_scatter.drain()
    gate_scatter.drain()
    for copy in row_copies + [up_copy, down_copy, gate_copy]:
        copy.wait()


def feed_forward(
    mid, cotangent, gain_ffn, normed_group, cot_near, cot_far, gate_w, up_w, w_down
):
    f32, bf16 = jnp.float32, jnp.bfloat16
    n_fsdp = lax.axis_size("fsdp")
    rows, width = mid.shape
    group_rows = n_fsdp * rows
    units = w_down.shape[0] * BLOCK
    blocks = units // BLOCK
    vmem, hbm = pl.BlockSpec(memory_space=pltpu.VMEM), pl.BlockSpec(memory_space=pl.ANY)
    shape = jax.ShapeDtypeStruct
    return pl.pallas_call(
        feed_forward_kernel,
        name="feed_forward",
        out_shape=[
            shape((rows, width), bf16),
            shape((rows, width), f32),
            shape((rows, width), bf16),
            shape((BLOCK, width), bf16),
            shape((BLOCK, width), bf16),
            shape((blocks // 2, BLOCK, width), bf16),
        ],
        in_specs=[hbm] + [vmem] * 5 + [hbm] * 3,
        out_specs=[hbm, vmem, hbm] + [hbm] * 3,
        scratch_shapes=[
            pltpu.VMEM((width // BLOCK, BLOCK, units), bf16),
            pltpu.VMEM((width // BLOCK, BLOCK, units), bf16),
            pltpu.VMEM((blocks, BLOCK, width), bf16),
            pltpu.VMEM((n_fsdp, rows, width), bf16),
            pltpu.VMEM((group_rows, units), bf16),
            pltpu.VMEM((group_rows, units), bf16),
            pltpu.VMEM((group_rows, units), bf16),
            pltpu.VMEM((n_fsdp, rows, width), bf16),
            pltpu.VMEM((n_fsdp, rows, width), bf16),
            pltpu.VMEM((group_rows, units // 2), bf16),
            pltpu.VMEM((group_rows, units // 2), bf16),
            pltpu.VMEM((group_rows, units // 2), bf16),
            pltpu.VMEM((2, n_fsdp, rows, width), bf16),
            pltpu.VMEM((2, n_fsdp - 1, rows, width), bf16),
            pltpu.VMEM((blocks // 2 - 1, BLOCK, width), bf16),
            pltpu.VMEM((BLOCK, width), bf16),
            pltpu.SemaphoreType.DMA((48,)),
            pltpu.SemaphoreType.DMA((48,)),
            pltpu.SemaphoreType.DMA((8,)),
            pltpu.SemaphoreType.DMA((3, blocks)),
            pltpu.SemaphoreType.REGULAR,
            pltpu.SemaphoreType.REGULAR,
        ],
        compiler_params=pltpu.CompilerParams(
            collective_id=2, has_side_effects=True, vmem_limit_bytes=62 * 2**20
        ),
    )(mid, cotangent, gain_ffn[None], normed_group, cot_near, cot_far, gate_w, up_w, w_down)


def attention_back_kernel(
    grad_proj_ref,
    grad_mid_ref,
    tokens_ref,
    gain_ref,
    w_head_ref,
    out_head_ref,
    qkv_ref,
    attended_ref,
    cos_ref,
    sin_ref,
    pair_ref,
    normed_hbm,
    gate_sum_hbm,
    up_part_hbm,
    grad_input_ref,
    qkv_sum,
    out_sum,
    gate_out,
    up_out,
    proj,
    normed,
    up_part,
    up_halves,
    up_sides,
    grad_att,
    grads,
    key_grad,
    value_grad,
    part,
    core_rx,
    half_rx,
    side_rx,
    out_stage,
    out_landed,
    out_summed,
    head_stage,
    head_summed,
    head_landed,
    pos_col_ref,
    pos_row_ref,
    send_sem,
    recv_sem,
    local_sem,
):
    f32, bf16 = jnp.float32, jnp.bfloat16
    ctx, fsdp = lax.axis_index("ctx"), lax.axis_index("fsdp")
    links = Links((send_sem, recv_sem, local_sem), ctx, fsdp)
    chip, core = ctx // 2, lax.rem(ctx, 2)
    n_ctx, rows, width = proj.shape
    n_fsdp = out_landed.shape[0]
    seq_rows = n_ctx * rows
    head_columns = out_head_ref.shape[0]
    strip_rows = out_landed.shape[1]
    score_scale = 1.0 / math.sqrt(HEAD_SIZE)
    loads = [links.here(normed_hbm, normed), links.here(up_part_hbm, up_part)]
    for copy in loads:
        copy.start()

    flips = [(a, 0) for a in range(1, n_ctx)] + COLUMN_FLIPS + [(1, b) for b in (1, 2, 3)]
    greet(ctx, fsdp, flips)

    proj[ctx] = grad_proj_ref[...]
    half = rows // 2
    gather = PlaneGather(
        links,
        lambda j: [proj.at[j]],
        lambda j, which: [proj.at[j, pl.ds(which * half, half)]],
    )
    gather.begin()
    place_positions(pair_ref, pos_col_ref, pos_row_ref, rows)

    def spread(source, dest):
        half_width = width // 2
        place = pl.ds(pl.multiple_of((2 * fsdp + core) * half_width, half_width), half_width)
        copies = []
        for a in (0, 1):
            for b in range(n_fsdp):
                plane = lax.bitwise_xor(fsdp, b)
                who = lax.bitwise_xor(core, a)
                at_row = (plane // 2) * (BLOCK // 2) + who * strip_rows
                block = source.at[
                    pl.ds(pl.multiple_of(at_row, strip_rows), strip_rows),
                    pl.ds(pl.multiple_of(lax.rem(plane, 2) * half_width, half_width), half_width),
                ]
                target = dest.at[:, place]
                if a or b:
                    copies.append(
                        links.to(block, target, lax.bitwise_xor(ctx, a), plane)
                    )
                else:
                    local = links.here(block, target)
                    locals_.append(local)
                    local.start()
        for copy in copies:
            copy.start()
        return copies

    locals_ = []
    up_scatter = ChipScatter(
        links,
        [up_part.at[lax.bitwise_xor(chip, flip)] for flip in range(4)],
        [up_halves.at[0], up_halves.at[1]],
        [up_sides.at[0], up_sides.at[1]],
    )
    gate_copies = spread(gate_sum_hbm, gate_out)
    gather.forward()
    gather.finish()

    total = jnp.zeros((head_columns, width), f32)
    for j in range(0, n_ctx, 2):
        total = total + lax.dot_general(
            attended_ref[pl.ds(j * rows, 2 * rows)],
            proj[pl.ds(j, 2)].reshape(2 * rows, width),
            (((0,), (0,)), ((), ())),
            preferred_element_type=f32,
        )
    out_stage[...] = total.astype(bf16).reshape(out_stage.shape)
    half_ctx = n_ctx // 2
    out_base = links.remote
    links.remote += half_ctx
    out_copies = []
    for j in range(half_ctx):
        target = half_ctx * core + j
        copy = pltpu.make_async_remote_copy(
            src_ref=out_stage.at[j],
            dst_ref=out_landed.at[chip],
            send_sem=send_sem.at[out_base + j],
            recv_sem=recv_sem.at[out_base + chip],
            device_id=(target, fsdp),
            device_id_type=MESH,
        )
        out_copies.append((target != ctx, copy))

        @pl.when(target != ctx)
        def _(copy=copy):
            copy.start()

    own_out = links.here(out_stage.at[lax.rem(ctx, half_ctx)], out_landed.at[chip])
    out_own_chip = lax.rem(ctx, 2) == ctx // half_ctx

    @pl.when(out_own_chip)
    def _():
        own_out.start()

    up_scatter.begin(up_part_hbm.at[lax.bitwise_xor(chip, 3)])

    def out_arrivals():
        for source in range(half_ctx):
            arrival = pltpu.make_async_remote_copy(
                src_ref=out_stage.at[0],
                dst_ref=out_landed.at[source],
                send_sem=send_sem.at[out_base],
                recv_sem=recv_sem.at[out_base + source],
                device_id=(lax.bitwise_xor(ctx, 1), fsdp),
                device_id_type=MESH,
            )

            @pl.when(2 * source + ctx // half_ctx != ctx)
            def _(arrival=arrival):
                arrival.wait_recv()

        @pl.when(out_own_chip)
        def _():
            own_out.wait()

    def out_begin():
        out_arrivals()
        copies = [
            links.column(
                out_landed.at[lax.bitwise_xor(fsdp, flip)], out_summed.at[slot], 1
            )
            for flip, slot in ((3, 1), (1, 0))
        ]
        start_all(copies)
        return copies

    def out_relay(copies):
        copies[0].wait_recv()
        across = lax.bitwise_xor(fsdp, 2)
        out_landed[across] = (
            out_landed[across].astype(f32) + out_summed[1].astype(f32)
        ).astype(bf16)
        copy = links.column(out_landed.at[across], out_summed.at[2], 2)
        copy.start()
        return copy

    def back(step, carry):
        at = pl.multiple_of(step * 2 * rows, 2 * rows)
        tile = proj[pl.ds(2 * step, 2)].reshape(2 * rows, width)
        grad_att[pl.ds(at, 2 * rows)] = contract_last(tile, out_head_ref[...]).astype(bf16)
        return carry

    lax.fori_loop(0, n_ctx // 2, back, 0)

    key_grad[...] = jnp.zeros_like(key_grad)
    value_grad[...] = jnp.zeros_like(value_grad)

    def attend_head(column):
        cols = pl.ds(column, HEAD_SIZE)

        def step(index, carry):
            at = pl.ds(pl.multiple_of(index * 2 * rows, 2 * rows), 2 * rows)
            keys = qkv_ref[:, pl.ds(head_columns, HEAD_SIZE)]
            values = qkv_ref[:, pl.ds(head_columns + HEAD_SIZE, HEAD_SIZE)]
            causal = pos_row_ref[...] <= pos_col_ref[at]
            query, grad_mixed = qkv_ref[at, cols], grad_att[at, cols]
            scores = contract_last(query, keys) * score_scale
            scores = jnp.where(causal, scores, -1e30)
            shifted = jnp.exp(scores - jnp.max(scores, axis=-1, keepdims=True))
            probs = shifted * (1.0 / jnp.sum(shifted, axis=-1, keepdims=True))
            grad_probs = contract_last(grad_mixed, values)
            delta = jnp.sum(grad_probs * probs, axis=-1, keepdims=True)
            grad_scores = (probs * (grad_probs - delta)).astype(bf16)
            value_grad[...] += contract_first(probs.astype(bf16), grad_mixed)
            key_grad[...] += contract_first(grad_scores, query)
            grad_query = jnp.dot(grad_scores, keys, preferred_element_type=f32) * score_scale
            grads[at, cols] = turn(grad_query, cos_ref[at], sin_ref[at], -1.0).astype(bf16)
            return carry

        lax.fori_loop(0, n_ctx // 2, step, 0)

    depth = n_ctx * strip_rows
    head_near, head_far = [], []

    def head_part(cols, slot):
        flip = (0, 2, 1, 3)[slot]
        places = pl.ds(pl.multiple_of(lax.bitwise_xor(fsdp, flip) * depth, depth), depth)
        total = contract_first(normed[:, :, places].reshape(seq_rows, depth), grads[:, cols])
        head_stage[slot, :, :, cols] = total.astype(bf16).reshape(n_ctx, strip_rows, -1)

    def head_begin(cols):
        copies = []
        for slot in (3, 2):
            head_part(cols, slot)
            copy = links.flip(
                head_stage.at[slot, :, :, cols],
                head_summed.at[slot - 2, :, :, cols],
                0,
                1,
            )
            copy.start()
            copies.append(copy)
        head_near.append(copies)
        for slot in (1, 0):
            head_part(cols, slot)

    def head_relay(index, cols):
        head_near[index][0].wait_recv()
        head_stage[1, :, :, cols] = (
            head_stage[1, :, :, cols].astype(f32) + head_summed[1, :, :, cols].astype(f32)
        ).astype(bf16)
        copy = links.flip(
            head_stage.at[1, :, :, cols], head_summed.at[2, :, :, cols], 0, 2
        )
        copy.start()
        head_far.append(copy)

    first_cols = pl.ds(0, HEAD_SIZE)
    rest_cols = pl.ds(HEAD_SIZE, grads.shape[1] - HEAD_SIZE)
    attend_head(0)
    loads[0].wait()
    head_begin(first_cols)
    out_near = out_begin()
    for column in range(HEAD_SIZE, head_columns, HEAD_SIZE):
        attend_head(column)
    loads[1].wait()
    up_scatter.middle()
    turned = turn(key_grad[...] * score_scale, cos_ref[...], sin_ref[...], -1.0)
    grads[:, pl.ds(head_columns, HEAD_SIZE)] = turned.astype(bf16)
    grads[:, pl.ds(head_columns + HEAD_SIZE, HEAD_SIZE)] = value_grad[...].astype(bf16)
    head_begin(rest_cols)

    scatter = PlaneScatter(links, part, core_rx, half_rx, side_rx)
    for flip, q in scatter.order():
        at = pl.multiple_of(q * 2 * rows, 2 * rows)
        out = contract_last(grads[pl.ds(at, 2 * rows)], w_head_ref[...])
        part[pl.ds(2 * q, 2)] = out.astype(bf16).reshape(2, rows, width)
        scatter.give(flip, q)

    scatter.begin()
    head_relay(0, first_cols)
    out_far = out_relay(out_near)
    head_relay(1, rest_cols)
    scatter.middle()
    up_copies = spread(up_scatter.finish(), up_out)
    grad_normed = scatter.finish()
    inputs = tokens_ref[...].astype(f32)
    scale = lax.rsqrt(jnp.mean(inputs * inputs, axis=-1, keepdims=True) + norm_eps)
    u = grad_normed * gain_ref[...]
    inner = jnp.mean(u * inputs, axis=-1, keepdims=True)
    grad_input_ref[...] = (
        grad_mid_ref[...] + scale * u - inputs * (scale * scale * scale * inner)
    )
    for copy in [pair[1] for pair in head_near] + head_far:
        copy.wait_recv()
    head_stage[0] = (
        head_stage[0].astype(f32) + head_summed[0].astype(f32) + head_summed[2].astype(f32)
    ).astype(bf16)
    head_copies = [
        links.plane(
            head_stage.at[0, lax.bitwise_xor(ctx, a)], head_landed.at[ctx], a
        )
        for a in range(1, n_ctx)
    ]
    start_all(head_copies)
    head_landed[ctx] = head_stage[0, ctx]

    for copy in (out_near[1], out_far):
        copy.wait_recv()
    out_sum[...] = (
        out_landed[fsdp].astype(f32) + out_summed[0].astype(f32) + out_summed[2].astype(f32)
    )
    for copy in head_copies:
        copy.wait_recv()
    for copy in locals_:
        copy.wait()
    query_columns = QUERY_HEADS * HEAD_SIZE
    key_columns = KEY_VALUE_HEADS * HEAD_SIZE
    for head in range(KEY_VALUE_HEADS):
        total = head_landed[head].astype(f32)
        qkv_sum[:, pl.ds(head * head_columns, head_columns)] = total[:, :head_columns]
        qkv_sum[:, pl.ds(query_columns + head * HEAD_SIZE, HEAD_SIZE)] = total[
            :, head_columns : head_columns + HEAD_SIZE
        ]
        qkv_sum[:, pl.ds(query_columns + key_columns + head * HEAD_SIZE, HEAD_SIZE)] = total[
            :, head_columns + HEAD_SIZE :
        ]
    for copy in gate_copies + up_copies:
        copy.wait_recv()
    for copy in gate_copies + up_copies + head_copies + head_far + head_near[0] + head_near[1]:
        copy.wait_send()
    for copy in out_near + [out_far]:
        copy.wait_send()
    for away, copy in out_copies:

        @pl.when(away)
        def _(copy=copy):
            copy.wait_send()

    gather.drain()
    scatter.drain()
    up_scatter.drain()


def attention_back(
    grad_proj,
    grad_mid,
    tokens,
    gain_attn,
    w_head,
    out_head,
    qkv,
    attended,
    cos,
    sin,
    pair_block,
    normed,
    gate_sum,
    up_part,
):
    f32, bf16 = jnp.float32, jnp.bfloat16
    n_ctx, n_fsdp = lax.axis_size("ctx"), lax.axis_size("fsdp")
    rows, width = tokens.shape
    seq_rows = n_ctx * rows
    strip_rows = width // (n_ctx * n_fsdp)
    head_columns, all_columns = attended.shape[1], qkv.shape[1]
    vmem, hbm = pl.BlockSpec(memory_space=pltpu.VMEM), pl.BlockSpec(memory_space=pl.ANY)
    shape = jax.ShapeDtypeStruct
    return pl.pallas_call(
        attention_back_kernel,
        name="attention_back",
        out_shape=[
            shape((rows, width), f32),
            shape((strip_rows, (QUERY_HEADS + 2 * KEY_VALUE_HEADS) * HEAD_SIZE), f32),
            shape((strip_rows, width), f32),
            shape((strip_rows, n_fsdp * width), bf16),
            shape((strip_rows, n_fsdp * width), bf16),
        ],
        in_specs=[vmem] * 10 + [pl.BlockSpec(memory_space=pltpu.SMEM)] + [hbm] * 3,
        out_specs=[vmem] * 3 + [hbm] * 2,
        scratch_shapes=[
            pltpu.VMEM((n_ctx, rows, width), bf16),
            pltpu.VMEM((n_ctx, rows, width), bf16),
            pltpu.VMEM(up_part.shape, bf16),
            pltpu.VMEM((2, BLOCK // 2, width), bf16),
            pltpu.VMEM((2, BLOCK, width), bf16),
            pltpu.VMEM((seq_rows, head_columns), bf16),
            pltpu.VMEM((seq_rows, all_columns), bf16),
            pltpu.VMEM((seq_rows, HEAD_SIZE), f32),
            pltpu.VMEM((seq_rows, HEAD_SIZE), f32),
            pltpu.VMEM((n_ctx, rows, width), bf16),
            pltpu.VMEM((n_ctx // 2, rows, width), bf16),
            pltpu.VMEM((2, rows // 2, width), bf16),
            pltpu.VMEM((2, rows, width), bf16),
            pltpu.VMEM((n_ctx // 2, strip_rows, width), bf16),
            pltpu.VMEM((n_fsdp, strip_rows, width), bf16),
            pltpu.VMEM((n_fsdp - 1, strip_rows, width), bf16),
            pltpu.VMEM((n_fsdp, n_ctx, strip_rows, all_columns), bf16),
            pltpu.VMEM((n_fsdp - 1, n_ctx, strip_rows, all_columns), bf16),
            pltpu.VMEM((n_ctx, strip_rows, all_columns), bf16),
            pltpu.VMEM((seq_rows, 1), jnp.int32),
            pltpu.VMEM((1, seq_rows), jnp.int32),
            pltpu.SemaphoreType.DMA((96,)),
            pltpu.SemaphoreType.DMA((96,)),
            pltpu.SemaphoreType.DMA((8,)),
        ],
        compiler_params=pltpu.CompilerParams(
            collective_id=3, has_side_effects=True, vmem_limit_bytes=62 * 2**20
        ),
    )(
        grad_proj,
        grad_mid,
        tokens,
        gain_attn[None],
        w_head,
        out_head,
        qkv,
        attended,
        cos,
        sin,
        pair_block,
        normed,
        gate_sum,
        up_part,
    )


def copier(sem):
    copies = []

    def copy(source, dest):
        copies.append(pltpu.make_async_copy(source, dest, sem.at[len(copies)]))
        copies[-1].start()
        return copies[-1]

    return copy


def widen_kernel(gain_attn, gain_ffn, qkv, gate, up, qkv_hbm, gate_hbm, up_hbm, *refs):
    (qkv_out, gate_out, up_out, sums_ref), refs = refs[:4], refs[4:]
    (qkv_v, gate_v, up_v, qkv_w, gate_w, up_w, gate_f, up_f, sem) = refs
    f32 = jnp.float32
    rows = gate_w.shape[0]
    ctx, fsdp = lax.axis_index("ctx"), lax.axis_index("fsdp")
    at = pl.ds(pl.multiple_of(ctx * rows, rows), rows)
    copy = copier(sem)
    loads, stores = [], []
    for source, dest, weight, rows_v in (
        (gate, gate_v, gate_hbm, gate_w),
        (up, up_v, up_hbm, up_w),
        (qkv, qkv_v, qkv_hbm, qkv_w),
    ):
        loads.append((copy(source, dest), copy(weight.at[at], rows_v)))

    def widen(index, source, weight, wide, out):
        for load in loads[index]:
            load.wait()
        values = source[...].astype(f32)
        if wide is None:
            stores.append(copy(source, out))
        else:
            wide[...] = values
            stores.append(copy(wide, out))
        return jnp.sum(weight[...].astype(f32) * values, axis=1, keepdims=True)

    ffn = widen(0, gate_v, gate_w, gate_f, gate_out)
    ffn = ffn + widen(1, up_v, up_w, up_f, up_out)
    attn = widen(2, qkv_v, qkv_w, None, qkv_out)
    which = fsdp * lax.axis_size("ctx") + ctx
    lanes = pl.ds(pl.multiple_of((which // 2) * 2 * rows, 2 * rows), 2 * rows)
    for index, (total, gain_ref) in enumerate(((attn, gain_attn), (ffn, gain_ffn))):
        turned = jnp.broadcast_to(total, (rows, HEAD_SIZE)).T
        gain = gain_ref[:, lanes]
        gain = jnp.where(lax.rem(which, 2) == 1, pltpu.roll(gain, rows, 1), gain)
        sums_ref[pl.ds(index, 1)] = turned[:1] / gain[:, :rows]
    for store in stores:
        store.wait()


def widen(qkv_sum, gate_low, up_low, qkv_w, w_gate, w_up, gain_attn, gain_ffn):
    f32, bf16 = jnp.float32, jnp.bfloat16
    rows = gate_low.shape[0]
    vmem, hbm = pl.BlockSpec(memory_space=pltpu.VMEM), pl.BlockSpec(memory_space=pl.ANY)
    arrays = (qkv_sum, gate_low, up_low)
    return pl.pallas_call(
        widen_kernel,
        name="widen",
        out_shape=[jax.ShapeDtypeStruct(a.shape, f32) for a in arrays]
        + [jax.ShapeDtypeStruct((2, rows), f32)],
        in_specs=[vmem] * 2 + [hbm] * 6,
        out_specs=[hbm] * 3 + [vmem],
        scratch_shapes=[pltpu.VMEM(a.shape, a.dtype) for a in arrays]
        + [pltpu.VMEM(a.shape, bf16) for a in arrays]
        + [pltpu.VMEM(a.shape, f32) for a in (gate_low, up_low)]
        + [pltpu.SemaphoreType.DMA((9,))],
        compiler_params=pltpu.CompilerParams(vmem_limit_bytes=62 * 2**20),
    )(gain_attn[None], gain_ffn[None], *arrays, qkv_w, w_gate, w_up)


def pass_on_kernel(count, *refs):
    sources, outs, held, (wide, sem) = (
        refs[: count + 1],
        refs[count + 1 : 2 * count + 2],
        refs[2 * count + 2 : 3 * count + 3],
        refs[3 * count + 3 :],
    )
    copy = copier(sem)
    loads = [copy(source, dest) for source, dest in zip(sources, held)]
    stores = []
    for load, source, dest in zip(loads, held, outs):
        load.wait()
        if len(stores) == count:
            wide[...] = source[...].astype(jnp.float32)
            source = wide
        stores.append(copy(source, dest))
    for store in stores:
        store.wait()


def pass_on(passed, last):
    hbm = pl.BlockSpec(memory_space=pl.ANY)
    count = len(passed)
    arrays = list(passed) + [last]
    kinds = [a.dtype for a in passed] + [jnp.float32]
    moved = 2 * sum(a.size * a.dtype.itemsize for a in arrays)
    return pl.pallas_call(
        functools.partial(pass_on_kernel, count),
        name="pass_on",
        out_shape=[jax.ShapeDtypeStruct(a.shape, kind) for a, kind in zip(arrays, kinds)],
        in_specs=[hbm] * (count + 1),
        out_specs=[hbm] * (count + 1),
        scratch_shapes=[pltpu.VMEM(a.shape, a.dtype) for a in arrays]
        + [pltpu.VMEM(last.shape, jnp.float32), pltpu.SemaphoreType.DMA((2 * count + 2,))],
        compiler_params=pltpu.CompilerParams(vmem_limit_bytes=62 * 2**20),
        cost_estimate=pl.CostEstimate(flops=last.size, bytes_accessed=moved, transcendentals=0),
    )(*arrays)


def local_heads(
    tokens,
    cotangent,
    gain_attn,
    gain_ffn,
    query_key_value_weight,
    w_out,
    w_gate,
    w_up,
    w_down,
    pair_block,
):
    n_ctx, n_fsdp = lax.axis_size("ctx"), lax.axis_size("fsdp")
    width = tokens.shape[1]
    depth = query_key_value_weight.shape[0]

    (
        mid,
        normed_two_group,
        cot_near,
        cot_far,
        gate_w,
        up_w,
        qkv,
        attended,
        normed_one_seq,
        w_head,
        out_head,
        cos,
        sin,
    ) = attention_forward(
        tokens,
        cotangent,
        gain_attn,
        gain_ffn,
        query_key_value_weight,
        w_out,
        w_gate,
        w_up,
        pair_block,
    )
    result, grad_mid, grad_proj, down_sum, gate_sum, up_part = feed_forward(
        mid,
        cotangent,
        gain_ffn,
        normed_two_group,
        cot_near,
        cot_far,
        gate_w,
        up_w,
        w_down.reshape(-1, BLOCK, width),
    )
    grad_input, qkv_sum, grad_out, gate_low, up_low = attention_back(
        grad_proj,
        grad_mid,
        tokens,
        gain_attn,
        w_head,
        out_head,
        qkv,
        attended,
        cos,
        sin,
        pair_block,
        normed_one_seq,
        gate_sum,
        up_part,
    )
    grad_qkv, grad_gate, grad_up, sums = widen(
        qkv_sum, gate_low, up_low, query_key_value_weight, w_gate, w_up, gain_attn, gain_ffn
    )
    result, grad_input, grad_out, grad_down = pass_on((result, grad_input, grad_out), down_sum)
    gain_pairs = [(c * n_fsdp + f, f * n_ctx + c) for c in range(n_ctx) for f in range(n_fsdp)]
    grad_gain_attn, grad_gain_ffn = lax.ppermute(sums, ("ctx", "fsdp"), gain_pairs)
    return (
        result,
        grad_input,
        grad_gain_attn,
        grad_gain_ffn,
        grad_qkv,
        grad_out,
        grad_gate,
        grad_up,
        grad_down,
    )


def solution(mesh):
    fits = mesh.shape["ctx"] == KEY_VALUE_HEADS and mesh.shape["fsdp"] == KEY_VALUE_HEADS // 2
    local = local_heads if fits else local_general
    return jax.shard_map(
        local,
        mesh=mesh,
        in_specs=(
            P(("ctx", "fsdp"), None),
            P(("ctx", "fsdp"), None),
            P(),
            P(),
            P("fsdp", None),
            P("fsdp", None),
            P("fsdp", None),
            P("fsdp", None),
            P("fsdp", None),
            P(),
        ),
        out_specs=(
            P(("ctx", "fsdp"), None),
            P(("ctx", "fsdp"), None),
            P(("ctx", "fsdp")),
            P(("ctx", "fsdp")),
            P(("fsdp", "ctx"), None),
            P(("fsdp", "ctx"), None),
            P(("fsdp", "ctx"), None),
            P(("fsdp", "ctx"), None),
            P(("fsdp", "ctx"), None),
        ),
        check_vma=False,
    )
```

```python
import functools
import math

import jax
import jax.numpy as jnp
from jax import lax
from jax.experimental import pallas as pl
from jax.experimental.pallas import tpu as pltpu
from jax.sharding import PartitionSpec as P

QUERY_HEADS = 16
KEY_VALUE_HEADS = 8
HEAD_SIZE = 128


norm_eps = 1e-05
rope_base = 1000000.0


def rms_norm(vectors, gain_vec):
    return (
        vectors
        * lax.rsqrt(jnp.mean(vectors * vectors, axis=-1, keepdims=True) + norm_eps)
        * gain_vec
    )


def apply_rotation(vectors, where_pos):
    half_dim = vectors.shape[-1] // 2
    frequency = jnp.exp(
        jnp.arange(half_dim, dtype=jnp.float32) * (-2.0 * math.log(rope_base) / vectors.shape[-1])
    )
    angles = where_pos.astype(jnp.float32)[:, None] * frequency[None, :]
    cosine = jnp.cos(angles)[:, None, :]
    sine_val = jnp.sin(angles)[:, None, :]
    first_half = vectors[..., :half_dim]
    second_half = vectors[..., half_dim:]
    return jnp.concatenate(
        [
            first_half * cosine - second_half * sine_val,
            second_half * cosine + first_half * sine_val,
        ],
        axis=-1,
    )


def positions(pair_block, token_rows):
    n_ctx = lax.axis_size("ctx")
    half_rows = token_rows // 2
    row_index = jnp.arange(token_rows, dtype=jnp.int32)
    first_block = pair_block[:, None]
    which_block = jnp.where(
        row_index[None, :] < half_rows, first_block, 2 * n_ctx - 1 - first_block
    )
    pos_table = which_block * half_rows + (row_index % half_rows)[None, :]
    own_pos = lax.dynamic_slice(pos_table, (lax.axis_index("ctx"), 0), (1, token_rows)).reshape(
        token_rows
    )
    return (pos_table.reshape(-1), own_pos)


def to_groups(input_array, group_count):
    token_rows = input_array.shape[0]
    head_length = input_array.shape[-1] // (group_count * KEY_VALUE_HEADS)
    return (
        input_array.reshape(token_rows, KEY_VALUE_HEADS, group_count, head_length)
        .transpose(1, 2, 0, 3)
        .reshape(KEY_VALUE_HEADS, group_count * token_rows, head_length)
    )


def from_groups(input_array, group_count):
    head_length = input_array.shape[-1]
    token_rows = input_array.shape[1] // group_count
    return (
        input_array.reshape(KEY_VALUE_HEADS, group_count, token_rows, head_length)
        .transpose(2, 0, 1, 3)
        .reshape(token_rows, KEY_VALUE_HEADS * group_count * head_length)
    )


def split_keys(every_key, every_value, key_pos):
    total_keys = every_key.shape[0]
    block_length = min(1024, total_keys)
    block_count = total_keys // block_length
    return (
        every_key.reshape(block_count, block_length, KEY_VALUE_HEADS, HEAD_SIZE),
        every_value.reshape(block_count, block_length, KEY_VALUE_HEADS, HEAD_SIZE),
        key_pos.reshape(block_count, block_length),
    )


def contract_last(left, right):
    return lax.dot_general(
        left, right, (((1,), (1,)), ((), ())), preferred_element_type=jnp.float32
    )


def contract_first(left, right):
    return lax.dot_general(
        left, right, (((0,), (0,)), ((), ())), preferred_element_type=jnp.float32
    )


def local_general(
    tokens,
    cotangent,
    gain_attn,
    gain_ffn,
    query_key_value_weight,
    w_out,
    w_gate,
    w_up,
    w_down,
    pair_block,
):
    token_rows = tokens.shape[0]
    query_columns = QUERY_HEADS * HEAD_SIZE
    key_value_columns = KEY_VALUE_HEADS * HEAD_SIZE
    group_count = QUERY_HEADS // KEY_VALUE_HEADS
    score_scale = 1.0 / math.sqrt(HEAD_SIZE)
    ff_cols = w_gate.shape[1]
    key_pos, own_pos = positions(pair_block, token_rows)
    query_pos = jnp.tile(own_pos, group_count)
    inputs_f = tokens.astype(jnp.float32)
    qkv_full, out_full = (
        lax.all_gather(query_key_value_weight, "fsdp", axis=0, tiled=True),
        lax.all_gather(w_out, "fsdp", axis=0, tiled=True),
    )
    normed_one_b = rms_norm(inputs_f, gain_attn).astype(jnp.bfloat16)
    projected_rows = jnp.dot(normed_one_b, qkv_full, preferred_element_type=jnp.float32)
    query_raw = projected_rows[:, :query_columns].reshape(token_rows, QUERY_HEADS, HEAD_SIZE)
    unrotated_key = projected_rows[:, query_columns : query_columns + key_value_columns].reshape(
        token_rows, KEY_VALUE_HEADS, HEAD_SIZE
    )
    query_b = (
        apply_rotation(query_raw, own_pos).astype(jnp.bfloat16).reshape(token_rows, query_columns)
    )
    keys_b = (
        apply_rotation(unrotated_key, own_pos)
        .astype(jnp.bfloat16)
        .reshape(token_rows, key_value_columns)
    )
    values_b = projected_rows[:, query_columns + key_value_columns :].astype(jnp.bfloat16)
    every_key, every_value = (
        lax.all_gather(keys_b, "ctx", axis=0, tiled=True),
        lax.all_gather(values_b, "ctx", axis=0, tiled=True),
    )
    query_grp = to_groups(query_b, group_count)
    key_blocks, value_blocks, pos_blocks = split_keys(every_key, every_value, key_pos)

    def forward_step(carry, block_in):
        run_max, run_total, weighted = carry
        key_block, value_block, block_pos = block_in
        causal = block_pos[None, None, :] <= query_pos[None, :, None]
        scores = (
            jnp.einsum("hqd,khd->hqk", query_grp, key_block, preferred_element_type=jnp.float32)
            * score_scale
        )
        scores = jnp.where(causal, scores, -1e30)
        new_max = jnp.maximum(run_max, jnp.max(scores, axis=-1))
        exp_scores = jnp.where(causal, jnp.exp(scores - new_max[..., None]), 0.0)
        fading = jnp.exp(run_max - new_max)
        run_total = run_total * fading + jnp.sum(exp_scores, axis=-1)
        weighted = weighted * fading[..., None] + jnp.einsum(
            "hqk,khd->hqd",
            exp_scores.astype(jnp.bfloat16),
            value_block,
            preferred_element_type=jnp.float32,
        )
        return ((new_max, run_total, weighted), None)

    initial_maximum = jnp.full((KEY_VALUE_HEADS, group_count * token_rows), -1e30, jnp.float32)
    initial_total = jnp.zeros((KEY_VALUE_HEADS, group_count * token_rows), jnp.float32)
    initial_weighted = jnp.zeros(
        (KEY_VALUE_HEADS, group_count * token_rows, HEAD_SIZE), jnp.float32
    )
    final_carry, ignored = lax.scan(
        forward_step,
        (initial_maximum, initial_total, initial_weighted),
        (key_blocks, value_blocks, pos_blocks),
    )
    run_max, run_total, weighted = final_carry
    log_total = run_max + jnp.log(run_total)
    attn_grp = weighted / run_total[..., None]
    attended_b = from_groups(attn_grp.astype(jnp.bfloat16), group_count)
    mid_rows = inputs_f + jnp.dot(attended_b, out_full, preferred_element_type=jnp.float32)
    gate_full, up_full, down_full = (
        lax.all_gather(w_gate, "fsdp", axis=0, tiled=True),
        lax.all_gather(w_up, "fsdp", axis=0, tiled=True),
        lax.all_gather(w_down, "fsdp", axis=0, tiled=True),
    )
    normed_two_b = rms_norm(mid_rows, gain_ffn).astype(jnp.bfloat16)
    gate_val = jnp.dot(normed_two_b, gate_full, preferred_element_type=jnp.float32)
    up_val = jnp.dot(normed_two_b, up_full, preferred_element_type=jnp.float32)
    hidden_b = (jax.nn.silu(gate_val) * up_val).astype(jnp.bfloat16)
    output_f = mid_rows + jnp.dot(hidden_b, down_full, preferred_element_type=jnp.float32)
    result = output_f.astype(jnp.bfloat16)
    normed_one_x, attended_x, normed_two_x, hidden_x = (
        lax.all_to_all(normed_one_b, "fsdp", split_axis=1, concat_axis=0, tiled=True),
        lax.all_to_all(attended_b, "fsdp", split_axis=1, concat_axis=0, tiled=True),
        lax.all_to_all(normed_two_b, "fsdp", split_axis=1, concat_axis=0, tiled=True),
        lax.all_to_all(hidden_b, "fsdp", split_axis=1, concat_axis=0, tiled=True),
    )
    grad_out_f = cotangent.astype(jnp.float32)
    gate_back, up_back, down_back = (
        lax.all_gather(w_gate, "fsdp", axis=0, tiled=True),
        lax.all_gather(w_up, "fsdp", axis=0, tiled=True),
        lax.all_gather(w_down, "fsdp", axis=0, tiled=True),
    )
    grad_hidden = contract_last(cotangent, down_back)
    ignored, ffn_back = jax.vjp(
        lambda gate_in, up_in: jax.nn.silu(gate_in) * up_in, gate_val, up_val
    )
    grad_gate_f, grad_up_f = ffn_back(grad_hidden)
    grad_gate_b = grad_gate_f.astype(jnp.bfloat16)
    grad_up_b = grad_up_f.astype(jnp.bfloat16)
    grad_normed_two = contract_last(grad_gate_b, gate_back) + contract_last(grad_up_b, up_back)
    ignored, norm_two_back = jax.vjp(rms_norm, mid_rows, gain_ffn)
    grad_mid_part, gain_ffn_part = norm_two_back(grad_normed_two)
    grad_mid = grad_out_f + grad_mid_part
    gate_up_b = jnp.concatenate([grad_gate_b, grad_up_b], axis=1)
    qkv_back, out_back = (
        lax.all_gather(query_key_value_weight, "fsdp", axis=0, tiled=True),
        lax.all_gather(w_out, "fsdp", axis=0, tiled=True),
    )
    grad_proj_b = grad_mid.astype(jnp.bfloat16)
    grad_att_b = contract_last(grad_proj_b, out_back).astype(jnp.bfloat16)
    grad_att_grp = to_groups(grad_att_b, group_count)
    delta_rows = jnp.sum(grad_att_grp.astype(jnp.float32) * attn_grp, axis=-1)

    def backward_step(grad_query, block_in):
        key_block, value_block, block_pos = block_in
        causal = block_pos[None, None, :] <= query_pos[None, :, None]
        scores = (
            jnp.einsum("hqd,khd->hqk", query_grp, key_block, preferred_element_type=jnp.float32)
            * score_scale
        )
        probs = jnp.where(causal, jnp.exp(scores - log_total[..., None]), 0.0)
        grad_values = jnp.einsum(
            "hqk,hqd->khd",
            probs.astype(jnp.bfloat16),
            grad_att_grp,
            preferred_element_type=jnp.float32,
        )
        grad_probs = jnp.einsum(
            "hqd,khd->hqk", grad_att_grp, value_block, preferred_element_type=jnp.float32
        )
        grad_scores = (probs * (grad_probs - delta_rows[..., None])).astype(jnp.bfloat16)
        grad_query = grad_query + score_scale * jnp.einsum(
            "hqk,khd->hqd", grad_scores, key_block, preferred_element_type=jnp.float32
        )
        grad_keys = score_scale * jnp.einsum(
            "hqk,hqd->khd", grad_scores, query_grp, preferred_element_type=jnp.float32
        )
        return (grad_query, (grad_keys, grad_values))

    grad_query_grp, key_grads = lax.scan(
        backward_step,
        jnp.zeros((KEY_VALUE_HEADS, group_count * token_rows, HEAD_SIZE), jnp.float32),
        (key_blocks, value_blocks, pos_blocks),
    )
    total_keys = key_pos.shape[0]
    grad_keys_all = key_grads[0].reshape(total_keys, key_value_columns)
    grad_values_all = key_grads[1].reshape(total_keys, key_value_columns)
    key_sums, summed_values = (
        lax.psum_scatter(
            grad_keys_all.astype(jnp.bfloat16), "ctx", scatter_dimension=0, tiled=True
        ).astype(jnp.float32),
        lax.psum_scatter(
            grad_values_all.astype(jnp.bfloat16), "ctx", scatter_dimension=0, tiled=True
        ).astype(jnp.float32),
    )
    grad_query_rows = from_groups(grad_query_grp, group_count).reshape(
        token_rows, QUERY_HEADS, HEAD_SIZE
    )
    ignored, query_rope_back = jax.vjp(lambda vectors: apply_rotation(vectors, own_pos), query_raw)
    ignored, key_rotation_backward = jax.vjp(
        lambda vectors: apply_rotation(vectors, own_pos), unrotated_key
    )
    grad_query_raw = query_rope_back(grad_query_rows)[0]
    unrotated_key_gradient = key_rotation_backward(
        key_sums.reshape(token_rows, KEY_VALUE_HEADS, HEAD_SIZE)
    )[0]
    grad_projected_b = jnp.concatenate(
        [
            grad_query_raw.reshape(token_rows, query_columns),
            unrotated_key_gradient.reshape(token_rows, key_value_columns),
            summed_values,
        ],
        axis=1,
    ).astype(jnp.bfloat16)
    grad_normed_one = contract_last(grad_projected_b, qkv_back)
    ignored, norm_one_back = jax.vjp(rms_norm, inputs_f, gain_attn)
    grad_in_part, gain_attn_part = norm_one_back(grad_normed_one)
    grad_input = grad_mid + grad_in_part
    cot_group, gate_up_group, projected_group, proj_group = (
        lax.all_gather(cotangent, "fsdp", axis=0, tiled=True),
        lax.all_gather(gate_up_b, "fsdp", axis=0, tiled=True),
        lax.all_gather(grad_projected_b, "fsdp", axis=0, tiled=True),
        lax.all_gather(grad_proj_b, "fsdp", axis=0, tiled=True),
    )
    qkv_part = contract_first(normed_one_x, projected_group)
    out_part = contract_first(attended_x, proj_group)
    gate_up_part = contract_first(normed_two_x, gate_up_group)
    gate_part = gate_up_part[:, :ff_cols]
    up_part = gate_up_part[:, ff_cols:]
    down_part = contract_first(hidden_x, cot_group)
    grad_qkv, grad_out, grad_down = (
        lax.psum_scatter(
            qkv_part.astype(jnp.bfloat16), "ctx", scatter_dimension=0, tiled=True
        ).astype(jnp.float32),
        lax.psum_scatter(
            out_part.astype(jnp.bfloat16), "ctx", scatter_dimension=0, tiled=True
        ).astype(jnp.float32),
        lax.psum_scatter(
            down_part.astype(jnp.bfloat16), "ctx", scatter_dimension=0, tiled=True
        ).astype(jnp.float32),
    )
    grad_gate, grad_up = (
        lax.psum_scatter(
            gate_part.astype(jnp.bfloat16), "ctx", scatter_dimension=0, tiled=True
        ).astype(jnp.float32),
        lax.psum_scatter(
            up_part.astype(jnp.bfloat16), "ctx", scatter_dimension=0, tiled=True
        ).astype(jnp.float32),
    )
    grad_gain_attn, grad_gain_ffn = (
        lax.psum_scatter(gain_attn_part, ("ctx", "fsdp"), scatter_dimension=0, tiled=True),
        lax.psum_scatter(gain_ffn_part, ("ctx", "fsdp"), scatter_dimension=0, tiled=True),
    )
    return (
        result,
        grad_input,
        grad_gain_attn,
        grad_gain_ffn,
        grad_qkv,
        grad_out,
        grad_gate,
        grad_up,
        grad_down,
    )


MESH = pl.DeviceIdType.MESH
ACROSS_X, ACROSS_Y, ACROSS_CORE = 2, 4, 1
BLOCK = 256


class Links:
    def __init__(self, sems, ctx, fsdp):
        self.send_sem, self.recv_sem, self.local_sem = sems
        self.ctx, self.fsdp = ctx, fsdp
        self.remote = self.locals = 0

    def to(self, src, dst, ctx, fsdp):
        index, self.remote = self.remote, self.remote + 1
        return pltpu.make_async_remote_copy(
            src_ref=src,
            dst_ref=dst,
            send_sem=self.send_sem.at[index],
            recv_sem=self.recv_sem.at[index],
            device_id=(ctx, fsdp),
            device_id_type=MESH,
        )

    def flip(self, src, dst, ctx_flip, fsdp_flip):
        return self.to(
            src, dst, lax.bitwise_xor(self.ctx, ctx_flip), lax.bitwise_xor(self.fsdp, fsdp_flip)
        )

    def plane(self, src, dst, flip):
        return self.flip(src, dst, flip, 0)

    def column(self, src, dst, flip):
        return self.flip(src, dst, 0, flip)

    def here(self, src, dst):
        index, self.locals = self.locals, self.locals + 1
        return pltpu.make_async_copy(src, dst, self.local_sem.at[index])


PLANE_FLIPS = [(1, 0), (2, 0), (4, 0)]
COLUMN_FLIPS = [(0, 1), (0, 2), (0, 3)]


def greet(ctx, fsdp, flips):
    barrier = pltpu.get_barrier_semaphore()
    for a, b in flips:
        pl.semaphore_signal(
            barrier,
            inc=1,
            device_id=(lax.bitwise_xor(ctx, a), lax.bitwise_xor(fsdp, b)),
            device_id_type=MESH,
        )
    pl.semaphore_wait(barrier, len(flips))


def start_all(copies):
    for copy in copies:
        copy.start()


class LineGather:
    def __init__(self, links, own, group):
        self.links, self.group = links, group
        self.home = links.here(own, group.at[0])
        self.near = links.column(own, group.at[2], 1)
        self.far = links.column(own, group.at[1], 2)
        self.relay = links.column(group.at[1], group.at[3], 1)

    def begin(self):
        start_all([self.far, self.near, self.home])

    def forward(self):
        self.far.wait_recv()
        self.relay.start()

    def finish(self):
        self.near.wait_recv()
        self.relay.wait_recv()
        for copy in (self.near, self.far, self.relay):
            copy.wait_send()
        self.home.wait()


class PlaneGather:
    def __init__(self, links, blocks, halves):
        self.links, self.blocks, self.halves = links, blocks, halves
        self.ctx = links.ctx
        self.sent = []
        self.cores = []

    def _go(self, copies):
        for copy in copies:
            copy.start()
        self.sent += copies
        return copies

    def _core(self, index):
        refs = self.blocks(index)
        self.cores += self._go([self.links.plane(r, r, ACROSS_CORE) for r in refs])

    def begin(self, sources=None):
        refs = self.blocks(self.ctx)
        pairs = list(zip(sources or refs, refs))
        self.from_x = self._go([self.links.plane(s, r, ACROSS_X) for s, r in pairs])
        self.from_y = self._go([self.links.plane(s, r, ACROSS_Y) for s, r in pairs])
        self.cores += self._go([self.links.plane(s, r, ACROSS_CORE) for s, r in pairs])

    def forward(self):
        index = lax.bitwise_xor(self.ctx, ACROSS_X)
        for copy in self.from_x:
            copy.wait_recv()
        refs = self.halves(index, 0)
        self.corner = self._go([self.links.plane(r, r, ACROSS_Y) for r in refs])
        self._core(index)
        index = lax.bitwise_xor(self.ctx, ACROSS_Y)
        for copy in self.from_y:
            copy.wait_recv()
        refs = self.halves(index, 1)
        self.corner += self._go([self.links.plane(r, r, ACROSS_X) for r in refs])
        self._core(index)

    def finish(self):
        for copy in self.corner:
            copy.wait_recv()
        self._core(lax.bitwise_xor(self.ctx, ACROSS_X | ACROSS_Y))
        for copy in self.cores:
            copy.wait_recv()

    def drain(self):
        for copy in self.sent:
            copy.wait_send()


class PlaneScatter:
    def __init__(self, links, part, core_rx, half_rx, side_rx):
        self.links, self.part = links, part
        self.core_rx, self.half_rx, self.side_rx = core_rx, half_rx, side_rx
        self.chip, self.core = links.ctx // 2, lax.rem(links.ctx, 2)
        self.sent = []
        self.from_core = {}

    def order(self):
        return [(flip, lax.bitwise_xor(self.chip, flip)) for flip in (3, 1, 2, 0)]

    def _go(self, copy):
        copy.start()
        self.sent.append(copy)
        return copy

    def give(self, flip, chip):
        self.from_core[flip] = self._go(
            self.links.plane(
                self.part.at[2 * chip + 1 - self.core], self.core_rx.at[chip], ACROSS_CORE
            )
        )

    def _summed(self, flip):
        chip = lax.bitwise_xor(self.chip, flip)
        self.from_core[flip].wait_recv()
        mine = self.part.at[2 * chip + self.core]
        total = mine[...].astype(jnp.float32) + self.core_rx[chip].astype(jnp.float32)
        return mine, total

    def begin(self):
        half = self.half = self.half_rx.shape[1]
        mine, total = self._summed(3)
        mine[...] = total.astype(jnp.bfloat16)
        self.corner = [
            self._go(self.links.plane(mine.at[pl.ds(0, half)], self.half_rx.at[0], ACROSS_Y)),
            self._go(
                self.links.plane(mine.at[pl.ds(half, half)], self.half_rx.at[1], ACROSS_X)
            ),
        ]

    def middle(self):
        self.sides = []
        for flip, across, slot in ((1, ACROSS_X, 0), (2, ACROSS_Y, 1)):
            mine, total = self._summed(flip)
            mine[...] = total.astype(jnp.bfloat16)
            self.corner[slot].wait_recv()
            rows = pl.ds(slot * self.half, self.half)
            mine[rows] = (
                total[slot * self.half : (slot + 1) * self.half]
                + self.half_rx[slot].astype(jnp.float32)
            ).astype(jnp.bfloat16)
            self.sides.append(self._go(self.links.plane(mine, self.side_rx.at[slot], across)))

    def finish(self):
        mine, total = self._summed(0)
        for slot, copy in enumerate(self.sides):
            copy.wait_recv()
            total = total + self.side_rx[slot].astype(jnp.float32)
        return total

    def drain(self):
        for copy in self.sent:
            copy.wait_send()


def swap_bits(fsdp):
    return 2 * lax.rem(fsdp, 2) + fsdp // 2


def place_positions(pair_ref, pos_col, pos_row, rows):
    half, n_ctx = rows // 2, pos_col.shape[0] // rows
    down = lax.broadcasted_iota(jnp.int32, (rows, 1), 0)
    along = lax.broadcasted_iota(jnp.int32, (1, rows), 1)
    for j in range(n_ctx):
        first = pair_ref[j] * half
        second = (2 * n_ctx - 1 - pair_ref[j]) * half - half
        pos_col[pl.ds(j * rows, rows)] = down + jnp.where(down < half, first, second)
        pos_row[:, pl.ds(j * rows, rows)] = along + jnp.where(along < half, first, second)


def turn(vectors, cos_rows, sin_rows, sign):
    return vectors * cos_rows + sign * pltpu.roll(vectors, HEAD_SIZE // 2, 1) * sin_rows


def attention_kernel(
    tokens_ref,
    cot_ref,
    gain_one_ref,
    gain_two_ref,
    qkv_w_ref,
    out_w_ref,
    gate_ref,
    up_ref,
    pair_ref,
    mid_ref,
    normed_two_group,
    cot_near,
    cot_far,
    gate_w,
    up_w,
    qkv_out,
    attended_out,
    normed_one_out,
    w_head_out,
    out_head_out,
    cos_out,
    sin_out,
    normed,
    w_head,
    out_head,
    out_relay,
    qkv,
    attended,
    part,
    core_rx,
    half_rx,
    side_rx,
    normed_two,
    cos_ref,
    sin_ref,
    pos_col_ref,
    pos_row_ref,
    send_sem,
    recv_sem,
    local_sem,
):
    f32, bf16 = jnp.float32, jnp.bfloat16
    ctx, fsdp = lax.axis_index("ctx"), lax.axis_index("fsdp")
    links = Links((send_sem, recv_sem, local_sem), ctx, fsdp)
    rows, width = tokens_ref.shape
    depth = qkv_w_ref.shape[0]
    head_columns = out_head.shape[0]
    n_ctx, n_fsdp = normed.shape[0], width // depth
    seq_rows = n_ctx * rows
    hidden = gate_w.shape[2]
    strip = hidden // n_ctx
    depth_blocks = gate_ref.shape[0]
    query_columns = QUERY_HEADS * HEAD_SIZE
    key_columns = KEY_VALUE_HEADS * HEAD_SIZE
    score_scale = 1.0 / math.sqrt(HEAD_SIZE)
    finals = []

    greet(ctx, fsdp, PLANE_FLIPS + COLUMN_FLIPS + [(6, 0)])

    out_block = out_w_ref.at[
        pl.ds(pl.multiple_of(lax.rem(ctx, 2) * head_columns, head_columns), head_columns)
    ]
    out_target = swap_bits(lax.bitwise_xor(ctx // 2, fsdp))
    out_away = out_target != fsdp
    out_copy = links.to(out_block, out_relay, ctx, out_target)
    out_home = links.here(out_block, out_relay)
    out_flip = 2 * swap_bits(fsdp)
    out_moves = fsdp != 0
    out_last = links.to(out_relay, out_head, lax.bitwise_xor(ctx, out_flip), fsdp)
    out_stays = links.here(out_relay, out_head)

    @pl.when(out_away)
    def _():
        out_copy.start()

    @pl.when(jnp.logical_not(out_away))
    def _():
        out_home.start()

    def rows_of(plane):
        return pl.ds(pl.multiple_of(plane * depth, depth), depth)

    head_parts, places = [], []
    for start, size, place in (
        (ctx * head_columns, head_columns, 0),
        (query_columns + ctx * HEAD_SIZE, HEAD_SIZE, head_columns),
        (query_columns + key_columns + ctx * HEAD_SIZE, HEAD_SIZE, head_columns + HEAD_SIZE),
    ):
        places.append(pl.ds(place, size))
        head_parts.append(
            (
                qkv_w_ref.at[:, pl.ds(pl.multiple_of(start, HEAD_SIZE), size)],
                w_head.at[rows_of(fsdp), pl.ds(place, size)],
            )
        )
    head_far = [links.column(src, dst, 2) for src, dst in head_parts]
    head_near = [links.column(src, dst, 1) for src, dst in head_parts]
    own_head = [links.here(src, dst) for src, dst in head_parts]
    start_all(head_far + head_near + own_head)

    def place_of(j):
        return pl.ds(pl.multiple_of(j * strip, strip), strip)

    def strips(target):
        cols = pl.ds(pl.multiple_of(target * hidden + ctx * strip, strip), strip)
        blocks = pl.ds(fsdp * depth_blocks, depth_blocks)
        for source, dest in ((gate_ref, gate_w), (up_ref, up_w)):
            yield source.at[:, :, cols], dest.at[blocks, :, place_of(ctx)]

    strip_copies = [[links.here(src, dst) for src, dst in strips(fsdp)]]
    for flip in (1, 2, 3):
        strip_copies.append(
            [links.column(s, d, flip) for s, d in strips(lax.bitwise_xor(fsdp, flip))]
        )
    start_all(strip_copies[0])

    def strip_gather(flip):
        first = lax.bitwise_xor(fsdp, flip) * depth_blocks
        blocks = pl.ds(first, depth_blocks)
        return PlaneGather(
            links,
            lambda j: [w.at[blocks, :, place_of(j)] for w in (gate_w, up_w)],
            lambda j, which: [w.at[first + which, :, place_of(j)] for w in (gate_w, up_w)],
        )

    weights = [strip_gather(flip) for flip in range(n_fsdp)]

    inputs = tokens_ref[...].astype(f32)
    scale = lax.rsqrt(jnp.mean(inputs * inputs, axis=-1, keepdims=True) + norm_eps)
    normed[ctx] = (inputs * scale * gain_one_ref[...]).astype(bf16)
    half = rows // 2
    gather = PlaneGather(
        links,
        lambda j: [normed.at[j]],
        lambda j, which: [normed.at[j, pl.ds(which * half, half)]],
    )
    gather.begin()

    place_positions(pair_ref, pos_col_ref, pos_row_ref, rows)
    lane = lax.broadcasted_iota(jnp.int32, (1, HEAD_SIZE), 1)
    lane_half = lax.rem(lane, HEAD_SIZE // 2).astype(f32)
    frequency = jnp.exp(lane_half * (-2.0 * math.log(rope_base) / HEAD_SIZE))
    side = jnp.where(lane < HEAD_SIZE // 2, -1.0, 1.0)

    def tables(step, carry):
        at = pl.ds(pl.multiple_of(step * rows, rows), rows)
        angles = pos_col_ref[at].astype(f32) * frequency
        cos_ref[at] = jnp.cos(angles)
        sin_ref[at] = side * jnp.sin(angles)
        return carry

    lax.fori_loop(0, n_ctx, tables, 0)
    for src, dst in ((cos_ref, cos_out), (sin_ref, sin_out)):
        finals.append(links.here(src, dst))
        finals[-1].start()
    gather.forward()
    weights[0].begin([source for source, dest in strips(fsdp)])
    gather.finish()

    @pl.when(out_away)
    def _():
        out_copy.wait_recv()

    @pl.when(jnp.logical_not(out_away))
    def _():
        out_home.wait()

    @pl.when(out_moves)
    def _():
        out_last.start()

    @pl.when(jnp.logical_not(out_moves))
    def _():
        out_stays.start()

    weights[0].forward()
    cot_copies = [links.column(cot_ref, cot_far, 2), links.column(cot_ref, cot_near, 1)]
    head_relay = []
    far_rows = rows_of(lax.bitwise_xor(fsdp, 2))
    for copy, place in zip(head_far, places):
        copy.wait_recv()
        block = w_head.at[far_rows, place]
        head_relay.append(links.column(block, block, 1))
        head_relay[-1].start()
    start_all(cot_copies[:1])
    weights[0].finish()
    finals.append(links.here(normed, normed_one_out))
    finals[-1].start()
    for copy in own_head:
        copy.wait()
    for copy in head_near + head_relay:
        copy.wait_recv()
    start_all(strip_copies[1] + strip_copies[2] + strip_copies[3])

    block_rows = 2 * rows

    def project(step, carry):
        at = pl.multiple_of(step * block_rows, block_rows)
        tile = normed[pl.ds(step * 2, 2)].reshape(block_rows, width)
        out = jnp.dot(tile, w_head[...], preferred_element_type=f32)
        cos_rows, sin_rows = cos_ref[pl.ds(at, block_rows)], sin_ref[pl.ds(at, block_rows)]
        for column in range(0, head_columns + HEAD_SIZE, HEAD_SIZE):
            turned = turn(out[:, column : column + HEAD_SIZE], cos_rows, sin_rows, 1.0)
            qkv[pl.ds(at, block_rows), pl.ds(column, HEAD_SIZE)] = turned.astype(bf16)
        column = head_columns + HEAD_SIZE
        qkv[pl.ds(at, block_rows), pl.ds(column, HEAD_SIZE)] = out[:, column:].astype(bf16)
        return carry

    lax.fori_loop(0, seq_rows // block_rows, project, 0)
    def attend(step, carry):
        at = pl.multiple_of(step * block_rows, block_rows)
        keys = qkv[:, pl.ds(head_columns, HEAD_SIZE)]
        values = qkv[:, pl.ds(head_columns + HEAD_SIZE, HEAD_SIZE)]
        causal = pos_row_ref[...] <= pos_col_ref[pl.ds(at, block_rows)]
        for column in range(0, head_columns, HEAD_SIZE):
            query = qkv[pl.ds(at, block_rows), pl.ds(column, HEAD_SIZE)]
            scores = contract_last(query, keys) * score_scale
            scores = jnp.where(causal, scores, -1e30)
            shifted = jnp.exp(scores - jnp.max(scores, axis=-1, keepdims=True))
            probs = shifted * (1.0 / jnp.sum(shifted, axis=-1, keepdims=True))
            mixed = jnp.dot(probs.astype(bf16), values, preferred_element_type=f32)
            attended[pl.ds(at, block_rows), pl.ds(column, HEAD_SIZE)] = mixed.astype(bf16)
        return carry

    lax.fori_loop(0, seq_rows // block_rows, attend, 0)

    @pl.when(out_moves)
    def _():
        out_last.wait_recv()

    @pl.when(jnp.logical_not(out_moves))
    def _():
        out_stays.wait()

    for src, dst in (        (qkv, qkv_out),
        (attended, attended_out),
        (w_head, w_head_out),
        (out_head, out_head_out),
    ):
        finals.append(links.here(src, dst))
        finals[-1].start()

    scatter = PlaneScatter(links, part, core_rx, half_rx, side_rx)
    for flip, chip in scatter.order():
        at = pl.multiple_of(chip * block_rows, block_rows)
        out = jnp.dot(
            attended[pl.ds(at, block_rows)], out_head[...], preferred_element_type=f32
        )
        part[pl.ds(chip * 2, 2)] = out.astype(bf16).reshape(2, rows, width)
        scatter.give(flip, chip)

    def arrived(flip):
        for copy in strip_copies[flip]:
            copy.wait_recv()
        weights[flip].begin()

    scatter.begin()
    scatter.middle()
    arrived(1)
    mid = tokens_ref[...].astype(f32) + scatter.finish()
    mid_ref[...] = mid
    mid_scale = lax.rsqrt(jnp.mean(mid * mid, axis=-1, keepdims=True) + norm_eps)
    normed_two[...] = (mid * mid_scale * gain_two_ref[...]).astype(bf16)

    group = LineGather(links, normed_two, normed_two_group)
    group.begin()
    arrived(2)
    weights[1].forward()
    group.forward()
    start_all(cot_copies[1:])
    arrived(3)
    weights[2].forward()
    weights[1].finish()
    weights[3].forward()
    weights[2].finish()
    weights[3].finish()
    group.finish()
    for copy in cot_copies:
        copy.wait()
    for copy in strip_copies[0]:
        copy.wait()

    for copies in [head_far, head_near, head_relay] + strip_copies[1:]:
        for copy in copies:
            copy.wait_send()

    @pl.when(out_away)
    def _():
        out_copy.wait_send()

    @pl.when(out_moves)
    def _():
        out_last.wait_send()

    gather.drain()
    scatter.drain()
    for item in weights:
        item.drain()
    for copy in finals:
        copy.wait()


def attention_forward(
    tokens, cotangent, gain_attn, gain_ffn, qkv_w, w_out, w_gate, w_up, pair_block
):
    f32, bf16 = jnp.float32, jnp.bfloat16
    n_ctx, n_fsdp = lax.axis_size("ctx"), lax.axis_size("fsdp")
    rows, width = tokens.shape
    depth = qkv_w.shape[0]
    hidden = w_gate.shape[1] // n_fsdp
    seq_rows = n_ctx * rows
    head_columns = QUERY_HEADS // KEY_VALUE_HEADS * HEAD_SIZE
    all_columns = head_columns + 2 * HEAD_SIZE
    vmem, hbm = pl.BlockSpec(memory_space=pltpu.VMEM), pl.BlockSpec(memory_space=pl.ANY)
    shape = jax.ShapeDtypeStruct
    return pl.pallas_call(
        attention_kernel,
        name="attention_forward",
        out_shape=[
            shape((rows, width), f32),
            shape((n_fsdp, rows, width), bf16),
            shape((rows, width), bf16),
            shape((rows, width), bf16),
            shape((width // BLOCK, BLOCK, hidden), bf16),
            shape((width // BLOCK, BLOCK, hidden), bf16),
            shape((seq_rows, all_columns), bf16),
            shape((seq_rows, head_columns), bf16),
            shape((n_ctx, rows, width), bf16),
            shape((width, all_columns), bf16),
            shape((head_columns, width), bf16),
            shape((seq_rows, HEAD_SIZE), f32),
            shape((seq_rows, HEAD_SIZE), f32),
        ],
        in_specs=[vmem] * 4 + [hbm] * 4 + [pl.BlockSpec(memory_space=pltpu.SMEM)],
        out_specs=[vmem] + [hbm] * 12,
        scratch_shapes=[
            pltpu.VMEM((n_ctx, rows, width), bf16),
            pltpu.VMEM((width, all_columns), bf16),
            pltpu.VMEM((head_columns, width), bf16),
            pltpu.VMEM((head_columns, width), bf16),
            pltpu.VMEM((seq_rows, all_columns), bf16),
            pltpu.VMEM((seq_rows, head_columns), bf16),
            pltpu.VMEM((n_ctx, rows, width), bf16),
            pltpu.VMEM((n_ctx // 2, rows, width), bf16),
            pltpu.VMEM((2, rows // 2, width), bf16),
            pltpu.VMEM((2, rows, width), bf16),
            pltpu.VMEM((rows, width), bf16),
            pltpu.VMEM((seq_rows, HEAD_SIZE), f32),
            pltpu.VMEM((seq_rows, HEAD_SIZE), f32),
            pltpu.VMEM((seq_rows, 1), jnp.int32),
            pltpu.VMEM((1, seq_rows), jnp.int32),
            pltpu.SemaphoreType.DMA((112,)),
            pltpu.SemaphoreType.DMA((112,)),
            pltpu.SemaphoreType.DMA((16,)),
        ],
        compiler_params=pltpu.CompilerParams(
            collective_id=1, has_side_effects=True, vmem_limit_bytes=58 * 2**20
        ),
    )(
        tokens,
        cotangent,
        gain_attn[None],
        gain_ffn[None],
        qkv_w,
        w_out,
        w_gate.reshape(depth // BLOCK, BLOCK, -1),
        w_up.reshape(depth // BLOCK, BLOCK, -1),
        pair_block,
    )


class ChipScatter:
    def __init__(self, links, parts, halves, sides):
        self.links, self.parts, self.halves, self.sides = links, parts, halves, sides
        self.sent = []

    def _go(self, copy):
        copy.start()
        self.sent.append(copy)
        return copy

    def begin(self, source=None):
        corner = self.parts[3] if source is None else source
        half = corner.shape[0] // 2
        self.half = half
        self.corner = [
            self._go(self.links.plane(corner.at[pl.ds(0, half)], self.halves[0], ACROSS_Y)),
            self._go(self.links.plane(corner.at[pl.ds(half, half)], self.halves[1], ACROSS_X)),
        ]

    def middle(self):
        self.side = []
        for slot, (flip, across) in enumerate(((1, ACROSS_X), (2, ACROSS_Y))):
            mine = self.parts[flip]
            self.corner[slot].wait_recv()
            rows = mine.at[pl.ds(slot * self.half, self.half)]
            rows[...] = (
                rows[...].astype(jnp.float32) + self.halves[slot][...].astype(jnp.float32)
            ).astype(jnp.bfloat16)
            self.side.append(self._go(self.links.plane(mine, self.sides[slot], across)))

    def finish(self):
        mine = self.parts[0]
        for copy in self.side:
            copy.wait_recv()
        mine[...] = (
            mine[...].astype(jnp.float32)
            + self.sides[0][...].astype(jnp.float32)
            + self.sides[1][...].astype(jnp.float32)
        ).astype(jnp.bfloat16)
        return mine

    def drain(self):
        for copy in self.sent:
            copy.wait_send()


def feed_forward_kernel(
    mid_ref,
    cot_ref,
    gain_ref,
    normed_ref,
    cot_near_ref,
    cot_far_ref,
    gate_hbm,
    up_hbm,
    down_hbm,
    result_ref,
    grad_mid_ref,
    grad_proj_ref,
    down_sum,
    gate_sum,
    up_part,
    gate_v,
    up_v,
    down_v,
    cots,
    hidden,
    grad_gate,
    grad_up,
    other_normed,
    other_cots,
    other_hidden,
    other_gate,
    other_up,
    stage,
    landed,
    down_parts,
    down_halves,
    send_sem,
    recv_sem,
    local_sem,
    load_sem,
    down_free,
    gate_free,
):
    f32, bf16 = jnp.float32, jnp.bfloat16
    ctx, fsdp = lax.axis_index("ctx"), lax.axis_index("fsdp")
    links = Links((send_sem, recv_sem, local_sem), ctx, fsdp)
    core = lax.rem(ctx, 2)
    rows, width = mid_ref.shape
    blocks = gate_v.shape[0]
    hidden_units = blocks * BLOCK
    half_units = hidden_units // 2
    n_fsdp = normed_ref.shape[0]
    group_rows = n_fsdp * rows

    def loads(j):
        cols = pl.ds(pl.multiple_of(j * BLOCK, BLOCK), BLOCK)
        return (
            pltpu.make_async_copy(
                gate_hbm.at[:, :, cols], gate_v.at[:, :, cols], load_sem.at[0, j]
            ),
            pltpu.make_async_copy(up_hbm.at[:, :, cols], up_v.at[:, :, cols], load_sem.at[1, j]),
            pltpu.make_async_copy(down_hbm.at[j], down_v.at[j], load_sem.at[2, j]),
        )

    for j in range(blocks):
        for copy in loads(j):
            copy.start()

    greet(ctx, fsdp, PLANE_FLIPS + COLUMN_FLIPS[:2])

    cot_relay = links.column(cot_far_ref, cots.at[3], 1)
    cot_relay.start()
    cots[0] = cot_ref[...]
    cots[1] = cot_far_ref[...]
    cots[2] = cot_near_ref[...]
    mid_load = links.here(mid_ref, grad_mid_ref)
    mid_load.start()

    swaps = [links.plane(normed_ref, other_normed, ACROSS_CORE)]
    cot_swaps = [links.plane(cots.at[s], other_cots.at[s], ACROSS_CORE) for s in range(n_fsdp)]
    start_all(swaps + cot_swaps[:3])

    half_slots, half_rows = n_fsdp // 2, group_rows // 2

    def activate(j, carry):
        for copy in loads(j):
            copy.wait()
        cols = pl.ds(pl.multiple_of(j * BLOCK, BLOCK), BLOCK)
        for first in (0, half_slots):
            at = pl.ds(first * rows, half_rows)
            normed = normed_ref[pl.ds(first, half_slots)].reshape(half_rows, width)
            gate = jnp.dot(
                normed, gate_v[:, :, cols].reshape(width, BLOCK), preferred_element_type=f32
            )
            up = jnp.dot(
                normed, up_v[:, :, cols].reshape(width, BLOCK), preferred_element_type=f32
            )
            sig = jax.nn.sigmoid(gate)
            silu = gate * sig
            hidden[at, cols] = (silu * up).astype(bf16)
            grad_gate[at, cols] = (up * (sig * (1.0 + gate * (1.0 - sig)))).astype(bf16)
            grad_up[at, cols] = silu.astype(bf16)
        return carry

    lax.fori_loop(0, blocks, activate, 0)

    hidden_acts = []
    for pair in range(blocks // 2):
        cols = pl.ds(pl.multiple_of((2 * pair + 1 - core) * BLOCK, BLOCK), BLOCK)
        hidden_acts.append(
            links.plane(
                hidden.at[:, cols], other_hidden.at[:, pl.ds(pair * BLOCK, BLOCK)], ACROSS_CORE
            )
        )
    start_all(hidden_acts)
    piece = 2 * BLOCK
    pieces = width // piece

    def spot(n):
        return pl.ds(n * piece, piece)

    def put(which, first, n, value):
        stage[which, pl.ds(first, half_slots), :, spot(n)] = value.astype(bf16).reshape(
            half_slots, rows, piece
        )

    def down_out(first, n):
        value = jnp.dot(
            hidden[pl.ds(first * rows, half_rows)],
            down_v[:, :, spot(n)].reshape(hidden_units, piece),
            preferred_element_type=f32,
        )
        put(0, first, n, value)

    def back_out(first, n):
        at, some = pl.ds(first * rows, half_rows), pl.ds(n * 2, 2)
        value = contract_last(grad_gate[at], gate_v[some].reshape(piece, hidden_units))
        value = value + contract_last(grad_up[at], up_v[some].reshape(piece, hidden_units))
        put(1, first, n, value)

    near, far = {}, []

    def send_near(which, n):
        near[which, n] = [
            links.column(stage.at[which, 3, :, spot(n)], landed.at[which, 1, :, spot(n)], 1),
            links.column(stage.at[which, 2, :, spot(n)], landed.at[which, 0, :, spot(n)], 1),
        ]
        start_all(near[which, n])

    def relay(which, n):
        near[which, n][0].wait_recv()
        stage[which, 1, :, spot(n)] = (
            stage[which, 1, :, spot(n)].astype(f32) + landed[which, 1, :, spot(n)].astype(f32)
        ).astype(bf16)
        copy = links.column(stage.at[which, 1, :, spot(n)], landed.at[which, 2, :, spot(n)], 2)
        copy.start()
        far.append(copy)

    for n in range(pieces):
        down_out(half_slots, n)
        send_near(0, n)
        down_out(0, n)

    def activation_grads(first):
        at = pl.ds(first * rows, half_rows)

        def step(j, carry):
            cols = pl.ds(pl.multiple_of(j * BLOCK, BLOCK), BLOCK)
            cot_rows = cots[pl.ds(first, half_slots)].reshape(half_rows, width)
            grad_hidden = contract_last(cot_rows, down_v[j])
            grad_gate[at, cols] = (grad_gate[at, cols].astype(f32) * grad_hidden).astype(bf16)
            grad_up[at, cols] = (grad_up[at, cols].astype(f32) * grad_hidden).astype(bf16)
            return carry

        lax.fori_loop(0, blocks, step, 0)

    for copy in [cot_relay]:
        copy.wait_recv()
    start_all(cot_swaps[3:])
    def flat(ref, cols):
        return ref[:, :, cols].reshape(group_rows, -1)

    for copy in cot_swaps + hidden_acts:
        copy.wait_recv()

    def down_block(pair, place):
        own = pl.ds(pl.multiple_of((2 * pair + core) * BLOCK, BLOCK), BLOCK)
        other = pl.ds(pl.multiple_of(pair * BLOCK, BLOCK), BLOCK)
        left, right = hidden[:, own].T, other_hidden[:, other].T
        for cols in (pl.ds(0, width // 2), pl.ds(width // 2, width // 2)):
            total = jnp.dot(left, flat(cots, cols), preferred_element_type=f32)
            total = total + jnp.dot(right, flat(other_cots, cols), preferred_element_type=f32)
            place[:, cols] = total.astype(bf16)

    def halves_of(ref):
        return [ref.at[pl.ds(0, BLOCK // 2)], ref.at[pl.ds(BLOCK // 2, BLOCK // 2)]]

    chip = ctx // 2
    down_scatter = ChipScatter(
        links,
        [down_v.at[2]] + [down_parts.at[flip - 1] for flip in (1, 2, 3)],
        halves_of(down_halves),
        [down_v.at[0], down_v.at[1]],
    )
    down_block(lax.bitwise_xor(chip, 3), down_parts.at[2])
    down_scatter.begin()

    def down_side(flip, carry):
        down_block(lax.bitwise_xor(chip, flip), down_parts.at[flip - 1])
        return carry

    lax.fori_loop(1, 3, down_side, 0)
    activation_grads(0)
    activation_grads(half_slots)
    down_block(chip, down_v.at[2])
    theirs = pl.ds(pl.multiple_of((1 - core) * half_units, half_units), half_units)
    acts = [
        links.plane(grad_gate.at[:, theirs], other_gate, ACROSS_CORE),
        links.plane(grad_up.at[:, theirs], other_up, ACROSS_CORE),
    ]
    start_all(acts)

    def free(sem):
        for flip in (ACROSS_X, ACROSS_Y):
            pl.semaphore_signal(
                sem,
                inc=1,
                device_id=(lax.bitwise_xor(ctx, flip), fsdp),
                device_id_type=MESH,
            )

    free(down_free)
    pl.semaphore_wait(down_free, 2)
    down_scatter.middle()

    for n in range(pieces):
        back_out(half_slots, n)
        send_near(1, n)
    for n in range(pieces):
        back_out(0, n)
    free(gate_free)
    relay(0, 0)
    relay(0, 1)

    mine = pl.ds(pl.multiple_of(core * half_units, half_units), half_units)

    def weight_block(b, carry):
        cols = pl.ds(pl.multiple_of(b * BLOCK, BLOCK), BLOCK)
        left, right = flat(normed_ref, cols).T, flat(other_normed, cols).T
        plane, first = b // 2, 2 * lax.rem(b, 2)
        at_row = pl.ds(pl.multiple_of((plane // 2) * (BLOCK // 2), BLOCK // 2), BLOCK // 2)
        at_col = pl.ds(pl.multiple_of(lax.rem(plane, 2) * (width // 2), width // 2), width // 2)
        for own_grad, other_grad, place in (
            (grad_gate, other_gate, gate_v),
            (grad_up, other_up, up_v),
        ):
            total = jnp.dot(left, own_grad[:, mine], preferred_element_type=f32)
            total = total + jnp.dot(right, other_grad[...], preferred_element_type=f32)
            low = total.astype(bf16)
            place[first, at_row, at_col] = low[: BLOCK // 2]
            place[first + 1, at_row, at_col] = low[BLOCK // 2 :]
        return carry

    for copy in swaps + acts:
        copy.wait_recv()
    lax.fori_loop(0, blocks // 2, weight_block, 0)
    relay(0, 2)
    lax.fori_loop(blocks // 2, blocks, weight_block, 0)
    pl.semaphore_wait(gate_free, 2)
    gate_scatter = ChipScatter(
        links,
        [gate_v.at[lax.bitwise_xor(chip, flip)] for flip in range(4)],
        halves_of(gate_v.at[4]),
        [gate_v.at[5], gate_v.at[6]],
    )
    gate_scatter.begin()
    up_copy = links.here(up_v.at[pl.ds(0, 4)], up_part)
    up_copy.start()
    relay(0, 3)
    relay(1, 0)
    relay(1, 1)
    relay(1, 2)
    relay(1, 3)
    gate_scatter.middle()
    down_copy = links.here(down_scatter.finish(), down_sum)
    down_copy.start()

    for copy in [pair[1] for pair in near.values()] + far:
        copy.wait_recv()
    for copies in near.values():
        for copy in copies:
            copy.wait_send()
    mid_load.wait()
    chunk = 32

    def close(step, carry):
        at = pl.ds(pl.multiple_of(step * chunk, chunk), chunk)

        def summed(which):
            total = stage[which, 0, at].astype(f32) + landed[which, 0, at].astype(f32)
            return total + landed[which, 2, at].astype(f32)

        mid = grad_mid_ref[at]
        stage[0, 2, at] = (mid + summed(0)).astype(bf16)
        scale = lax.rsqrt(jnp.mean(mid * mid, axis=-1, keepdims=True) + norm_eps)
        u = summed(1) * gain_ref[...]
        inner = jnp.mean(u * mid, axis=-1, keepdims=True)
        grad_mid = (
            cots[0, at].astype(f32) + scale * u - mid * (scale * scale * scale * inner)
        )
        grad_mid_ref[at] = grad_mid
        stage[1, 2, at] = grad_mid.astype(bf16)
        return carry

    lax.fori_loop(0, rows // chunk, close, 0)
    row_copies = [
        links.here(stage.at[0, 2], result_ref),
        links.here(stage.at[1, 2], grad_proj_ref),
    ]
    start_all(row_copies)

    gate_copy = links.here(gate_scatter.finish(), gate_sum)
    gate_copy.start()
    sent = far + swaps + cot_swaps
    for copy in sent + hidden_acts + acts + [cot_relay]:
        copy.wait_send()
    down_scatter.drain()
    gate_scatter.drain()
    for copy in row_copies + [up_copy, down_copy, gate_copy]:
        copy.wait()


def feed_forward(
    mid, cotangent, gain_ffn, normed_group, cot_near, cot_far, gate_w, up_w, w_down
):
    f32, bf16 = jnp.float32, jnp.bfloat16
    n_fsdp = lax.axis_size("fsdp")
    rows, width = mid.shape
    group_rows = n_fsdp * rows
    units = w_down.shape[0] * BLOCK
    blocks = units // BLOCK
    vmem, hbm = pl.BlockSpec(memory_space=pltpu.VMEM), pl.BlockSpec(memory_space=pl.ANY)
    shape = jax.ShapeDtypeStruct
    return pl.pallas_call(
        feed_forward_kernel,
        name="feed_forward",
        out_shape=[
            shape((rows, width), bf16),
            shape((rows, width), f32),
            shape((rows, width), bf16),
            shape((BLOCK, width), bf16),
            shape((BLOCK, width), bf16),
            shape((blocks // 2, BLOCK, width), bf16),
        ],
        in_specs=[hbm] + [vmem] * 5 + [hbm] * 3,
        out_specs=[hbm, vmem, hbm] + [hbm] * 3,
        scratch_shapes=[
            pltpu.VMEM((width // BLOCK, BLOCK, units), bf16),
            pltpu.VMEM((width // BLOCK, BLOCK, units), bf16),
            pltpu.VMEM((blocks, BLOCK, width), bf16),
            pltpu.VMEM((n_fsdp, rows, width), bf16),
            pltpu.VMEM((group_rows, units), bf16),
            pltpu.VMEM((group_rows, units), bf16),
            pltpu.VMEM((group_rows, units), bf16),
            pltpu.VMEM((n_fsdp, rows, width), bf16),
            pltpu.VMEM((n_fsdp, rows, width), bf16),
            pltpu.VMEM((group_rows, units // 2), bf16),
            pltpu.VMEM((group_rows, units // 2), bf16),
            pltpu.VMEM((group_rows, units // 2), bf16),
            pltpu.VMEM((2, n_fsdp, rows, width), bf16),
            pltpu.VMEM((2, n_fsdp - 1, rows, width), bf16),
            pltpu.VMEM((blocks // 2 - 1, BLOCK, width), bf16),
            pltpu.VMEM((BLOCK, width), bf16),
            pltpu.SemaphoreType.DMA((48,)),
            pltpu.SemaphoreType.DMA((48,)),
            pltpu.SemaphoreType.DMA((8,)),
            pltpu.SemaphoreType.DMA((3, blocks)),
            pltpu.SemaphoreType.REGULAR,
            pltpu.SemaphoreType.REGULAR,
        ],
        compiler_params=pltpu.CompilerParams(
            collective_id=2, has_side_effects=True, vmem_limit_bytes=62 * 2**20
        ),
    )(mid, cotangent, gain_ffn[None], normed_group, cot_near, cot_far, gate_w, up_w, w_down)


def attention_back_kernel(
    grad_proj_ref,
    grad_mid_ref,
    tokens_ref,
    gain_ref,
    w_head_ref,
    out_head_ref,
    qkv_ref,
    attended_ref,
    cos_ref,
    sin_ref,
    pair_ref,
    normed_hbm,
    gate_sum_hbm,
    up_part_hbm,
    grad_input_ref,
    qkv_sum,
    out_sum,
    gate_out,
    up_out,
    proj,
    normed,
    up_part,
    up_halves,
    up_sides,
    grad_att,
    grads,
    key_grad,
    value_grad,
    part,
    core_rx,
    half_rx,
    side_rx,
    out_stage,
    out_landed,
    out_summed,
    head_stage,
    head_summed,
    head_landed,
    pos_col_ref,
    pos_row_ref,
    send_sem,
    recv_sem,
    local_sem,
):
    f32, bf16 = jnp.float32, jnp.bfloat16
    ctx, fsdp = lax.axis_index("ctx"), lax.axis_index("fsdp")
    links = Links((send_sem, recv_sem, local_sem), ctx, fsdp)
    chip, core = ctx // 2, lax.rem(ctx, 2)
    n_ctx, rows, width = proj.shape
    n_fsdp = out_landed.shape[0]
    seq_rows = n_ctx * rows
    head_columns = out_head_ref.shape[0]
    strip_rows = out_landed.shape[1]
    score_scale = 1.0 / math.sqrt(HEAD_SIZE)
    loads = [links.here(normed_hbm, normed), links.here(up_part_hbm, up_part)]
    for copy in loads:
        copy.start()

    flips = [(a, 0) for a in range(1, n_ctx)] + COLUMN_FLIPS + [(1, b) for b in (1, 2, 3)]
    greet(ctx, fsdp, flips)

    proj[ctx] = grad_proj_ref[...]
    half = rows // 2
    gather = PlaneGather(
        links,
        lambda j: [proj.at[j]],
        lambda j, which: [proj.at[j, pl.ds(which * half, half)]],
    )
    gather.begin()
    place_positions(pair_ref, pos_col_ref, pos_row_ref, rows)

    def spread(source, dest):
        half_width = width // 2
        place = pl.ds(pl.multiple_of((2 * fsdp + core) * half_width, half_width), half_width)
        copies = []
        for a in (0, 1):
            for b in range(n_fsdp):
                plane = lax.bitwise_xor(fsdp, b)
                who = lax.bitwise_xor(core, a)
                at_row = (plane // 2) * (BLOCK // 2) + who * strip_rows
                block = source.at[
                    pl.ds(pl.multiple_of(at_row, strip_rows), strip_rows),
                    pl.ds(pl.multiple_of(lax.rem(plane, 2) * half_width, half_width), half_width),
                ]
                target = dest.at[:, place]
                if a or b:
                    copies.append(
                        links.to(block, target, lax.bitwise_xor(ctx, a), plane)
                    )
                else:
                    local = links.here(block, target)
                    locals_.append(local)
                    local.start()
        for copy in copies:
            copy.start()
        return copies

    locals_ = []
    up_scatter = ChipScatter(
        links,
        [up_part.at[lax.bitwise_xor(chip, flip)] for flip in range(4)],
        [up_halves.at[0], up_halves.at[1]],
        [up_sides.at[0], up_sides.at[1]],
    )
    gate_copies = spread(gate_sum_hbm, gate_out)
    gather.forward()
    gather.finish()

    total = jnp.zeros((head_columns, width), f32)
    for j in range(0, n_ctx, 2):
        total = total + lax.dot_general(
            attended_ref[pl.ds(j * rows, 2 * rows)],
            proj[pl.ds(j, 2)].reshape(2 * rows, width),
            (((0,), (0,)), ((), ())),
            preferred_element_type=f32,
        )
    out_stage[...] = total.astype(bf16).reshape(out_stage.shape)
    half_ctx = n_ctx // 2
    out_base = links.remote
    links.remote += half_ctx
    out_copies = []
    for j in range(half_ctx):
        target = half_ctx * core + j
        copy = pltpu.make_async_remote_copy(
            src_ref=out_stage.at[j],
            dst_ref=out_landed.at[chip],
            send_sem=send_sem.at[out_base + j],
            recv_sem=recv_sem.at[out_base + chip],
            device_id=(target, fsdp),
            device_id_type=MESH,
        )
        out_copies.append((target != ctx, copy))

        @pl.when(target != ctx)
        def _(copy=copy):
            copy.start()

    own_out = links.here(out_stage.at[lax.rem(ctx, half_ctx)], out_landed.at[chip])
    out_own_chip = lax.rem(ctx, 2) == ctx // half_ctx

    @pl.when(out_own_chip)
    def _():
        own_out.start()

    up_scatter.begin(up_part_hbm.at[lax.bitwise_xor(chip, 3)])

    def out_arrivals():
        for source in range(half_ctx):
            arrival = pltpu.make_async_remote_copy(
                src_ref=out_stage.at[0],
                dst_ref=out_landed.at[source],
                send_sem=send_sem.at[out_base],
                recv_sem=recv_sem.at[out_base + source],
                device_id=(lax.bitwise_xor(ctx, 1), fsdp),
                device_id_type=MESH,
            )

            @pl.when(2 * source + ctx // half_ctx != ctx)
            def _(arrival=arrival):
                arrival.wait_recv()

        @pl.when(out_own_chip)
        def _():
            own_out.wait()

    def out_begin():
        out_arrivals()
        copies = [
            links.column(
                out_landed.at[lax.bitwise_xor(fsdp, flip)], out_summed.at[slot], 1
            )
            for flip, slot in ((3, 1), (1, 0))
        ]
        start_all(copies)
        return copies

    def out_relay(copies):
        copies[0].wait_recv()
        across = lax.bitwise_xor(fsdp, 2)
        out_landed[across] = (
            out_landed[across].astype(f32) + out_summed[1].astype(f32)
        ).astype(bf16)
        copy = links.column(out_landed.at[across], out_summed.at[2], 2)
        copy.start()
        return copy

    def back(step, carry):
        at = pl.multiple_of(step * 2 * rows, 2 * rows)
        tile = proj[pl.ds(2 * step, 2)].reshape(2 * rows, width)
        grad_att[pl.ds(at, 2 * rows)] = contract_last(tile, out_head_ref[...]).astype(bf16)
        return carry

    lax.fori_loop(0, n_ctx // 2, back, 0)

    key_grad[...] = jnp.zeros_like(key_grad)
    value_grad[...] = jnp.zeros_like(value_grad)

    def attend_head(column):
        cols = pl.ds(column, HEAD_SIZE)

        def step(index, carry):
            at = pl.ds(pl.multiple_of(index * 2 * rows, 2 * rows), 2 * rows)
            keys = qkv_ref[:, pl.ds(head_columns, HEAD_SIZE)]
            values = qkv_ref[:, pl.ds(head_columns + HEAD_SIZE, HEAD_SIZE)]
            causal = pos_row_ref[...] <= pos_col_ref[at]
            query, grad_mixed = qkv_ref[at, cols], grad_att[at, cols]
            scores = contract_last(query, keys) * score_scale
            scores = jnp.where(causal, scores, -1e30)
            shifted = jnp.exp(scores - jnp.max(scores, axis=-1, keepdims=True))
            probs = shifted * (1.0 / jnp.sum(shifted, axis=-1, keepdims=True))
            grad_probs = contract_last(grad_mixed, values)
            delta = jnp.sum(grad_probs * probs, axis=-1, keepdims=True)
            grad_scores = (probs * (grad_probs - delta)).astype(bf16)
            value_grad[...] += contract_first(probs.astype(bf16), grad_mixed)
            key_grad[...] += contract_first(grad_scores, query)
            grad_query = jnp.dot(grad_scores, keys, preferred_element_type=f32) * score_scale
            grads[at, cols] = turn(grad_query, cos_ref[at], sin_ref[at], -1.0).astype(bf16)
            return carry

        lax.fori_loop(0, n_ctx // 2, step, 0)

    depth = n_ctx * strip_rows
    head_near, head_far = [], []

    def head_part(cols, slot):
        flip = (0, 2, 1, 3)[slot]
        places = pl.ds(pl.multiple_of(lax.bitwise_xor(fsdp, flip) * depth, depth), depth)
        total = contract_first(normed[:, :, places].reshape(seq_rows, depth), grads[:, cols])
        head_stage[slot, :, :, cols] = total.astype(bf16).reshape(n_ctx, strip_rows, -1)

    def head_begin(cols):
        copies = []
        for slot in (3, 2):
            head_part(cols, slot)
            copy = links.flip(
                head_stage.at[slot, :, :, cols],
                head_summed.at[slot - 2, :, :, cols],
                0,
                1,
            )
            copy.start()
            copies.append(copy)
        head_near.append(copies)
        for slot in (1, 0):
            head_part(cols, slot)

    def head_relay(index, cols):
        head_near[index][0].wait_recv()
        head_stage[1, :, :, cols] = (
            head_stage[1, :, :, cols].astype(f32) + head_summed[1, :, :, cols].astype(f32)
        ).astype(bf16)
        copy = links.flip(
            head_stage.at[1, :, :, cols], head_summed.at[2, :, :, cols], 0, 2
        )
        copy.start()
        head_far.append(copy)

    first_cols = pl.ds(0, HEAD_SIZE)
    rest_cols = pl.ds(HEAD_SIZE, grads.shape[1] - HEAD_SIZE)
    attend_head(0)
    loads[0].wait()
    head_begin(first_cols)
    out_near = out_begin()
    for column in range(HEAD_SIZE, head_columns, HEAD_SIZE):
        attend_head(column)
    loads[1].wait()
    up_scatter.middle()
    turned = turn(key_grad[...] * score_scale, cos_ref[...], sin_ref[...], -1.0)
    grads[:, pl.ds(head_columns, HEAD_SIZE)] = turned.astype(bf16)
    grads[:, pl.ds(head_columns + HEAD_SIZE, HEAD_SIZE)] = value_grad[...].astype(bf16)
    head_begin(rest_cols)

    scatter = PlaneScatter(links, part, core_rx, half_rx, side_rx)
    for flip, q in scatter.order():
        at = pl.multiple_of(q * 2 * rows, 2 * rows)
        out = contract_last(grads[pl.ds(at, 2 * rows)], w_head_ref[...])
        part[pl.ds(2 * q, 2)] = out.astype(bf16).reshape(2, rows, width)
        scatter.give(flip, q)

    scatter.begin()
    head_relay(0, first_cols)
    out_far = out_relay(out_near)
    head_relay(1, rest_cols)
    scatter.middle()
    up_copies = spread(up_scatter.finish(), up_out)
    grad_normed = scatter.finish()
    inputs = tokens_ref[...].astype(f32)
    scale = lax.rsqrt(jnp.mean(inputs * inputs, axis=-1, keepdims=True) + norm_eps)
    u = grad_normed * gain_ref[...]
    inner = jnp.mean(u * inputs, axis=-1, keepdims=True)
    grad_input_ref[...] = (
        grad_mid_ref[...] + scale * u - inputs * (scale * scale * scale * inner)
    )
    for copy in [pair[1] for pair in head_near] + head_far:
        copy.wait_recv()
    head_stage[0] = (
        head_stage[0].astype(f32) + head_summed[0].astype(f32) + head_summed[2].astype(f32)
    ).astype(bf16)
    head_copies = [
        links.plane(
            head_stage.at[0, lax.bitwise_xor(ctx, a)], head_landed.at[ctx], a
        )
        for a in range(1, n_ctx)
    ]
    start_all(head_copies)
    head_landed[ctx] = head_stage[0, ctx]

    for copy in (out_near[1], out_far):
        copy.wait_recv()
    out_sum[...] = (
        out_landed[fsdp].astype(f32) + out_summed[0].astype(f32) + out_summed[2].astype(f32)
    )
    for copy in head_copies:
        copy.wait_recv()
    for copy in locals_:
        copy.wait()
    query_columns = QUERY_HEADS * HEAD_SIZE
    key_columns = KEY_VALUE_HEADS * HEAD_SIZE
    for head in range(KEY_VALUE_HEADS):
        total = head_landed[head].astype(f32)
        qkv_sum[:, pl.ds(head * head_columns, head_columns)] = total[:, :head_columns]
        qkv_sum[:, pl.ds(query_columns + head * HEAD_SIZE, HEAD_SIZE)] = total[
            :, head_columns : head_columns + HEAD_SIZE
        ]
        qkv_sum[:, pl.ds(query_columns + key_columns + head * HEAD_SIZE, HEAD_SIZE)] = total[
            :, head_columns + HEAD_SIZE :
        ]
    for copy in gate_copies + up_copies:
        copy.wait_recv()
    for copy in gate_copies + up_copies + head_copies + head_far + head_near[0] + head_near[1]:
        copy.wait_send()
    for copy in out_near + [out_far]:
        copy.wait_send()
    for away, copy in out_copies:

        @pl.when(away)
        def _(copy=copy):
            copy.wait_send()

    gather.drain()
    scatter.drain()
    up_scatter.drain()


def attention_back(
    grad_proj,
    grad_mid,
    tokens,
    gain_attn,
    w_head,
    out_head,
    qkv,
    attended,
    cos,
    sin,
    pair_block,
    normed,
    gate_sum,
    up_part,
):
    f32, bf16 = jnp.float32, jnp.bfloat16
    n_ctx, n_fsdp = lax.axis_size("ctx"), lax.axis_size("fsdp")
    rows, width = tokens.shape
    seq_rows = n_ctx * rows
    strip_rows = width // (n_ctx * n_fsdp)
    head_columns, all_columns = attended.shape[1], qkv.shape[1]
    vmem, hbm = pl.BlockSpec(memory_space=pltpu.VMEM), pl.BlockSpec(memory_space=pl.ANY)
    shape = jax.ShapeDtypeStruct
    return pl.pallas_call(
        attention_back_kernel,
        name="attention_back",
        out_shape=[
            shape((rows, width), f32),
            shape((strip_rows, (QUERY_HEADS + 2 * KEY_VALUE_HEADS) * HEAD_SIZE), f32),
            shape((strip_rows, width), f32),
            shape((strip_rows, n_fsdp * width), bf16),
            shape((strip_rows, n_fsdp * width), bf16),
        ],
        in_specs=[vmem] * 10 + [pl.BlockSpec(memory_space=pltpu.SMEM)] + [hbm] * 3,
        out_specs=[vmem] * 3 + [hbm] * 2,
        scratch_shapes=[
            pltpu.VMEM((n_ctx, rows, width), bf16),
            pltpu.VMEM((n_ctx, rows, width), bf16),
            pltpu.VMEM(up_part.shape, bf16),
            pltpu.VMEM((2, BLOCK // 2, width), bf16),
            pltpu.VMEM((2, BLOCK, width), bf16),
            pltpu.VMEM((seq_rows, head_columns), bf16),
            pltpu.VMEM((seq_rows, all_columns), bf16),
            pltpu.VMEM((seq_rows, HEAD_SIZE), f32),
            pltpu.VMEM((seq_rows, HEAD_SIZE), f32),
            pltpu.VMEM((n_ctx, rows, width), bf16),
            pltpu.VMEM((n_ctx // 2, rows, width), bf16),
            pltpu.VMEM((2, rows // 2, width), bf16),
            pltpu.VMEM((2, rows, width), bf16),
            pltpu.VMEM((n_ctx // 2, strip_rows, width), bf16),
            pltpu.VMEM((n_fsdp, strip_rows, width), bf16),
            pltpu.VMEM((n_fsdp - 1, strip_rows, width), bf16),
            pltpu.VMEM((n_fsdp, n_ctx, strip_rows, all_columns), bf16),
            pltpu.VMEM((n_fsdp - 1, n_ctx, strip_rows, all_columns), bf16),
            pltpu.VMEM((n_ctx, strip_rows, all_columns), bf16),
            pltpu.VMEM((seq_rows, 1), jnp.int32),
            pltpu.VMEM((1, seq_rows), jnp.int32),
            pltpu.SemaphoreType.DMA((96,)),
            pltpu.SemaphoreType.DMA((96,)),
            pltpu.SemaphoreType.DMA((8,)),
        ],
        compiler_params=pltpu.CompilerParams(
            collective_id=3, has_side_effects=True, vmem_limit_bytes=62 * 2**20
        ),
    )(
        grad_proj,
        grad_mid,
        tokens,
        gain_attn[None],
        w_head,
        out_head,
        qkv,
        attended,
        cos,
        sin,
        pair_block,
        normed,
        gate_sum,
        up_part,
    )


def copier(sem):
    copies = []

    def copy(source, dest):
        copies.append(pltpu.make_async_copy(source, dest, sem.at[len(copies)]))
        copies[-1].start()
        return copies[-1]

    return copy


def widen_kernel(gain_attn, gain_ffn, qkv, gate, up, qkv_hbm, gate_hbm, up_hbm, *refs):
    (qkv_out, gate_out, up_out, sums_ref), refs = refs[:4], refs[4:]
    (qkv_v, gate_v, up_v, qkv_w, gate_w, up_w, gate_f, up_f, sem) = refs
    f32 = jnp.float32
    rows = gate_w.shape[0]
    ctx, fsdp = lax.axis_index("ctx"), lax.axis_index("fsdp")
    at = pl.ds(pl.multiple_of(ctx * rows, rows), rows)
    copy = copier(sem)
    loads, stores = [], []
    for source, dest, weight, rows_v in (
        (gate, gate_v, gate_hbm, gate_w),
        (up, up_v, up_hbm, up_w),
        (qkv, qkv_v, qkv_hbm, qkv_w),
    ):
        loads.append((copy(source, dest), copy(weight.at[at], rows_v)))

    def widen(index, source, weight, wide, out):
        for load in loads[index]:
            load.wait()
        values = source[...].astype(f32)
        if wide is None:
            stores.append(copy(source, out))
        else:
            wide[...] = values
            stores.append(copy(wide, out))
        return jnp.sum(weight[...].astype(f32) * values, axis=1, keepdims=True)

    ffn = widen(0, gate_v, gate_w, gate_f, gate_out)
    ffn = ffn + widen(1, up_v, up_w, up_f, up_out)
    attn = widen(2, qkv_v, qkv_w, None, qkv_out)
    which = fsdp * lax.axis_size("ctx") + ctx
    lanes = pl.ds(pl.multiple_of((which // 2) * 2 * rows, 2 * rows), 2 * rows)
    for index, (total, gain_ref) in enumerate(((attn, gain_attn), (ffn, gain_ffn))):
        turned = jnp.broadcast_to(total, (rows, HEAD_SIZE)).T
        gain = gain_ref[:, lanes]
        gain = jnp.where(lax.rem(which, 2) == 1, pltpu.roll(gain, rows, 1), gain)
        sums_ref[pl.ds(index, 1)] = turned[:1] / gain[:, :rows]
    for store in stores:
        store.wait()


def widen(qkv_sum, gate_low, up_low, qkv_w, w_gate, w_up, gain_attn, gain_ffn):
    f32, bf16 = jnp.float32, jnp.bfloat16
    rows = gate_low.shape[0]
    vmem, hbm = pl.BlockSpec(memory_space=pltpu.VMEM), pl.BlockSpec(memory_space=pl.ANY)
    arrays = (qkv_sum, gate_low, up_low)
    return pl.pallas_call(
        widen_kernel,
        name="widen",
        out_shape=[jax.ShapeDtypeStruct(a.shape, f32) for a in arrays]
        + [jax.ShapeDtypeStruct((2, rows), f32)],
        in_specs=[vmem] * 2 + [hbm] * 6,
        out_specs=[hbm] * 3 + [vmem],
        scratch_shapes=[pltpu.VMEM(a.shape, a.dtype) for a in arrays]
        + [pltpu.VMEM(a.shape, bf16) for a in arrays]
        + [pltpu.VMEM(a.shape, f32) for a in (gate_low, up_low)]
        + [pltpu.SemaphoreType.DMA((9,))],
        compiler_params=pltpu.CompilerParams(vmem_limit_bytes=62 * 2**20),
    )(gain_attn[None], gain_ffn[None], *arrays, qkv_w, w_gate, w_up)


def pass_on_kernel(count, *refs):
    sources, outs, held, (wide, sem) = (
        refs[: count + 1],
        refs[count + 1 : 2 * count + 2],
        refs[2 * count + 2 : 3 * count + 3],
        refs[3 * count + 3 :],
    )
    copy = copier(sem)
    loads = [copy(source, dest) for source, dest in zip(sources, held)]
    stores = []
    for load, source, dest in zip(loads, held, outs):
        load.wait()
        if len(stores) == count:
            wide[...] = source[...].astype(jnp.float32)
            source = wide
        stores.append(copy(source, dest))
    for store in stores:
        store.wait()


def pass_on(passed, last):
    hbm = pl.BlockSpec(memory_space=pl.ANY)
    count = len(passed)
    arrays = list(passed) + [last]
    kinds = [a.dtype for a in passed] + [jnp.float32]
    moved = 2 * sum(a.size * a.dtype.itemsize for a in arrays)
    return pl.pallas_call(
        functools.partial(pass_on_kernel, count),
        name="pass_on",
        out_shape=[jax.ShapeDtypeStruct(a.shape, kind) for a, kind in zip(arrays, kinds)],
        in_specs=[hbm] * (count + 1),
        out_specs=[hbm] * (count + 1),
        scratch_shapes=[pltpu.VMEM(a.shape, a.dtype) for a in arrays]
        + [pltpu.VMEM(last.shape, jnp.float32), pltpu.SemaphoreType.DMA((2 * count + 2,))],
        compiler_params=pltpu.CompilerParams(vmem_limit_bytes=62 * 2**20),
        cost_estimate=pl.CostEstimate(flops=last.size, bytes_accessed=moved, transcendentals=0),
    )(*arrays)


def local_heads(
    tokens,
    cotangent,
    gain_attn,
    gain_ffn,
    query_key_value_weight,
    w_out,
    w_gate,
    w_up,
    w_down,
    pair_block,
):
    n_ctx, n_fsdp = lax.axis_size("ctx"), lax.axis_size("fsdp")
    width = tokens.shape[1]
    depth = query_key_value_weight.shape[0]

    (
        mid,
        normed_two_group,
        cot_near,
        cot_far,
        gate_w,
        up_w,
        qkv,
        attended,
        normed_one_seq,
        w_head,
        out_head,
        cos,
        sin,
    ) = attention_forward(
        tokens,
        cotangent,
        gain_attn,
        gain_ffn,
        query_key_value_weight,
        w_out,
        w_gate,
        w_up,
        pair_block,
    )
    result, grad_mid, grad_proj, down_sum, gate_sum, up_part = feed_forward(
        mid,
        cotangent,
        gain_ffn,
        normed_two_group,
        cot_near,
        cot_far,
        gate_w,
        up_w,
        w_down.reshape(-1, BLOCK, width),
    )
    grad_input, qkv_sum, grad_out, gate_low, up_low = attention_back(
        grad_proj,
        grad_mid,
        tokens,
        gain_attn,
        w_head,
        out_head,
        qkv,
        attended,
        cos,
        sin,
        pair_block,
        normed_one_seq,
        gate_sum,
        up_part,
    )
    grad_qkv, grad_gate, grad_up, sums = widen(
        qkv_sum, gate_low, up_low, query_key_value_weight, w_gate, w_up, gain_attn, gain_ffn
    )
    result, grad_input, grad_out, grad_down = pass_on((result, grad_input, grad_out), down_sum)
    gain_pairs = [(c * n_fsdp + f, f * n_ctx + c) for c in range(n_ctx) for f in range(n_fsdp)]
    grad_gain_attn, grad_gain_ffn = lax.ppermute(sums, ("ctx", "fsdp"), gain_pairs)
    return (
        result,
        grad_input,
        grad_gain_attn,
        grad_gain_ffn,
        grad_qkv,
        grad_out,
        grad_gate,
        grad_up,
        grad_down,
    )


def solution(mesh):
    fits = mesh.shape["ctx"] == KEY_VALUE_HEADS and mesh.shape["fsdp"] == KEY_VALUE_HEADS // 2
    local = local_heads if fits else local_general
    return jax.shard_map(
        local,
        mesh=mesh,
        in_specs=(
            P(("ctx", "fsdp"), None),
            P(("ctx", "fsdp"), None),
            P(),
            P(),
            P("fsdp", None),
            P("fsdp", None),
            P("fsdp", None),
            P("fsdp", None),
            P("fsdp", None),
            P(),
        ),
        out_specs=(
            P(("ctx", "fsdp"), None),
            P(("ctx", "fsdp"), None),
            P(("ctx", "fsdp")),
            P(("ctx", "fsdp")),
            P(("fsdp", "ctx"), None),
            P(("fsdp", "ctx"), None),
            P(("fsdp", "ctx"), None),
            P(("fsdp", "ctx"), None),
            P(("fsdp", "ctx"), None),
        ),
        check_vma=False,
    )
```

```python
import functools
import math

import jax
import jax.numpy as jnp
from jax import lax
from jax.experimental import pallas as pl
from jax.experimental.pallas import tpu as pltpu
from jax.sharding import PartitionSpec as P

QUERY_HEADS = 16
KEY_VALUE_HEADS = 8
HEAD_SIZE = 128


norm_eps = 1e-05
rope_base = 1000000.0


def rms_norm(vectors, gain_vec):
    return (
        vectors
        * lax.rsqrt(jnp.mean(vectors * vectors, axis=-1, keepdims=True) + norm_eps)
        * gain_vec
    )


def apply_rotation(vectors, where_pos):
    half_dim = vectors.shape[-1] // 2
    frequency = jnp.exp(
        jnp.arange(half_dim, dtype=jnp.float32) * (-2.0 * math.log(rope_base) / vectors.shape[-1])
    )
    angles = where_pos.astype(jnp.float32)[:, None] * frequency[None, :]
    cosine = jnp.cos(angles)[:, None, :]
    sine_val = jnp.sin(angles)[:, None, :]
    first_half = vectors[..., :half_dim]
    second_half = vectors[..., half_dim:]
    return jnp.concatenate(
        [
            first_half * cosine - second_half * sine_val,
            second_half * cosine + first_half * sine_val,
        ],
        axis=-1,
    )


def positions(pair_block, token_rows):
    n_ctx = lax.axis_size("ctx")
    half_rows = token_rows // 2
    row_index = jnp.arange(token_rows, dtype=jnp.int32)
    first_block = pair_block[:, None]
    which_block = jnp.where(
        row_index[None, :] < half_rows, first_block, 2 * n_ctx - 1 - first_block
    )
    pos_table = which_block * half_rows + (row_index % half_rows)[None, :]
    own_pos = lax.dynamic_slice(pos_table, (lax.axis_index("ctx"), 0), (1, token_rows)).reshape(
        token_rows
    )
    return (pos_table.reshape(-1), own_pos)


def to_groups(input_array, group_count):
    token_rows = input_array.shape[0]
    head_length = input_array.shape[-1] // (group_count * KEY_VALUE_HEADS)
    return (
        input_array.reshape(token_rows, KEY_VALUE_HEADS, group_count, head_length)
        .transpose(1, 2, 0, 3)
        .reshape(KEY_VALUE_HEADS, group_count * token_rows, head_length)
    )


def from_groups(input_array, group_count):
    head_length = input_array.shape[-1]
    token_rows = input_array.shape[1] // group_count
    return (
        input_array.reshape(KEY_VALUE_HEADS, group_count, token_rows, head_length)
        .transpose(2, 0, 1, 3)
        .reshape(token_rows, KEY_VALUE_HEADS * group_count * head_length)
    )


def split_keys(every_key, every_value, key_pos):
    total_keys = every_key.shape[0]
    block_length = min(1024, total_keys)
    block_count = total_keys // block_length
    return (
        every_key.reshape(block_count, block_length, KEY_VALUE_HEADS, HEAD_SIZE),
        every_value.reshape(block_count, block_length, KEY_VALUE_HEADS, HEAD_SIZE),
        key_pos.reshape(block_count, block_length),
    )


def contract_last(left, right):
    return lax.dot_general(
        left, right, (((1,), (1,)), ((), ())), preferred_element_type=jnp.float32
    )


def contract_first(left, right):
    return lax.dot_general(
        left, right, (((0,), (0,)), ((), ())), preferred_element_type=jnp.float32
    )


def local_general(
    tokens,
    cotangent,
    gain_attn,
    gain_ffn,
    query_key_value_weight,
    w_out,
    w_gate,
    w_up,
    w_down,
    pair_block,
):
    token_rows = tokens.shape[0]
    query_columns = QUERY_HEADS * HEAD_SIZE
    key_value_columns = KEY_VALUE_HEADS * HEAD_SIZE
    group_count = QUERY_HEADS // KEY_VALUE_HEADS
    score_scale = 1.0 / math.sqrt(HEAD_SIZE)
    ff_cols = w_gate.shape[1]
    key_pos, own_pos = positions(pair_block, token_rows)
    query_pos = jnp.tile(own_pos, group_count)
    inputs_f = tokens.astype(jnp.float32)
    qkv_full, out_full = (
        lax.all_gather(query_key_value_weight, "fsdp", axis=0, tiled=True),
        lax.all_gather(w_out, "fsdp", axis=0, tiled=True),
    )
    normed_one_b = rms_norm(inputs_f, gain_attn).astype(jnp.bfloat16)
    projected_rows = jnp.dot(normed_one_b, qkv_full, preferred_element_type=jnp.float32)
    query_raw = projected_rows[:, :query_columns].reshape(token_rows, QUERY_HEADS, HEAD_SIZE)
    unrotated_key = projected_rows[:, query_columns : query_columns + key_value_columns].reshape(
        token_rows, KEY_VALUE_HEADS, HEAD_SIZE
    )
    query_b = (
        apply_rotation(query_raw, own_pos).astype(jnp.bfloat16).reshape(token_rows, query_columns)
    )
    keys_b = (
        apply_rotation(unrotated_key, own_pos)
        .astype(jnp.bfloat16)
        .reshape(token_rows, key_value_columns)
    )
    values_b = projected_rows[:, query_columns + key_value_columns :].astype(jnp.bfloat16)
    every_key, every_value = (
        lax.all_gather(keys_b, "ctx", axis=0, tiled=True),
        lax.all_gather(values_b, "ctx", axis=0, tiled=True),
    )
    query_grp = to_groups(query_b, group_count)
    key_blocks, value_blocks, pos_blocks = split_keys(every_key, every_value, key_pos)

    def forward_step(carry, block_in):
        run_max, run_total, weighted = carry
        key_block, value_block, block_pos = block_in
        causal = block_pos[None, None, :] <= query_pos[None, :, None]
        scores = (
            jnp.einsum("hqd,khd->hqk", query_grp, key_block, preferred_element_type=jnp.float32)
            * score_scale
        )
        scores = jnp.where(causal, scores, -1e30)
        new_max = jnp.maximum(run_max, jnp.max(scores, axis=-1))
        exp_scores = jnp.where(causal, jnp.exp(scores - new_max[..., None]), 0.0)
        fading = jnp.exp(run_max - new_max)
        run_total = run_total * fading + jnp.sum(exp_scores, axis=-1)
        weighted = weighted * fading[..., None] + jnp.einsum(
            "hqk,khd->hqd",
            exp_scores.astype(jnp.bfloat16),
            value_block,
            preferred_element_type=jnp.float32,
        )
        return ((new_max, run_total, weighted), None)

    initial_maximum = jnp.full((KEY_VALUE_HEADS, group_count * token_rows), -1e30, jnp.float32)
    initial_total = jnp.zeros((KEY_VALUE_HEADS, group_count * token_rows), jnp.float32)
    initial_weighted = jnp.zeros(
        (KEY_VALUE_HEADS, group_count * token_rows, HEAD_SIZE), jnp.float32
    )
    final_carry, ignored = lax.scan(
        forward_step,
        (initial_maximum, initial_total, initial_weighted),
        (key_blocks, value_blocks, pos_blocks),
    )
    run_max, run_total, weighted = final_carry
    log_total = run_max + jnp.log(run_total)
    attn_grp = weighted / run_total[..., None]
    attended_b = from_groups(attn_grp.astype(jnp.bfloat16), group_count)
    mid_rows = inputs_f + jnp.dot(attended_b, out_full, preferred_element_type=jnp.float32)
    gate_full, up_full, down_full = (
        lax.all_gather(w_gate, "fsdp", axis=0, tiled=True),
        lax.all_gather(w_up, "fsdp", axis=0, tiled=True),
        lax.all_gather(w_down, "fsdp", axis=0, tiled=True),
    )
    normed_two_b = rms_norm(mid_rows, gain_ffn).astype(jnp.bfloat16)
    gate_val = jnp.dot(normed_two_b, gate_full, preferred_element_type=jnp.float32)
    up_val = jnp.dot(normed_two_b, up_full, preferred_element_type=jnp.float32)
    hidden_b = (jax.nn.silu(gate_val) * up_val).astype(jnp.bfloat16)
    output_f = mid_rows + jnp.dot(hidden_b, down_full, preferred_element_type=jnp.float32)
    result = output_f.astype(jnp.bfloat16)
    normed_one_x, attended_x, normed_two_x, hidden_x = (
        lax.all_to_all(normed_one_b, "fsdp", split_axis=1, concat_axis=0, tiled=True),
        lax.all_to_all(attended_b, "fsdp", split_axis=1, concat_axis=0, tiled=True),
        lax.all_to_all(normed_two_b, "fsdp", split_axis=1, concat_axis=0, tiled=True),
        lax.all_to_all(hidden_b, "fsdp", split_axis=1, concat_axis=0, tiled=True),
    )
    grad_out_f = cotangent.astype(jnp.float32)
    gate_back, up_back, down_back = (
        lax.all_gather(w_gate, "fsdp", axis=0, tiled=True),
        lax.all_gather(w_up, "fsdp", axis=0, tiled=True),
        lax.all_gather(w_down, "fsdp", axis=0, tiled=True),
    )
    grad_hidden = contract_last(cotangent, down_back)
    ignored, ffn_back = jax.vjp(
        lambda gate_in, up_in: jax.nn.silu(gate_in) * up_in, gate_val, up_val
    )
    grad_gate_f, grad_up_f = ffn_back(grad_hidden)
    grad_gate_b = grad_gate_f.astype(jnp.bfloat16)
    grad_up_b = grad_up_f.astype(jnp.bfloat16)
    grad_normed_two = contract_last(grad_gate_b, gate_back) + contract_last(grad_up_b, up_back)
    ignored, norm_two_back = jax.vjp(rms_norm, mid_rows, gain_ffn)
    grad_mid_part, gain_ffn_part = norm_two_back(grad_normed_two)
    grad_mid = grad_out_f + grad_mid_part
    gate_up_b = jnp.concatenate([grad_gate_b, grad_up_b], axis=1)
    qkv_back, out_back = (
        lax.all_gather(query_key_value_weight, "fsdp", axis=0, tiled=True),
        lax.all_gather(w_out, "fsdp", axis=0, tiled=True),
    )
    grad_proj_b = grad_mid.astype(jnp.bfloat16)
    grad_att_b = contract_last(grad_proj_b, out_back).astype(jnp.bfloat16)
    grad_att_grp = to_groups(grad_att_b, group_count)
    delta_rows = jnp.sum(grad_att_grp.astype(jnp.float32) * attn_grp, axis=-1)

    def backward_step(grad_query, block_in):
        key_block, value_block, block_pos = block_in
        causal = block_pos[None, None, :] <= query_pos[None, :, None]
        scores = (
            jnp.einsum("hqd,khd->hqk", query_grp, key_block, preferred_element_type=jnp.float32)
            * score_scale
        )
        probs = jnp.where(causal, jnp.exp(scores - log_total[..., None]), 0.0)
        grad_values = jnp.einsum(
            "hqk,hqd->khd",
            probs.astype(jnp.bfloat16),
            grad_att_grp,
            preferred_element_type=jnp.float32,
        )
        grad_probs = jnp.einsum(
            "hqd,khd->hqk", grad_att_grp, value_block, preferred_element_type=jnp.float32
        )
        grad_scores = (probs * (grad_probs - delta_rows[..., None])).astype(jnp.bfloat16)
        grad_query = grad_query + score_scale * jnp.einsum(
            "hqk,khd->hqd", grad_scores, key_block, preferred_element_type=jnp.float32
        )
        grad_keys = score_scale * jnp.einsum(
            "hqk,hqd->khd", grad_scores, query_grp, preferred_element_type=jnp.float32
        )
        return (grad_query, (grad_keys, grad_values))

    grad_query_grp, key_grads = lax.scan(
        backward_step,
        jnp.zeros((KEY_VALUE_HEADS, group_count * token_rows, HEAD_SIZE), jnp.float32),
        (key_blocks, value_blocks, pos_blocks),
    )
    total_keys = key_pos.shape[0]
    grad_keys_all = key_grads[0].reshape(total_keys, key_value_columns)
    grad_values_all = key_grads[1].reshape(total_keys, key_value_columns)
    key_sums, summed_values = (
        lax.psum_scatter(
            grad_keys_all.astype(jnp.bfloat16), "ctx", scatter_dimension=0, tiled=True
        ).astype(jnp.float32),
        lax.psum_scatter(
            grad_values_all.astype(jnp.bfloat16), "ctx", scatter_dimension=0, tiled=True
        ).astype(jnp.float32),
    )
    grad_query_rows = from_groups(grad_query_grp, group_count).reshape(
        token_rows, QUERY_HEADS, HEAD_SIZE
    )
    ignored, query_rope_back = jax.vjp(lambda vectors: apply_rotation(vectors, own_pos), query_raw)
    ignored, key_rotation_backward = jax.vjp(
        lambda vectors: apply_rotation(vectors, own_pos), unrotated_key
    )
    grad_query_raw = query_rope_back(grad_query_rows)[0]
    unrotated_key_gradient = key_rotation_backward(
        key_sums.reshape(token_rows, KEY_VALUE_HEADS, HEAD_SIZE)
    )[0]
    grad_projected_b = jnp.concatenate(
        [
            grad_query_raw.reshape(token_rows, query_columns),
            unrotated_key_gradient.reshape(token_rows, key_value_columns),
            summed_values,
        ],
        axis=1,
    ).astype(jnp.bfloat16)
    grad_normed_one = contract_last(grad_projected_b, qkv_back)
    ignored, norm_one_back = jax.vjp(rms_norm, inputs_f, gain_attn)
    grad_in_part, gain_attn_part = norm_one_back(grad_normed_one)
    grad_input = grad_mid + grad_in_part
    cot_group, gate_up_group, projected_group, proj_group = (
        lax.all_gather(cotangent, "fsdp", axis=0, tiled=True),
        lax.all_gather(gate_up_b, "fsdp", axis=0, tiled=True),
        lax.all_gather(grad_projected_b, "fsdp", axis=0, tiled=True),
        lax.all_gather(grad_proj_b, "fsdp", axis=0, tiled=True),
    )
    qkv_part = contract_first(normed_one_x, projected_group)
    out_part = contract_first(attended_x, proj_group)
    gate_up_part = contract_first(normed_two_x, gate_up_group)
    gate_part = gate_up_part[:, :ff_cols]
    up_part = gate_up_part[:, ff_cols:]
    down_part = contract_first(hidden_x, cot_group)
    grad_qkv, grad_out, grad_down = (
        lax.psum_scatter(
            qkv_part.astype(jnp.bfloat16), "ctx", scatter_dimension=0, tiled=True
        ).astype(jnp.float32),
        lax.psum_scatter(
            out_part.astype(jnp.bfloat16), "ctx", scatter_dimension=0, tiled=True
        ).astype(jnp.float32),
        lax.psum_scatter(
            down_part.astype(jnp.bfloat16), "ctx", scatter_dimension=0, tiled=True
        ).astype(jnp.float32),
    )
    grad_gate, grad_up = (
        lax.psum_scatter(
            gate_part.astype(jnp.bfloat16), "ctx", scatter_dimension=0, tiled=True
        ).astype(jnp.float32),
        lax.psum_scatter(
            up_part.astype(jnp.bfloat16), "ctx", scatter_dimension=0, tiled=True
        ).astype(jnp.float32),
    )
    grad_gain_attn, grad_gain_ffn = (
        lax.psum_scatter(gain_attn_part, ("ctx", "fsdp"), scatter_dimension=0, tiled=True),
        lax.psum_scatter(gain_ffn_part, ("ctx", "fsdp"), scatter_dimension=0, tiled=True),
    )
    return (
        result,
        grad_input,
        grad_gain_attn,
        grad_gain_ffn,
        grad_qkv,
        grad_out,
        grad_gate,
        grad_up,
        grad_down,
    )


MESH = pl.DeviceIdType.MESH
ACROSS_X, ACROSS_Y, ACROSS_CORE = 2, 4, 1
BLOCK = 256


class Links:
    def __init__(self, sems, ctx, fsdp):
        self.send_sem, self.recv_sem, self.local_sem = sems
        self.ctx, self.fsdp = ctx, fsdp
        self.remote = self.locals = 0

    def to(self, src, dst, ctx, fsdp):
        index, self.remote = self.remote, self.remote + 1
        return pltpu.make_async_remote_copy(
            src_ref=src,
            dst_ref=dst,
            send_sem=self.send_sem.at[index],
            recv_sem=self.recv_sem.at[index],
            device_id=(ctx, fsdp),
            device_id_type=MESH,
        )

    def flip(self, src, dst, ctx_flip, fsdp_flip):
        return self.to(
            src, dst, lax.bitwise_xor(self.ctx, ctx_flip), lax.bitwise_xor(self.fsdp, fsdp_flip)
        )

    def plane(self, src, dst, flip):
        return self.flip(src, dst, flip, 0)

    def column(self, src, dst, flip):
        return self.flip(src, dst, 0, flip)

    def here(self, src, dst):
        index, self.locals = self.locals, self.locals + 1
        return pltpu.make_async_copy(src, dst, self.local_sem.at[index])


PLANE_FLIPS = [(1, 0), (2, 0), (4, 0)]
COLUMN_FLIPS = [(0, 1), (0, 2), (0, 3)]


def greet(ctx, fsdp, flips):
    barrier = pltpu.get_barrier_semaphore()
    for a, b in flips:
        pl.semaphore_signal(
            barrier,
            inc=1,
            device_id=(lax.bitwise_xor(ctx, a), lax.bitwise_xor(fsdp, b)),
            device_id_type=MESH,
        )
    pl.semaphore_wait(barrier, len(flips))


def start_all(copies):
    for copy in copies:
        copy.start()


class LineGather:
    def __init__(self, links, own, group):
        self.links, self.group = links, group
        self.home = links.here(own, group.at[0])
        self.near = links.column(own, group.at[2], 1)
        self.far = links.column(own, group.at[1], 2)
        self.relay = links.column(group.at[1], group.at[3], 1)

    def begin(self):
        start_all([self.far, self.near, self.home])

    def forward(self):
        self.far.wait_recv()
        self.relay.start()

    def finish(self):
        self.near.wait_recv()
        self.relay.wait_recv()
        for copy in (self.near, self.far, self.relay):
            copy.wait_send()
        self.home.wait()


class PlaneGather:
    def __init__(self, links, blocks, halves):
        self.links, self.blocks, self.halves = links, blocks, halves
        self.ctx = links.ctx
        self.sent = []
        self.cores = []

    def _go(self, copies):
        for copy in copies:
            copy.start()
        self.sent += copies
        return copies

    def _core(self, index):
        refs = self.blocks(index)
        self.cores += self._go([self.links.plane(r, r, ACROSS_CORE) for r in refs])

    def begin(self, sources=None):
        refs = self.blocks(self.ctx)
        pairs = list(zip(sources or refs, refs))
        self.from_x = self._go([self.links.plane(s, r, ACROSS_X) for s, r in pairs])
        self.from_y = self._go([self.links.plane(s, r, ACROSS_Y) for s, r in pairs])
        self.cores += self._go([self.links.plane(s, r, ACROSS_CORE) for s, r in pairs])

    def forward(self):
        index = lax.bitwise_xor(self.ctx, ACROSS_X)
        for copy in self.from_x:
            copy.wait_recv()
        refs = self.halves(index, 0)
        self.corner = self._go([self.links.plane(r, r, ACROSS_Y) for r in refs])
        self._core(index)
        index = lax.bitwise_xor(self.ctx, ACROSS_Y)
        for copy in self.from_y:
            copy.wait_recv()
        refs = self.halves(index, 1)
        self.corner += self._go([self.links.plane(r, r, ACROSS_X) for r in refs])
        self._core(index)

    def finish(self):
        for copy in self.corner:
            copy.wait_recv()
        self._core(lax.bitwise_xor(self.ctx, ACROSS_X | ACROSS_Y))
        for copy in self.cores:
            copy.wait_recv()

    def drain(self):
        for copy in self.sent:
            copy.wait_send()


class PlaneScatter:
    def __init__(self, links, part, core_rx, half_rx, side_rx):
        self.links, self.part = links, part
        self.core_rx, self.half_rx, self.side_rx = core_rx, half_rx, side_rx
        self.chip, self.core = links.ctx // 2, lax.rem(links.ctx, 2)
        self.sent = []
        self.from_core = {}

    def order(self):
        return [(flip, lax.bitwise_xor(self.chip, flip)) for flip in (3, 1, 2, 0)]

    def _go(self, copy):
        copy.start()
        self.sent.append(copy)
        return copy

    def give(self, flip, chip):
        self.from_core[flip] = self._go(
            self.links.plane(
                self.part.at[2 * chip + 1 - self.core], self.core_rx.at[chip], ACROSS_CORE
            )
        )

    def _summed(self, flip):
        chip = lax.bitwise_xor(self.chip, flip)
        self.from_core[flip].wait_recv()
        mine = self.part.at[2 * chip + self.core]
        total = mine[...].astype(jnp.float32) + self.core_rx[chip].astype(jnp.float32)
        return mine, total

    def begin(self):
        half = self.half = self.half_rx.shape[1]
        mine, total = self._summed(3)
        mine[...] = total.astype(jnp.bfloat16)
        self.corner = [
            self._go(self.links.plane(mine.at[pl.ds(0, half)], self.half_rx.at[0], ACROSS_Y)),
            self._go(
                self.links.plane(mine.at[pl.ds(half, half)], self.half_rx.at[1], ACROSS_X)
            ),
        ]

    def middle(self):
        self.sides = []
        for flip, across, slot in ((1, ACROSS_X, 0), (2, ACROSS_Y, 1)):
            mine, total = self._summed(flip)
            mine[...] = total.astype(jnp.bfloat16)
            self.corner[slot].wait_recv()
            rows = pl.ds(slot * self.half, self.half)
            mine[rows] = (
                total[slot * self.half : (slot + 1) * self.half]
                + self.half_rx[slot].astype(jnp.float32)
            ).astype(jnp.bfloat16)
            self.sides.append(self._go(self.links.plane(mine, self.side_rx.at[slot], across)))

    def finish(self):
        mine, total = self._summed(0)
        for slot, copy in enumerate(self.sides):
            copy.wait_recv()
            total = total + self.side_rx[slot].astype(jnp.float32)
        return total

    def drain(self):
        for copy in self.sent:
            copy.wait_send()


def swap_bits(fsdp):
    return 2 * lax.rem(fsdp, 2) + fsdp // 2


def place_positions(pair_ref, pos_col, pos_row, rows):
    half, n_ctx = rows // 2, pos_col.shape[0] // rows
    down = lax.broadcasted_iota(jnp.int32, (rows, 1), 0)
    along = lax.broadcasted_iota(jnp.int32, (1, rows), 1)
    for j in range(n_ctx):
        first = pair_ref[j] * half
        second = (2 * n_ctx - 1 - pair_ref[j]) * half - half
        pos_col[pl.ds(j * rows, rows)] = down + jnp.where(down < half, first, second)
        pos_row[:, pl.ds(j * rows, rows)] = along + jnp.where(along < half, first, second)


def turn(vectors, cos_rows, sin_rows, sign):
    return vectors * cos_rows + sign * pltpu.roll(vectors, HEAD_SIZE // 2, 1) * sin_rows


def attention_kernel(
    tokens_ref,
    cot_ref,
    gain_one_ref,
    gain_two_ref,
    qkv_w_ref,
    out_w_ref,
    gate_ref,
    up_ref,
    pair_ref,
    mid_ref,
    normed_two_group,
    cot_near,
    cot_far,
    gate_w,
    up_w,
    qkv_out,
    attended_out,
    normed_one_out,
    w_head_out,
    out_head_out,
    cos_out,
    sin_out,
    normed,
    w_head,
    out_head,
    out_relay,
    qkv,
    attended,
    part,
    core_rx,
    half_rx,
    side_rx,
    normed_two,
    cos_ref,
    sin_ref,
    pos_col_ref,
    pos_row_ref,
    send_sem,
    recv_sem,
    local_sem,
):
    f32, bf16 = jnp.float32, jnp.bfloat16
    ctx, fsdp = lax.axis_index("ctx"), lax.axis_index("fsdp")
    links = Links((send_sem, recv_sem, local_sem), ctx, fsdp)
    rows, width = tokens_ref.shape
    depth = qkv_w_ref.shape[0]
    head_columns = out_head.shape[0]
    n_ctx, n_fsdp = normed.shape[0], width // depth
    seq_rows = n_ctx * rows
    hidden = gate_w.shape[2]
    strip = hidden // n_ctx
    depth_blocks = gate_ref.shape[0]
    query_columns = QUERY_HEADS * HEAD_SIZE
    key_columns = KEY_VALUE_HEADS * HEAD_SIZE
    score_scale = 1.0 / math.sqrt(HEAD_SIZE)
    finals = []

    greet(ctx, fsdp, PLANE_FLIPS + COLUMN_FLIPS + [(6, 0)])

    out_block = out_w_ref.at[
        pl.ds(pl.multiple_of(lax.rem(ctx, 2) * head_columns, head_columns), head_columns)
    ]
    out_target = swap_bits(lax.bitwise_xor(ctx // 2, fsdp))
    out_away = out_target != fsdp
    out_copy = links.to(out_block, out_relay, ctx, out_target)
    out_home = links.here(out_block, out_relay)
    out_flip = 2 * swap_bits(fsdp)
    out_moves = fsdp != 0
    out_last = links.to(out_relay, out_head, lax.bitwise_xor(ctx, out_flip), fsdp)
    out_stays = links.here(out_relay, out_head)

    @pl.when(out_away)
    def _():
        out_copy.start()

    @pl.when(jnp.logical_not(out_away))
    def _():
        out_home.start()

    def rows_of(plane):
        return pl.ds(pl.multiple_of(plane * depth, depth), depth)

    head_parts, places = [], []
    for start, size, place in (
        (ctx * head_columns, head_columns, 0),
        (query_columns + ctx * HEAD_SIZE, HEAD_SIZE, head_columns),
        (query_columns + key_columns + ctx * HEAD_SIZE, HEAD_SIZE, head_columns + HEAD_SIZE),
    ):
        places.append(pl.ds(place, size))
        head_parts.append(
            (
                qkv_w_ref.at[:, pl.ds(pl.multiple_of(start, HEAD_SIZE), size)],
                w_head.at[rows_of(fsdp), pl.ds(place, size)],
            )
        )
    head_far = [links.column(src, dst, 2) for src, dst in head_parts]
    head_near = [links.column(src, dst, 1) for src, dst in head_parts]
    own_head = [links.here(src, dst) for src, dst in head_parts]
    start_all(head_far + head_near + own_head)

    def place_of(j):
        return pl.ds(pl.multiple_of(j * strip, strip), strip)

    def strips(target):
        cols = pl.ds(pl.multiple_of(target * hidden + ctx * strip, strip), strip)
        blocks = pl.ds(fsdp * depth_blocks, depth_blocks)
        for source, dest in ((gate_ref, gate_w), (up_ref, up_w)):
            yield source.at[:, :, cols], dest.at[blocks, :, place_of(ctx)]

    strip_copies = [[links.here(src, dst) for src, dst in strips(fsdp)]]
    for flip in (1, 2, 3):
        strip_copies.append(
            [links.column(s, d, flip) for s, d in strips(lax.bitwise_xor(fsdp, flip))]
        )
    start_all(strip_copies[0])

    def strip_gather(flip):
        first = lax.bitwise_xor(fsdp, flip) * depth_blocks
        blocks = pl.ds(first, depth_blocks)
        return PlaneGather(
            links,
            lambda j: [w.at[blocks, :, place_of(j)] for w in (gate_w, up_w)],
            lambda j, which: [w.at[first + which, :, place_of(j)] for w in (gate_w, up_w)],
        )

    weights = [strip_gather(flip) for flip in range(n_fsdp)]

    inputs = tokens_ref[...].astype(f32)
    scale = lax.rsqrt(jnp.mean(inputs * inputs, axis=-1, keepdims=True) + norm_eps)
    normed[ctx] = (inputs * scale * gain_one_ref[...]).astype(bf16)
    half = rows // 2
    gather = PlaneGather(
        links,
        lambda j: [normed.at[j]],
        lambda j, which: [normed.at[j, pl.ds(which * half, half)]],
    )
    gather.begin()

    place_positions(pair_ref, pos_col_ref, pos_row_ref, rows)
    lane = lax.broadcasted_iota(jnp.int32, (1, HEAD_SIZE), 1)
    lane_half = lax.rem(lane, HEAD_SIZE // 2).astype(f32)
    frequency = jnp.exp(lane_half * (-2.0 * math.log(rope_base) / HEAD_SIZE))
    side = jnp.where(lane < HEAD_SIZE // 2, -1.0, 1.0)

    def tables(step, carry):
        at = pl.ds(pl.multiple_of(step * rows, rows), rows)
        angles = pos_col_ref[at].astype(f32) * frequency
        cos_ref[at] = jnp.cos(angles)
        sin_ref[at] = side * jnp.sin(angles)
        return carry

    lax.fori_loop(0, n_ctx, tables, 0)
    for src, dst in ((cos_ref, cos_out), (sin_ref, sin_out)):
        finals.append(links.here(src, dst))
        finals[-1].start()
    gather.forward()
    weights[0].begin([source for source, dest in strips(fsdp)])
    gather.finish()

    @pl.when(out_away)
    def _():
        out_copy.wait_recv()

    @pl.when(jnp.logical_not(out_away))
    def _():
        out_home.wait()

    @pl.when(out_moves)
    def _():
        out_last.start()

    @pl.when(jnp.logical_not(out_moves))
    def _():
        out_stays.start()

    weights[0].forward()
    cot_copies = [links.column(cot_ref, cot_far, 2), links.column(cot_ref, cot_near, 1)]
    head_relay = []
    far_rows = rows_of(lax.bitwise_xor(fsdp, 2))
    for copy, place in zip(head_far, places):
        copy.wait_recv()
        block = w_head.at[far_rows, place]
        head_relay.append(links.column(block, block, 1))
        head_relay[-1].start()
    start_all(cot_copies[:1])
    weights[0].finish()
    finals.append(links.here(normed, normed_one_out))
    finals[-1].start()
    for copy in own_head:
        copy.wait()
    for copy in head_near + head_relay:
        copy.wait_recv()
    start_all(strip_copies[1] + strip_copies[2] + strip_copies[3])

    block_rows = 2 * rows

    def project(step, carry):
        at = pl.multiple_of(step * block_rows, block_rows)
        tile = normed[pl.ds(step * 2, 2)].reshape(block_rows, width)
        out = jnp.dot(tile, w_head[...], preferred_element_type=f32)
        cos_rows, sin_rows = cos_ref[pl.ds(at, block_rows)], sin_ref[pl.ds(at, block_rows)]
        for column in range(0, head_columns + HEAD_SIZE, HEAD_SIZE):
            turned = turn(out[:, column : column + HEAD_SIZE], cos_rows, sin_rows, 1.0)
            qkv[pl.ds(at, block_rows), pl.ds(column, HEAD_SIZE)] = turned.astype(bf16)
        column = head_columns + HEAD_SIZE
        qkv[pl.ds(at, block_rows), pl.ds(column, HEAD_SIZE)] = out[:, column:].astype(bf16)
        return carry

    lax.fori_loop(0, seq_rows // block_rows, project, 0)
    def attend(step, carry):
        at = pl.multiple_of(step * block_rows, block_rows)
        keys = qkv[:, pl.ds(head_columns, HEAD_SIZE)]
        values = qkv[:, pl.ds(head_columns + HEAD_SIZE, HEAD_SIZE)]
        causal = pos_row_ref[...] <= pos_col_ref[pl.ds(at, block_rows)]
        for column in range(0, head_columns, HEAD_SIZE):
            query = qkv[pl.ds(at, block_rows), pl.ds(column, HEAD_SIZE)]
            scores = contract_last(query, keys) * score_scale
            scores = jnp.where(causal, scores, -1e30)
            shifted = jnp.exp(scores - jnp.max(scores, axis=-1, keepdims=True))
            probs = shifted * (1.0 / jnp.sum(shifted, axis=-1, keepdims=True))
            mixed = jnp.dot(probs.astype(bf16), values, preferred_element_type=f32)
            attended[pl.ds(at, block_rows), pl.ds(column, HEAD_SIZE)] = mixed.astype(bf16)
        return carry

    lax.fori_loop(0, seq_rows // block_rows, attend, 0)

    @pl.when(out_moves)
    def _():
        out_last.wait_recv()

    @pl.when(jnp.logical_not(out_moves))
    def _():
        out_stays.wait()

    for src, dst in (        (qkv, qkv_out),
        (attended, attended_out),
        (w_head, w_head_out),
        (out_head, out_head_out),
    ):
        finals.append(links.here(src, dst))
        finals[-1].start()

    scatter = PlaneScatter(links, part, core_rx, half_rx, side_rx)
    for flip, chip in scatter.order():
        at = pl.multiple_of(chip * block_rows, block_rows)
        out = jnp.dot(
            attended[pl.ds(at, block_rows)], out_head[...], preferred_element_type=f32
        )
        part[pl.ds(chip * 2, 2)] = out.astype(bf16).reshape(2, rows, width)
        scatter.give(flip, chip)

    def arrived(flip):
        for copy in strip_copies[flip]:
            copy.wait_recv()
        weights[flip].begin()

    scatter.begin()
    scatter.middle()
    arrived(1)
    mid = tokens_ref[...].astype(f32) + scatter.finish()
    mid_ref[...] = mid
    mid_scale = lax.rsqrt(jnp.mean(mid * mid, axis=-1, keepdims=True) + norm_eps)
    normed_two[...] = (mid * mid_scale * gain_two_ref[...]).astype(bf16)

    group = LineGather(links, normed_two, normed_two_group)
    group.begin()
    arrived(2)
    weights[1].forward()
    group.forward()
    start_all(cot_copies[1:])
    arrived(3)
    weights[2].forward()
    weights[1].finish()
    weights[3].forward()
    weights[2].finish()
    weights[3].finish()
    group.finish()
    for copy in cot_copies:
        copy.wait()
    for copy in strip_copies[0]:
        copy.wait()

    for copies in [head_far, head_near, head_relay] + strip_copies[1:]:
        for copy in copies:
            copy.wait_send()

    @pl.when(out_away)
    def _():
        out_copy.wait_send()

    @pl.when(out_moves)
    def _():
        out_last.wait_send()

    gather.drain()
    scatter.drain()
    for item in weights:
        item.drain()
    for copy in finals:
        copy.wait()


def attention_forward(
    tokens, cotangent, gain_attn, gain_ffn, qkv_w, w_out, w_gate, w_up, pair_block
):
    f32, bf16 = jnp.float32, jnp.bfloat16
    n_ctx, n_fsdp = lax.axis_size("ctx"), lax.axis_size("fsdp")
    rows, width = tokens.shape
    depth = qkv_w.shape[0]
    hidden = w_gate.shape[1] // n_fsdp
    seq_rows = n_ctx * rows
    head_columns = QUERY_HEADS // KEY_VALUE_HEADS * HEAD_SIZE
    all_columns = head_columns + 2 * HEAD_SIZE
    vmem, hbm = pl.BlockSpec(memory_space=pltpu.VMEM), pl.BlockSpec(memory_space=pl.ANY)
    shape = jax.ShapeDtypeStruct
    return pl.pallas_call(
        attention_kernel,
        name="attention_forward",
        out_shape=[
            shape((rows, width), f32),
            shape((n_fsdp, rows, width), bf16),
            shape((rows, width), bf16),
            shape((rows, width), bf16),
            shape((width // BLOCK, BLOCK, hidden), bf16),
            shape((width // BLOCK, BLOCK, hidden), bf16),
            shape((seq_rows, all_columns), bf16),
            shape((seq_rows, head_columns), bf16),
            shape((n_ctx, rows, width), bf16),
            shape((width, all_columns), bf16),
            shape((head_columns, width), bf16),
            shape((seq_rows, HEAD_SIZE), f32),
            shape((seq_rows, HEAD_SIZE), f32),
        ],
        in_specs=[vmem] * 4 + [hbm] * 4 + [pl.BlockSpec(memory_space=pltpu.SMEM)],
        out_specs=[vmem] + [hbm] * 12,
        scratch_shapes=[
            pltpu.VMEM((n_ctx, rows, width), bf16),
            pltpu.VMEM((width, all_columns), bf16),
            pltpu.VMEM((head_columns, width), bf16),
            pltpu.VMEM((head_columns, width), bf16),
            pltpu.VMEM((seq_rows, all_columns), bf16),
            pltpu.VMEM((seq_rows, head_columns), bf16),
            pltpu.VMEM((n_ctx, rows, width), bf16),
            pltpu.VMEM((n_ctx // 2, rows, width), bf16),
            pltpu.VMEM((2, rows // 2, width), bf16),
            pltpu.VMEM((2, rows, width), bf16),
            pltpu.VMEM((rows, width), bf16),
            pltpu.VMEM((seq_rows, HEAD_SIZE), f32),
            pltpu.VMEM((seq_rows, HEAD_SIZE), f32),
            pltpu.VMEM((seq_rows, 1), jnp.int32),
            pltpu.VMEM((1, seq_rows), jnp.int32),
            pltpu.SemaphoreType.DMA((112,)),
            pltpu.SemaphoreType.DMA((112,)),
            pltpu.SemaphoreType.DMA((16,)),
        ],
        compiler_params=pltpu.CompilerParams(
            collective_id=1, has_side_effects=True, vmem_limit_bytes=58 * 2**20
        ),
    )(
        tokens,
        cotangent,
        gain_attn[None],
        gain_ffn[None],
        qkv_w,
        w_out,
        w_gate.reshape(depth // BLOCK, BLOCK, -1),
        w_up.reshape(depth // BLOCK, BLOCK, -1),
        pair_block,
    )


class ChipScatter:
    def __init__(self, links, parts, halves, sides):
        self.links, self.parts, self.halves, self.sides = links, parts, halves, sides
        self.sent = []

    def _go(self, copy):
        copy.start()
        self.sent.append(copy)
        return copy

    def begin(self, source=None):
        corner = self.parts[3] if source is None else source
        half = corner.shape[0] // 2
        self.half = half
        self.corner = [
            self._go(self.links.plane(corner.at[pl.ds(0, half)], self.halves[0], ACROSS_Y)),
            self._go(self.links.plane(corner.at[pl.ds(half, half)], self.halves[1], ACROSS_X)),
        ]

    def middle(self):
        self.side = []
        for slot, (flip, across) in enumerate(((1, ACROSS_X), (2, ACROSS_Y))):
            mine = self.parts[flip]
            self.corner[slot].wait_recv()
            rows = mine.at[pl.ds(slot * self.half, self.half)]
            rows[...] = (
                rows[...].astype(jnp.float32) + self.halves[slot][...].astype(jnp.float32)
            ).astype(jnp.bfloat16)
            self.side.append(self._go(self.links.plane(mine, self.sides[slot], across)))

    def finish(self):
        mine = self.parts[0]
        for copy in self.side:
            copy.wait_recv()
        mine[...] = (
            mine[...].astype(jnp.float32)
            + self.sides[0][...].astype(jnp.float32)
            + self.sides[1][...].astype(jnp.float32)
        ).astype(jnp.bfloat16)
        return mine

    def drain(self):
        for copy in self.sent:
            copy.wait_send()


def feed_forward_kernel(
    mid_ref,
    cot_ref,
    gain_ref,
    normed_ref,
    cot_near_ref,
    cot_far_ref,
    gate_hbm,
    up_hbm,
    down_hbm,
    result_ref,
    grad_mid_ref,
    grad_proj_ref,
    down_sum,
    gate_sum,
    up_part,
    gate_v,
    up_v,
    down_v,
    cots,
    hidden,
    grad_gate,
    grad_up,
    other_normed,
    other_cots,
    other_hidden,
    other_gate,
    other_up,
    stage,
    landed,
    down_parts,
    down_halves,
    send_sem,
    recv_sem,
    local_sem,
    load_sem,
    down_free,
    gate_free,
):
    f32, bf16 = jnp.float32, jnp.bfloat16
    ctx, fsdp = lax.axis_index("ctx"), lax.axis_index("fsdp")
    links = Links((send_sem, recv_sem, local_sem), ctx, fsdp)
    core = lax.rem(ctx, 2)
    rows, width = mid_ref.shape
    blocks = gate_v.shape[0]
    hidden_units = blocks * BLOCK
    half_units = hidden_units // 2
    n_fsdp = normed_ref.shape[0]
    group_rows = n_fsdp * rows

    def loads(j):
        cols = pl.ds(pl.multiple_of(j * BLOCK, BLOCK), BLOCK)
        return (
            pltpu.make_async_copy(
                gate_hbm.at[:, :, cols], gate_v.at[:, :, cols], load_sem.at[0, j]
            ),
            pltpu.make_async_copy(up_hbm.at[:, :, cols], up_v.at[:, :, cols], load_sem.at[1, j]),
            pltpu.make_async_copy(down_hbm.at[j], down_v.at[j], load_sem.at[2, j]),
        )

    for j in range(blocks):
        for copy in loads(j):
            copy.start()

    greet(ctx, fsdp, PLANE_FLIPS + COLUMN_FLIPS[:2])

    cot_relay = links.column(cot_far_ref, cots.at[3], 1)
    cot_relay.start()
    cots[0] = cot_ref[...]
    cots[1] = cot_far_ref[...]
    cots[2] = cot_near_ref[...]
    mid_load = links.here(mid_ref, grad_mid_ref)
    mid_load.start()

    swaps = [links.plane(normed_ref, other_normed, ACROSS_CORE)]
    cot_swaps = [links.plane(cots.at[s], other_cots.at[s], ACROSS_CORE) for s in range(n_fsdp)]
    start_all(swaps + cot_swaps[:3])

    half_slots, half_rows = n_fsdp // 2, group_rows // 2

    def activate(j, carry):
        for copy in loads(j):
            copy.wait()
        cols = pl.ds(pl.multiple_of(j * BLOCK, BLOCK), BLOCK)
        for first in (0, half_slots):
            at = pl.ds(first * rows, half_rows)
            normed = normed_ref[pl.ds(first, half_slots)].reshape(half_rows, width)
            gate = jnp.dot(
                normed, gate_v[:, :, cols].reshape(width, BLOCK), preferred_element_type=f32
            )
            up = jnp.dot(
                normed, up_v[:, :, cols].reshape(width, BLOCK), preferred_element_type=f32
            )
            sig = jax.nn.sigmoid(gate)
            silu = gate * sig
            hidden[at, cols] = (silu * up).astype(bf16)
            grad_gate[at, cols] = (up * (sig * (1.0 + gate * (1.0 - sig)))).astype(bf16)
            grad_up[at, cols] = silu.astype(bf16)
        return carry

    lax.fori_loop(0, blocks, activate, 0)

    hidden_acts = []
    for pair in range(blocks // 2):
        cols = pl.ds(pl.multiple_of((2 * pair + 1 - core) * BLOCK, BLOCK), BLOCK)
        hidden_acts.append(
            links.plane(
                hidden.at[:, cols], other_hidden.at[:, pl.ds(pair * BLOCK, BLOCK)], ACROSS_CORE
            )
        )
    start_all(hidden_acts)
    piece = 2 * BLOCK
    pieces = width // piece

    def spot(n):
        return pl.ds(n * piece, piece)

    def put(which, first, n, value):
        stage[which, pl.ds(first, half_slots), :, spot(n)] = value.astype(bf16).reshape(
            half_slots, rows, piece
        )

    def down_out(first, n):
        value = jnp.dot(
            hidden[pl.ds(first * rows, half_rows)],
            down_v[:, :, spot(n)].reshape(hidden_units, piece),
            preferred_element_type=f32,
        )
        put(0, first, n, value)

    def back_out(first, n):
        at, some = pl.ds(first * rows, half_rows), pl.ds(n * 2, 2)
        value = contract_last(grad_gate[at], gate_v[some].reshape(piece, hidden_units))
        value = value + contract_last(grad_up[at], up_v[some].reshape(piece, hidden_units))
        put(1, first, n, value)

    near, far = {}, []

    def send_near(which, n):
        near[which, n] = [
            links.column(stage.at[which, 3, :, spot(n)], landed.at[which, 1, :, spot(n)], 1),
            links.column(stage.at[which, 2, :, spot(n)], landed.at[which, 0, :, spot(n)], 1),
        ]
        start_all(near[which, n])

    def relay(which, n):
        near[which, n][0].wait_recv()
        stage[which, 1, :, spot(n)] = (
            stage[which, 1, :, spot(n)].astype(f32) + landed[which, 1, :, spot(n)].astype(f32)
        ).astype(bf16)
        copy = links.column(stage.at[which, 1, :, spot(n)], landed.at[which, 2, :, spot(n)], 2)
        copy.start()
        far.append(copy)

    for n in range(pieces):
        down_out(half_slots, n)
        send_near(0, n)
        down_out(0, n)

    def activation_grads(first):
        at = pl.ds(first * rows, half_rows)

        def step(j, carry):
            cols = pl.ds(pl.multiple_of(j * BLOCK, BLOCK), BLOCK)
            cot_rows = cots[pl.ds(first, half_slots)].reshape(half_rows, width)
            grad_hidden = contract_last(cot_rows, down_v[j])
            grad_gate[at, cols] = (grad_gate[at, cols].astype(f32) * grad_hidden).astype(bf16)
            grad_up[at, cols] = (grad_up[at, cols].astype(f32) * grad_hidden).astype(bf16)
            return carry

        lax.fori_loop(0, blocks, step, 0)

    for copy in [cot_relay]:
        copy.wait_recv()
    start_all(cot_swaps[3:])
    def flat(ref, cols):
        return ref[:, :, cols].reshape(group_rows, -1)

    for copy in cot_swaps + hidden_acts:
        copy.wait_recv()

    def down_block(pair, place):
        own = pl.ds(pl.multiple_of((2 * pair + core) * BLOCK, BLOCK), BLOCK)
        other = pl.ds(pl.multiple_of(pair * BLOCK, BLOCK), BLOCK)
        left, right = hidden[:, own].T, other_hidden[:, other].T
        for cols in (pl.ds(0, width // 2), pl.ds(width // 2, width // 2)):
            total = jnp.dot(left, flat(cots, cols), preferred_element_type=f32)
            total = total + jnp.dot(right, flat(other_cots, cols), preferred_element_type=f32)
            place[:, cols] = total.astype(bf16)

    def halves_of(ref):
        return [ref.at[pl.ds(0, BLOCK // 2)], ref.at[pl.ds(BLOCK // 2, BLOCK // 2)]]

    chip = ctx // 2
    down_scatter = ChipScatter(
        links,
        [down_v.at[2]] + [down_parts.at[flip - 1] for flip in (1, 2, 3)],
        halves_of(down_halves),
        [down_v.at[0], down_v.at[1]],
    )
    down_block(lax.bitwise_xor(chip, 3), down_parts.at[2])
    down_scatter.begin()

    def down_side(flip, carry):
        down_block(lax.bitwise_xor(chip, flip), down_parts.at[flip - 1])
        return carry

    lax.fori_loop(1, 3, down_side, 0)
    activation_grads(0)
    activation_grads(half_slots)
    down_block(chip, down_v.at[2])
    theirs = pl.ds(pl.multiple_of((1 - core) * half_units, half_units), half_units)
    acts = [
        links.plane(grad_gate.at[:, theirs], other_gate, ACROSS_CORE),
        links.plane(grad_up.at[:, theirs], other_up, ACROSS_CORE),
    ]
    start_all(acts)

    def free(sem):
        for flip in (ACROSS_X, ACROSS_Y):
            pl.semaphore_signal(
                sem,
                inc=1,
                device_id=(lax.bitwise_xor(ctx, flip), fsdp),
                device_id_type=MESH,
            )

    free(down_free)
    pl.semaphore_wait(down_free, 2)
    down_scatter.middle()

    for n in range(pieces):
        back_out(half_slots, n)
        send_near(1, n)
    for n in range(pieces):
        back_out(0, n)
    free(gate_free)
    relay(0, 0)
    relay(0, 1)

    mine = pl.ds(pl.multiple_of(core * half_units, half_units), half_units)

    def weight_block(b, carry):
        cols = pl.ds(pl.multiple_of(b * BLOCK, BLOCK), BLOCK)
        left, right = flat(normed_ref, cols).T, flat(other_normed, cols).T
        plane, first = b // 2, 2 * lax.rem(b, 2)
        at_row = pl.ds(pl.multiple_of((plane // 2) * (BLOCK // 2), BLOCK // 2), BLOCK // 2)
        at_col = pl.ds(pl.multiple_of(lax.rem(plane, 2) * (width // 2), width // 2), width // 2)
        for own_grad, other_grad, place in (
            (grad_gate, other_gate, gate_v),
            (grad_up, other_up, up_v),
        ):
            total = jnp.dot(left, own_grad[:, mine], preferred_element_type=f32)
            total = total + jnp.dot(right, other_grad[...], preferred_element_type=f32)
            low = total.astype(bf16)
            place[first, at_row, at_col] = low[: BLOCK // 2]
            place[first + 1, at_row, at_col] = low[BLOCK // 2 :]
        return carry

    for copy in swaps + acts:
        copy.wait_recv()
    lax.fori_loop(0, blocks // 2, weight_block, 0)
    relay(0, 2)
    lax.fori_loop(blocks // 2, blocks, weight_block, 0)
    pl.semaphore_wait(gate_free, 2)
    gate_scatter = ChipScatter(
        links,
        [gate_v.at[lax.bitwise_xor(chip, flip)] for flip in range(4)],
        halves_of(gate_v.at[4]),
        [gate_v.at[5], gate_v.at[6]],
    )
    gate_scatter.begin()
    up_copy = links.here(up_v.at[pl.ds(0, 4)], up_part)
    up_copy.start()
    relay(0, 3)
    relay(1, 0)
    relay(1, 1)
    relay(1, 2)
    relay(1, 3)
    gate_scatter.middle()
    down_copy = links.here(down_scatter.finish(), down_sum)
    down_copy.start()

    for copy in [pair[1] for pair in near.values()] + far:
        copy.wait_recv()
    for copies in near.values():
        for copy in copies:
            copy.wait_send()
    mid_load.wait()
    chunk = 32

    def close(step, carry):
        at = pl.ds(pl.multiple_of(step * chunk, chunk), chunk)

        def summed(which):
            total = stage[which, 0, at].astype(f32) + landed[which, 0, at].astype(f32)
            return total + landed[which, 2, at].astype(f32)

        mid = grad_mid_ref[at]
        stage[0, 2, at] = (mid + summed(0)).astype(bf16)
        scale = lax.rsqrt(jnp.mean(mid * mid, axis=-1, keepdims=True) + norm_eps)
        u = summed(1) * gain_ref[...]
        inner = jnp.mean(u * mid, axis=-1, keepdims=True)
        grad_mid = (
            cots[0, at].astype(f32) + scale * u - mid * (scale * scale * scale * inner)
        )
        grad_mid_ref[at] = grad_mid
        stage[1, 2, at] = grad_mid.astype(bf16)
        return carry

    lax.fori_loop(0, rows // chunk, close, 0)
    row_copies = [
        links.here(stage.at[0, 2], result_ref),
        links.here(stage.at[1, 2], grad_proj_ref),
    ]
    start_all(row_copies)

    gate_copy = links.here(gate_scatter.finish(), gate_sum)
    gate_copy.start()
    sent = far + swaps + cot_swaps
    for copy in sent + hidden_acts + acts + [cot_relay]:
        copy.wait_send()
    down_scatter.drain()
    gate_scatter.drain()
    for copy in row_copies + [up_copy, down_copy, gate_copy]:
        copy.wait()


def feed_forward(
    mid, cotangent, gain_ffn, normed_group, cot_near, cot_far, gate_w, up_w, w_down
):
    f32, bf16 = jnp.float32, jnp.bfloat16
    n_fsdp = lax.axis_size("fsdp")
    rows, width = mid.shape
    group_rows = n_fsdp * rows
    units = w_down.shape[0] * BLOCK
    blocks = units // BLOCK
    vmem, hbm = pl.BlockSpec(memory_space=pltpu.VMEM), pl.BlockSpec(memory_space=pl.ANY)
    shape = jax.ShapeDtypeStruct
    return pl.pallas_call(
        feed_forward_kernel,
        name="feed_forward",
        out_shape=[
            shape((rows, width), bf16),
            shape((rows, width), f32),
            shape((rows, width), bf16),
            shape((BLOCK, width), bf16),
            shape((BLOCK, width), bf16),
            shape((blocks // 2, BLOCK, width), bf16),
        ],
        in_specs=[hbm] + [vmem] * 5 + [hbm] * 3,
        out_specs=[hbm, vmem, hbm] + [hbm] * 3,
        scratch_shapes=[
            pltpu.VMEM((width // BLOCK, BLOCK, units), bf16),
            pltpu.VMEM((width // BLOCK, BLOCK, units), bf16),
            pltpu.VMEM((blocks, BLOCK, width), bf16),
            pltpu.VMEM((n_fsdp, rows, width), bf16),
            pltpu.VMEM((group_rows, units), bf16),
            pltpu.VMEM((group_rows, units), bf16),
            pltpu.VMEM((group_rows, units), bf16),
            pltpu.VMEM((n_fsdp, rows, width), bf16),
            pltpu.VMEM((n_fsdp, rows, width), bf16),
            pltpu.VMEM((group_rows, units // 2), bf16),
            pltpu.VMEM((group_rows, units // 2), bf16),
            pltpu.VMEM((group_rows, units // 2), bf16),
            pltpu.VMEM((2, n_fsdp, rows, width), bf16),
            pltpu.VMEM((2, n_fsdp - 1, rows, width), bf16),
            pltpu.VMEM((blocks // 2 - 1, BLOCK, width), bf16),
            pltpu.VMEM((BLOCK, width), bf16),
            pltpu.SemaphoreType.DMA((48,)),
            pltpu.SemaphoreType.DMA((48,)),
            pltpu.SemaphoreType.DMA((8,)),
            pltpu.SemaphoreType.DMA((3, blocks)),
            pltpu.SemaphoreType.REGULAR,
            pltpu.SemaphoreType.REGULAR,
        ],
        compiler_params=pltpu.CompilerParams(
            collective_id=2, has_side_effects=True, vmem_limit_bytes=62 * 2**20
        ),
    )(mid, cotangent, gain_ffn[None], normed_group, cot_near, cot_far, gate_w, up_w, w_down)


def attention_back_kernel(
    grad_proj_ref,
    grad_mid_ref,
    tokens_ref,
    gain_ref,
    w_head_ref,
    out_head_ref,
    qkv_ref,
    attended_ref,
    cos_ref,
    sin_ref,
    pair_ref,
    normed_hbm,
    gate_sum_hbm,
    up_part_hbm,
    grad_input_ref,
    qkv_sum,
    out_sum,
    gate_out,
    up_out,
    proj,
    normed,
    up_part,
    up_halves,
    up_sides,
    grad_att,
    grads,
    key_grad,
    value_grad,
    part,
    core_rx,
    half_rx,
    side_rx,
    out_stage,
    out_landed,
    out_summed,
    head_stage,
    head_summed,
    head_landed,
    pos_col_ref,
    pos_row_ref,
    send_sem,
    recv_sem,
    local_sem,
):
    f32, bf16 = jnp.float32, jnp.bfloat16
    ctx, fsdp = lax.axis_index("ctx"), lax.axis_index("fsdp")
    links = Links((send_sem, recv_sem, local_sem), ctx, fsdp)
    chip, core = ctx // 2, lax.rem(ctx, 2)
    n_ctx, rows, width = proj.shape
    n_fsdp = out_landed.shape[0]
    seq_rows = n_ctx * rows
    head_columns = out_head_ref.shape[0]
    strip_rows = out_landed.shape[1]
    score_scale = 1.0 / math.sqrt(HEAD_SIZE)
    loads = [links.here(normed_hbm, normed), links.here(up_part_hbm, up_part)]
    for copy in loads:
        copy.start()

    flips = [(a, 0) for a in range(1, n_ctx)] + COLUMN_FLIPS + [(1, b) for b in (1, 2, 3)]
    greet(ctx, fsdp, flips)

    proj[ctx] = grad_proj_ref[...]
    half = rows // 2
    gather = PlaneGather(
        links,
        lambda j: [proj.at[j]],
        lambda j, which: [proj.at[j, pl.ds(which * half, half)]],
    )
    gather.begin()
    place_positions(pair_ref, pos_col_ref, pos_row_ref, rows)

    def spread(source, dest):
        half_width = width // 2
        place = pl.ds(pl.multiple_of((2 * fsdp + core) * half_width, half_width), half_width)
        copies = []
        for a in (0, 1):
            for b in range(n_fsdp):
                plane = lax.bitwise_xor(fsdp, b)
                who = lax.bitwise_xor(core, a)
                at_row = (plane // 2) * (BLOCK // 2) + who * strip_rows
                block = source.at[
                    pl.ds(pl.multiple_of(at_row, strip_rows), strip_rows),
                    pl.ds(pl.multiple_of(lax.rem(plane, 2) * half_width, half_width), half_width),
                ]
                target = dest.at[:, place]
                if a or b:
                    copies.append(
                        links.to(block, target, lax.bitwise_xor(ctx, a), plane)
                    )
                else:
                    local = links.here(block, target)
                    locals_.append(local)
                    local.start()
        for copy in copies:
            copy.start()
        return copies

    locals_ = []
    up_scatter = ChipScatter(
        links,
        [up_part.at[lax.bitwise_xor(chip, flip)] for flip in range(4)],
        [up_halves.at[0], up_halves.at[1]],
        [up_sides.at[0], up_sides.at[1]],
    )
    gate_copies = spread(gate_sum_hbm, gate_out)
    gather.forward()
    gather.finish()

    total = jnp.zeros((head_columns, width), f32)
    for j in range(0, n_ctx, 2):
        total = total + lax.dot_general(
            attended_ref[pl.ds(j * rows, 2 * rows)],
            proj[pl.ds(j, 2)].reshape(2 * rows, width),
            (((0,), (0,)), ((), ())),
            preferred_element_type=f32,
        )
    out_stage[...] = total.astype(bf16).reshape(out_stage.shape)
    half_ctx = n_ctx // 2
    out_base = links.remote
    links.remote += half_ctx
    out_copies = []
    for j in range(half_ctx):
        target = half_ctx * core + j
        copy = pltpu.make_async_remote_copy(
            src_ref=out_stage.at[j],
            dst_ref=out_landed.at[chip],
            send_sem=send_sem.at[out_base + j],
            recv_sem=recv_sem.at[out_base + chip],
            device_id=(target, fsdp),
            device_id_type=MESH,
        )
        out_copies.append((target != ctx, copy))

        @pl.when(target != ctx)
        def _(copy=copy):
            copy.start()

    own_out = links.here(out_stage.at[lax.rem(ctx, half_ctx)], out_landed.at[chip])
    out_own_chip = lax.rem(ctx, 2) == ctx // half_ctx

    @pl.when(out_own_chip)
    def _():
        own_out.start()

    up_scatter.begin(up_part_hbm.at[lax.bitwise_xor(chip, 3)])

    def out_arrivals():
        for source in range(half_ctx):
            arrival = pltpu.make_async_remote_copy(
                src_ref=out_stage.at[0],
                dst_ref=out_landed.at[source],
                send_sem=send_sem.at[out_base],
                recv_sem=recv_sem.at[out_base + source],
                device_id=(lax.bitwise_xor(ctx, 1), fsdp),
                device_id_type=MESH,
            )

            @pl.when(2 * source + ctx // half_ctx != ctx)
            def _(arrival=arrival):
                arrival.wait_recv()

        @pl.when(out_own_chip)
        def _():
            own_out.wait()

    def out_begin():
        out_arrivals()
        copies = [
            links.column(
                out_landed.at[lax.bitwise_xor(fsdp, flip)], out_summed.at[slot], 1
            )
            for flip, slot in ((3, 1), (1, 0))
        ]
        start_all(copies)
        return copies

    def out_relay(copies):
        copies[0].wait_recv()
        across = lax.bitwise_xor(fsdp, 2)
        out_landed[across] = (
            out_landed[across].astype(f32) + out_summed[1].astype(f32)
        ).astype(bf16)
        copy = links.column(out_landed.at[across], out_summed.at[2], 2)
        copy.start()
        return copy

    def back(step, carry):
        at = pl.multiple_of(step * 2 * rows, 2 * rows)
        tile = proj[pl.ds(2 * step, 2)].reshape(2 * rows, width)
        grad_att[pl.ds(at, 2 * rows)] = contract_last(tile, out_head_ref[...]).astype(bf16)
        return carry

    lax.fori_loop(0, n_ctx // 2, back, 0)

    key_grad[...] = jnp.zeros_like(key_grad)
    value_grad[...] = jnp.zeros_like(value_grad)

    def attend_head(column):
        cols = pl.ds(column, HEAD_SIZE)

        def step(index, carry):
            at = pl.ds(pl.multiple_of(index * 2 * rows, 2 * rows), 2 * rows)
            keys = qkv_ref[:, pl.ds(head_columns, HEAD_SIZE)]
            values = qkv_ref[:, pl.ds(head_columns + HEAD_SIZE, HEAD_SIZE)]
            causal = pos_row_ref[...] <= pos_col_ref[at]
            query, grad_mixed = qkv_ref[at, cols], grad_att[at, cols]
            scores = contract_last(query, keys) * score_scale
            scores = jnp.where(causal, scores, -1e30)
            shifted = jnp.exp(scores - jnp.max(scores, axis=-1, keepdims=True))
            probs = shifted * (1.0 / jnp.sum(shifted, axis=-1, keepdims=True))
            grad_probs = contract_last(grad_mixed, values)
            delta = jnp.sum(grad_probs * probs, axis=-1, keepdims=True)
            grad_scores = (probs * (grad_probs - delta)).astype(bf16)
            value_grad[...] += contract_first(probs.astype(bf16), grad_mixed)
            key_grad[...] += contract_first(grad_scores, query)
            grad_query = jnp.dot(grad_scores, keys, preferred_element_type=f32) * score_scale
            grads[at, cols] = turn(grad_query, cos_ref[at], sin_ref[at], -1.0).astype(bf16)
            return carry

        lax.fori_loop(0, n_ctx // 2, step, 0)

    depth = n_ctx * strip_rows
    head_near, head_far = [], []

    def head_part(cols, slot):
        flip = (0, 2, 1, 3)[slot]
        places = pl.ds(pl.multiple_of(lax.bitwise_xor(fsdp, flip) * depth, depth), depth)
        total = contract_first(normed[:, :, places].reshape(seq_rows, depth), grads[:, cols])
        head_stage[slot, :, :, cols] = total.astype(bf16).reshape(n_ctx, strip_rows, -1)

    def head_begin(cols):
        copies = []
        for slot in (3, 2):
            head_part(cols, slot)
            copy = links.flip(
                head_stage.at[slot, :, :, cols],
                head_summed.at[slot - 2, :, :, cols],
                0,
                1,
            )
            copy.start()
            copies.append(copy)
        head_near.append(copies)
        for slot in (1, 0):
            head_part(cols, slot)

    def head_relay(index, cols):
        head_near[index][0].wait_recv()
        head_stage[1, :, :, cols] = (
            head_stage[1, :, :, cols].astype(f32) + head_summed[1, :, :, cols].astype(f32)
        ).astype(bf16)
        copy = links.flip(
            head_stage.at[1, :, :, cols], head_summed.at[2, :, :, cols], 0, 2
        )
        copy.start()
        head_far.append(copy)

    first_cols = pl.ds(0, HEAD_SIZE)
    rest_cols = pl.ds(HEAD_SIZE, grads.shape[1] - HEAD_SIZE)
    attend_head(0)
    loads[0].wait()
    head_begin(first_cols)
    out_near = out_begin()
    for column in range(HEAD_SIZE, head_columns, HEAD_SIZE):
        attend_head(column)
    loads[1].wait()
    up_scatter.middle()
    turned = turn(key_grad[...] * score_scale, cos_ref[...], sin_ref[...], -1.0)
    grads[:, pl.ds(head_columns, HEAD_SIZE)] = turned.astype(bf16)
    grads[:, pl.ds(head_columns + HEAD_SIZE, HEAD_SIZE)] = value_grad[...].astype(bf16)
    head_begin(rest_cols)

    scatter = PlaneScatter(links, part, core_rx, half_rx, side_rx)
    for flip, q in scatter.order():
        at = pl.multiple_of(q * 2 * rows, 2 * rows)
        out = contract_last(grads[pl.ds(at, 2 * rows)], w_head_ref[...])
        part[pl.ds(2 * q, 2)] = out.astype(bf16).reshape(2, rows, width)
        scatter.give(flip, q)

    scatter.begin()
    head_relay(0, first_cols)
    out_far = out_relay(out_near)
    head_relay(1, rest_cols)
    up_copies = spread(up_scatter.finish(), up_out)
    scatter.middle()
    grad_normed = scatter.finish()
    inputs = tokens_ref[...].astype(f32)
    scale = lax.rsqrt(jnp.mean(inputs * inputs, axis=-1, keepdims=True) + norm_eps)
    u = grad_normed * gain_ref[...]
    inner = jnp.mean(u * inputs, axis=-1, keepdims=True)
    grad_input_ref[...] = (
        grad_mid_ref[...] + scale * u - inputs * (scale * scale * scale * inner)
    )
    for copy in [pair[1] for pair in head_near] + head_far:
        copy.wait_recv()
    head_stage[0] = (
        head_stage[0].astype(f32) + head_summed[0].astype(f32) + head_summed[2].astype(f32)
    ).astype(bf16)
    head_copies = [
        links.plane(
            head_stage.at[0, lax.bitwise_xor(ctx, a)], head_landed.at[ctx], a
        )
        for a in range(1, n_ctx)
    ]
    start_all(head_copies)
    head_landed[ctx] = head_stage[0, ctx]

    for copy in (out_near[1], out_far):
        copy.wait_recv()
    out_sum[...] = (
        out_landed[fsdp].astype(f32) + out_summed[0].astype(f32) + out_summed[2].astype(f32)
    )
    for copy in head_copies:
        copy.wait_recv()
    for copy in locals_:
        copy.wait()
    query_columns = QUERY_HEADS * HEAD_SIZE
    key_columns = KEY_VALUE_HEADS * HEAD_SIZE
    for head in range(KEY_VALUE_HEADS):
        total = head_landed[head].astype(f32)
        qkv_sum[:, pl.ds(head * head_columns, head_columns)] = total[:, :head_columns]
        qkv_sum[:, pl.ds(query_columns + head * HEAD_SIZE, HEAD_SIZE)] = total[
            :, head_columns : head_columns + HEAD_SIZE
        ]
        qkv_sum[:, pl.ds(query_columns + key_columns + head * HEAD_SIZE, HEAD_SIZE)] = total[
            :, head_columns + HEAD_SIZE :
        ]
    for copy in gate_copies + up_copies:
        copy.wait_recv()
    for copy in gate_copies + up_copies + head_copies + head_far + head_near[0] + head_near[1]:
        copy.wait_send()
    for copy in out_near + [out_far]:
        copy.wait_send()
    for away, copy in out_copies:

        @pl.when(away)
        def _(copy=copy):
            copy.wait_send()

    gather.drain()
    scatter.drain()
    up_scatter.drain()


def attention_back(
    grad_proj,
    grad_mid,
    tokens,
    gain_attn,
    w_head,
    out_head,
    qkv,
    attended,
    cos,
    sin,
    pair_block,
    normed,
    gate_sum,
    up_part,
):
    f32, bf16 = jnp.float32, jnp.bfloat16
    n_ctx, n_fsdp = lax.axis_size("ctx"), lax.axis_size("fsdp")
    rows, width = tokens.shape
    seq_rows = n_ctx * rows
    strip_rows = width // (n_ctx * n_fsdp)
    head_columns, all_columns = attended.shape[1], qkv.shape[1]
    vmem, hbm = pl.BlockSpec(memory_space=pltpu.VMEM), pl.BlockSpec(memory_space=pl.ANY)
    shape = jax.ShapeDtypeStruct
    return pl.pallas_call(
        attention_back_kernel,
        name="attention_back",
        out_shape=[
            shape((rows, width), f32),
            shape((strip_rows, (QUERY_HEADS + 2 * KEY_VALUE_HEADS) * HEAD_SIZE), f32),
            shape((strip_rows, width), f32),
            shape((strip_rows, n_fsdp * width), bf16),
            shape((strip_rows, n_fsdp * width), bf16),
        ],
        in_specs=[vmem] * 10 + [pl.BlockSpec(memory_space=pltpu.SMEM)] + [hbm] * 3,
        out_specs=[vmem] * 3 + [hbm] * 2,
        scratch_shapes=[
            pltpu.VMEM((n_ctx, rows, width), bf16),
            pltpu.VMEM((n_ctx, rows, width), bf16),
            pltpu.VMEM(up_part.shape, bf16),
            pltpu.VMEM((2, BLOCK // 2, width), bf16),
            pltpu.VMEM((2, BLOCK, width), bf16),
            pltpu.VMEM((seq_rows, head_columns), bf16),
            pltpu.VMEM((seq_rows, all_columns), bf16),
            pltpu.VMEM((seq_rows, HEAD_SIZE), f32),
            pltpu.VMEM((seq_rows, HEAD_SIZE), f32),
            pltpu.VMEM((n_ctx, rows, width), bf16),
            pltpu.VMEM((n_ctx // 2, rows, width), bf16),
            pltpu.VMEM((2, rows // 2, width), bf16),
            pltpu.VMEM((2, rows, width), bf16),
            pltpu.VMEM((n_ctx // 2, strip_rows, width), bf16),
            pltpu.VMEM((n_fsdp, strip_rows, width), bf16),
            pltpu.VMEM((n_fsdp - 1, strip_rows, width), bf16),
            pltpu.VMEM((n_fsdp, n_ctx, strip_rows, all_columns), bf16),
            pltpu.VMEM((n_fsdp - 1, n_ctx, strip_rows, all_columns), bf16),
            pltpu.VMEM((n_ctx, strip_rows, all_columns), bf16),
            pltpu.VMEM((seq_rows, 1), jnp.int32),
            pltpu.VMEM((1, seq_rows), jnp.int32),
            pltpu.SemaphoreType.DMA((96,)),
            pltpu.SemaphoreType.DMA((96,)),
            pltpu.SemaphoreType.DMA((8,)),
        ],
        compiler_params=pltpu.CompilerParams(
            collective_id=3, has_side_effects=True, vmem_limit_bytes=62 * 2**20
        ),
    )(
        grad_proj,
        grad_mid,
        tokens,
        gain_attn[None],
        w_head,
        out_head,
        qkv,
        attended,
        cos,
        sin,
        pair_block,
        normed,
        gate_sum,
        up_part,
    )


def copier(sem):
    copies = []

    def copy(source, dest):
        copies.append(pltpu.make_async_copy(source, dest, sem.at[len(copies)]))
        copies[-1].start()
        return copies[-1]

    return copy


def widen_kernel(gain_attn, gain_ffn, qkv, gate, up, qkv_hbm, gate_hbm, up_hbm, *refs):
    (qkv_out, gate_out, up_out, sums_ref), refs = refs[:4], refs[4:]
    (qkv_v, gate_v, up_v, qkv_w, gate_w, up_w, gate_f, up_f, sem) = refs
    f32 = jnp.float32
    rows = gate_w.shape[0]
    ctx, fsdp = lax.axis_index("ctx"), lax.axis_index("fsdp")
    at = pl.ds(pl.multiple_of(ctx * rows, rows), rows)
    copy = copier(sem)
    loads, stores = [], []
    for source, dest, weight, rows_v in (
        (gate, gate_v, gate_hbm, gate_w),
        (up, up_v, up_hbm, up_w),
        (qkv, qkv_v, qkv_hbm, qkv_w),
    ):
        loads.append((copy(source, dest), copy(weight.at[at], rows_v)))

    def widen(index, source, weight, wide, out):
        for load in loads[index]:
            load.wait()
        values = source[...].astype(f32)
        if wide is None:
            stores.append(copy(source, out))
        else:
            wide[...] = values
            stores.append(copy(wide, out))
        return jnp.sum(weight[...].astype(f32) * values, axis=1, keepdims=True)

    ffn = widen(0, gate_v, gate_w, gate_f, gate_out)
    ffn = ffn + widen(1, up_v, up_w, up_f, up_out)
    attn = widen(2, qkv_v, qkv_w, None, qkv_out)
    which = fsdp * lax.axis_size("ctx") + ctx
    lanes = pl.ds(pl.multiple_of((which // 2) * 2 * rows, 2 * rows), 2 * rows)
    for index, (total, gain_ref) in enumerate(((attn, gain_attn), (ffn, gain_ffn))):
        turned = jnp.broadcast_to(total, (rows, HEAD_SIZE)).T
        gain = gain_ref[:, lanes]
        gain = jnp.where(lax.rem(which, 2) == 1, pltpu.roll(gain, rows, 1), gain)
        sums_ref[pl.ds(index, 1)] = turned[:1] / gain[:, :rows]
    for store in stores:
        store.wait()


def widen(qkv_sum, gate_low, up_low, qkv_w, w_gate, w_up, gain_attn, gain_ffn):
    f32, bf16 = jnp.float32, jnp.bfloat16
    rows = gate_low.shape[0]
    vmem, hbm = pl.BlockSpec(memory_space=pltpu.VMEM), pl.BlockSpec(memory_space=pl.ANY)
    arrays = (qkv_sum, gate_low, up_low)
    return pl.pallas_call(
        widen_kernel,
        name="widen",
        out_shape=[jax.ShapeDtypeStruct(a.shape, f32) for a in arrays]
        + [jax.ShapeDtypeStruct((2, rows), f32)],
        in_specs=[vmem] * 2 + [hbm] * 6,
        out_specs=[hbm] * 3 + [vmem],
        scratch_shapes=[pltpu.VMEM(a.shape, a.dtype) for a in arrays]
        + [pltpu.VMEM(a.shape, bf16) for a in arrays]
        + [pltpu.VMEM(a.shape, f32) for a in (gate_low, up_low)]
        + [pltpu.SemaphoreType.DMA((9,))],
        compiler_params=pltpu.CompilerParams(vmem_limit_bytes=62 * 2**20),
    )(gain_attn[None], gain_ffn[None], *arrays, qkv_w, w_gate, w_up)


def pass_on_kernel(count, *refs):
    sources, outs, held, (wide, sem) = (
        refs[: count + 1],
        refs[count + 1 : 2 * count + 2],
        refs[2 * count + 2 : 3 * count + 3],
        refs[3 * count + 3 :],
    )
    copy = copier(sem)
    loads = [copy(source, dest) for source, dest in zip(sources, held)]
    stores = []
    for load, source, dest in zip(loads, held, outs):
        load.wait()
        if len(stores) == count:
            wide[...] = source[...].astype(jnp.float32)
            source = wide
        stores.append(copy(source, dest))
    for store in stores:
        store.wait()


def pass_on(passed, last):
    hbm = pl.BlockSpec(memory_space=pl.ANY)
    count = len(passed)
    arrays = list(passed) + [last]
    kinds = [a.dtype for a in passed] + [jnp.float32]
    moved = 2 * sum(a.size * a.dtype.itemsize for a in arrays)
    return pl.pallas_call(
        functools.partial(pass_on_kernel, count),
        name="pass_on",
        out_shape=[jax.ShapeDtypeStruct(a.shape, kind) for a, kind in zip(arrays, kinds)],
        in_specs=[hbm] * (count + 1),
        out_specs=[hbm] * (count + 1),
        scratch_shapes=[pltpu.VMEM(a.shape, a.dtype) for a in arrays]
        + [pltpu.VMEM(last.shape, jnp.float32), pltpu.SemaphoreType.DMA((2 * count + 2,))],
        compiler_params=pltpu.CompilerParams(vmem_limit_bytes=62 * 2**20),
        cost_estimate=pl.CostEstimate(flops=last.size, bytes_accessed=moved, transcendentals=0),
    )(*arrays)


def local_heads(
    tokens,
    cotangent,
    gain_attn,
    gain_ffn,
    query_key_value_weight,
    w_out,
    w_gate,
    w_up,
    w_down,
    pair_block,
):
    n_ctx, n_fsdp = lax.axis_size("ctx"), lax.axis_size("fsdp")
    width = tokens.shape[1]
    depth = query_key_value_weight.shape[0]

    (
        mid,
        normed_two_group,
        cot_near,
        cot_far,
        gate_w,
        up_w,
        qkv,
        attended,
        normed_one_seq,
        w_head,
        out_head,
        cos,
        sin,
    ) = attention_forward(
        tokens,
        cotangent,
        gain_attn,
        gain_ffn,
        query_key_value_weight,
        w_out,
        w_gate,
        w_up,
        pair_block,
    )
    result, grad_mid, grad_proj, down_sum, gate_sum, up_part = feed_forward(
        mid,
        cotangent,
        gain_ffn,
        normed_two_group,
        cot_near,
        cot_far,
        gate_w,
        up_w,
        w_down.reshape(-1, BLOCK, width),
    )
    grad_input, qkv_sum, grad_out, gate_low, up_low = attention_back(
        grad_proj,
        grad_mid,
        tokens,
        gain_attn,
        w_head,
        out_head,
        qkv,
        attended,
        cos,
        sin,
        pair_block,
        normed_one_seq,
        gate_sum,
        up_part,
    )
    grad_qkv, grad_gate, grad_up, sums = widen(
        qkv_sum, gate_low, up_low, query_key_value_weight, w_gate, w_up, gain_attn, gain_ffn
    )
    result, grad_input, grad_out, grad_down = pass_on((result, grad_input, grad_out), down_sum)
    gain_pairs = [(c * n_fsdp + f, f * n_ctx + c) for c in range(n_ctx) for f in range(n_fsdp)]
    grad_gain_attn, grad_gain_ffn = lax.ppermute(sums, ("ctx", "fsdp"), gain_pairs)
    return (
        result,
        grad_input,
        grad_gain_attn,
        grad_gain_ffn,
        grad_qkv,
        grad_out,
        grad_gate,
        grad_up,
        grad_down,
    )


def solution(mesh):
    fits = mesh.shape["ctx"] == KEY_VALUE_HEADS and mesh.shape["fsdp"] == KEY_VALUE_HEADS // 2
    local = local_heads if fits else local_general
    return jax.shard_map(
        local,
        mesh=mesh,
        in_specs=(
            P(("ctx", "fsdp"), None),
            P(("ctx", "fsdp"), None),
            P(),
            P(),
            P("fsdp", None),
            P("fsdp", None),
            P("fsdp", None),
            P("fsdp", None),
            P("fsdp", None),
            P(),
        ),
        out_specs=(
            P(("ctx", "fsdp"), None),
            P(("ctx", "fsdp"), None),
            P(("ctx", "fsdp")),
            P(("ctx", "fsdp")),
            P(("fsdp", "ctx"), None),
            P(("fsdp", "ctx"), None),
            P(("fsdp", "ctx"), None),
            P(("fsdp", "ctx"), None),
            P(("fsdp", "ctx"), None),
        ),
        check_vma=False,
    )
```
